32 devices in a mesh: fsdp: 32 (over z, y, x, core).
Axes of the slice: x: 2, y: 2, z: 4, core: 2. Of those that a mesh axis runs over, the one named last changes fastest.
Arguments:
- tokens: bfloat16 [8192, 2048], P('fsdp'), may hold values from -6 to 6
- cotangent: bfloat16 [8192, 2048], P('fsdp'), may hold values from -6 to 6
- dealt_lengths: int32 [96], replicated, may hold values from 16 to 128, as said below
- deal: int32 [96], replicated, may hold values from 0 to 95, each once
- norm_gain: bfloat16 [2048], P('fsdp'), may hold values from 0.5 to 1.5
- mixer_in: bfloat16 [2048, 6144], P('fsdp'), may hold values from -0.125 to 0.125
- forget_floor: bfloat16 [2048], P('fsdp'), may hold values from 0.099609375 to 0.96875
- group_gain: bfloat16 [2048], P('fsdp'), may hold values from 0.25 to 1.75
- out_proj: bfloat16 [2048, 2048], P('fsdp'), may hold values from -0.125 to 0.125
- ffn_gain: bfloat16 [2048], P('fsdp'), may hold values from 0.5 to 1.5
- gate_up: bfloat16 [2048, 11264], P('fsdp'), may hold values from -0.125 to 0.125
- down_proj: bfloat16 [2048, 5632], P('fsdp'), may hold values from -0.078125 to 0.078125
Outputs:
- layer_out: float32 [8192, 2048], P('fsdp')
- input_grad: float32 [8192, 2048], P('fsdp')
- d_norm_gain: float32 [2048], P('fsdp')
- d_mixer_in: float32 [2048, 6144], P('fsdp')
- d_forget_floor: float32 [2048], P('fsdp')
- d_group_gain: float32 [2048], P('fsdp')
- d_out_proj: float32 [2048, 2048], P('fsdp')
- d_ffn_gain: float32 [2048], P('fsdp')
- d_gate_up: float32 [2048, 11264], P('fsdp')
- d_down_proj: float32 [2048, 5632], P('fsdp')
The draws below stay inside these ranges and needn't reach their ends.
Inputs may be any that keep to these rules, and one draw needn't show every extreme that they name: The 3 entries dealt_lengths[d * 3] onward of each device d sum to 256, and exactly one of them is 128. `deal`: each sequence is dealt once.
All inputs are finite; a program needn't handle non-finite values.
Results may differ from the reference program's by a relative error of at most 0.009.
Values may be sent and summed in bfloat16 or wider, within the bound.
A program may use at most 448 MiB of HBM per device.

```python
from functools import partial
import jax
import jax.numpy as jnp
from jax import lax

D = 2048
HEADS = 16
FF = 5632
HEAD_DIM = 128
TOK_DEV = 256
SEQ_DEV = 3
BLOCK = 32
MAXLEN = 128
MINLEN = 16
NSEQ = 96
TOKENS = 8192
N_FSDP = 32


def draw_dealt_lengths(key, part):
    key = jax.random.fold_in(key, 7)
    cut_key, turn_key = jax.random.split(key)
    device_total = NSEQ // SEQ_DEV
    spare = TOK_DEV - MAXLEN - (SEQ_DEV - 1) * MINLEN
    cut_points = jnp.sort(jax.random.randint(cut_key, (device_total, SEQ_DEV - 2), 0, spare + 1), axis=1).astype(jnp.int32)
    edges = jnp.concatenate([jnp.zeros((device_total, 1), jnp.int32), cut_points, jnp.full((device_total, 1), spare, jnp.int32)], axis=1)
    others = MINLEN + edges[:, 1:] - edges[:, :-1]
    lengths = jnp.concatenate([jnp.full((device_total, 1), MAXLEN, jnp.int32), others], axis=1)
    turns = jax.random.randint(turn_key, (device_total, 1), 0, SEQ_DEV).astype(jnp.int32)
    placing = (jnp.arange(SEQ_DEV, dtype=jnp.int32)[None, :] + turns) % SEQ_DEV
    return jnp.take_along_axis(lengths, placing, axis=1).reshape(-1).astype(jnp.int32)


def level_of(own_key, dims, pieces, smallest, high):
    level, own = 1.0, jax.random.fold_in(own_key, 6)
    for axis_at, shards_of in pieces:
        draws = jnp.exp(jax.random.uniform(jax.random.fold_in(own, axis_at), (shards_of,), jnp.float32, smallest / len(pieces), high / len(pieces)))
        level = level * jnp.repeat(draws, dims[axis_at] // shards_of).reshape([-1 if axis == axis_at else 1 for axis in range(len(dims))])
    return level


def noise(rng, shape, spread, reach, cuts=(), kind=jnp.bfloat16):
    loudness = level_of(rng, shape, cuts, -0.22, 0.18) if cuts else 1.0
    drawn = jax.random.normal(rng, shape, jnp.float32) * spread * loudness
    return jnp.minimum(jnp.maximum(drawn, -reach), reach).astype(kind)


def setup_inputs(seed: int = 0) -> dict:
    arg_keys = jax.random.split(jax.random.key(seed), 13)
    return {
        "tokens": noise(arg_keys[0], (TOKENS, D), 1.0, 6.0, ((0, 32),)),
        "cotangent": noise(arg_keys[1], (TOKENS, D), 1.0, 6.0, ((0, 32),)),
        "dealt_lengths": draw_dealt_lengths(jax.random.fold_in(arg_keys[12], 71), 0),
        "deal": jax.random.permutation(arg_keys[3], NSEQ).astype(jnp.int32),
        "norm_gain": jnp.clip(1.0 + 0.1 * jax.random.normal(arg_keys[4], (D,), jnp.float32), 0.5, 1.5).astype(jnp.bfloat16),
        "mixer_in": noise(arg_keys[5], (D, 3 * D), D ** -0.5, 0.125, ((0, 32),)),
        "forget_floor": jnp.clip(0.099609375 + 0.8691406 * jax.random.uniform(arg_keys[6], (D,), jnp.float32) ** level_of(arg_keys[6], (D,), ((0, 32),), -0.2, 0.2), 0.099609375, 0.96875).astype(jnp.bfloat16),
        "group_gain": jnp.clip(1.0 + 0.15 * jax.random.normal(arg_keys[7], (D,), jnp.float32), 0.25, 1.75).astype(jnp.bfloat16),
        "out_proj": noise(arg_keys[8], (D, D), D ** -0.5, 0.125, ((0, 32),)),
        "ffn_gain": jnp.clip(1.0 + 0.1 * jax.random.normal(arg_keys[9], (D,), jnp.float32), 0.5, 1.5).astype(jnp.bfloat16),
        "gate_up": noise(arg_keys[10], (D, 2 * FF), D ** -0.5, 0.125, ((0, 32),)),
        "down_proj": noise(arg_keys[11], (D, FF), FF ** -0.5, 0.078125, ((0, 32),)),
    }


@jax.custom_vjp
def low(v):
    return lax.optimization_barrier(v.astype(jnp.bfloat16)).astype(jnp.float32)

@jax.custom_vjp
def low_back(v):
    return v

def low_keep(v):
    return (low(v), None)

def low_pass(kept, grad):
    return (grad,)

def back_keep(v):
    return (v, None)

def back_low(kept, grad):
    return (low(grad),)
low.defvjp(low_keep, low_pass)
low_back.defvjp(back_keep, back_low)
norm_eps = 1e-05

def exact_dot(left_side, right_side):
    return jnp.dot(left_side, right_side, precision=lax.Precision.HIGHEST, preferred_element_type=jnp.float32)

def rms_scaled(values):
    return values * lax.rsqrt(lax.optimization_barrier(jnp.mean(values * values, axis=-1, keepdims=True)) + norm_eps)

def run_block(state_now, block_items):

    def advance(state_step, token_items):
        query_row, key_row, value_row, forget_row, reset_row = token_items
        state_step = state_step * (forget_row * (1.0 - reset_row))[:, :, None] + key_row[:, :, None] * value_row[:, None, :]
        return (state_step, jnp.einsum('hc,hce->he', query_row, state_step, precision=lax.Precision.HIGHEST))
    return lax.scan(advance, state_now, block_items)

def recurrence(query, key_gate, value, forget, resets):
    row_count = query.shape[0]
    block_total = row_count // BLOCK
    shaped = (block_total, BLOCK, HEADS, HEAD_DIM)
    block_items = (query.reshape(shaped), key_gate.reshape(shaped), value.reshape(shaped), forget.reshape(shaped), resets.reshape(block_total, BLOCK))
    start_state = jnp.zeros((HEADS, HEAD_DIM, HEAD_DIM), jnp.float32)
    _, outputs = lax.scan(jax.checkpoint(run_block), start_state, block_items)
    return outputs.reshape(row_count, HEADS, HEAD_DIM)

def layer(resets, inputs, norm_gain, mixer_in, forget_floor, group_gain, out_proj, ffn_gain, gate_up, down_proj):
    row_count = inputs.shape[0]
    first_normed = low(rms_scaled(inputs) * norm_gain)
    projected = low_back(exact_dot(first_normed, mixer_in))
    query = low(jax.nn.silu(projected[:, :D]))
    forget = forget_floor + (1.0 - forget_floor) * jax.nn.sigmoid(projected[:, D:2 * D])
    key_gate = low(1.0 - forget)
    value = low(projected[:, 2 * D:])
    head_shape = (row_count, HEADS, HEAD_DIM)
    state_out = recurrence(query.reshape(head_shape), key_gate.reshape(head_shape), value.reshape(head_shape), forget.reshape(head_shape), resets)
    group_normed = rms_scaled(state_out).reshape(row_count, D)
    mixer_input = low(group_normed * group_gain)
    residual = inputs + low_back(exact_dot(mixer_input, out_proj))
    second_normed = low(rms_scaled(residual) * ffn_gain)
    gate_pre = low_back(exact_dot(second_normed, gate_up))
    hidden_act = low(jax.nn.silu(gate_pre[:, :FF]) * gate_pre[:, FF:])
    return residual + exact_dot(hidden_act, down_proj.T)

def reference(tokens, cotangent, dealt_lengths, deal, norm_gain, mixer_in, forget_floor, group_gain, out_proj, ffn_gain, gate_up, down_proj):
    total_rows = tokens.shape[0]
    seq_count = deal.shape[0]
    given_lengths = jnp.zeros((seq_count,), jnp.int32).at[deal].set(dealt_lengths)
    given_starts = (jnp.cumsum(given_lengths) - given_lengths).astype(jnp.int32)
    dealt_starts = (jnp.cumsum(dealt_lengths) - dealt_lengths).astype(jnp.int32)
    row_ids = jnp.arange(total_rows, dtype=jnp.int32)
    start_flags = jnp.zeros((total_rows,), jnp.int32).at[dealt_starts].add(1)
    slot_ids = (jnp.cumsum(start_flags) - 1).astype(jnp.int32)
    source_rows = (given_starts[deal[slot_ids]] + row_ids - dealt_starts[slot_ids]).astype(jnp.int32)
    device_shape = (N_FSDP, TOK_DEV, D)
    dealt_inputs = tokens.astype(jnp.float32)[source_rows].reshape(device_shape)
    dealt_cotangent = cotangent.astype(jnp.float32)[source_rows].reshape(device_shape)
    dealt_resets = start_flags.astype(jnp.float32).reshape(N_FSDP, TOK_DEV)
    params = (norm_gain.astype(jnp.float32), mixer_in.astype(jnp.float32), forget_floor.astype(jnp.float32), group_gain.astype(jnp.float32), out_proj.astype(jnp.float32), ffn_gain.astype(jnp.float32), gate_up.astype(jnp.float32), down_proj.astype(jnp.float32))

    def device_step(grad_sums, step_items):
        step_inputs, step_cotangent, step_resets = step_items
        outputs, pullback = jax.vjp(partial(layer, step_resets), step_inputs, *params)
        pulled = pullback(step_cotangent)
        new_sums = tuple((running + fresh for running, fresh in zip(grad_sums, pulled[1:])))
        return (new_sums, (outputs, pulled[0]))
    zero_sums = tuple((jnp.zeros(weight.shape, jnp.float32) for weight in params))
    grad_sums, (dealt_out, dealt_grad) = lax.scan(device_step, zero_sums, (dealt_inputs, dealt_cotangent, dealt_resets))
    layer_out = jnp.zeros((total_rows, D), jnp.float32).at[source_rows].set(dealt_out.reshape(total_rows, D))
    input_grad = jnp.zeros((total_rows, D), jnp.float32).at[source_rows].set(dealt_grad.reshape(total_rows, D))
    return (layer_out, input_grad, grad_sums[0], grad_sums[1], grad_sums[2], grad_sums[3], grad_sums[4], grad_sums[5], grad_sums[6], grad_sums[7])
```

```python
import functools

import jax
import jax.numpy as jnp
from jax import lax
from jax.experimental import pallas as pl
from jax.experimental.pallas import tpu as pltpu
from jax.sharding import PartitionSpec as P

HEADS = 16
CHUNK = 64
HALF = 32
MAXLEN = 128
GROUP = 8
MESH_ID = pl.DeviceIdType.MESH
VMEM = pl.BlockSpec(memory_space=pltpu.VMEM)
SMEM = pl.BlockSpec(memory_space=pltpu.SMEM)
ANY = pl.BlockSpec(memory_space=pl.ANY)

norm_eps = 1e-05
f32 = jnp.float32
bf16 = jnp.bfloat16


def inverse_rms(values):
    return lax.rsqrt(jnp.mean(values * values, axis=-1, keepdims=True) + norm_eps)


def rms_back(grad_scaled, scaled, inverse):
    return inverse * (grad_scaled - scaled * jnp.mean(grad_scaled * scaled, axis=-1, keepdims=True))


def dot_nt(left, right):
    return lax.dot_general(left, right, (((1,), (1,)), ((), ())), preferred_element_type=f32)


def dot_nn(left, right):
    return lax.dot_general(left, right, (((1,), (0,)), ((), ())), preferred_element_type=f32)


def dot_tn(left, right):
    return lax.dot_general(left, right, (((0,), (0,)), ((), ())), preferred_element_type=f32)


def places():
    me = lax.axis_index("fsdp")
    slot = lax.rem(me, GROUP)
    core = lax.rem(slot, 2)
    step_low = 2 - 4 * lax.rem(slot // 2, 2)
    step_high = 4 - 8 * (slot // 4)
    step_core = 1 - 2 * core
    first_step = (1 - core) * step_low + core * step_high
    second_step = core * step_low + (1 - core) * step_high
    return me, slot, step_core, first_step, second_step


def greet(others):
    barrier = pltpu.get_barrier_semaphore()
    for other in others:
        pl.semaphore_signal(barrier, inc=1, device_id=(other,), device_id_type=MESH_ID)
    pl.semaphore_wait(barrier, len(others))


def remote(source, target, send_sem, recv_sem, device):
    return pltpu.make_async_remote_copy(
        src_ref=source,
        dst_ref=target,
        send_sem=send_sem,
        recv_sem=recv_sem,
        device_id=(device,),
        device_id_type=MESH_ID,
    )


def group_gather_kernel(x_ref, out_ref, send_sem, recv_sem, own_sem):
    me, slot, step_core, first_step, second_step = places()
    first, second, mate = me + first_step, me + second_step, me + step_core
    greet((first, second, mate))

    def block(place):
        return out_ref.at[:, place]

    own = pltpu.make_async_copy(x_ref, block(slot), own_sem)
    sent = []

    def send(source, place, number, target):
        copy = remote(source, block(place), send_sem.at[number], recv_sem.at[number], target)
        copy.start()
        sent.append(copy)

    def arrived(place, number, source):
        remote(
            block(place), block(place), send_sem.at[number], recv_sem.at[number], source
        ).wait_recv()

    from_first, from_second = slot + first_step, slot + second_step
    corner = slot + first_step + second_step
    send(x_ref, slot, 0, first)
    send(x_ref, slot, 1, second)
    send(x_ref, slot, 2, mate)
    own.start()
    arrived(from_first, 0, first)
    send(block(from_first), from_first, 3, second)
    send(block(from_first), from_first, 4, mate)
    arrived(from_second, 1, second)
    send(block(from_second), from_second, 5, mate)
    arrived(corner, 3, second)
    send(block(corner), corner, 6, mate)
    arrived(slot + step_core, 2, mate)
    arrived(slot + step_core + second_step, 4, mate)
    arrived(slot + step_core + first_step, 5, mate)
    arrived(corner + step_core, 6, mate)
    for copy in sent:
        copy.wait_send()
    own.wait()


def group_gather(x, number):
    parts, rows, columns = x.shape
    return pl.pallas_call(
        group_gather_kernel,
        out_shape=jax.ShapeDtypeStruct((parts, GROUP, rows, columns), x.dtype),
        in_specs=[ANY],
        out_specs=ANY,
        scratch_shapes=[
            pltpu.SemaphoreType.DMA((7,)),
            pltpu.SemaphoreType.DMA((7,)),
            pltpu.SemaphoreType.DMA,
        ],
        compiler_params=pltpu.CompilerParams(collective_id=number, has_side_effects=True),
        cost_estimate=pl.CostEstimate(flops=0, transcendentals=0, bytes_accessed=150_000_000),
    )(x)


def group_scatter_kernel(slab_rows, x_ref, out_ref, near, far, going, send_sem, recv_sem):
    me, slot, step_core, first_step, second_step = places()
    first, second, mate = me + first_step, me + second_step, me + step_core
    greet((first, second, mate))
    parts, rows, _ = out_ref.shape
    corner_step = first_step + second_step
    steps = (corner_step, first_step, second_step, corner_step * 0)
    mate_steps = (corner_step, second_step, first_step, corner_step * 0)
    sent = []

    def send(source, target, number, device):
        copy = remote(source, target, send_sem.at[number], recv_sem.at[number], device)
        copy.start()
        sent.append(copy)

    def arrived(ref, number, source):
        remote(ref, ref, send_sem.at[number], recv_sem.at[number], source).wait_recv()

    def add(kind, extra, target):
        place = slot + steps[kind]

        def slab(i, _):
            part = i // (rows // slab_rows)
            at = pl.ds(
                pl.multiple_of(lax.rem(i, rows // slab_rows) * slab_rows, slab_rows), slab_rows
            )
            total = x_ref[part, place, at, :].astype(f32) + near[kind, part, at, :].astype(f32)
            for ref in extra:
                total = total + ref[part, at, :].astype(f32)
            target[part, at, :] = total.astype(target.dtype)
            return 0

        lax.fori_loop(0, parts * (rows // slab_rows), slab, 0)

    for kind in (0, 2, 1, 3):
        send(x_ref.at[:, slot + step_core + mate_steps[kind]], near.at[kind], kind, mate)
    arrived(near.at[0], 0, mate)
    add(0, (), going.at[0])
    send(going.at[0], far.at[0], 4, second)
    arrived(near.at[2], 2, mate)
    add(2, (), going.at[2])
    send(going.at[2], far.at[2], 5, second)
    arrived(near.at[1], 1, mate)
    arrived(far.at[0], 4, second)
    add(1, (far.at[0],), going.at[1])
    send(going.at[1], far.at[1], 6, first)
    arrived(near.at[3], 3, mate)
    arrived(far.at[2], 5, second)
    arrived(far.at[1], 6, first)
    add(3, (far.at[1], far.at[2]), out_ref)
    for copy in sent:
        copy.wait_send()


def group_scatter(x, number, out_type):
    parts, _, rows, columns = x.shape
    return pl.pallas_call(
        functools.partial(group_scatter_kernel, min(32, rows)),
        out_shape=jax.ShapeDtypeStruct((parts, rows, columns), out_type),
        in_specs=[VMEM],
        out_specs=VMEM,
        scratch_shapes=[
            pltpu.VMEM((4, parts, rows, columns), x.dtype),
            pltpu.VMEM((3, parts, rows, columns), x.dtype),
            pltpu.VMEM((3, parts, rows, columns), x.dtype),
            pltpu.SemaphoreType.DMA((7,)),
            pltpu.SemaphoreType.DMA((7,)),
        ],
        compiler_params=pltpu.CompilerParams(
            collective_id=number, has_side_effects=True, vmem_limit_bytes=48 * 2**20
        ),
        cost_estimate=pl.CostEstimate(flops=0, transcendentals=0, bytes_accessed=130_000_000),
    )(x)


def low(values):
    return values.astype(bf16).astype(f32)


def gates(proj_ref, floor_ref, rows, head, heads):
    dim = floor_ref.shape[1] // heads
    wide = heads * dim
    lo = head * dim
    q_pre = proj_ref[rows, lo : lo + dim]
    f_pre = proj_ref[rows, wide + lo : wide + lo + dim]
    value = proj_ref[rows, 2 * wide + lo : 2 * wide + lo + dim].astype(bf16)
    floor = floor_ref[:, lo : lo + dim]
    q_sigmoid = jax.nn.sigmoid(q_pre)
    query = low(q_pre * q_sigmoid)
    f_sigmoid = jax.nn.sigmoid(f_pre)
    forget = floor + (1.0 - floor) * f_sigmoid
    key = low(1.0 - forget)
    row = lax.broadcasted_iota(jnp.int32, (CHUNK, dim), 0)
    in_half = lax.rem(row, HALF)
    product = forget
    step = 1
    while step < HALF:
        product = jnp.where(in_half >= step, product * pltpu.roll(product, step, 0), product)
        step *= 2
    middle = product[HALF - 1 : HALF, :]
    end = product[CHUNK - 1 : CHUNK, :]
    ratio = jnp.where(row < HALF, product / middle, product)
    inverse = 1.0 / ratio
    return {
        "q_pre": q_pre,
        "q_sigmoid": q_sigmoid,
        "f_sigmoid": f_sigmoid,
        "forget": forget,
        "value": value,
        "floor": floor,
        "middle": middle,
        "end": end,
        "ratio": ratio,
        "inverse": inverse,
        "row": row,
        "query_mid": query * ratio,
        "key_mid": key * inverse,
    }


def whole_fade(g, last):
    return g["middle"] * g["end"] * jnp.where(last < 0, 1.0, 0.0)


def tail_keys(g, last):
    return jnp.where(g["row"] >= last, g["key_mid"] * g["end"], 0.0).astype(bf16)


def entry_queries(g, carried):
    return jnp.where(carried, g["query_mid"] * g["middle"], 0.0).astype(bf16)


def next_state(g, last, state):
    return state * whole_fade(g, last) + dot_tn(g["value"], tail_keys(g, last))


def forward_kernel(
    heads, last_ref, proj_ref, start_ref, floor_ref, gain_ref, in_ref, mix_ref, out_ref, enter_ref, state
):
    dim = floor_ref.shape[1] // heads
    state[...] = in_ref[...]

    def step(n, _):
        base = pl.multiple_of(n * CHUNK, CHUNK)
        rows = pl.ds(base, CHUNK)
        starts = start_ref[rows, :] - base
        last = last_ref[n] - base
        column = lax.broadcasted_iota(jnp.int32, (CHUNK, CHUNK), 1)
        line = lax.broadcasted_iota(jnp.int32, (CHUNK, CHUNK), 0)
        within = (column <= line) & (column >= starts)
        carried = starts < 0
        for head in range(heads):
            lo = head * dim
            g = gates(proj_ref, floor_ref, rows, head, heads)
            now = state[head]
            enter_ref[n, head] = now
            scores = dot_nt(g["query_mid"].astype(bf16), g["key_mid"].astype(bf16))
            scores = jnp.where(within, scores, 0.0).astype(bf16)
            out = dot_nn(scores, g["value"]) + dot_nt(entry_queries(g, carried), now.astype(bf16))
            state[head] = next_state(g, last, now)
            out_ref[rows, lo : lo + dim] = out
            mix_ref[rows, lo : lo + dim] = (
                out * inverse_rms(out) * gain_ref[:, lo : lo + dim]
            ).astype(bf16)
        return 0

    lax.fori_loop(0, proj_ref.shape[0] // CHUNK, step, 0)


def last_state_kernel(heads, last_ref, proj_ref, floor_ref, out_ref):
    for head in range(heads):
        state = jnp.zeros(out_ref.shape[1:], f32)
        for n in range(proj_ref.shape[0] // CHUNK):
            g = gates(proj_ref, floor_ref, pl.ds(n * CHUNK, CHUNK), head, heads)
            state = next_state(g, last_ref[n] - n * CHUNK, state)
        out_ref[head] = state


def state_grad(out_ref, dmix_ref, gain_ref, rows, lo, dim):
    out = out_ref[rows, lo : lo + dim]
    inverse = inverse_rms(out)
    scaled = out * inverse
    dmix = dmix_ref[rows, lo : lo + dim].astype(f32)
    grad = rms_back(dmix * gain_ref[:, lo : lo + dim], scaled, inverse)
    return grad, jnp.sum(dmix * scaled, axis=0, keepdims=True)


def backward_kernel(
    heads,
    last_ref,
    proj_ref,
    start_ref,
    floor_ref,
    gain_ref,
    out_ref,
    dmix_ref,
    enter_ref,
    in_ref,
    dproj_ref,
    dfloor_ref,
    dgain_ref,
    later,
):
    dim = floor_ref.shape[1] // heads
    wide = heads * dim
    chunks = proj_ref.shape[0] // CHUNK
    later[...] = in_ref[...]
    dfloor_ref[...] = jnp.zeros_like(dfloor_ref)
    dgain_ref[...] = jnp.zeros_like(dgain_ref)

    def step(i, _):
        n = chunks - 1 - i
        base = pl.multiple_of(n * CHUNK, CHUNK)
        rows = pl.ds(base, CHUNK)
        starts = start_ref[rows, :] - base
        last = last_ref[n] - base
        column = lax.broadcasted_iota(jnp.int32, (CHUNK, CHUNK), 1)
        line = lax.broadcasted_iota(jnp.int32, (CHUNK, CHUNK), 0)
        within = (column <= line) & (column >= starts)
        carried = starts < 0
        for head in range(heads):
            lo = head * dim
            g = gates(proj_ref, floor_ref, rows, head, heads)
            grad, dgain = state_grad(out_ref, dmix_ref, gain_ref, rows, lo, dim)
            grad_hi = grad.astype(bf16)
            grad_lo = (grad - grad_hi.astype(f32)).astype(bf16)
            state = enter_ref[n, head]
            after = later[head]
            after_low = after.astype(bf16)
            query_mid = g["query_mid"].astype(bf16)
            key_mid = g["key_mid"].astype(bf16)
            scores = jnp.where(within, dot_nt(query_mid, key_mid), 0.0).astype(bf16)
            d_scores = dot_nt(grad_hi, g["value"]) + dot_nt(grad_lo, g["value"])
            d_scores = jnp.where(within, d_scores, 0.0).astype(bf16)
            query_in = entry_queries(g, carried)
            key_out = tail_keys(g, last)
            d_query_mid = dot_nn(d_scores, key_mid)
            d_query_in = jnp.where(carried, dot_nn(grad_hi, state.astype(bf16)), 0.0)
            d_key_mid = dot_tn(d_scores, query_mid)
            d_key_out = jnp.where(g["row"] >= last, dot_nn(g["value"], after_low), 0.0)
            d_value = dot_tn(scores, grad_hi) + dot_nt(key_out, after_low)
            d_query = (d_query_mid + d_query_in * g["middle"]) * g["ratio"]
            d_key = (d_key_mid + d_key_out * g["end"]) * g["inverse"]
            tail = d_key_out * key_out.astype(f32)
            term = (
                d_query_mid * query_mid.astype(f32)
                + d_query_in * query_in.astype(f32)
                - d_key_mid * key_mid.astype(f32)
                - tail
            )
            fade = whole_fade(g, last)
            final = jnp.sum(tail, axis=0, keepdims=True) + fade * jnp.sum(
                state * after, axis=0, keepdims=True
            )
            step_rows = 1
            while step_rows < CHUNK:
                term = jnp.where(
                    g["row"] < CHUNK - step_rows,
                    term + pltpu.roll(term, CHUNK - step_rows, 0),
                    term,
                )
                step_rows *= 2
            d_forget = (term + final) / g["forget"] - d_key
            q_sigmoid, f_sigmoid = g["q_sigmoid"], g["f_sigmoid"]
            d_q_pre = d_query * q_sigmoid * (1.0 + g["q_pre"] * (1.0 - q_sigmoid))
            d_floor = d_forget * (1.0 - f_sigmoid)
            d_f_pre = d_floor * (1.0 - g["floor"]) * f_sigmoid
            dproj_ref[rows, lo : lo + dim] = d_q_pre.astype(bf16)
            dproj_ref[rows, wide + lo : wide + lo + dim] = d_f_pre.astype(bf16)
            dproj_ref[rows, 2 * wide + lo : 2 * wide + lo + dim] = d_value.astype(bf16)
            dfloor_ref[:, lo : lo + dim] += jnp.sum(d_floor, axis=0, keepdims=True)
            dgain_ref[:, lo : lo + dim] += dgain
            later[head] = after * fade + dot_tn(grad_hi, query_in)
        return 0

    lax.fori_loop(0, chunks, step, 0)


def first_grad_kernel(
    heads, last_ref, proj_ref, start_ref, floor_ref, gain_ref, out_ref, dmix_ref, grad_ref
):
    dim = floor_ref.shape[1] // heads
    for head in range(heads):
        after = jnp.zeros((dim, dim), f32)
        for n in range(proj_ref.shape[0] // CHUNK - 1, -1, -1):
            rows = pl.ds(n * CHUNK, CHUNK)
            g = gates(proj_ref, floor_ref, rows, head, heads)
            grad, _ = state_grad(out_ref, dmix_ref, gain_ref, rows, head * dim, dim)
            queries = entry_queries(g, start_ref[rows, :] < n * CHUNK)
            after = after * whole_fade(g, last_ref[n] - n * CHUNK) + dot_tn(
                grad.astype(bf16), queries
            )
        grad_ref[head] = after


def local_call(kernel, heads, out_shape, scratch, *operands):
    return pl.pallas_call(
        functools.partial(kernel, heads),
        out_shape=out_shape,
        in_specs=[SMEM] + [VMEM] * (len(operands) - 1),
        out_specs=jax.tree.map(lambda _: VMEM, out_shape),
        scratch_shapes=scratch,
        compiler_params=pltpu.CompilerParams(vmem_limit_bytes=48 * 2**20),
    )(*operands)


def body(
    tokens,
    cotangent,
    dealt_lengths,
    deal,
    norm_gain,
    mixer_in,
    forget_floor,
    group_gain,
    out_proj,
    ffn_gain,
    gate_up,
    down_proj,
):
    row_count, width = tokens.shape
    weight_rows = mixer_in.shape[0]
    device_count = lax.axis_size("fsdp")
    groups = device_count // GROUP
    own_index = lax.axis_index("fsdp")
    slot = lax.rem(own_index, GROUP)
    group = own_index // GROUP
    group_rows = GROUP * row_count
    heads = HEADS // GROUP
    own_width = width // GROUP
    dim = width // HEADS
    ffn_width = down_proj.shape[1]
    own_ffn = ffn_width // GROUP
    planes = [[g * GROUP + s for s in range(GROUP)] for g in range(groups)]
    lines = [[g * GROUP + s for g in range(groups)] for s in range(GROUP)]

    def swap(x):
        return lax.all_to_all(x, "fsdp", 0, 0, axis_index_groups=planes, tiled=True)

    def line_gather(x):
        return lax.all_gather(x, "fsdp", axis=0, axis_index_groups=lines, tiled=True)

    def line_scatter(x):
        return lax.psum_scatter(
            x, "fsdp", scatter_dimension=0, axis_index_groups=lines, tiled=True
        )

    def own_columns(weight, pieces):
        columns = weight.shape[1] // (pieces * GROUP)
        parted = weight.reshape(weight_rows, pieces, GROUP, columns).transpose(2, 0, 1, 3)
        swapped = swap(parted.reshape(GROUP, weight_rows, pieces * columns))
        return line_gather(swapped.reshape(GROUP * weight_rows, pieces * columns))

    def home_rows(grad, pieces):
        columns = grad.shape[1] // pieces
        summed = line_scatter(grad.astype(bf16)).reshape(GROUP, weight_rows, pieces * columns)
        swapped = swap(summed).reshape(GROUP, weight_rows, pieces, columns)
        return swapped.transpose(1, 2, 0, 3).reshape(weight_rows, -1).astype(f32)

    seq_count = deal.shape[0]
    seq_ids = jnp.arange(seq_count, dtype=jnp.int32)
    matches = deal[:, None] == seq_ids[None, :]
    lengths = jnp.sum(jnp.where(matches, dealt_lengths[:, None], 0), axis=0)
    seq_starts = jnp.sum(
        jnp.where(seq_ids[:, None] < seq_ids[None, :], lengths[:, None], 0), axis=0
    )
    group_start = group * group_rows
    rows_here = group_start + jnp.arange(group_rows, dtype=jnp.int32)
    starts = (
        jnp.max(jnp.where(seq_starts[None, :] <= rows_here[:, None], seq_starts[None, :], 0), axis=1)
        - group_start
    )
    start_column = starts[:, None]
    last_starts = starts[CHUNK - 1 :: CHUNK]

    gains = lax.all_gather(
        jnp.stack([norm_gain, forget_floor, group_gain, ffn_gain]), "fsdp", axis=1, tiled=True
    ).astype(f32)
    first_gain = gains[0:1]
    second_gain = gains[3:4]
    own_gains = lax.dynamic_slice_in_dim(gains, slot * own_width, own_width, 1)
    own_floor = own_gains[1:2]
    own_group_gain = own_gains[2:3]

    mixer_weight = own_columns(mixer_in, 3)
    out_lines = lax.all_gather(out_proj, "fsdp", axis=0, axis_index_groups=lines)
    ffn_weight = own_columns(gate_up, 2)
    down_weight = own_columns(down_proj, 1)

    inputs = tokens.astype(f32)
    first_inverse = inverse_rms(inputs)
    first_scaled = inputs * first_inverse
    first_normed = (first_scaled * first_gain).astype(bf16)
    first_all = group_gather(first_normed[None], 0).reshape(group_rows, width)
    tail_projected = dot_nn(first_all[group_rows - MAXLEN :], mixer_weight)
    edge = MAXLEN // CHUNK
    state_type = jax.ShapeDtypeStruct((heads, dim, dim), f32)
    last_state = local_call(
        last_state_kernel,
        heads,
        state_type,
        [],
        last_starts[-edge:] - (group_rows - MAXLEN),
        tail_projected,
        own_floor,
    )
    up_line = [(i, i + GROUP) for i in range(device_count - GROUP)]
    down_line = [(i + GROUP, i) for i in range(device_count - GROUP)]
    entering_state = lax.ppermute(last_state, "fsdp", up_line)
    projected = dot_nn(first_all, mixer_weight)
    chunks = group_rows // CHUNK
    mixed_heads, state_out, entering = local_call(
        forward_kernel,
        heads,
        (
            jax.ShapeDtypeStruct((group_rows, own_width), bf16),
            jax.ShapeDtypeStruct((group_rows, own_width), f32),
            jax.ShapeDtypeStruct((chunks, heads, dim, dim), f32),
        ),
        [pltpu.VMEM((heads, dim, dim), f32)],
        last_starts,
        projected,
        start_column,
        own_floor,
        own_group_gain,
        entering_state,
    )
    mixer_input = (
        swap(mixed_heads.reshape(GROUP, row_count, own_width))
        .transpose(1, 0, 2)
        .reshape(row_count, width)
    )
    out_weight = group_gather(out_lines, 1).reshape(width, width)
    residual = inputs + dot_nn(mixer_input, out_weight)
    second_inverse = inverse_rms(residual)
    second_scaled = residual * second_inverse
    second_normed = (second_scaled * second_gain).astype(bf16)
    second_all = group_gather(second_normed[None], 0).reshape(group_rows, width)
    cot_late, second_all = lax.optimization_barrier((cotangent, second_all))
    cot_all = group_gather(cot_late[None], 0).reshape(group_rows, width)
    gate_pre = dot_nn(second_all, ffn_weight)
    gate_part = gate_pre[:, :own_ffn]
    up_part = gate_pre[:, own_ffn:]
    gate_sigmoid = jax.nn.sigmoid(gate_part)
    gate_act = gate_part * gate_sigmoid
    hidden_act = (gate_act * up_part).astype(bf16)
    d_down_proj = home_rows(dot_tn(cot_all, hidden_act), 1)
    ffn_part = dot_nt(hidden_act, down_weight).astype(bf16)
    d_hidden = dot_nn(cot_all, down_weight)
    d_gate_pre = jnp.concatenate(
        [
            d_hidden * up_part * gate_sigmoid * (1.0 + gate_part * (1.0 - gate_sigmoid)),
            d_hidden * gate_act,
        ],
        axis=1,
    ).astype(bf16)
    d_gate_up = home_rows(dot_tn(second_all, d_gate_pre), 2)
    second_part = dot_nt(d_gate_pre, ffn_weight).astype(bf16)
    d_second = group_scatter(second_part.reshape(1, GROUP, row_count, width), 2, f32)[0]
    d_residual = cotangent.astype(f32) + rms_back(
        d_second * second_gain, second_scaled, second_inverse
    )
    d_mix_out = d_residual.astype(bf16)
    d_mixer_input = dot_nt(d_mix_out, out_weight).astype(bf16)
    d_mixed_heads = swap(
        d_mixer_input.reshape(row_count, GROUP, own_width).transpose(1, 0, 2)
    ).reshape(group_rows, own_width)
    first_grad = local_call(
        first_grad_kernel,
        heads,
        state_type,
        [],
        last_starts[:edge],
        projected[:MAXLEN],
        start_column[:MAXLEN],
        own_floor,
        own_group_gain,
        state_out[:MAXLEN],
        d_mixed_heads[:MAXLEN],
    )
    entering_grad = lax.ppermute(first_grad, "fsdp", down_line)
    d_projected, floor_grad, group_gain_grad = local_call(
        backward_kernel,
        heads,
        (
            jax.ShapeDtypeStruct((group_rows, 3 * own_width), bf16),
            jax.ShapeDtypeStruct((1, own_width), f32),
            jax.ShapeDtypeStruct((1, own_width), f32),
        ),
        [pltpu.VMEM((heads, dim, dim), f32)],
        last_starts,
        projected,
        start_column,
        own_floor,
        own_group_gain,
        state_out,
        d_mixed_heads,
        entering,
        entering_grad,
    )
    d_mixer_in = home_rows(dot_tn(first_all, d_projected), 3)
    first_part = dot_nt(d_projected, mixer_weight).astype(bf16)
    d_first = group_scatter(first_part.reshape(1, GROUP, row_count, width), 2, f32)[0]
    d_dealt = d_residual + rms_back(d_first * first_gain, first_scaled, first_inverse)

    ffn_out = group_scatter(ffn_part.reshape(1, GROUP, row_count, width), 2, f32)[0]
    layer_out = residual + ffn_out
    out_part = dot_tn(mixer_input, d_mix_out).astype(bf16)
    out_sum = group_scatter(out_part.reshape(groups, GROUP, weight_rows, width), 3, bf16)
    d_out_proj = line_scatter(out_sum.reshape(groups * weight_rows, width)).astype(f32)

    spread = jnp.zeros((2, width), f32)
    own_grads = jnp.concatenate([floor_grad, group_gain_grad])
    gain_grads = jnp.concatenate(
        [
            jnp.sum(d_first * first_scaled, axis=0, keepdims=True),
            lax.dynamic_update_slice_in_dim(spread, own_grads, slot * own_width, 1),
            jnp.sum(d_second * second_scaled, axis=0, keepdims=True),
        ]
    )
    gain_sums = lax.psum_scatter(gain_grads, "fsdp", scatter_dimension=1, tiled=True)
    return (
        layer_out,
        d_dealt,
        gain_sums[0],
        d_mixer_in,
        gain_sums[1],
        gain_sums[2],
        d_out_proj,
        gain_sums[3],
        d_gate_up,
        d_down_proj,
    )


def solution(mesh):
    by_rows = P("fsdp", None)
    by_one = P("fsdp")
    return jax.shard_map(
        body,
        mesh=mesh,
        in_specs=(
            by_rows,
            by_rows,
            P(),
            P(),
            by_one,
            by_rows,
            by_one,
            by_one,
            by_rows,
            by_one,
            by_rows,
            by_rows,
        ),
        out_specs=(
            by_rows,
            by_rows,
            by_one,
            by_rows,
            by_one,
            by_one,
            by_rows,
            by_one,
            by_rows,
            by_rows,
        ),
        check_vma=False,
    )
```

```python
import functools

import jax
import jax.numpy as jnp
from jax import lax
from jax.experimental import pallas as pl
from jax.experimental.pallas import tpu as pltpu
from jax.sharding import PartitionSpec as P

HEADS = 16
CHUNK = 64
HALF = 32
MAXLEN = 128
GROUP = 8
MESH_ID = pl.DeviceIdType.MESH
VMEM = pl.BlockSpec(memory_space=pltpu.VMEM)
SMEM = pl.BlockSpec(memory_space=pltpu.SMEM)
ANY = pl.BlockSpec(memory_space=pl.ANY)

norm_eps = 1e-05
f32 = jnp.float32
bf16 = jnp.bfloat16


def inverse_rms(values):
    return lax.rsqrt(jnp.mean(values * values, axis=-1, keepdims=True) + norm_eps)


def rms_back(grad_scaled, scaled, inverse):
    return inverse * (grad_scaled - scaled * jnp.mean(grad_scaled * scaled, axis=-1, keepdims=True))


def dot_nt(left, right):
    return lax.dot_general(left, right, (((1,), (1,)), ((), ())), preferred_element_type=f32)


def dot_nn(left, right):
    return lax.dot_general(left, right, (((1,), (0,)), ((), ())), preferred_element_type=f32)


def dot_tn(left, right):
    return lax.dot_general(left, right, (((0,), (0,)), ((), ())), preferred_element_type=f32)


def cost(micros):
    return pl.CostEstimate(flops=0, transcendentals=0, bytes_accessed=int(micros * 3_690_000))


def places():
    me = lax.axis_index("fsdp")
    slot = lax.rem(me, GROUP)
    core = lax.rem(slot, 2)
    step_low = 2 - 4 * lax.rem(slot // 2, 2)
    step_high = 4 - 8 * (slot // 4)
    step_core = 1 - 2 * core
    first_step = (1 - core) * step_low + core * step_high
    second_step = core * step_low + (1 - core) * step_high
    return me, slot, step_core, first_step, second_step


def greet(others):
    barrier = pltpu.get_barrier_semaphore()
    for other in others:
        pl.semaphore_signal(barrier, inc=1, device_id=(other,), device_id_type=MESH_ID)
    pl.semaphore_wait(barrier, len(others))


def remote(source, target, send_sem, recv_sem, device):
    return pltpu.make_async_remote_copy(
        src_ref=source,
        dst_ref=target,
        send_sem=send_sem,
        recv_sem=recv_sem,
        device_id=(device,),
        device_id_type=MESH_ID,
    )


def plane_steps(step_core, step_low, step_high):
    return [
        (number, (number & 1) * step_core + ((number >> 1) & 1) * step_low + (number >> 2) * step_high)
        for number in range(1, GROUP)
    ]


def exchange_kernel(plan, *refs):
    count = len(plan)
    ins, outs = refs[:count], refs[count : 2 * count]
    send_sem, recv_sem, own_sem = refs[2 * count :]
    me, slot, step_core, first_step, second_step = places()
    core = lax.rem(slot, 2)
    step_low = (1 - core) * first_step + core * second_step
    step_high = core * first_step + (1 - core) * second_step
    others = plane_steps(step_core, step_low, step_high)
    group = me // GROUP
    groups = lax.axis_size("fsdp") // GROUP
    greeted = [me + first_step, me + second_step, me + step_core]
    if set(plan) != {"gather"}:
        greeted = [me + step for _, step in others]
    line = []
    if "all" in plan:
        line = [
            (
                number,
                lax.rem(group + number, groups) * GROUP + slot,
                lax.rem(group + groups - number, groups),
            )
            for number in range(1, groups)
        ]
        greeted = greeted + [target for _, target, _ in line]
    greet(greeted)
    sent = []

    def copy_of(item, source, target, number, device):
        return remote(source, target, send_sem.at[item, number], recv_sem.at[item, number], device)

    def send(item, source, target, number, device):
        copy = copy_of(item, source, target, number, device)
        copy.start()
        sent.append(copy)

    def arrived(item, target, number):
        copy_of(item, target, target, number, me).wait_recv()

    def keep(item, source, target):
        copy = pltpu.make_async_copy(source, target, own_sem.at[item])
        copy.start()
        return copy

    def block(item, place):
        kind, out = plan[item], outs[item]
        if kind == "widen":
            columns = out.shape[1] // GROUP
            return out.at[:, pl.ds(pl.multiple_of(place * columns, columns), columns)]
        if kind == "gather":
            return out.at[:, place]
        return out.at[place]

    def piece(item, place):
        if plan[item] == "narrow":
            columns = ins[item].shape[1] // GROUP
            return ins[item].at[:, pl.ds(pl.multiple_of(place * columns, columns), columns)]
        return ins[item].at[place]

    own = []
    for item, kind in enumerate(plan):
        if kind == "all":
            own.append(keep(item, ins[item], outs[item].at[group, slot]))
            for number, target, _ in line:
                send(item, ins[item], outs[item].at[group, slot], GROUP - 1 + number, target)
        elif kind == "gather":
            for number, step in enumerate((first_step, second_step, step_core)):
                send(item, ins[item], block(item, slot), number, me + step)
            own.append(keep(item, ins[item], block(item, slot)))
    for item, kind in enumerate(plan):
        if kind in ("swap", "widen", "narrow"):
            for number, step in others:
                send(item, piece(item, slot + step), block(item, slot), number - 1, me + step)
            own.append(keep(item, piece(item, slot), block(item, slot)))
    for copy in own:
        copy.wait()
    for item, kind in enumerate(plan):
        if kind == "all":
            for number, _, sender in line:
                arrived(item, outs[item].at[sender, slot], GROUP - 1 + number)
            for number, step in others:
                send(item, outs[item].at[:, slot], outs[item].at[:, slot], number - 1, me + step)
    corner_step = first_step + second_step
    for item, kind in enumerate(plan):
        if kind == "gather":
            for place, number, onward in (
                (slot + first_step, 0, ((3, second_step), (4, step_core))),
                (slot + second_step, 1, ((5, step_core),)),
                (slot + corner_step, 3, ((6, step_core),)),
            ):
                arrived(item, block(item, place), number)
                for then, step in onward:
                    send(item, block(item, place), block(item, place), then, me + step)
    for item, kind in enumerate(plan):
        if kind == "gather":
            for step, number in ((0, 2), (second_step, 4), (first_step, 5), (corner_step, 6)):
                arrived(item, block(item, slot + step_core + step), number)
        elif kind == "all":
            for number, step in others:
                arrived(item, outs[item].at[:, slot + step], number - 1)
        else:
            for number, step in others:
                arrived(item, block(item, slot + step), number - 1)
    for copy in sent:
        copy.wait_send()


def exchange(number, micros, *items):
    groups = lax.axis_size("fsdp") // GROUP
    kinds = [kind for kind, _ in items]
    arrays = [array for _, array in items]
    shapes = []
    for kind, array in items:
        if kind == "gather":
            shape = (array.shape[0], GROUP) + array.shape[1:]
        elif kind == "swap":
            shape = array.shape
        elif kind == "widen":
            shape = (array.shape[1], GROUP * array.shape[2])
        elif kind == "narrow":
            shape = (GROUP, array.shape[0], array.shape[1] // GROUP)
        else:
            shape = (groups, GROUP) + array.shape
        shapes.append(jax.ShapeDtypeStruct(shape, array.dtype))
    numbers = GROUP - 1 + (groups if "all" in kinds else 0)
    return pl.pallas_call(
        functools.partial(exchange_kernel, kinds),
        out_shape=tuple(shapes),
        in_specs=[ANY] * len(items),
        out_specs=tuple([ANY] * len(items)),
        scratch_shapes=[
            pltpu.SemaphoreType.DMA((len(items), numbers)),
            pltpu.SemaphoreType.DMA((len(items), numbers)),
            pltpu.SemaphoreType.DMA((len(items),)),
        ],
        compiler_params=pltpu.CompilerParams(collective_id=number, has_side_effects=True),
        cost_estimate=cost(micros),
    )(*arrays)


def home_kernel(pieces, x_ref, out_ref, got, send_sem, recv_sem, own_sem):
    me, slot, step_core, first_step, second_step = places()
    core = lax.rem(slot, 2)
    step_low = (1 - core) * first_step + core * second_step
    step_high = core * first_step + (1 - core) * second_step
    others = plane_steps(step_core, step_low, step_high)
    greet([me + step for _, step in others])
    sent = []
    for number, step in others:
        copy = remote(
            x_ref.at[slot + step], got.at[slot], send_sem.at[number - 1], recv_sem.at[number - 1], me + step
        )
        copy.start()
        sent.append(copy)
    own = pltpu.make_async_copy(x_ref.at[slot], got.at[slot], own_sem)
    own.start()
    own.wait()
    for number, step in others:
        target = got.at[slot + step]
        remote(target, target, send_sem.at[number - 1], recv_sem.at[number - 1], me + step).wait_recv()
    columns = x_ref.shape[2] // pieces
    for piece in range(pieces):
        for sender in range(GROUP):
            lo = (piece * GROUP + sender) * columns
            out_ref[:, lo : lo + columns] = got[sender, :, piece * columns : (piece + 1) * columns].astype(f32)
    for copy in sent:
        copy.wait_send()


def home(x, pieces, number):
    _, rows, columns = x.shape
    return pl.pallas_call(
        functools.partial(home_kernel, pieces),
        out_shape=jax.ShapeDtypeStruct((rows, GROUP * columns), f32),
        in_specs=[VMEM],
        out_specs=VMEM,
        scratch_shapes=[
            pltpu.VMEM(x.shape, x.dtype),
            pltpu.SemaphoreType.DMA((GROUP - 1,)),
            pltpu.SemaphoreType.DMA((GROUP - 1,)),
            pltpu.SemaphoreType.DMA,
        ],
        compiler_params=pltpu.CompilerParams(
            collective_id=number, has_side_effects=True, vmem_limit_bytes=32 * 2**20
        ),
        cost_estimate=cost(20),
    )(x)


def group_scatter_kernel(slab_rows, x_ref, out_ref, near, far, going, send_sem, recv_sem):
    me, slot, step_core, first_step, second_step = places()
    first, second, mate = me + first_step, me + second_step, me + step_core
    greet((first, second, mate))
    parts, rows, _ = out_ref.shape
    corner_step = first_step + second_step
    steps = (corner_step, first_step, second_step, corner_step * 0)
    mate_steps = (corner_step, second_step, first_step, corner_step * 0)
    sent = []

    def send(source, target, number, device):
        copy = remote(source, target, send_sem.at[number], recv_sem.at[number], device)
        copy.start()
        sent.append(copy)

    def arrived(ref, number, source):
        remote(ref, ref, send_sem.at[number], recv_sem.at[number], source).wait_recv()

    def add(kind, extra, target):
        place = slot + steps[kind]

        def slab(i, _):
            part = i // (rows // slab_rows)
            at = pl.ds(
                pl.multiple_of(lax.rem(i, rows // slab_rows) * slab_rows, slab_rows), slab_rows
            )
            total = x_ref[part, place, at, :].astype(f32) + near[kind, part, at, :].astype(f32)
            for ref in extra:
                total = total + ref[part, at, :].astype(f32)
            target[part, at, :] = total.astype(target.dtype)
            return 0

        lax.fori_loop(0, parts * (rows // slab_rows), slab, 0)

    for kind in (0, 2, 1, 3):
        send(x_ref.at[:, slot + step_core + mate_steps[kind]], near.at[kind], kind, mate)
    arrived(near.at[0], 0, mate)
    add(0, (), going.at[0])
    send(going.at[0], far.at[0], 4, second)
    arrived(near.at[2], 2, mate)
    add(2, (), going.at[2])
    send(going.at[2], far.at[2], 5, second)
    arrived(near.at[1], 1, mate)
    arrived(far.at[0], 4, second)
    add(1, (far.at[0],), going.at[1])
    send(going.at[1], far.at[1], 6, first)
    arrived(near.at[3], 3, mate)
    arrived(far.at[2], 5, second)
    arrived(far.at[1], 6, first)
    add(3, (far.at[1], far.at[2]), out_ref)
    for copy in sent:
        copy.wait_send()


def group_scatter(x, number, out_type):
    parts, _, rows, columns = x.shape
    return pl.pallas_call(
        functools.partial(group_scatter_kernel, min(32, rows)),
        out_shape=jax.ShapeDtypeStruct((parts, rows, columns), out_type),
        in_specs=[VMEM],
        out_specs=VMEM,
        scratch_shapes=[
            pltpu.VMEM((4, parts, rows, columns), x.dtype),
            pltpu.VMEM((3, parts, rows, columns), x.dtype),
            pltpu.VMEM((3, parts, rows, columns), x.dtype),
            pltpu.SemaphoreType.DMA((7,)),
            pltpu.SemaphoreType.DMA((7,)),
        ],
        compiler_params=pltpu.CompilerParams(
            collective_id=number, has_side_effects=True, vmem_limit_bytes=48 * 2**20
        ),
        cost_estimate=cost(43),
    )(x)


def plane_permutes(device_count):
    first, second, mate = [], [], []
    for i in range(device_count):
        low_bit, high_bit = (2, 4) if i % 2 == 0 else (4, 2)
        first.append((i, i ^ low_bit))
        second.append((i, i ^ high_bit))
        mate.append((i, i ^ 1))
    return first, second, mate


def after(values, *earlier):
    return lax.optimization_barrier((values, earlier))[0]


def meet(*values):
    return lax.optimization_barrier(values)


def assemble_kernel(*refs):
    blocks, out_ref = refs[:GROUP], refs[GROUP]
    _, slot, step_core, first_step, second_step = places()
    corner_step = first_step + second_step
    here = (0, first_step, second_step, corner_step)
    there = (step_core, step_core + second_step, step_core + first_step, step_core + corner_step)
    for number, step in enumerate(here + there):
        out_ref[:, slot + step] = blocks[number][...]


def assemble(x, from_first, from_second, from_corner, mates):
    parts, rows, columns = x.shape
    return pl.pallas_call(
        assemble_kernel,
        out_shape=jax.ShapeDtypeStruct((parts, GROUP, rows, columns), x.dtype),
        in_specs=[VMEM] * GROUP,
        out_specs=VMEM,
        compiler_params=pltpu.CompilerParams(vmem_limit_bytes=32 * 2**20),
        cost_estimate=cost(8),
    )(x, from_first, from_second, from_corner, *mates)


class SlowScatter:
    def __init__(self, x, moves, device_count):
        self.x = x
        self.slot, self.step_core, self.first_step, self.second_step = moves
        self.first, self.second, self.mate = plane_permutes(device_count)

    def block(self, step):
        return lax.dynamic_index_in_dim(self.x, self.slot + step, 1, keepdims=False)

    def pair(self, near, kind, step):
        return self.block(step).astype(f32) + near[kind].astype(f32)

    def to_mate(self):
        steps = (self.first_step + self.second_step, self.second_step, self.first_step, 0)
        away = jnp.stack([self.block(self.step_core + step) for step in steps])
        return lax.ppermute(away, "fsdp", self.mate)

    def to_second(self, near):
        corner = self.pair(near, 0, self.first_step + self.second_step)
        onward = jnp.stack([corner, self.pair(near, 2, self.second_step)]).astype(bf16)
        return lax.ppermute(onward, "fsdp", self.second)

    def to_first(self, near, far):
        both = self.pair(near, 1, self.first_step) + far[0].astype(f32)
        return lax.ppermute(both.astype(bf16), "fsdp", self.first)

    def total(self, near, far, last):
        return self.pair(near, 3, 0) + far[1].astype(f32) + last.astype(f32)


def low(values):
    return values.astype(bf16).astype(f32)


def gates(proj_ref, floor_ref, rows, head, heads):
    dim = floor_ref.shape[1] // heads
    wide = heads * dim
    lo = head * dim
    q_pre = proj_ref[rows, lo : lo + dim]
    f_pre = proj_ref[rows, wide + lo : wide + lo + dim]
    value = proj_ref[rows, 2 * wide + lo : 2 * wide + lo + dim].astype(bf16)
    floor = floor_ref[:, lo : lo + dim]
    q_sigmoid = jax.nn.sigmoid(q_pre)
    query = low(q_pre * q_sigmoid)
    f_sigmoid = jax.nn.sigmoid(f_pre)
    forget = floor + (1.0 - floor) * f_sigmoid
    key = low(1.0 - forget)
    row = lax.broadcasted_iota(jnp.int32, (CHUNK, dim), 0)
    in_half = lax.rem(row, HALF)
    product = forget
    step = 1
    while step < HALF:
        product = jnp.where(in_half >= step, product * pltpu.roll(product, step, 0), product)
        step *= 2
    middle = product[HALF - 1 : HALF, :]
    end = product[CHUNK - 1 : CHUNK, :]
    ratio = jnp.where(row < HALF, product / middle, product)
    inverse = 1.0 / ratio
    return {
        "q_pre": q_pre,
        "q_sigmoid": q_sigmoid,
        "f_sigmoid": f_sigmoid,
        "forget": forget,
        "value": value,
        "floor": floor,
        "middle": middle,
        "end": end,
        "ratio": ratio,
        "inverse": inverse,
        "row": row,
        "query_mid": query * ratio,
        "key_mid": key * inverse,
    }


def whole_fade(g, last):
    return g["middle"] * g["end"] * jnp.where(last < 0, 1.0, 0.0)


def tail_keys(g, last):
    return jnp.where(g["row"] >= last, g["key_mid"] * g["end"], 0.0).astype(bf16)


def entry_queries(g, carried):
    return jnp.where(carried, g["query_mid"] * g["middle"], 0.0).astype(bf16)


def next_state(g, last, state):
    return state * whole_fade(g, last) + dot_tn(g["value"], tail_keys(g, last))


def forward_kernel(
    heads, last_ref, proj_ref, start_ref, floor_ref, gain_ref, in_ref, mix_ref, out_ref, enter_ref, state
):
    dim = floor_ref.shape[1] // heads
    state[...] = in_ref[...]

    def step(n, _):
        base = pl.multiple_of(n * CHUNK, CHUNK)
        rows = pl.ds(base, CHUNK)
        starts = start_ref[rows, :] - base
        last = last_ref[n] - base
        column = lax.broadcasted_iota(jnp.int32, (CHUNK, CHUNK), 1)
        line = lax.broadcasted_iota(jnp.int32, (CHUNK, CHUNK), 0)
        within = (column <= line) & (column >= starts)
        carried = starts < 0
        for head in range(heads):
            lo = head * dim
            g = gates(proj_ref, floor_ref, rows, head, heads)
            now = state[head]
            enter_ref[n, head] = now
            scores = dot_nt(g["query_mid"].astype(bf16), g["key_mid"].astype(bf16))
            scores = jnp.where(within, scores, 0.0).astype(bf16)
            out = dot_nn(scores, g["value"]) + dot_nt(entry_queries(g, carried), now.astype(bf16))
            state[head] = next_state(g, last, now)
            out_ref[rows, lo : lo + dim] = out
            mix_ref[rows, lo : lo + dim] = (
                out * inverse_rms(out) * gain_ref[:, lo : lo + dim]
            ).astype(bf16)
        return 0

    lax.fori_loop(0, proj_ref.shape[0] // CHUNK, step, 0)


def last_state_kernel(heads, last_ref, proj_ref, floor_ref, out_ref):
    for head in range(heads):
        state = jnp.zeros(out_ref.shape[1:], f32)
        for n in range(proj_ref.shape[0] // CHUNK):
            g = gates(proj_ref, floor_ref, pl.ds(n * CHUNK, CHUNK), head, heads)
            state = next_state(g, last_ref[n] - n * CHUNK, state)
        out_ref[head] = state


def state_grad(out_ref, dmix_ref, gain_ref, rows, lo, dim):
    out = out_ref[rows, lo : lo + dim]
    inverse = inverse_rms(out)
    scaled = out * inverse
    dmix = dmix_ref[rows, lo : lo + dim].astype(f32)
    return rms_back(dmix * gain_ref[:, lo : lo + dim], scaled, inverse)


def backward_kernel(
    heads,
    last_ref,
    proj_ref,
    start_ref,
    floor_ref,
    gain_ref,
    out_ref,
    dmix_ref,
    enter_ref,
    in_ref,
    dproj_ref,
    dfloor_ref,
    later,
):
    dim = floor_ref.shape[1] // heads
    wide = heads * dim
    chunks = proj_ref.shape[0] // CHUNK
    later[...] = in_ref[...]
    dfloor_ref[...] = jnp.zeros_like(dfloor_ref)

    def step(i, _):
        n = chunks - 1 - i
        base = pl.multiple_of(n * CHUNK, CHUNK)
        rows = pl.ds(base, CHUNK)
        starts = start_ref[rows, :] - base
        last = last_ref[n] - base
        column = lax.broadcasted_iota(jnp.int32, (CHUNK, CHUNK), 1)
        line = lax.broadcasted_iota(jnp.int32, (CHUNK, CHUNK), 0)
        within = (column <= line) & (column >= starts)
        carried = starts < 0
        for head in range(heads):
            lo = head * dim
            g = gates(proj_ref, floor_ref, rows, head, heads)
            grad = state_grad(out_ref, dmix_ref, gain_ref, rows, lo, dim)
            grad_hi = grad.astype(bf16)
            grad_lo = (grad - grad_hi.astype(f32)).astype(bf16)
            state = enter_ref[n, head]
            after = later[head]
            after_low = after.astype(bf16)
            query_mid = g["query_mid"].astype(bf16)
            key_mid = g["key_mid"].astype(bf16)
            scores = jnp.where(within, dot_nt(query_mid, key_mid), 0.0).astype(bf16)
            d_scores = dot_nt(grad_hi, g["value"]) + dot_nt(grad_lo, g["value"])
            d_scores = jnp.where(within, d_scores, 0.0).astype(bf16)
            query_in = entry_queries(g, carried)
            key_out = tail_keys(g, last)
            d_query_mid = dot_nn(d_scores, key_mid)
            d_query_in = jnp.where(carried, dot_nn(grad_hi, state.astype(bf16)), 0.0)
            d_key_mid = dot_tn(d_scores, query_mid)
            d_key_out = jnp.where(g["row"] >= last, dot_nn(g["value"], after_low), 0.0)
            d_value = dot_tn(scores, grad_hi) + dot_nt(key_out, after_low)
            d_query = (d_query_mid + d_query_in * g["middle"]) * g["ratio"]
            d_key = (d_key_mid + d_key_out * g["end"]) * g["inverse"]
            tail = d_key_out * key_out.astype(f32)
            term = (
                d_query_mid * query_mid.astype(f32)
                + d_query_in * query_in.astype(f32)
                - d_key_mid * key_mid.astype(f32)
                - tail
            )
            fade = whole_fade(g, last)
            final = jnp.sum(tail, axis=0, keepdims=True) + fade * jnp.sum(
                state * after, axis=0, keepdims=True
            )
            step_rows = 1
            while step_rows < CHUNK:
                term = jnp.where(
                    g["row"] < CHUNK - step_rows,
                    term + pltpu.roll(term, CHUNK - step_rows, 0),
                    term,
                )
                step_rows *= 2
            d_forget = (term + final) / g["forget"] - d_key
            q_sigmoid, f_sigmoid = g["q_sigmoid"], g["f_sigmoid"]
            d_q_pre = d_query * q_sigmoid * (1.0 + g["q_pre"] * (1.0 - q_sigmoid))
            d_floor = d_forget * (1.0 - f_sigmoid)
            d_f_pre = d_floor * (1.0 - g["floor"]) * f_sigmoid
            dproj_ref[rows, lo : lo + dim] = d_q_pre.astype(bf16)
            dproj_ref[rows, wide + lo : wide + lo + dim] = d_f_pre.astype(bf16)
            dproj_ref[rows, 2 * wide + lo : 2 * wide + lo + dim] = d_value.astype(bf16)
            dfloor_ref[:, lo : lo + dim] += jnp.sum(d_floor, axis=0, keepdims=True)
            later[head] = after * fade + dot_tn(grad_hi, query_in)
        return 0

    lax.fori_loop(0, chunks, step, 0)


def first_grad_kernel(
    heads, last_ref, proj_ref, start_ref, floor_ref, gain_ref, out_ref, dmix_ref, grad_ref
):
    dim = floor_ref.shape[1] // heads
    for head in range(heads):
        after = jnp.zeros((dim, dim), f32)
        for n in range(proj_ref.shape[0] // CHUNK - 1, -1, -1):
            rows = pl.ds(n * CHUNK, CHUNK)
            g = gates(proj_ref, floor_ref, rows, head, heads)
            grad = state_grad(out_ref, dmix_ref, gain_ref, rows, head * dim, dim)
            queries = entry_queries(g, start_ref[rows, :] < n * CHUNK)
            after = after * whole_fade(g, last_ref[n] - n * CHUNK) + dot_tn(
                grad.astype(bf16), queries
            )
        grad_ref[head] = after


def local_call(kernel, heads, micros, out_shape, scratch, *operands):
    return pl.pallas_call(
        functools.partial(kernel, heads),
        out_shape=out_shape,
        in_specs=[SMEM] + [VMEM] * (len(operands) - 1),
        out_specs=jax.tree.map(lambda _: VMEM, out_shape),
        scratch_shapes=scratch,
        compiler_params=pltpu.CompilerParams(vmem_limit_bytes=48 * 2**20),
        cost_estimate=cost(micros),
    )(*operands)


def body(
    tokens,
    cotangent,
    dealt_lengths,
    deal,
    norm_gain,
    mixer_in,
    forget_floor,
    group_gain,
    out_proj,
    ffn_gain,
    gate_up,
    down_proj,
):
    row_count, width = tokens.shape
    weight_rows = mixer_in.shape[0]
    device_count = lax.axis_size("fsdp")
    groups = device_count // GROUP
    own_index = lax.axis_index("fsdp")
    slot = lax.rem(own_index, GROUP)
    group = own_index // GROUP
    group_rows = GROUP * row_count
    heads = HEADS // GROUP
    own_width = width // GROUP
    dim = width // HEADS
    ffn_width = down_proj.shape[1]
    own_ffn = ffn_width // GROUP
    planes = [[g * GROUP + s for s in range(GROUP)] for g in range(groups)]
    lines = [[g * GROUP + s for g in range(groups)] for s in range(GROUP)]

    def line_gather(x):
        return lax.all_gather(x, "fsdp", axis=0, axis_index_groups=lines, tiled=True)

    def line_scatter(x):
        return lax.psum_scatter(
            x, "fsdp", scatter_dimension=0, axis_index_groups=lines, tiled=True
        )

    def by_owner(weight, pieces):
        columns = weight.shape[1] // (pieces * GROUP)
        parted = weight.reshape(weight_rows, pieces, GROUP, columns).transpose(2, 0, 1, 3)
        return parted.reshape(GROUP, weight_rows, pieces * columns)

    def whole_rows(x):
        return line_gather(x.reshape(GROUP * weight_rows, -1))

    def home_rows(summed, pieces, number):
        return home(summed.reshape(GROUP, weight_rows, -1), pieces, number)

    low_step = 2 - 4 * (slot // 2 % 2)
    high_step = 4 - 8 * (slot // 4)
    odd = slot % 2
    moves = (
        slot,
        1 - 2 * odd,
        jnp.where(odd == 0, low_step, high_step),
        jnp.where(odd == 0, high_step, low_step),
    )

    seq_count = deal.shape[0]
    seq_ids = jnp.arange(seq_count, dtype=jnp.int32)
    matches = deal[:, None] == seq_ids[None, :]
    lengths = jnp.sum(jnp.where(matches, dealt_lengths[:, None], 0), axis=0)
    seq_starts = jnp.sum(
        jnp.where(seq_ids[:, None] < seq_ids[None, :], lengths[:, None], 0), axis=0
    )
    group_start = group * group_rows
    rows_here = group_start + jnp.arange(group_rows, dtype=jnp.int32)
    starts = (
        jnp.max(jnp.where(seq_starts[None, :] <= rows_here[:, None], seq_starts[None, :], 0), axis=1)
        - group_start
    )
    start_column = starts[:, None]
    last_starts = starts[CHUNK - 1 :: CHUNK]

    out_lines = lax.all_gather(out_proj, "fsdp", axis=0, axis_index_groups=lines)
    gain_block = jnp.zeros((16, 128), bf16)
    for number, gain in enumerate((norm_gain, forget_floor, group_gain, ffn_gain)):
        gain_block = gain_block.at[number, :weight_rows].set(gain)
    gain_blocks, mixer_swapped = exchange(
        0, 15, ("all", gain_block), ("swap", by_owner(mixer_in, 3))
    )
    mixer_weight = whole_rows(mixer_swapped)
    gains = (
        gain_blocks[:, :, :4, :weight_rows].transpose(2, 0, 1, 3).reshape(4, width).astype(f32)
    )
    first_gain = gains[0:1]
    second_gain = gains[3:4]
    own_gains = lax.dynamic_slice_in_dim(gains, slot * own_width, own_width, 1)
    own_floor = own_gains[1:2]
    own_group_gain = own_gains[2:3]

    inputs = tokens.astype(f32)
    first_inverse = inverse_rms(inputs)
    first_scaled = inputs * first_inverse
    first_normed = (first_scaled * first_gain).astype(bf16)
    first_all, ffn_swapped, down_swapped = exchange(
        1,
        65,
        ("gather", first_normed[None]),
        ("swap", by_owner(gate_up, 2)),
        ("swap", by_owner(down_proj, 1)),
    )
    first_all = first_all.reshape(group_rows, width)
    ffn_weight = whole_rows(ffn_swapped)
    first, second, mate = plane_permutes(device_count)
    out_own = after(out_lines, first_all)
    from_first = lax.ppermute(out_own, "fsdp", first)
    from_second = lax.ppermute(out_own, "fsdp", second)
    tail_projected = dot_nn(first_all[group_rows - MAXLEN :], mixer_weight)
    edge = MAXLEN // CHUNK
    state_type = jax.ShapeDtypeStruct((heads, dim, dim), f32)
    last_state = local_call(
        last_state_kernel,
        heads,
        3,
        state_type,
        [],
        last_starts[-edge:] - (group_rows - MAXLEN),
        tail_projected,
        own_floor,
    )
    up_line = [(i, i + GROUP) for i in range(device_count - GROUP)]
    down_line = [(i + GROUP, i) for i in range(device_count - GROUP)]
    entering_state = lax.ppermute(last_state, "fsdp", up_line)
    projected = dot_nn(after(first_all, last_state), mixer_weight)
    projected, entering_state = meet(projected, entering_state)
    chunks = group_rows // CHUNK
    mixed_heads, state_out, entering = local_call(
        forward_kernel,
        heads,
        18,
        (
            jax.ShapeDtypeStruct((group_rows, own_width), bf16),
            jax.ShapeDtypeStruct((group_rows, own_width), f32),
            jax.ShapeDtypeStruct((chunks, heads, dim, dim), f32),
        ),
        [pltpu.VMEM((heads, dim, dim), f32)],
        last_starts,
        projected,
        start_column,
        own_floor,
        own_group_gain,
        entering_state,
    )
    mixed_heads, from_first, from_second = meet(mixed_heads, from_first, from_second)
    from_corner = lax.ppermute(from_first, "fsdp", second)
    mates = [lax.ppermute(block, "fsdp", mate) for block in (out_own, from_first, from_second)]
    [mixer_input] = exchange(
        3, 15, ("widen", mixed_heads.reshape(GROUP, row_count, own_width))
    )
    mixer_input, from_corner, mates = meet(mixer_input, from_corner, mates)
    mates = mates + [lax.ppermute(from_corner, "fsdp", mate)]
    out_weight = assemble(out_own, from_first, from_second, from_corner, mates).reshape(width, width)
    down_weight = whole_rows(after(down_swapped, mixed_heads))
    residual = inputs + dot_nn(mixer_input, out_weight)
    second_inverse = inverse_rms(residual)
    second_scaled = residual * second_inverse
    second_normed = (second_scaled * second_gain).astype(bf16)
    [second_all] = exchange(2, 43, ("gather", second_normed[None]))
    second_all = second_all.reshape(group_rows, width)
    [cot_all] = exchange(2, 43, ("gather", after(cotangent, second_all)[None]))
    cot_all = cot_all.reshape(group_rows, width)
    gate_pre = dot_nn(second_all, ffn_weight)
    gate_part = gate_pre[:, :own_ffn]
    up_part = gate_pre[:, own_ffn:]
    gate_sigmoid = jax.nn.sigmoid(gate_part)
    gate_act = gate_part * gate_sigmoid
    hidden_act = (gate_act * up_part).astype(bf16)
    down_summed = line_scatter(dot_tn(cot_all, hidden_act).astype(bf16))
    d_hidden = dot_nn(cot_all, down_weight)
    d_gate_pre = jnp.concatenate(
        [
            d_hidden * up_part * gate_sigmoid * (1.0 + gate_part * (1.0 - gate_sigmoid)),
            d_hidden * gate_act,
        ],
        axis=1,
    ).astype(bf16)
    ffn_part = dot_nt(hidden_act, after(down_weight, d_gate_pre)).astype(bf16)
    ffn_sum = SlowScatter(ffn_part.reshape(1, GROUP, row_count, width), moves, device_count)
    ffn_near = ffn_sum.to_mate()
    ffn_grad = dot_tn(after(second_all, ffn_part), d_gate_pre).astype(bf16)
    ffn_grad, ffn_near = meet(ffn_grad, ffn_near)
    ffn_summed = line_scatter(ffn_grad)
    ffn_far = ffn_sum.to_second(ffn_near)
    second_part = dot_nt(d_gate_pre, after(ffn_weight, ffn_grad)).astype(bf16)
    d_second = group_scatter(second_part.reshape(1, GROUP, row_count, width), 4, f32)[0]
    d_second, ffn_far, down_summed = meet(d_second, ffn_far, down_summed)
    ffn_last = ffn_sum.to_first(ffn_near, ffn_far)
    d_residual = cotangent.astype(f32) + rms_back(
        d_second * second_gain, second_scaled, second_inverse
    )
    d_mix_out = d_residual.astype(bf16)
    out_part = dot_tn(mixer_input, d_mix_out).astype(bf16)
    out_sum = SlowScatter(
        out_part.reshape(groups, GROUP, weight_rows, width), moves, device_count
    )
    out_near = out_sum.to_mate()
    d_mixer_input = dot_nt(after(d_mix_out, out_part), out_weight).astype(bf16)
    [d_mixed_heads] = exchange(5, 15, ("narrow", d_mixer_input))
    d_mixed_heads, out_near, ffn_last = meet(
        d_mixed_heads.reshape(group_rows, own_width), out_near, ffn_last
    )
    layer_out = residual + ffn_sum.total(ffn_near, ffn_far, ffn_last)[0]
    out_far = out_sum.to_second(out_near)
    first_grad = local_call(
        first_grad_kernel,
        heads,
        3,
        state_type,
        [],
        last_starts[:edge],
        projected[:MAXLEN],
        start_column[:MAXLEN],
        own_floor,
        own_group_gain,
        state_out[:MAXLEN],
        d_mixed_heads[:MAXLEN],
    )
    entering_grad = lax.ppermute(first_grad, "fsdp", down_line)
    d_projected, floor_grad = local_call(
        backward_kernel,
        heads,
        30,
        (
            jax.ShapeDtypeStruct((group_rows, 3 * own_width), bf16),
            jax.ShapeDtypeStruct((1, own_width), f32),
        ),
        [pltpu.VMEM((heads, dim, dim), f32)],
        last_starts,
        projected,
        start_column,
        own_floor,
        own_group_gain,
        state_out,
        d_mixed_heads,
        entering,
        entering_grad,
    )
    d_projected, out_far = meet(d_projected, out_far)
    out_last = out_sum.to_first(out_near, out_far)
    mixer_grad = dot_tn(first_all, d_projected).astype(bf16)
    mixer_summed = line_scatter(after(mixer_grad, ffn_summed))
    first_part = dot_nt(d_projected, after(mixer_weight, mixer_grad)).astype(bf16)
    first_part, out_last = meet(first_part, out_last)
    out_total = out_sum.total(out_near, out_far, out_last).astype(bf16)
    d_first = group_scatter(first_part.reshape(1, GROUP, row_count, width), 4, f32)[0]
    d_first, mixer_summed = meet(d_first, mixer_summed)
    d_out_proj = line_scatter(
        after(out_total, mixer_summed).reshape(groups * weight_rows, width)
    ).astype(f32)
    d_down_proj = home_rows(after(down_summed, d_first), 1, 6)
    d_gate_up = home_rows(after(ffn_summed, d_down_proj), 2, 7)
    d_mixer_in = home_rows(after(mixer_summed, d_gate_up), 3, 8)
    d_dealt = d_residual + rms_back(d_first * first_gain, first_scaled, first_inverse)

    def gain_grad(weight, weight_grad, gain):
        return jnp.sum(weight.astype(f32) * weight_grad, axis=1) / gain.astype(f32)

    floor_block = jnp.zeros((8, 128), f32).at[: own_width // 128].set(
        floor_grad.reshape(own_width // 128, 128)
    )
    [floor_blocks] = exchange(9, 8, ("all", after(floor_block, d_gate_up)))
    floor_sums = jnp.sum(floor_blocks[:, :, : own_width // 128], axis=0).reshape(width)
    d_forget_floor = lax.dynamic_slice_in_dim(floor_sums, own_index * weight_rows, weight_rows, 0)
    return (
        layer_out,
        d_dealt,
        gain_grad(mixer_in, d_mixer_in, norm_gain),
        d_mixer_in,
        d_forget_floor,
        gain_grad(out_proj, d_out_proj, group_gain),
        d_out_proj,
        gain_grad(gate_up, d_gate_up, ffn_gain),
        d_gate_up,
        d_down_proj,
    )


def solution(mesh):
    by_rows = P("fsdp", None)
    by_one = P("fsdp")
    return jax.shard_map(
        body,
        mesh=mesh,
        in_specs=(
            by_rows,
            by_rows,
            P(),
            P(),
            by_one,
            by_rows,
            by_one,
            by_one,
            by_rows,
            by_one,
            by_rows,
            by_rows,
        ),
        out_specs=(
            by_rows,
            by_rows,
            by_one,
            by_rows,
            by_one,
            by_one,
            by_rows,
            by_one,
            by_rows,
            by_rows,
        ),
        check_vma=False,
    )
```

```python
import functools

import jax
import jax.numpy as jnp
from jax import lax
from jax.experimental import pallas as pl
from jax.experimental.pallas import tpu as pltpu
from jax.sharding import PartitionSpec as P

HEADS = 16
CHUNK = 64
HALF = 32
MAXLEN = 128
GROUP = 8
MESH_ID = pl.DeviceIdType.MESH
VMEM = pl.BlockSpec(memory_space=pltpu.VMEM)
SMEM = pl.BlockSpec(memory_space=pltpu.SMEM)
ANY = pl.BlockSpec(memory_space=pl.ANY)

norm_eps = 1e-05
f32 = jnp.float32
bf16 = jnp.bfloat16


def inverse_rms(values):
    return lax.rsqrt(jnp.mean(values * values, axis=-1, keepdims=True) + norm_eps)


def rms_back(grad_scaled, scaled, inverse):
    return inverse * (grad_scaled - scaled * jnp.mean(grad_scaled * scaled, axis=-1, keepdims=True))


def dot_nt(left, right):
    return lax.dot_general(left, right, (((1,), (1,)), ((), ())), preferred_element_type=f32)


def dot_nn(left, right):
    return lax.dot_general(left, right, (((1,), (0,)), ((), ())), preferred_element_type=f32)


def dot_tn(left, right):
    return lax.dot_general(left, right, (((0,), (0,)), ((), ())), preferred_element_type=f32)


def cost(micros):
    return pl.CostEstimate(flops=0, transcendentals=0, bytes_accessed=int(micros * 3_690_000))


def places():
    me = lax.axis_index("fsdp")
    slot = lax.rem(me, GROUP)
    core = lax.rem(slot, 2)
    step_low = 2 - 4 * lax.rem(slot // 2, 2)
    step_high = 4 - 8 * (slot // 4)
    step_core = 1 - 2 * core
    first_step = (1 - core) * step_low + core * step_high
    second_step = core * step_low + (1 - core) * step_high
    return me, slot, step_core, first_step, second_step


def greet(others):
    barrier = pltpu.get_barrier_semaphore()
    for other in others:
        pl.semaphore_signal(barrier, inc=1, device_id=(other,), device_id_type=MESH_ID)
    pl.semaphore_wait(barrier, len(others))


def remote(source, target, send_sem, recv_sem, device):
    return pltpu.make_async_remote_copy(
        src_ref=source,
        dst_ref=target,
        send_sem=send_sem,
        recv_sem=recv_sem,
        device_id=(device,),
        device_id_type=MESH_ID,
    )


def plane_steps(step_core, step_low, step_high):
    return [
        (number, (number & 1) * step_core + ((number >> 1) & 1) * step_low + (number >> 2) * step_high)
        for number in range(1, GROUP)
    ]


def exchange_kernel(plan, *refs):
    count = len(plan)
    ins, outs = refs[:count], refs[count : 2 * count]
    send_sem, recv_sem, own_sem = refs[2 * count :]
    me, slot, step_core, first_step, second_step = places()
    core = lax.rem(slot, 2)
    step_low = (1 - core) * first_step + core * second_step
    step_high = core * first_step + (1 - core) * second_step
    others = plane_steps(step_core, step_low, step_high)
    group = me // GROUP
    groups = lax.axis_size("fsdp") // GROUP
    greeted = [me + first_step, me + second_step, me + step_core]
    if set(plan) != {"gather"}:
        greeted = [me + step for _, step in others]
    line = []
    if "all" in plan:
        line = [
            (
                number,
                lax.rem(group + number, groups) * GROUP + slot,
                lax.rem(group + groups - number, groups),
            )
            for number in range(1, groups)
        ]
        greeted = greeted + [target for _, target, _ in line]
    greet(greeted)
    sent = []

    def copy_of(item, source, target, number, device):
        return remote(source, target, send_sem.at[item, number], recv_sem.at[item, number], device)

    def send(item, source, target, number, device):
        copy = copy_of(item, source, target, number, device)
        copy.start()
        sent.append(copy)

    def arrived(item, target, number):
        copy_of(item, target, target, number, me).wait_recv()

    def keep(item, source, target):
        copy = pltpu.make_async_copy(source, target, own_sem.at[item])
        copy.start()
        return copy

    def block(item, place):
        kind, out = plan[item], outs[item]
        if kind == "widen":
            columns = out.shape[1] // GROUP
            return out.at[:, pl.ds(pl.multiple_of(place * columns, columns), columns)]
        if kind == "gather":
            return out.at[:, place]
        return out.at[place]

    def piece(item, place):
        if plan[item] == "narrow":
            columns = ins[item].shape[1] // GROUP
            return ins[item].at[:, pl.ds(pl.multiple_of(place * columns, columns), columns)]
        return ins[item].at[place]

    own = []
    for item, kind in enumerate(plan):
        if kind == "all":
            keep(item, ins[item], outs[item].at[group, slot]).wait()
            for number, target, _ in line:
                send(item, ins[item], outs[item].at[group, slot], GROUP - 1 + number, target)
        elif kind == "gather":
            for number, step in enumerate((first_step, second_step, step_core)):
                send(item, ins[item], block(item, slot), number, me + step)
            own.append(keep(item, ins[item], block(item, slot)))
    for item, kind in enumerate(plan):
        if kind in ("swap", "widen", "narrow"):
            for number, step in others:
                send(item, piece(item, slot + step), block(item, slot), number - 1, me + step)
            own.append(keep(item, piece(item, slot), block(item, slot)))
    for item, kind in enumerate(plan):
        if kind == "all":
            for number, _, sender in line:
                arrived(item, outs[item].at[sender, slot], GROUP - 1 + number)
            for number, step in others:
                send(item, outs[item].at[:, slot], outs[item].at[:, slot], number - 1, me + step)
    corner_step = first_step + second_step
    for item, kind in enumerate(plan):
        if kind == "gather":
            for place, number, onward in (
                (slot + first_step, 0, ((3, second_step), (4, step_core))),
                (slot + second_step, 1, ((5, step_core),)),
                (slot + corner_step, 3, ((6, step_core),)),
            ):
                arrived(item, block(item, place), number)
                for then, step in onward:
                    send(item, block(item, place), block(item, place), then, me + step)
    for item, kind in enumerate(plan):
        if kind == "gather":
            for step, number in ((0, 2), (second_step, 4), (first_step, 5), (corner_step, 6)):
                arrived(item, block(item, slot + step_core + step), number)
        elif kind == "all":
            for number, step in others:
                arrived(item, outs[item].at[:, slot + step], number - 1)
        else:
            for number, step in others:
                arrived(item, block(item, slot + step), number - 1)
    for copy in sent:
        copy.wait_send()
    for copy in own:
        copy.wait()


def exchange(number, micros, *items):
    groups = lax.axis_size("fsdp") // GROUP
    kinds = [kind for kind, _ in items]
    arrays = [array for _, array in items]
    shapes = []
    for kind, array in items:
        if kind == "gather":
            shape = (array.shape[0], GROUP) + array.shape[1:]
        elif kind == "swap":
            shape = array.shape
        elif kind == "widen":
            shape = (array.shape[1], GROUP * array.shape[2])
        elif kind == "narrow":
            shape = (GROUP, array.shape[0], array.shape[1] // GROUP)
        else:
            shape = (groups, GROUP) + array.shape
        shapes.append(jax.ShapeDtypeStruct(shape, array.dtype))
    numbers = GROUP - 1 + (groups if "all" in kinds else 0)
    return pl.pallas_call(
        functools.partial(exchange_kernel, kinds),
        out_shape=tuple(shapes),
        in_specs=[ANY] * len(items),
        out_specs=tuple([ANY] * len(items)),
        scratch_shapes=[
            pltpu.SemaphoreType.DMA((len(items), numbers)),
            pltpu.SemaphoreType.DMA((len(items), numbers)),
            pltpu.SemaphoreType.DMA((len(items),)),
        ],
        compiler_params=pltpu.CompilerParams(collective_id=number, has_side_effects=True),
        cost_estimate=cost(micros),
    )(*arrays)


def home_kernel(pieces, got_ref, weight_ref, out_ref, gain_ref):
    columns = got_ref.shape[2] // pieces
    for piece in range(pieces):
        for sender in range(GROUP):
            lo = (piece * GROUP + sender) * columns
            out_ref[:, lo : lo + columns] = got_ref[
                sender, :, piece * columns : (piece + 1) * columns
            ].astype(f32)
    gain_ref[...] = jnp.sum(out_ref[...] * weight_ref[...].astype(f32), axis=1, keepdims=True)


def home(got, weight, pieces):
    rows, columns = weight.shape
    return pl.pallas_call(
        functools.partial(home_kernel, pieces),
        out_shape=(
            jax.ShapeDtypeStruct((rows, columns), f32),
            jax.ShapeDtypeStruct((rows, 1), f32),
        ),
        in_specs=[VMEM, VMEM],
        out_specs=(VMEM, VMEM),
        compiler_params=pltpu.CompilerParams(vmem_limit_bytes=32 * 2**20),
        cost_estimate=cost(5),
    )(got, weight)


TILE = 256


def product_scatter_kernel(a_ref, w_ref, out_ref, near, far, away, going, send_sem, recv_sem):
    me, slot, step_core, first_step, second_step = places()
    first, second, mate = me + first_step, me + second_step, me + step_core
    greet((first, second, mate))
    corner_step = first_step + second_step
    steps = (corner_step, first_step, second_step, corner_step * 0)
    mate_steps = (corner_step, second_step, first_step, corner_step * 0)
    sent = []

    def send(source, target, number, device):
        copy = remote(source, target, send_sem.at[number], recv_sem.at[number], device)
        copy.start()
        sent.append(copy)

    def arrived(ref, number, source):
        remote(ref, ref, send_sem.at[number], recv_sem.at[number], source).wait_recv()

    def product(place, extra, target):
        def tile(i, _):
            at = pl.ds(pl.multiple_of(i * TILE, TILE), TILE)
            total = dot_nt(a_ref[place], w_ref[at, :])
            for ref in extra:
                total = total + ref[:, at].astype(f32)
            target[:, at] = total.astype(target.dtype)
            return 0

        lax.fori_loop(0, out_ref.shape[1] // TILE, tile, 0)

    def to_mate(kind):
        product(slot + step_core + mate_steps[kind], (), away.at[kind])
        send(away.at[kind], near.at[kind], kind, mate)

    def add(ref):
        def tile(i, _):
            at = pl.ds(pl.multiple_of(i * TILE, TILE), TILE)
            out_ref[:, at] = out_ref[:, at] + ref[:, at].astype(f32)
            return 0

        lax.fori_loop(0, out_ref.shape[1] // TILE, tile, 0)

    to_mate(0)
    to_mate(2)
    arrived(near.at[0], 0, mate)
    product(slot + steps[0], (near.at[0],), going.at[0])
    send(going.at[0], far.at[0], 4, second)
    arrived(near.at[2], 2, mate)
    product(slot + steps[2], (near.at[2],), going.at[2])
    send(going.at[2], far.at[2], 5, second)
    to_mate(1)
    to_mate(3)
    arrived(near.at[3], 3, mate)
    product(slot + steps[3], (near.at[3],), out_ref)
    arrived(near.at[1], 1, mate)
    arrived(far.at[0], 4, second)
    product(slot + steps[1], (near.at[1], far.at[0]), going.at[1])
    send(going.at[1], far.at[1], 6, first)
    arrived(far.at[2], 5, second)
    add(far.at[2])
    arrived(far.at[1], 6, first)
    add(far.at[1])
    for copy in sent:
        copy.wait_send()


def product_scatter(a, w, number):
    _, rows, depth = a.shape
    columns = w.shape[0]
    return pl.pallas_call(
        product_scatter_kernel,
        out_shape=jax.ShapeDtypeStruct((rows, columns), f32),
        in_specs=[VMEM, VMEM],
        out_specs=VMEM,
        scratch_shapes=[
            pltpu.VMEM((4, rows, columns), bf16),
            pltpu.VMEM((3, rows, columns), bf16),
            pltpu.VMEM((4, rows, columns), bf16),
            pltpu.VMEM((3, rows, columns), bf16),
            pltpu.SemaphoreType.DMA((7,)),
            pltpu.SemaphoreType.DMA((7,)),
        ],
        compiler_params=pltpu.CompilerParams(
            collective_id=number, has_side_effects=True, vmem_limit_bytes=56 * 2**20
        ),
        cost_estimate=cost(50),
    )(a, w)


def gate_gather_kernel(own_ref, x_ref, w_ref, all_ref, gate_ref, up_ref, hidden_ref, send_sem, recv_sem, own_sem):
    me, slot, step_core, first_step, second_step = places()
    first, second, mate = me + first_step, me + second_step, me + step_core
    greet((first, second, mate))
    sent = []

    def send(source, place, number, device):
        copy = remote(source, all_ref.at[place], send_sem.at[number], recv_sem.at[number], device)
        copy.start()
        sent.append(copy)

    def arrived(place, number):
        target = all_ref.at[place]
        remote(target, target, send_sem.at[number], recv_sem.at[number], me).wait_recv()

    own = pltpu.make_async_copy(own_ref, all_ref.at[slot], own_sem)
    send(own_ref, slot, 0, first)
    send(own_ref, slot, 1, second)
    send(own_ref, slot, 2, mate)
    own.start()
    half = gate_ref.shape[1]
    tile_rows = own_ref.shape[0]

    def tile(i, _):
        at = pl.ds(pl.multiple_of(i * tile_rows, tile_rows), tile_rows)
        both = dot_nn(x_ref[at, :], w_ref[...])
        gate = both[:, :half]
        up = both[:, half:]
        gate_ref[at, :] = gate
        up_ref[at, :] = up
        hidden_ref[at, :] = (gate * jax.nn.sigmoid(gate) * up).astype(bf16)
        return 0

    tiles = x_ref.shape[0] // tile_rows
    lax.fori_loop(0, tiles // 2, tile, 0)
    corner = slot + first_step + second_step
    arrived(slot + first_step, 0)
    send(all_ref.at[slot + first_step], slot + first_step, 3, second)
    send(all_ref.at[slot + first_step], slot + first_step, 4, mate)
    arrived(slot + second_step, 1)
    send(all_ref.at[slot + second_step], slot + second_step, 5, mate)
    lax.fori_loop(tiles // 2, tiles, tile, 0)
    arrived(corner, 3)
    send(all_ref.at[corner], corner, 6, mate)
    arrived(slot + step_core, 2)
    arrived(slot + step_core + second_step, 4)
    arrived(slot + step_core + first_step, 5)
    arrived(corner + step_core, 6)
    for copy in sent:
        copy.wait_send()
    own.wait()


def gate_gather(own, x, w, number):
    rows, columns = own.shape
    half = w.shape[1] // 2
    wide = jax.ShapeDtypeStruct((x.shape[0], half), f32)
    return pl.pallas_call(
        gate_gather_kernel,
        out_shape=(
            jax.ShapeDtypeStruct((GROUP, rows, columns), own.dtype),
            wide,
            wide,
            jax.ShapeDtypeStruct((x.shape[0], half), bf16),
        ),
        in_specs=[ANY, VMEM, VMEM],
        out_specs=(ANY, VMEM, VMEM, VMEM),
        scratch_shapes=[
            pltpu.SemaphoreType.DMA((7,)),
            pltpu.SemaphoreType.DMA((7,)),
            pltpu.SemaphoreType.DMA,
        ],
        compiler_params=pltpu.CompilerParams(
            collective_id=number, has_side_effects=True, vmem_limit_bytes=56 * 2**20
        ),
        cost_estimate=cost(45),
    )(own, x, w)


def hidden_back_kernel(cot_ref, gate_ref, up_ref, hidden_ref, w_ref, grad_ref, out_ref):
    half = gate_ref.shape[1]
    d_hidden = dot_nn(cot_ref[...], w_ref[...])
    gate = gate_ref[...]
    sigmoid = jax.nn.sigmoid(gate)
    grad_ref[:, :half] = (
        d_hidden * up_ref[...] * sigmoid * (1.0 + gate * (1.0 - sigmoid))
    ).astype(bf16)
    grad_ref[:, half:] = (d_hidden * gate * sigmoid).astype(bf16)
    out_ref[...] = dot_nt(hidden_ref[...], w_ref[...]).astype(bf16)


def hidden_back(cot, gate, up, hidden, w):
    rows, columns = cot.shape
    half = w.shape[1]
    tile_rows = 256

    def tiles(width):
        return pl.BlockSpec((tile_rows, width), lambda i: (i, 0))

    return pl.pallas_call(
        hidden_back_kernel,
        grid=(rows // tile_rows,),
        in_specs=[
            tiles(columns),
            tiles(half),
            tiles(half),
            tiles(half),
            pl.BlockSpec(w.shape, lambda i: (0, 0)),
        ],
        out_specs=(tiles(2 * half), tiles(columns)),
        out_shape=(
            jax.ShapeDtypeStruct((rows, 2 * half), bf16),
            jax.ShapeDtypeStruct((rows, columns), bf16),
        ),
        compiler_params=pltpu.CompilerParams(vmem_limit_bytes=48 * 2**20),
        cost_estimate=cost(20),
    )(cot, gate, up, hidden, w)


def rows_product_kernel(x_ref, y_ref, out_ref):
    out_ref[...] = dot_tn(x_ref[...], y_ref[...]).astype(bf16)


def rows_product(x, y, micros):
    rows, columns = x.shape
    wide = y.shape[1]
    tile_columns = 512
    return pl.pallas_call(
        rows_product_kernel,
        grid=(columns // tile_columns,),
        in_specs=[
            pl.BlockSpec((rows, tile_columns), lambda i: (0, i)),
            pl.BlockSpec((rows, wide), lambda i: (0, 0)),
        ],
        out_specs=pl.BlockSpec((tile_columns, wide), lambda i: (i, 0)),
        out_shape=jax.ShapeDtypeStruct((columns, wide), bf16),
        compiler_params=pltpu.CompilerParams(vmem_limit_bytes=48 * 2**20),
        cost_estimate=cost(micros),
    )(x, y)


def plane_permutes(device_count):
    first, second, mate = [], [], []
    for i in range(device_count):
        low_bit, high_bit = (2, 4) if i % 2 == 0 else (4, 2)
        first.append((i, i ^ low_bit))
        second.append((i, i ^ high_bit))
        mate.append((i, i ^ 1))
    return first, second, mate


def after(values, *earlier):
    return lax.optimization_barrier((values, earlier))[0]


def meet(*values):
    return lax.optimization_barrier(values)


def assemble_kernel(*refs):
    blocks, out_ref = refs[:GROUP], refs[GROUP]
    _, slot, step_core, first_step, second_step = places()
    corner_step = first_step + second_step
    here = (0, first_step, second_step, corner_step)
    there = (step_core, step_core + second_step, step_core + first_step, step_core + corner_step)
    for number, step in enumerate(here + there):
        out_ref[:, slot + step] = blocks[number][...]


def assemble(x, from_first, from_second, from_corner, mates):
    parts, rows, columns = x.shape
    return pl.pallas_call(
        assemble_kernel,
        out_shape=jax.ShapeDtypeStruct((parts, GROUP, rows, columns), x.dtype),
        in_specs=[VMEM] * GROUP,
        out_specs=VMEM,
        compiler_params=pltpu.CompilerParams(vmem_limit_bytes=32 * 2**20),
        cost_estimate=cost(8),
    )(x, from_first, from_second, from_corner, *mates)


class SlowScatter:
    def __init__(self, x, moves, device_count):
        self.x = x
        self.slot, self.step_core, self.first_step, self.second_step = moves
        self.first, self.second, self.mate = plane_permutes(device_count)

    def block(self, step):
        return lax.dynamic_index_in_dim(self.x, self.slot + step, 1, keepdims=False)

    def pair(self, near, kind, step):
        return self.block(step).astype(f32) + near[kind].astype(f32)

    def to_mate(self):
        steps = (self.first_step + self.second_step, self.second_step, self.first_step, 0)
        away = jnp.stack([self.block(self.step_core + step) for step in steps])
        return lax.ppermute(away, "fsdp", self.mate)

    def to_second(self, near):
        corner = self.pair(near, 0, self.first_step + self.second_step)
        onward = jnp.stack([corner, self.pair(near, 2, self.second_step)]).astype(bf16)
        return lax.ppermute(onward, "fsdp", self.second)

    def to_first(self, near, far):
        both = self.pair(near, 1, self.first_step) + far[0].astype(f32)
        return lax.ppermute(both.astype(bf16), "fsdp", self.first)

    def total(self, near, far, last):
        return self.pair(near, 3, 0) + far[1].astype(f32) + last.astype(f32)


def low(values):
    return values.astype(bf16).astype(f32)


def gates(proj_ref, floor_ref, rows, head, heads):
    dim = floor_ref.shape[1] // heads
    wide = heads * dim
    lo = head * dim
    q_pre = proj_ref[rows, lo : lo + dim]
    f_pre = proj_ref[rows, wide + lo : wide + lo + dim]
    value = proj_ref[rows, 2 * wide + lo : 2 * wide + lo + dim].astype(bf16)
    floor = floor_ref[:, lo : lo + dim]
    q_sigmoid = jax.nn.sigmoid(q_pre)
    query = low(q_pre * q_sigmoid)
    f_sigmoid = jax.nn.sigmoid(f_pre)
    forget = floor + (1.0 - floor) * f_sigmoid
    key = low(1.0 - forget)
    row = lax.broadcasted_iota(jnp.int32, (CHUNK, dim), 0)
    in_half = lax.rem(row, HALF)
    product = forget
    step = 1
    while step < HALF:
        product = jnp.where(in_half >= step, product * pltpu.roll(product, step, 0), product)
        step *= 2
    middle = product[HALF - 1 : HALF, :]
    end = product[CHUNK - 1 : CHUNK, :]
    ratio = jnp.where(row < HALF, product / middle, product)
    inverse = 1.0 / ratio
    return {
        "q_pre": q_pre,
        "q_sigmoid": q_sigmoid,
        "f_sigmoid": f_sigmoid,
        "forget": forget,
        "value": value,
        "floor": floor,
        "middle": middle,
        "end": end,
        "ratio": ratio,
        "inverse": inverse,
        "row": row,
        "query_mid": query * ratio,
        "key_mid": key * inverse,
    }


def whole_fade(g, last):
    return g["middle"] * g["end"] * jnp.where(last < 0, 1.0, 0.0)


def tail_keys(g, last):
    return jnp.where(g["row"] >= last, g["key_mid"] * g["end"], 0.0).astype(bf16)


def entry_queries(g, carried):
    return jnp.where(carried, g["query_mid"] * g["middle"], 0.0).astype(bf16)


def next_state(g, last, state):
    return state * whole_fade(g, last) + dot_tn(g["value"], tail_keys(g, last))


def forward_kernel(
    heads, last_ref, proj_ref, start_ref, floor_ref, gain_ref, in_ref, mix_ref, out_ref, enter_ref, state
):
    dim = floor_ref.shape[1] // heads
    state[...] = in_ref[...]

    def step(n, _):
        base = pl.multiple_of(n * CHUNK, CHUNK)
        rows = pl.ds(base, CHUNK)
        starts = start_ref[rows, :] - base
        last = last_ref[n] - base
        column = lax.broadcasted_iota(jnp.int32, (CHUNK, CHUNK), 1)
        line = lax.broadcasted_iota(jnp.int32, (CHUNK, CHUNK), 0)
        within = (column <= line) & (column >= starts)
        carried = starts < 0
        for head in range(heads):
            lo = head * dim
            g = gates(proj_ref, floor_ref, rows, head, heads)
            now = state[head]
            enter_ref[n, head] = now
            scores = dot_nt(g["query_mid"].astype(bf16), g["key_mid"].astype(bf16))
            scores = jnp.where(within, scores, 0.0).astype(bf16)
            out = dot_nn(scores, g["value"]) + dot_nt(entry_queries(g, carried), now.astype(bf16))
            state[head] = next_state(g, last, now)
            out_ref[rows, lo : lo + dim] = out
            mix_ref[rows, lo : lo + dim] = (
                out * inverse_rms(out) * gain_ref[:, lo : lo + dim]
            ).astype(bf16)
        return 0

    lax.fori_loop(0, proj_ref.shape[0] // CHUNK, step, 0)


def last_state_kernel(heads, last_ref, proj_ref, floor_ref, out_ref):
    for head in range(heads):
        state = jnp.zeros(out_ref.shape[1:], f32)
        for n in range(proj_ref.shape[0] // CHUNK):
            g = gates(proj_ref, floor_ref, pl.ds(n * CHUNK, CHUNK), head, heads)
            state = next_state(g, last_ref[n] - n * CHUNK, state)
        out_ref[head] = state


def state_grad(out_ref, dmix_ref, gain_ref, rows, lo, dim):
    out = out_ref[rows, lo : lo + dim]
    inverse = inverse_rms(out)
    scaled = out * inverse
    dmix = dmix_ref[rows, lo : lo + dim].astype(f32)
    return rms_back(dmix * gain_ref[:, lo : lo + dim], scaled, inverse)


def backward_kernel(
    heads,
    last_ref,
    proj_ref,
    start_ref,
    floor_ref,
    gain_ref,
    out_ref,
    dmix_ref,
    enter_ref,
    in_ref,
    dproj_ref,
    dfloor_ref,
    later,
):
    dim = floor_ref.shape[1] // heads
    wide = heads * dim
    chunks = proj_ref.shape[0] // CHUNK
    later[...] = in_ref[...]
    dfloor_ref[...] = jnp.zeros_like(dfloor_ref)

    def step(i, _):
        n = chunks - 1 - i
        base = pl.multiple_of(n * CHUNK, CHUNK)
        rows = pl.ds(base, CHUNK)
        starts = start_ref[rows, :] - base
        last = last_ref[n] - base
        column = lax.broadcasted_iota(jnp.int32, (CHUNK, CHUNK), 1)
        line = lax.broadcasted_iota(jnp.int32, (CHUNK, CHUNK), 0)
        within = (column <= line) & (column >= starts)
        carried = starts < 0
        for head in range(heads):
            lo = head * dim
            g = gates(proj_ref, floor_ref, rows, head, heads)
            grad = state_grad(out_ref, dmix_ref, gain_ref, rows, lo, dim)
            grad_hi = grad.astype(bf16)
            grad_lo = (grad - grad_hi.astype(f32)).astype(bf16)
            state = enter_ref[n, head]
            after = later[head]
            after_low = after.astype(bf16)
            query_mid = g["query_mid"].astype(bf16)
            key_mid = g["key_mid"].astype(bf16)
            scores = jnp.where(within, dot_nt(query_mid, key_mid), 0.0).astype(bf16)
            d_scores = dot_nt(grad_hi, g["value"]) + dot_nt(grad_lo, g["value"])
            d_scores = jnp.where(within, d_scores, 0.0).astype(bf16)
            query_in = entry_queries(g, carried)
            key_out = tail_keys(g, last)
            d_query_mid = dot_nn(d_scores, key_mid)
            d_query_in = jnp.where(carried, dot_nn(grad_hi, state.astype(bf16)), 0.0)
            d_key_mid = dot_tn(d_scores, query_mid)
            d_key_out = jnp.where(g["row"] >= last, dot_nn(g["value"], after_low), 0.0)
            d_value = dot_tn(scores, grad_hi) + dot_nt(key_out, after_low)
            d_query = (d_query_mid + d_query_in * g["middle"]) * g["ratio"]
            d_key = (d_key_mid + d_key_out * g["end"]) * g["inverse"]
            tail = d_key_out * key_out.astype(f32)
            term = (
                d_query_mid * query_mid.astype(f32)
                + d_query_in * query_in.astype(f32)
                - d_key_mid * key_mid.astype(f32)
                - tail
            )
            fade = whole_fade(g, last)
            final = jnp.sum(tail, axis=0, keepdims=True) + fade * jnp.sum(
                state * after, axis=0, keepdims=True
            )
            step_rows = 1
            while step_rows < CHUNK:
                term = jnp.where(
                    g["row"] < CHUNK - step_rows,
                    term + pltpu.roll(term, CHUNK - step_rows, 0),
                    term,
                )
                step_rows *= 2
            d_forget = (term + final) / g["forget"] - d_key
            q_sigmoid, f_sigmoid = g["q_sigmoid"], g["f_sigmoid"]
            d_q_pre = d_query * q_sigmoid * (1.0 + g["q_pre"] * (1.0 - q_sigmoid))
            d_floor = d_forget * (1.0 - f_sigmoid)
            d_f_pre = d_floor * (1.0 - g["floor"]) * f_sigmoid
            dproj_ref[rows, lo : lo + dim] = d_q_pre.astype(bf16)
            dproj_ref[rows, wide + lo : wide + lo + dim] = d_f_pre.astype(bf16)
            dproj_ref[rows, 2 * wide + lo : 2 * wide + lo + dim] = d_value.astype(bf16)
            dfloor_ref[:, lo : lo + dim] += jnp.sum(d_floor, axis=0, keepdims=True)
            later[head] = after * fade + dot_tn(grad_hi, query_in)
        return 0

    lax.fori_loop(0, chunks, step, 0)


def first_grad_kernel(
    heads, last_ref, proj_ref, start_ref, floor_ref, gain_ref, out_ref, dmix_ref, grad_ref
):
    dim = floor_ref.shape[1] // heads
    for head in range(heads):
        after = jnp.zeros((dim, dim), f32)
        for n in range(proj_ref.shape[0] // CHUNK - 1, -1, -1):
            rows = pl.ds(n * CHUNK, CHUNK)
            g = gates(proj_ref, floor_ref, rows, head, heads)
            grad = state_grad(out_ref, dmix_ref, gain_ref, rows, head * dim, dim)
            queries = entry_queries(g, start_ref[rows, :] < n * CHUNK)
            after = after * whole_fade(g, last_ref[n] - n * CHUNK) + dot_tn(
                grad.astype(bf16), queries
            )
        grad_ref[head] = after


def local_call(kernel, heads, micros, out_shape, scratch, *operands):
    return pl.pallas_call(
        functools.partial(kernel, heads),
        out_shape=out_shape,
        in_specs=[SMEM] + [VMEM] * (len(operands) - 1),
        out_specs=jax.tree.map(lambda _: VMEM, out_shape),
        scratch_shapes=scratch,
        compiler_params=pltpu.CompilerParams(vmem_limit_bytes=48 * 2**20),
        cost_estimate=cost(micros),
    )(*operands)


def body(
    tokens,
    cotangent,
    dealt_lengths,
    deal,
    norm_gain,
    mixer_in,
    forget_floor,
    group_gain,
    out_proj,
    ffn_gain,
    gate_up,
    down_proj,
):
    row_count, width = tokens.shape
    weight_rows = mixer_in.shape[0]
    device_count = lax.axis_size("fsdp")
    groups = device_count // GROUP
    own_index = lax.axis_index("fsdp")
    slot = lax.rem(own_index, GROUP)
    group = own_index // GROUP
    group_rows = GROUP * row_count
    heads = HEADS // GROUP
    own_width = width // GROUP
    dim = width // HEADS
    ffn_width = down_proj.shape[1]
    own_ffn = ffn_width // GROUP
    planes = [[g * GROUP + s for s in range(GROUP)] for g in range(groups)]
    lines = [[g * GROUP + s for g in range(groups)] for s in range(GROUP)]

    def line_gather(x):
        return lax.all_gather(x, "fsdp", axis=0, axis_index_groups=lines, tiled=True)

    def line_scatter(x):
        return lax.psum_scatter(
            x, "fsdp", scatter_dimension=0, axis_index_groups=lines, tiled=True
        )

    def by_owner(weight, pieces):
        columns = weight.shape[1] // (pieces * GROUP)
        parted = weight.reshape(weight_rows, pieces, GROUP, columns).transpose(2, 0, 1, 3)
        return parted.reshape(GROUP, weight_rows, pieces * columns)

    def whole_rows(x):
        return line_gather(x.reshape(GROUP * weight_rows, -1))

    low_step = 2 - 4 * (slot // 2 % 2)
    high_step = 4 - 8 * (slot // 4)
    odd = slot % 2
    moves = (
        slot,
        1 - 2 * odd,
        jnp.where(odd == 0, low_step, high_step),
        jnp.where(odd == 0, high_step, low_step),
    )

    seq_count = deal.shape[0]
    seq_ids = jnp.arange(seq_count, dtype=jnp.int32)
    matches = deal[:, None] == seq_ids[None, :]
    lengths = jnp.sum(jnp.where(matches, dealt_lengths[:, None], 0), axis=0)
    seq_starts = jnp.sum(
        jnp.where(seq_ids[:, None] < seq_ids[None, :], lengths[:, None], 0), axis=0
    )
    group_start = group * group_rows
    rows_here = group_start + jnp.arange(group_rows, dtype=jnp.int32)
    starts = (
        jnp.max(jnp.where(seq_starts[None, :] <= rows_here[:, None], seq_starts[None, :], 0), axis=1)
        - group_start
    )
    start_column = starts[:, None]
    last_starts = starts[CHUNK - 1 :: CHUNK]

    out_lines = lax.all_gather(out_proj, "fsdp", axis=0, axis_index_groups=lines)
    gain_block = jnp.zeros((16, 128), bf16)
    for number, gain in enumerate((norm_gain, forget_floor, group_gain, ffn_gain)):
        gain_block = gain_block.at[number, :weight_rows].set(gain)
    gain_blocks, mixer_swapped = exchange(
        0, 15, ("all", gain_block), ("swap", by_owner(mixer_in, 3))
    )
    mixer_weight = whole_rows(mixer_swapped)
    gains = (
        gain_blocks[:, :, :4, :weight_rows].transpose(2, 0, 1, 3).reshape(4, width).astype(f32)
    )
    first_gain = gains[0:1]
    second_gain = gains[3:4]
    own_gains = lax.dynamic_slice_in_dim(gains, slot * own_width, own_width, 1)
    own_floor = own_gains[1:2]
    own_group_gain = own_gains[2:3]

    inputs = tokens.astype(f32)
    first_inverse = inverse_rms(inputs)
    first_scaled = inputs * first_inverse
    first_normed = (first_scaled * first_gain).astype(bf16)
    first_all, ffn_swapped, down_swapped = exchange(
        1,
        65,
        ("gather", first_normed[None]),
        ("swap", by_owner(gate_up, 2)),
        ("swap", by_owner(down_proj, 1)),
    )
    first_all = first_all.reshape(group_rows, width)
    ffn_weight = whole_rows(ffn_swapped)
    first, second, mate = plane_permutes(device_count)
    out_own = after(out_lines, first_all)
    from_first = lax.ppermute(out_own, "fsdp", first)
    from_second = lax.ppermute(out_own, "fsdp", second)
    tail_projected = dot_nn(first_all[group_rows - MAXLEN :], mixer_weight)
    edge = MAXLEN // CHUNK
    state_type = jax.ShapeDtypeStruct((heads, dim, dim), f32)
    last_state = local_call(
        last_state_kernel,
        heads,
        3,
        state_type,
        [],
        last_starts[-edge:] - (group_rows - MAXLEN),
        tail_projected,
        own_floor,
    )
    up_line = [(i, i + GROUP) for i in range(device_count - GROUP)]
    down_line = [(i + GROUP, i) for i in range(device_count - GROUP)]
    entering_state = lax.ppermute(last_state, "fsdp", up_line)
    projected = dot_nn(after(first_all, last_state), mixer_weight)
    projected, entering_state = meet(projected, entering_state)
    chunks = group_rows // CHUNK
    mixed_heads, state_out, entering = local_call(
        forward_kernel,
        heads,
        18,
        (
            jax.ShapeDtypeStruct((group_rows, own_width), bf16),
            jax.ShapeDtypeStruct((group_rows, own_width), f32),
            jax.ShapeDtypeStruct((chunks, heads, dim, dim), f32),
        ),
        [pltpu.VMEM((heads, dim, dim), f32)],
        last_starts,
        projected,
        start_column,
        own_floor,
        own_group_gain,
        entering_state,
    )
    mixed_heads, from_first, from_second = meet(mixed_heads, from_first, from_second)
    from_corner = lax.ppermute(from_first, "fsdp", second)
    mates = [lax.ppermute(block, "fsdp", mate) for block in (out_own, from_first, from_second)]
    [mixer_input] = exchange(
        3, 15, ("widen", mixed_heads.reshape(GROUP, row_count, own_width))
    )
    mixer_input, from_corner, mates = meet(mixer_input, from_corner, mates)
    mates = mates + [lax.ppermute(from_corner, "fsdp", mate)]
    out_weight = assemble(out_own, from_first, from_second, from_corner, mates).reshape(width, width)
    down_weight = whole_rows(after(down_swapped, mixed_heads))
    residual = inputs + dot_nn(mixer_input, out_weight)
    second_inverse = inverse_rms(residual)
    second_scaled = residual * second_inverse
    second_normed = (second_scaled * second_gain).astype(bf16)
    [second_all] = exchange(2, 43, ("gather", second_normed[None]))
    second_all = second_all.reshape(group_rows, width)
    cot_blocks, gate_part, up_part, hidden_act = gate_gather(
        cotangent, second_all, ffn_weight, 6
    )
    cot_all = cot_blocks.reshape(group_rows, width)
    down_grad = rows_product(cot_all, hidden_act, 11)
    down_summed = line_scatter(down_grad)
    d_gate_pre, ffn_part = hidden_back(
        after(cot_all, down_grad), gate_part, up_part, hidden_act, down_weight
    )
    ffn_sum = SlowScatter(ffn_part.reshape(1, GROUP, row_count, width), moves, device_count)
    ffn_near = ffn_sum.to_mate()
    ffn_grad = rows_product(second_all, d_gate_pre, 18)
    ffn_grad, ffn_near = meet(ffn_grad, ffn_near)
    ffn_summed = line_scatter(ffn_grad)
    ffn_far = ffn_sum.to_second(ffn_near)
    d_second = product_scatter(
        d_gate_pre.reshape(GROUP, row_count, -1), after(ffn_weight, ffn_grad), 4
    )
    d_second, ffn_far, down_summed = meet(d_second, ffn_far, down_summed)
    ffn_last = ffn_sum.to_first(ffn_near, ffn_far)
    d_residual = cotangent.astype(f32) + rms_back(
        d_second * second_gain, second_scaled, second_inverse
    )
    d_mix_out = d_residual.astype(bf16)
    out_part = dot_tn(mixer_input, d_mix_out).astype(bf16)
    out_sum = SlowScatter(
        out_part.reshape(groups, GROUP, weight_rows, width), moves, device_count
    )
    out_near = out_sum.to_mate()
    d_mixer_input = dot_nt(after(d_mix_out, out_part), out_weight).astype(bf16)
    [d_mixed_heads] = exchange(5, 15, ("narrow", d_mixer_input))
    d_mixed_heads, out_near, ffn_last = meet(
        d_mixed_heads.reshape(group_rows, own_width), out_near, ffn_last
    )
    layer_out = residual + ffn_sum.total(ffn_near, ffn_far, ffn_last)[0]
    first_grad = local_call(
        first_grad_kernel,
        heads,
        3,
        state_type,
        [],
        last_starts[:edge],
        projected[:MAXLEN],
        start_column[:MAXLEN],
        own_floor,
        own_group_gain,
        state_out[:MAXLEN],
        d_mixed_heads[:MAXLEN],
    )
    entering_grad = lax.ppermute(first_grad, "fsdp", down_line)
    out_near = after(out_near, first_grad)
    out_far = out_sum.to_second(out_near)
    d_projected, floor_grad = local_call(
        backward_kernel,
        heads,
        30,
        (
            jax.ShapeDtypeStruct((group_rows, 3 * own_width), bf16),
            jax.ShapeDtypeStruct((1, own_width), f32),
        ),
        [pltpu.VMEM((heads, dim, dim), f32)],
        last_starts,
        projected,
        start_column,
        own_floor,
        own_group_gain,
        state_out,
        d_mixed_heads,
        entering,
        entering_grad,
    )
    d_projected, out_far = meet(d_projected, out_far)
    out_last = out_sum.to_first(out_near, out_far)
    mixer_grad = dot_tn(first_all, d_projected).astype(bf16)
    mixer_summed = line_scatter(after(mixer_grad, ffn_summed))
    d_first = product_scatter(
        d_projected.reshape(GROUP, row_count, -1), after(mixer_weight, mixer_grad), 8
    )
    d_first, out_last = meet(d_first, out_last)
    out_total = out_sum.total(out_near, out_far, out_last).astype(bf16)
    d_out_proj = line_scatter(
        after(out_total, mixer_summed).reshape(groups * weight_rows, width)
    ).astype(f32)
    floor_block = jnp.zeros((8, 128), f32).at[: own_width // 128].set(
        floor_grad.reshape(own_width // 128, 128)
    )
    down_summed, ffn_summed, floor_block = after((down_summed, ffn_summed, floor_block), d_first)
    by_sender = (GROUP, weight_rows, -1)
    down_swapped, ffn_swapped, floor_blocks = exchange(
        7,
        30,
        ("swap", down_summed.reshape(by_sender)),
        ("swap", ffn_summed.reshape(by_sender)),
        ("all", floor_block),
    )
    d_down_proj, _ = home(down_swapped, down_proj, 1)
    d_gate_up, ffn_gain_sum = home(ffn_swapped, gate_up, 2)
    [mixer_swapped] = exchange(
        9, 12, ("swap", after(mixer_summed, floor_blocks).reshape(by_sender))
    )
    d_mixer_in, norm_gain_sum = home(mixer_swapped, mixer_in, 3)
    d_dealt = d_residual + rms_back(d_first * first_gain, first_scaled, first_inverse)

    group_gain_sum = jnp.sum(out_proj.astype(f32) * d_out_proj, axis=1)
    floor_sums = jnp.sum(floor_blocks[:, :, : own_width // 128], axis=0).reshape(width)
    d_forget_floor = lax.dynamic_slice_in_dim(floor_sums, own_index * weight_rows, weight_rows, 0)
    return (
        layer_out,
        d_dealt,
        norm_gain_sum[:, 0] / norm_gain.astype(f32),
        d_mixer_in,
        d_forget_floor,
        group_gain_sum / group_gain.astype(f32),
        d_out_proj,
        ffn_gain_sum[:, 0] / ffn_gain.astype(f32),
        d_gate_up,
        d_down_proj,
    )


def solution(mesh):
    by_rows = P("fsdp", None)
    by_one = P("fsdp")
    return jax.shard_map(
        body,
        mesh=mesh,
        in_specs=(
            by_rows,
            by_rows,
            P(),
            P(),
            by_one,
            by_rows,
            by_one,
            by_one,
            by_rows,
            by_one,
            by_rows,
            by_rows,
        ),
        out_specs=(
            by_rows,
            by_rows,
            by_one,
            by_rows,
            by_one,
            by_one,
            by_rows,
            by_one,
            by_rows,
            by_rows,
        ),
        check_vma=False,
    )
```

```python
import functools

import jax
import jax.numpy as jnp
from jax import lax
from jax.experimental import pallas as pl
from jax.experimental.pallas import tpu as pltpu
from jax.sharding import PartitionSpec as P

HEADS = 16
CHUNK = 64
HALF = 32
TILE_ROWS = 512
UNROLL = 2
MAXLEN = 128
GROUP = 8
MESH_ID = pl.DeviceIdType.MESH
VMEM = pl.BlockSpec(memory_space=pltpu.VMEM)
SMEM = pl.BlockSpec(memory_space=pltpu.SMEM)
ANY = pl.BlockSpec(memory_space=pl.ANY)

norm_eps = 1e-05
f32 = jnp.float32
bf16 = jnp.bfloat16


def inverse_rms(values):
    return lax.rsqrt(jnp.mean(values * values, axis=-1, keepdims=True) + norm_eps)


def rms_back(grad_scaled, scaled, inverse):
    return inverse * (grad_scaled - scaled * jnp.mean(grad_scaled * scaled, axis=-1, keepdims=True))


def dot_nt(left, right):
    return lax.dot_general(left, right, (((1,), (1,)), ((), ())), preferred_element_type=f32)


def dot_nn(left, right):
    return lax.dot_general(left, right, (((1,), (0,)), ((), ())), preferred_element_type=f32)


def dot_tn(left, right):
    return lax.dot_general(left, right, (((0,), (0,)), ((), ())), preferred_element_type=f32)


def cost(micros):
    return pl.CostEstimate(flops=0, transcendentals=0, bytes_accessed=int(micros * 36_900))


def places():
    me = lax.axis_index("fsdp")
    slot = lax.rem(me, GROUP)
    core = lax.rem(slot, 2)
    step_low = 2 - 4 * lax.rem(slot // 2, 2)
    step_high = 4 - 8 * (slot // 4)
    step_core = 1 - 2 * core
    first_step = (1 - core) * step_low + core * step_high
    second_step = core * step_low + (1 - core) * step_high
    return me, slot, step_core, first_step, second_step


def greet(others):
    barrier = pltpu.get_barrier_semaphore()
    for other in others:
        pl.semaphore_signal(barrier, inc=1, device_id=(other,), device_id_type=MESH_ID)
    pl.semaphore_wait(barrier, len(others))


def remote(source, target, send_sem, recv_sem, device):
    return pltpu.make_async_remote_copy(
        src_ref=source,
        dst_ref=target,
        send_sem=send_sem,
        recv_sem=recv_sem,
        device_id=(device,),
        device_id_type=MESH_ID,
    )


def plane_steps(step_core, step_low, step_high):
    return [
        (number, (number & 1) * step_core + ((number >> 1) & 1) * step_low + (number >> 2) * step_high)
        for number in range(1, GROUP)
    ]


AROUND = (1, 2, 4, 3, 5, 6, 7)


def exchange_kernel(plan, *refs):
    count = len(plan)
    ins, outs = refs[:count], refs[count : 2 * count]
    send_sem, recv_sem, own_sem = refs[2 * count :]
    me, slot, step_core, first_step, second_step = places()
    core = lax.rem(slot, 2)
    step_low = (1 - core) * first_step + core * second_step
    step_high = core * first_step + (1 - core) * second_step
    others = plane_steps(step_core, step_low, step_high)
    group = me // GROUP
    groups = lax.axis_size("fsdp") // GROUP
    greeted = [me + first_step, me + second_step, me + step_core]
    if not set(plan) <= {"gather", "around"}:
        greeted = [me + step for _, step in others]
    line = []
    if "all" in plan:
        line = [
            (
                number,
                lax.rem(group + number, groups) * GROUP + slot,
                lax.rem(group + groups - number, groups),
            )
            for number in range(1, groups)
        ]
        greeted = greeted + [target for _, target, _ in line]
    greet(greeted)
    sent = []

    def copy_of(item, source, target, number, device):
        return remote(source, target, send_sem.at[item, number], recv_sem.at[item, number], device)

    def send(item, source, target, number, device):
        copy = copy_of(item, source, target, number, device)
        copy.start()
        sent.append(copy)

    def arrived(item, target, number):
        copy_of(item, target, target, number, me).wait_recv()

    def keep(item, source, target):
        copy = pltpu.make_async_copy(source, target, own_sem.at[item])
        copy.start()
        return copy

    def block(item, place):
        kind, out = plan[item], outs[item]
        if kind == "widen":
            columns = out.shape[1] // GROUP
            return out.at[:, pl.ds(pl.multiple_of(place * columns, columns), columns)]
        if kind in ("gather", "around"):
            return out.at[:, place]
        return out.at[place]

    def landing(item, place, number):
        return block(item, AROUND[number] if plan[item] == "around" else place)

    def piece(item, place):
        if plan[item] == "narrow":
            columns = ins[item].shape[1] // GROUP
            return ins[item].at[:, pl.ds(pl.multiple_of(place * columns, columns), columns)]
        return ins[item].at[place]

    own = []
    for item, kind in enumerate(plan):
        if kind == "all":
            keep(item, ins[item], outs[item].at[group, slot]).wait()
            for number, target, _ in line:
                send(item, ins[item], outs[item].at[group, slot], GROUP - 1 + number, target)
        elif kind in ("gather", "around"):
            for number, step in enumerate((first_step, second_step, step_core)):
                send(item, ins[item], landing(item, slot, number), number, me + step)
            own.append(keep(item, ins[item], block(item, 0 if kind == "around" else slot)))
    for item, kind in enumerate(plan):
        if kind in ("swap", "widen", "narrow"):
            for number, step in others:
                send(item, piece(item, slot + step), block(item, slot), number - 1, me + step)
            own.append(keep(item, piece(item, slot), block(item, slot)))
    for item, kind in enumerate(plan):
        if kind == "all":
            for number, _, sender in line:
                arrived(item, outs[item].at[sender, slot], GROUP - 1 + number)
            for number, step in others:
                send(item, outs[item].at[:, slot], outs[item].at[:, slot], number - 1, me + step)
    corner_step = first_step + second_step
    for item, kind in enumerate(plan):
        if kind in ("gather", "around"):
            for place, number, onward in (
                (slot + first_step, 0, ((3, second_step), (4, step_core))),
                (slot + second_step, 1, ((5, step_core),)),
                (slot + corner_step, 3, ((6, step_core),)),
            ):
                here = landing(item, place, number)
                arrived(item, here, number)
                for then, step in onward:
                    send(item, here, landing(item, place, then), then, me + step)
    for item, kind in enumerate(plan):
        if kind in ("gather", "around"):
            for step, number in ((0, 2), (second_step, 4), (first_step, 5), (corner_step, 6)):
                arrived(item, landing(item, slot + step_core + step, number), number)
        elif kind == "all":
            for number, step in others:
                arrived(item, outs[item].at[:, slot + step], number - 1)
        else:
            for number, step in others:
                arrived(item, block(item, slot + step), number - 1)
    for copy in sent:
        copy.wait_send()
    for copy in own:
        copy.wait()


def exchange(number, micros, *items):
    groups = lax.axis_size("fsdp") // GROUP
    kinds = [kind for kind, _ in items]
    arrays = [array for _, array in items]
    shapes = []
    for kind, array in items:
        if kind in ("gather", "around"):
            shape = (array.shape[0], GROUP) + array.shape[1:]
        elif kind == "swap":
            shape = array.shape
        elif kind == "widen":
            shape = (array.shape[1], GROUP * array.shape[2])
        elif kind == "narrow":
            shape = (GROUP, array.shape[0], array.shape[1] // GROUP)
        else:
            shape = (groups, GROUP) + array.shape
        shapes.append(jax.ShapeDtypeStruct(shape, array.dtype))
    numbers = GROUP - 1 + (groups if "all" in kinds else 0)
    return pl.pallas_call(
        functools.partial(exchange_kernel, kinds),
        out_shape=tuple(shapes),
        in_specs=[ANY] * len(items),
        out_specs=tuple([ANY] * len(items)),
        scratch_shapes=[
            pltpu.SemaphoreType.DMA((len(items), numbers)),
            pltpu.SemaphoreType.DMA((len(items), numbers)),
            pltpu.SemaphoreType.DMA((len(items),)),
        ],
        compiler_params=pltpu.CompilerParams(collective_id=number, has_side_effects=True),
        cost_estimate=cost(micros),
    )(*arrays)


def owners_kernel(pieces, in_ref, out_ref):
    columns = out_ref.shape[2] // pieces
    for piece in range(pieces):
        for owner in range(GROUP):
            lo = (piece * GROUP + owner) * columns
            out_ref[owner, :, piece * columns : (piece + 1) * columns] = in_ref[:, lo : lo + columns]


def by_owner(weight, pieces):
    rows, columns = weight.shape
    return pl.pallas_call(
        functools.partial(owners_kernel, pieces),
        out_shape=jax.ShapeDtypeStruct((GROUP, rows, columns // GROUP), weight.dtype),
        in_specs=[VMEM],
        out_specs=VMEM,
        compiler_params=pltpu.CompilerParams(vmem_limit_bytes=32 * 2**20),
        cost_estimate=cost(3),
    )(weight)


def dealt_columns_kernel(piece, in_ref, out_ref):
    for owner in range(GROUP):
        for part in range(out_ref.shape[2] // piece):
            lo = (part * GROUP + owner) * piece
            out_ref[owner, :, part * piece : (part + 1) * piece] = in_ref[:, lo : lo + piece]


def dealt_columns(x, piece):
    rows, columns = x.shape
    return pl.pallas_call(
        functools.partial(dealt_columns_kernel, piece),
        out_shape=jax.ShapeDtypeStruct((GROUP, rows, columns // GROUP), x.dtype),
        in_specs=[VMEM],
        out_specs=VMEM,
        compiler_params=pltpu.CompilerParams(vmem_limit_bytes=32 * 2**20),
        cost_estimate=cost(2),
    )(x)


def home_kernel(pieces, got_ref, weight_ref, out_ref, gain_ref, more_ref):
    columns = weight_ref.shape[1] // GROUP // pieces
    more_ref[...] = jnp.zeros_like(more_ref)
    for sender in range(GROUP):
        for piece in range(pieces):
            lo = (piece * GROUP + sender) * columns
            out_ref[:, lo : lo + columns] = got_ref[
                sender, :, piece * columns : (piece + 1) * columns
            ].astype(f32)
        if got_ref.shape[2] > pieces * columns:
            more_ref[...] += got_ref[sender, :, pieces * columns :].astype(f32)
    gain_ref[...] = jnp.sum(out_ref[...] * weight_ref[...].astype(f32), axis=1, keepdims=True)


def home(got, weight, pieces):
    rows, columns = weight.shape
    return pl.pallas_call(
        functools.partial(home_kernel, pieces),
        out_shape=(
            jax.ShapeDtypeStruct((rows, columns), f32),
            jax.ShapeDtypeStruct((rows, 1), f32),
            jax.ShapeDtypeStruct((rows, 128), f32),
        ),
        in_specs=[VMEM, VMEM],
        out_specs=(VMEM, VMEM, VMEM),
        compiler_params=pltpu.CompilerParams(vmem_limit_bytes=32 * 2**20),
        cost_estimate=cost(5),
    )(got, weight)


TILE = 1024


def product_scatter_kernel(swaps, around, a_far, w_far, *refs):
    swap_refs, out_ref, swapped_refs = refs[:swaps], refs[swaps], refs[swaps + 1 : 2 * swaps + 1]
    near, far, away, going, send_sem, recv_sem, a_ref, w_ref, a_sem, w_sem = refs[
        2 * swaps + 1 : 2 * swaps + 11
    ]
    me, slot, step_core, first_step, second_step = places()
    first, second, mate = me + first_step, me + second_step, me + step_core
    core = lax.rem(slot, 2)
    others = plane_steps(
        step_core,
        (1 - core) * first_step + core * second_step,
        core * first_step + (1 - core) * second_step,
    )
    corner_step = first_step + second_step
    if around:
        own_places, mate_places = (3, 1, 2, 0), (7, 5, 6, 4)
    else:
        own_places = (slot + corner_step, slot + first_step, slot + second_step, slot)
        mate_slot = slot + step_core
        mate_places = (
            mate_slot + corner_step,
            mate_slot + second_step,
            mate_slot + first_step,
            mate_slot,
        )

    def a_load(place):
        return pltpu.make_async_copy(a_far.at[place], a_ref.at[place], a_sem.at[place])

    def w_load(i):
        at = pl.ds(i * TILE, TILE)
        return pltpu.make_async_copy(w_far.at[at, :], w_ref.at[at, :], w_sem.at[i])

    a_load(mate_places[0]).start()
    for i in range(out_ref.shape[1] // TILE):
        w_load(i).start()
    for place in (
        mate_places[2],
        own_places[0],
        own_places[2],
        mate_places[1],
        mate_places[3],
        own_places[3],
        own_places[1],
    ):
        a_load(place).start()
    greet([me + step for _, step in others] if swaps else (first, second, mate))
    sent = []

    def send(source, target, number, device):
        copy = remote(source, target, send_sem.at[number], recv_sem.at[number], device)
        copy.start()
        sent.append(copy)

    def arrived(ref, number, source):
        remote(ref, ref, send_sem.at[number], recv_sem.at[number], source).wait_recv()

    def product(place, extra, target):
        a_load(place).wait()

        def tile(i, _):
            at = pl.ds(pl.multiple_of(i * TILE, TILE), TILE)
            total = dot_nt(a_ref[place], w_ref[at, :])
            for ref in extra:
                total = total + ref[:, at].astype(f32)
            target[:, at] = total.astype(target.dtype)
            return 0

        lax.fori_loop(0, out_ref.shape[1] // TILE, tile, 0)

    def to_mate(kind):
        product(mate_places[kind], (), away.at[kind])
        send(away.at[kind], near.at[kind], kind, mate)

    def add(ref):
        def tile(i, _):
            at = pl.ds(pl.multiple_of(i * TILE, TILE), TILE)
            out_ref[:, at] = out_ref[:, at] + ref[:, at].astype(f32)
            return 0

        lax.fori_loop(0, out_ref.shape[1] // TILE, tile, 0)

    swapping, kept = [], []
    if swaps:
        swap_send, swap_recv, swap_own = refs[2 * swaps + 11 :]

    def start_swaps():
        for item in range(swaps):
            for number, step in others:
                copy = remote(
                    swap_refs[item].at[slot + step],
                    swapped_refs[item].at[slot],
                    swap_send.at[item, number - 1],
                    swap_recv.at[item, number - 1],
                    me + step,
                )
                copy.start()
                swapping.append(copy)
            copy = pltpu.make_async_copy(
                swap_refs[item].at[slot], swapped_refs[item].at[slot], swap_own.at[item]
            )
            copy.start()
            kept.append(copy)

    for i in range(out_ref.shape[1] // TILE):
        w_load(i).wait()
    to_mate(0)
    to_mate(2)
    arrived(near.at[0], 0, mate)
    product(own_places[0], (near.at[0],), going.at[0])
    send(going.at[0], far.at[0], 4, second)
    arrived(near.at[2], 2, mate)
    product(own_places[2], (near.at[2],), going.at[2])
    send(going.at[2], far.at[2], 5, second)
    start_swaps()
    to_mate(1)
    to_mate(3)
    arrived(near.at[3], 3, mate)
    product(own_places[3], (near.at[3],), out_ref)
    arrived(near.at[1], 1, mate)
    arrived(far.at[0], 4, second)
    product(own_places[1], (near.at[1], far.at[0]), going.at[1])
    send(going.at[1], far.at[1], 6, first)
    arrived(far.at[2], 5, second)
    add(far.at[2])
    arrived(far.at[1], 6, first)
    add(far.at[1])
    for item in range(swaps):
        for number, step in others:
            target = swapped_refs[item].at[slot + step]
            remote(
                target,
                target,
                swap_send.at[item, number - 1],
                swap_recv.at[item, number - 1],
                me + step,
            ).wait_recv()
    for copy in sent + swapping:
        copy.wait_send()
    for copy in kept:
        copy.wait()


def product_scatter(a, w, number, around, *swaps):
    _, rows, depth = a.shape
    columns = w.shape[0]
    count = len(swaps)
    swap_sems = [
        pltpu.SemaphoreType.DMA((count, GROUP - 1)),
        pltpu.SemaphoreType.DMA((count, GROUP - 1)),
        pltpu.SemaphoreType.DMA((count,)),
    ]
    return pl.pallas_call(
        functools.partial(product_scatter_kernel, count, around),
        out_shape=(jax.ShapeDtypeStruct((rows, columns), f32),)
        + tuple(jax.ShapeDtypeStruct(x.shape, x.dtype) for x in swaps),
        in_specs=[ANY, ANY] + [ANY] * count,
        out_specs=(VMEM,) + (ANY,) * count,
        scratch_shapes=[
            pltpu.VMEM((4, rows, columns), bf16),
            pltpu.VMEM((3, rows, columns), bf16),
            pltpu.VMEM((4, rows, columns), bf16),
            pltpu.VMEM((3, rows, columns), bf16),
            pltpu.SemaphoreType.DMA((7,)),
            pltpu.SemaphoreType.DMA((7,)),
            pltpu.VMEM(a.shape, bf16),
            pltpu.VMEM(w.shape, bf16),
            pltpu.SemaphoreType.DMA((GROUP,)),
            pltpu.SemaphoreType.DMA((columns // TILE,)),
        ]
        + (swap_sems if swaps else []),
        compiler_params=pltpu.CompilerParams(
            collective_id=number, has_side_effects=True, vmem_limit_bytes=56 * 2**20
        ),
        cost_estimate=cost(50),
    )(a, w, *swaps)


def gate_gather_kernel(
    own_ref,
    x_far,
    w_far,
    all_ref,
    gate_far,
    up_far,
    hidden_far,
    x_ref,
    w_ref,
    gate_ref,
    up_ref,
    hidden_ref,
    send_sem,
    recv_sem,
    own_sem,
    x_sem,
    w_sem,
    store_sem,
):
    me, slot, step_core, first_step, second_step = places()
    first, second, mate = me + first_step, me + second_step, me + step_core
    w_load = pltpu.make_async_copy(w_far, w_ref, w_sem)
    w_load.start()
    tiles, tile_rows = x_ref.shape[:2]
    half = gate_ref.shape[2]

    def rows_of(i):
        return pl.ds(pl.multiple_of(i * tile_rows, tile_rows), tile_rows)

    def x_load(i):
        return pltpu.make_async_copy(x_far.at[rows_of(i), :], x_ref.at[i], x_sem.at[i])

    for i in range(tiles):
        x_load(i).start()
    greet((first, second, mate))
    sent = []

    def send(source, number, device):
        copy = remote(
            source, all_ref.at[AROUND[number]], send_sem.at[number], recv_sem.at[number], device
        )
        copy.start()
        sent.append(copy)

    def arrived(number):
        target = all_ref.at[AROUND[number]]
        remote(target, target, send_sem.at[number], recv_sem.at[number], me).wait_recv()
        return target

    own = pltpu.make_async_copy(own_ref, all_ref.at[0], own_sem)
    send(own_ref, 0, first)
    send(own_ref, 1, second)
    send(own_ref, 2, mate)
    own.start()

    def stores(i, spot):
        return [
            pltpu.make_async_copy(near.at[spot], far.at[rows_of(i), :], store_sem.at[spot, number])
            for number, (near, far) in enumerate(
                ((gate_ref, gate_far), (up_ref, up_far), (hidden_ref, hidden_far))
            )
        ]

    def tile(i, _):
        spot = lax.rem(i, 2)
        x_load(i).wait()

        @pl.when(i >= 2)
        def _():
            for copy in stores(i - 2, spot):
                copy.wait()

        both = dot_nn(x_ref[i], w_ref[...])
        gate = both[:, :half]
        up = both[:, half:]
        gate_ref[spot] = gate
        up_ref[spot] = up
        hidden_ref[spot] = (gate * jax.nn.sigmoid(gate) * up).astype(bf16)
        for copy in stores(i, spot):
            copy.start()
        return 0

    w_load.wait()
    lax.fori_loop(0, tiles // 2, tile, 0)
    block = arrived(0)
    send(block, 3, second)
    send(block, 4, mate)
    send(arrived(1), 5, mate)
    lax.fori_loop(tiles // 2, tiles, tile, 0)
    for i in (tiles - 2, tiles - 1):
        for copy in stores(i, i % 2):
            copy.wait()
    send(arrived(3), 6, mate)
    for number in (2, 4, 5, 6):
        arrived(number)
    for copy in sent:
        copy.wait_send()
    own.wait()


def gate_gather(own, x, w, number):
    rows, columns = own.shape
    half = w.shape[1] // 2
    tiles = x.shape[0] // rows
    wide = jax.ShapeDtypeStruct((x.shape[0], half), f32)
    return pl.pallas_call(
        gate_gather_kernel,
        out_shape=(
            jax.ShapeDtypeStruct((GROUP, rows, columns), own.dtype),
            wide,
            wide,
            jax.ShapeDtypeStruct((x.shape[0], half), bf16),
        ),
        in_specs=[ANY, ANY, ANY],
        out_specs=(ANY, ANY, ANY, ANY),
        scratch_shapes=[
            pltpu.VMEM((tiles, rows, x.shape[1]), bf16),
            pltpu.VMEM(w.shape, bf16),
            pltpu.VMEM((2, rows, half), f32),
            pltpu.VMEM((2, rows, half), f32),
            pltpu.VMEM((2, rows, half), bf16),
            pltpu.SemaphoreType.DMA((7,)),
            pltpu.SemaphoreType.DMA((7,)),
            pltpu.SemaphoreType.DMA,
            pltpu.SemaphoreType.DMA((tiles,)),
            pltpu.SemaphoreType.DMA,
            pltpu.SemaphoreType.DMA((2, 3)),
        ],
        compiler_params=pltpu.CompilerParams(
            collective_id=number, has_side_effects=True, vmem_limit_bytes=56 * 2**20
        ),
        cost_estimate=cost(45),
    )(own, x, w)


def hidden_back_kernel(cot_ref, gate_ref, up_ref, w_ref, grad_ref):
    half = gate_ref.shape[1]
    d_hidden = dot_nn(cot_ref[...], w_ref[...])
    gate = gate_ref[...]
    sigmoid = jax.nn.sigmoid(gate)
    grad_ref[:, :half] = (
        d_hidden * up_ref[...] * sigmoid * (1.0 + gate * (1.0 - sigmoid))
    ).astype(bf16)
    grad_ref[:, half:] = (d_hidden * gate * sigmoid).astype(bf16)


def hidden_back(cot, gate, up, w):
    rows, columns = cot.shape
    half = w.shape[1]
    tile_rows = 256

    def tiles(width):
        return pl.BlockSpec((tile_rows, width), lambda i: (i, 0))

    return pl.pallas_call(
        hidden_back_kernel,
        grid=(rows // tile_rows,),
        in_specs=[
            tiles(columns),
            tiles(half),
            tiles(half),
            pl.BlockSpec(w.shape, lambda i: (0, 0)),
        ],
        out_specs=tiles(2 * half),
        out_shape=jax.ShapeDtypeStruct((rows, 2 * half), bf16),
        compiler_params=pltpu.CompilerParams(vmem_limit_bytes=56 * 2**20),
        cost_estimate=cost(20),
    )(cot, gate, up, w)


def away_product_kernel(x_ref, w_ref, out_ref):
    out_ref[...] = dot_nt(x_ref[...], w_ref[...]).astype(bf16)


def away_product(x, w, tile_rows):
    rows, depth = x.shape
    tiles = rows // tile_rows // 2
    return pl.pallas_call(
        away_product_kernel,
        grid=(tiles,),
        in_specs=[
            pl.BlockSpec((tile_rows, depth), lambda i: (tiles + i, 0)),
            pl.BlockSpec(w.shape, lambda i: (0, 0)),
        ],
        out_specs=pl.BlockSpec((tile_rows, w.shape[0]), lambda i: (i, 0)),
        out_shape=jax.ShapeDtypeStruct((rows // 2, w.shape[0]), bf16),
        compiler_params=pltpu.CompilerParams(vmem_limit_bytes=56 * 2**20),
        cost_estimate=cost(6),
    )(x, w)


def rows_product_kernel(x_ref, y_ref, *refs):
    out_ref = refs[-1]
    wide = y_ref.shape[1]
    out_ref[:, :wide] = dot_tn(x_ref[...], y_ref[...]).astype(bf16)
    for more_ref in refs[:-1]:
        out_ref[:, wide:] = more_ref[...]


def rows_product(x, y, micros, *more):
    rows, columns = x.shape
    wide = y.shape[1]
    tile_columns = 512
    more_wide = sum(m.shape[1] for m in more)
    return pl.pallas_call(
        rows_product_kernel,
        grid=(columns // tile_columns,),
        in_specs=[
            pl.BlockSpec((rows, tile_columns), lambda i: (0, i)),
            pl.BlockSpec((rows, wide), lambda i: (0, 0)),
        ]
        + [pl.BlockSpec((tile_columns, m.shape[1]), lambda i: (i, 0)) for m in more],
        out_specs=pl.BlockSpec((tile_columns, wide + more_wide), lambda i: (i, 0)),
        out_shape=jax.ShapeDtypeStruct((columns, wide + more_wide), bf16),
        compiler_params=pltpu.CompilerParams(vmem_limit_bytes=56 * 2**20),
        cost_estimate=cost(micros),
    )(x, y, *more)


def plane_permutes(device_count):
    first, second, mate = [], [], []
    for i in range(device_count):
        low_bit, high_bit = (2, 4) if i % 2 == 0 else (4, 2)
        first.append((i, i ^ low_bit))
        second.append((i, i ^ high_bit))
        mate.append((i, i ^ 1))
    return first, second, mate


def after(values, *earlier):
    return lax.optimization_barrier((values, earlier))[0]


def meet(*values):
    return lax.optimization_barrier(values)


def assemble_kernel(*refs):
    blocks, out_ref = refs[:GROUP], refs[GROUP]
    _, slot, step_core, first_step, second_step = places()
    corner_step = first_step + second_step
    here = (0, first_step, second_step, corner_step)
    there = (step_core, step_core + second_step, step_core + first_step, step_core + corner_step)
    for number, step in enumerate(here + there):
        out_ref[:, slot + step] = blocks[number][...]


def assemble(x, from_first, from_second, from_corner, mates):
    parts, rows, columns = x.shape
    return pl.pallas_call(
        assemble_kernel,
        out_shape=jax.ShapeDtypeStruct((parts, GROUP, rows, columns), x.dtype),
        in_specs=[VMEM] * GROUP,
        out_specs=VMEM,
        compiler_params=pltpu.CompilerParams(vmem_limit_bytes=32 * 2**20),
        cost_estimate=cost(8),
    )(x, from_first, from_second, from_corner, *mates)


class SlowScatter:
    def __init__(self, keep, away, device_count):
        self.keep = keep
        self.away = away
        self.first, self.second, self.mate = plane_permutes(device_count)

    def to_mate(self):
        return lax.ppermute(self.away, "fsdp", self.mate)

    def onward(self, near):
        return (self.keep(2, 2) + near[2:].astype(f32)).astype(bf16)

    def to_second(self, sums):
        return lax.ppermute(sums, "fsdp", self.second)

    def both(self, near, far):
        return (self.keep(1, 1)[0] + near[1].astype(f32) + far[1].astype(f32)).astype(bf16)

    def to_first(self, both):
        return lax.ppermute(both, "fsdp", self.first)

    def total(self, near, far, last):
        own = self.keep(0, 1)[0] + near[0].astype(f32)
        return own + far[0].astype(f32) + last.astype(f32)


def low(values):
    return values.astype(bf16).astype(f32)


def gates(proj_ref, floor_ref, rows, head, heads):
    dim = floor_ref.shape[1] // heads
    wide = heads * dim
    lo = head * dim
    q_pre = proj_ref[rows, lo : lo + dim]
    f_pre = proj_ref[rows, wide + lo : wide + lo + dim]
    value = proj_ref[rows, 2 * wide + lo : 2 * wide + lo + dim].astype(bf16)
    floor = floor_ref[:, lo : lo + dim]
    q_sigmoid = jax.nn.sigmoid(q_pre)
    query = low(q_pre * q_sigmoid)
    f_sigmoid = jax.nn.sigmoid(f_pre)
    forget = floor + (1.0 - floor) * f_sigmoid
    key = low(1.0 - forget)
    row = lax.broadcasted_iota(jnp.int32, (CHUNK, dim), 0)
    in_half = lax.rem(row, HALF)
    product = forget
    step = 1
    while step < HALF:
        product = jnp.where(in_half >= step, product * pltpu.roll(product, step, 0), product)
        step *= 2
    middle = product[HALF - 1 : HALF, :]
    end = product[CHUNK - 1 : CHUNK, :]
    ratio = jnp.where(row < HALF, product / middle, product)
    inverse = 1.0 / ratio
    return {
        "q_pre": q_pre,
        "q_sigmoid": q_sigmoid,
        "f_sigmoid": f_sigmoid,
        "forget": forget,
        "value": value,
        "floor": floor,
        "middle": middle,
        "end": end,
        "ratio": ratio,
        "inverse": inverse,
        "row": row,
        "query_mid": query * ratio,
        "key_mid": key * inverse,
    }


def whole_fade(g, last):
    return g["middle"] * g["end"] * jnp.where(last < 0, 1.0, 0.0)


def tail_keys(g, last):
    return jnp.where(g["row"] >= last, g["key_mid"] * g["end"], 0.0).astype(bf16)


def entry_queries(g, carried):
    return jnp.where(carried, g["query_mid"] * g["middle"], 0.0).astype(bf16)


def next_state(g, last, state):
    return state * whole_fade(g, last) + dot_tn(g["value"], tail_keys(g, last))


def forward_kernel(
    heads, last_ref, proj_ref, start_ref, floor_ref, gain_ref, in_ref, mix_ref, out_ref, enter_ref, state
):
    dim = floor_ref.shape[1] // heads
    chunks = proj_ref.shape[0] // CHUNK
    tile = pl.program_id(0)

    @pl.when(tile == 0)
    def _():
        state[...] = in_ref[...]

    def step(n, _):
        base = pl.multiple_of(n * CHUNK, CHUNK)
        rows = pl.ds(base, CHUNK)
        place = (tile * chunks + n) * CHUNK
        starts = start_ref[rows, :] - place
        last = last_ref[tile * chunks + n] - place
        column = lax.broadcasted_iota(jnp.int32, (CHUNK, CHUNK), 1)
        line = lax.broadcasted_iota(jnp.int32, (CHUNK, CHUNK), 0)
        within = (column <= line) & (column >= starts)
        carried = starts < 0
        for head in range(heads):
            lo = head * dim
            g = gates(proj_ref, floor_ref, rows, head, heads)
            now = state[head]
            enter_ref[n, head] = now
            scores = dot_nt(g["query_mid"].astype(bf16), g["key_mid"].astype(bf16))
            scores = jnp.where(within, scores, 0.0).astype(bf16)
            out = dot_nn(scores, g["value"]) + dot_nt(entry_queries(g, carried), now.astype(bf16))
            state[head] = next_state(g, last, now)
            out_ref[rows, lo : lo + dim] = out
            mix_ref[rows, lo : lo + dim] = (
                out * inverse_rms(out) * gain_ref[:, lo : lo + dim]
            ).astype(bf16)
        return 0

    lax.fori_loop(0, chunks, step, 0, unroll=UNROLL)


def last_state_kernel(heads, last_ref, proj_ref, floor_ref, out_ref):
    for head in range(heads):
        state = jnp.zeros(out_ref.shape[1:], f32)
        for n in range(proj_ref.shape[0] // CHUNK):
            g = gates(proj_ref, floor_ref, pl.ds(n * CHUNK, CHUNK), head, heads)
            state = next_state(g, last_ref[n] - n * CHUNK, state)
        out_ref[head] = state


def state_grad(out_ref, dmix_ref, gain_ref, rows, lo, dim):
    out = out_ref[rows, lo : lo + dim]
    inverse = inverse_rms(out)
    scaled = out * inverse
    dmix = dmix_ref[rows, lo : lo + dim].astype(f32)
    return rms_back(dmix * gain_ref[:, lo : lo + dim], scaled, inverse)


def backward_chunk(heads, n, at, refs, outs, later, before=0):
    last_ref, proj_ref, start_ref, floor_ref, gain_ref, out_ref, dmix_ref, enter_ref = refs
    dproj_ref, dfloor_ref = outs
    dim = floor_ref.shape[1] // heads
    wide = heads * dim
    base = n * CHUNK
    rows = pl.ds(base, CHUNK)
    place = (before + n) * CHUNK
    starts = start_ref[rows, :] - place
    last = last_ref[before + n] - place
    column = lax.broadcasted_iota(jnp.int32, (CHUNK, CHUNK), 1)
    line = lax.broadcasted_iota(jnp.int32, (CHUNK, CHUNK), 0)
    within = (column <= line) & (column >= starts)
    carried = starts < 0
    for head in range(heads):
        lo = head * dim
        g = gates(proj_ref, floor_ref, rows, head, heads)
        grad = state_grad(out_ref, dmix_ref, gain_ref, rows, lo, dim)
        grad_hi = grad.astype(bf16)
        grad_lo = (grad - grad_hi.astype(f32)).astype(bf16)
        state = enter_ref[n, head]
        after = later[head]
        after_low = after.astype(bf16)
        query_mid = g["query_mid"].astype(bf16)
        key_mid = g["key_mid"].astype(bf16)
        scores = jnp.where(within, dot_nt(query_mid, key_mid), 0.0).astype(bf16)
        d_scores = dot_nt(grad_hi, g["value"]) + dot_nt(grad_lo, g["value"])
        d_scores = jnp.where(within, d_scores, 0.0).astype(bf16)
        query_in = entry_queries(g, carried)
        key_out = tail_keys(g, last)
        d_query_mid = dot_nn(d_scores, key_mid)
        d_query_in = jnp.where(carried, dot_nn(grad_hi, state.astype(bf16)), 0.0)
        d_key_mid = dot_tn(d_scores, query_mid)
        d_key_out = jnp.where(g["row"] >= last, dot_nn(g["value"], after_low), 0.0)
        d_value = dot_tn(scores, grad_hi) + dot_nt(key_out, after_low)
        d_query = (d_query_mid + d_query_in * g["middle"]) * g["ratio"]
        d_key = (d_key_mid + d_key_out * g["end"]) * g["inverse"]
        tail = d_key_out * key_out.astype(f32)
        term = (
            d_query_mid * query_mid.astype(f32)
            + d_query_in * query_in.astype(f32)
            - d_key_mid * key_mid.astype(f32)
            - tail
        )
        fade = whole_fade(g, last)
        final = jnp.sum(tail, axis=0, keepdims=True) + fade * jnp.sum(
            state * after, axis=0, keepdims=True
        )
        step_rows = 1
        while step_rows < CHUNK:
            term = jnp.where(
                g["row"] < CHUNK - step_rows,
                term + pltpu.roll(term, CHUNK - step_rows, 0),
                term,
            )
            step_rows *= 2
        d_forget = (term + final) / g["forget"] - d_key
        q_sigmoid, f_sigmoid = g["q_sigmoid"], g["f_sigmoid"]
        d_q_pre = d_query * q_sigmoid * (1.0 + g["q_pre"] * (1.0 - q_sigmoid))
        d_floor = d_forget * (1.0 - f_sigmoid)
        d_f_pre = d_floor * (1.0 - g["floor"]) * f_sigmoid
        dproj_ref[at, lo : lo + dim] = d_q_pre.astype(bf16)
        dproj_ref[at, wide + lo : wide + lo + dim] = d_f_pre.astype(bf16)
        dproj_ref[at, 2 * wide + lo : 2 * wide + lo + dim] = d_value.astype(bf16)
        dfloor_ref[:, lo : lo + dim] += jnp.sum(d_floor, axis=0, keepdims=True)
        later[head] = after * fade + dot_tn(grad_hi, query_in)


def backward_rest(heads, n, refs, later, before=0):
    last_ref, proj_ref, start_ref, floor_ref, gain_ref, out_ref, dmix_ref = refs
    dim = floor_ref.shape[1] // heads
    rows = pl.ds(n * CHUNK, CHUNK)
    for head in range(heads):
        g = gates(proj_ref, floor_ref, rows, head, heads)
        grad = state_grad(out_ref, dmix_ref, gain_ref, rows, head * dim, dim)
        place = (before + n) * CHUNK
        queries = entry_queries(g, start_ref[rows, :] < place)
        fade = whole_fade(g, last_ref[before + n] - place)
        later[head] = later[head] * fade + dot_tn(grad.astype(bf16), queries)


def backward_kernel(heads, *refs):
    ins, outs, later = refs[:8], refs[8:10], refs[10]
    chunks = ins[1].shape[0] // CHUNK
    edge = MAXLEN // CHUNK
    tile = pl.num_programs(0) - 1 - pl.program_id(0)
    before = tile * chunks

    def step(i, first):
        n = first - i
        at = pl.ds(pl.multiple_of(n * CHUNK, CHUNK), CHUNK)
        backward_chunk(heads, n, at, ins, outs, later, before)
        return first

    @pl.when(pl.program_id(0) == 0)
    def _():
        later[...] = jnp.zeros_like(later)
        outs[1][...] = jnp.zeros_like(outs[1])
        for n in range(chunks - 1, chunks - 1 - edge, -1):
            backward_rest(heads, n, ins[:7], later, before)
        lax.fori_loop(0, chunks - edge, step, chunks - 1 - edge, unroll=UNROLL)

    @pl.when(pl.program_id(0) != 0)
    def _():
        lax.fori_loop(0, chunks, step, chunks - 1, unroll=UNROLL)


def backward_edge_kernel(heads, *refs):
    ins, in_ref, _, outs, later = refs[:8], refs[8], refs[9], refs[10:12], refs[12]
    later[...] = in_ref[...]
    outs[1][...] = jnp.zeros_like(outs[1])
    edge = MAXLEN // CHUNK
    before = ins[0].shape[0] - edge
    for n in range(edge - 1, -1, -1):
        backward_chunk(heads, n, pl.ds(n * CHUNK, CHUNK), ins, outs, later, before)


def first_grad_kernel(heads, *refs):
    ins, grad_ref = refs[:7], refs[7]
    grad_ref[...] = jnp.zeros_like(grad_ref)
    for n in range(ins[1].shape[0] // CHUNK - 1, -1, -1):
        backward_rest(heads, n, ins, grad_ref)


def local_call(kernel, heads, micros, out_shape, scratch, *operands):
    return pl.pallas_call(
        functools.partial(kernel, heads),
        out_shape=out_shape,
        in_specs=[SMEM] + [VMEM] * (len(operands) - 1),
        out_specs=jax.tree.map(lambda _: VMEM, out_shape),
        scratch_shapes=scratch,
        compiler_params=pltpu.CompilerParams(vmem_limit_bytes=56 * 2**20),
        cost_estimate=cost(micros),
    )(*operands)


def body(
    tokens,
    cotangent,
    dealt_lengths,
    deal,
    norm_gain,
    mixer_in,
    forget_floor,
    group_gain,
    out_proj,
    ffn_gain,
    gate_up,
    down_proj,
):
    row_count, width = tokens.shape
    weight_rows = mixer_in.shape[0]
    device_count = lax.axis_size("fsdp")
    groups = device_count // GROUP
    own_index = lax.axis_index("fsdp")
    slot = lax.rem(own_index, GROUP)
    group = own_index // GROUP
    group_rows = GROUP * row_count
    heads = HEADS // GROUP
    own_width = width // GROUP
    dim = width // HEADS
    ffn_width = down_proj.shape[1]
    own_ffn = ffn_width // GROUP
    planes = [[g * GROUP + s for s in range(GROUP)] for g in range(groups)]
    lines = [[g * GROUP + s for g in range(groups)] for s in range(GROUP)]

    def line_gather(x):
        return lax.all_gather(x, "fsdp", axis=0, axis_index_groups=lines, tiled=True)

    def line_scatter(x):
        return lax.psum_scatter(
            x, "fsdp", scatter_dimension=0, axis_index_groups=lines, tiled=True
        )

    def whole_rows(x):
        return line_gather(x.reshape(GROUP * weight_rows, -1))

    low_step = 2 - 4 * (slot // 2 % 2)
    high_step = 4 - 8 * (slot // 4)
    odd = slot % 2
    moves = (
        slot,
        1 - 2 * odd,
        jnp.where(odd == 0, low_step, high_step),
        jnp.where(odd == 0, high_step, low_step),
    )

    seq_count = deal.shape[0]
    seq_ids = jnp.arange(seq_count, dtype=jnp.int32)
    matches = deal[:, None] == seq_ids[None, :]
    lengths = jnp.sum(jnp.where(matches, dealt_lengths[:, None], 0), axis=0)
    seq_starts = jnp.sum(
        jnp.where(seq_ids[:, None] < seq_ids[None, :], lengths[:, None], 0), axis=0
    )
    group_start = group * group_rows
    rows_here = group_start + jnp.arange(group_rows, dtype=jnp.int32)
    starts = (
        jnp.max(jnp.where(seq_starts[None, :] <= rows_here[:, None], seq_starts[None, :], 0), axis=1)
        - group_start
    )
    start_column = starts[:, None]
    last_starts = starts[CHUNK - 1 :: CHUNK]

    out_lines = lax.all_gather(out_proj, "fsdp", axis=0, axis_index_groups=lines)
    gain_block = jnp.zeros((16, 128), bf16)
    for number, gain in enumerate((norm_gain, forget_floor, group_gain, ffn_gain)):
        gain_block = gain_block.at[number, :weight_rows].set(gain)
    gain_blocks, mixer_swapped = exchange(
        0, 15, ("all", gain_block), ("swap", by_owner(mixer_in, 3))
    )
    mixer_weight = whole_rows(mixer_swapped)
    gains = (
        gain_blocks[:, :, :4, :weight_rows].transpose(2, 0, 1, 3).reshape(4, width).astype(f32)
    )
    first_gain = gains[0:1]
    second_gain = gains[3:4]
    own_gains = lax.dynamic_slice_in_dim(gains, slot * own_width, own_width, 1)
    own_floor = own_gains[1:2]
    own_group_gain = own_gains[2:3]

    inputs = tokens.astype(f32)
    first_inverse = inverse_rms(inputs)
    first_scaled = inputs * first_inverse
    first_normed = (first_scaled * first_gain).astype(bf16)
    late_gate_up, late_down = after((gate_up, down_proj), mixer_swapped)
    first_all, ffn_swapped, down_swapped = exchange(
        1,
        58,
        ("gather", first_normed[None]),
        ("swap", by_owner(late_gate_up, 2)),
        ("swap", by_owner(late_down, 1)),
    )
    first_all = first_all.reshape(group_rows, width)
    ffn_weight = whole_rows(ffn_swapped)
    first, second, mate = plane_permutes(device_count)
    out_own = after(out_lines, first_all)
    from_first = lax.ppermute(out_own, "fsdp", first)
    from_second = lax.ppermute(out_own, "fsdp", second)
    tail_projected = dot_nn(first_all[group_rows - MAXLEN :], mixer_weight)
    edge = MAXLEN // CHUNK
    state_type = jax.ShapeDtypeStruct((heads, dim, dim), f32)
    last_state = local_call(
        last_state_kernel,
        heads,
        3,
        state_type,
        [],
        last_starts[-edge:] - (group_rows - MAXLEN),
        tail_projected,
        own_floor,
    )
    up_line = [(i, i + GROUP) for i in range(device_count - GROUP)]
    down_line = [(i + GROUP, i) for i in range(device_count - GROUP)]
    entering_state = lax.ppermute(last_state, "fsdp", up_line)
    projected = dot_nn(after(first_all, last_state), mixer_weight)
    projected, entering_state, from_first, from_second = meet(
        projected, entering_state, from_first, from_second
    )
    from_corner = lax.ppermute(from_first, "fsdp", second)
    mates = [lax.ppermute(block, "fsdp", mate) for block in (out_own, from_first, from_second)]
    chunks = group_rows // CHUNK
    tile_count = group_rows // TILE_ROWS

    def row_tiles(columns, turned=False):
        return pl.BlockSpec(
            (TILE_ROWS, columns), lambda i: (tile_count - 1 - i if turned else i, 0)
        )

    def state_tiles(turned=False):
        return pl.BlockSpec(
            (TILE_ROWS // CHUNK, heads, dim, dim),
            lambda i: (tile_count - 1 - i if turned else i, 0, 0, 0),
        )

    state_scratch = pltpu.VMEM((heads, dim, dim), f32)
    mixed_heads, state_out, entering = pl.pallas_call(
        functools.partial(forward_kernel, heads),
        grid=(tile_count,),
        out_shape=(
            jax.ShapeDtypeStruct((group_rows, own_width), bf16),
            jax.ShapeDtypeStruct((group_rows, own_width), f32),
            jax.ShapeDtypeStruct((chunks, heads, dim, dim), f32),
        ),
        in_specs=[SMEM, row_tiles(3 * own_width), row_tiles(1), VMEM, VMEM, VMEM],
        out_specs=(row_tiles(own_width), row_tiles(own_width), state_tiles()),
        scratch_shapes=[state_scratch],
        compiler_params=pltpu.CompilerParams(vmem_limit_bytes=56 * 2**20),
        cost_estimate=cost(18),
    )(last_starts, projected, start_column, own_floor, own_group_gain, entering_state)
    mixed_heads, from_corner = meet(mixed_heads, from_corner)
    mates = mates + [lax.ppermute(from_corner, "fsdp", mate)]
    [mixer_input] = exchange(
        3, 15, ("widen", mixed_heads.reshape(GROUP, row_count, own_width))
    )
    mixer_input, mates = meet(mixer_input, mates)
    _, step_core, first_step, second_step = moves
    steps = (0, first_step, second_step, first_step + second_step)
    mate_steps = [step_core + steps[kind] for kind in (0, 2, 1, 3)]
    mixer_blocks = dealt_columns(mixer_input, weight_rows)
    mixer_around = [
        lax.dynamic_index_in_dim(mixer_blocks, slot + step, 0) for step in (*steps, *mate_steps)
    ]
    mixer_keep = jnp.concatenate(mixer_around[:4])
    mixer_away = jnp.concatenate(mixer_around[4:])
    out_weight = assemble(out_own, from_first, from_second, from_corner, mates).reshape(width, width)
    down_weight = whole_rows(after(down_swapped, mixed_heads))
    residual = inputs + dot_nn(mixer_input, out_weight)
    second_inverse = inverse_rms(residual)
    second_scaled = residual * second_inverse
    second_normed = (second_scaled * second_gain).astype(bf16)
    second_normed, mixer_keep, mixer_away = meet(second_normed, mixer_keep, mixer_away)
    [second_all] = exchange(2, 43, ("around", second_normed[None]))
    second_all = second_all.reshape(group_rows, width)
    cot_blocks, gate_part, up_part, hidden_act = gate_gather(
        cotangent, second_all, ffn_weight, 6
    )
    cot_all = cot_blocks.reshape(group_rows, width)
    down_grad = rows_product(cot_all, hidden_act, 11)
    down_summed = line_scatter(down_grad)
    hidden_act = after(hidden_act, down_grad)

    def ffn_blocks(begin, number):
        rows = hidden_act[begin * row_count : (begin + number) * row_count]
        return dot_nt(rows, down_weight).reshape(number, row_count, width)

    ffn_away = away_product(hidden_act, down_weight, row_count).reshape(4, row_count, width)
    ffn_sum = SlowScatter(ffn_blocks, ffn_away, device_count)
    ffn_near = ffn_sum.to_mate()
    d_gate_pre = hidden_back(after(cot_all, ffn_away), gate_part, up_part, down_weight)
    d_gate_pre, ffn_near = meet(d_gate_pre, ffn_near)
    ffn_sums = ffn_sum.onward(ffn_near)
    ffn_grad = rows_product(after(second_all, ffn_sums), d_gate_pre, 18)
    ffn_grad, ffn_far = meet(ffn_grad, ffn_sum.to_second(ffn_sums))
    ffn_both = ffn_sum.both(ffn_near, ffn_far)
    ffn_summed = line_scatter(ffn_grad)
    [d_second] = product_scatter(
        d_gate_pre.reshape(GROUP, row_count, -1), after(ffn_weight, ffn_grad, ffn_both), 4, True
    )
    d_second, ffn_last, down_summed = meet(d_second, ffn_sum.to_first(ffn_both), down_summed)

    d_residual = cotangent.astype(f32) + rms_back(
        d_second * second_gain, second_scaled, second_inverse
    )
    d_mix_out = d_residual.astype(bf16)

    def out_blocks(blocks):
        return lax.dot_general(
            blocks, d_mix_out, (((1,), (0,)), ((), ())), preferred_element_type=f32
        )

    out_away = out_blocks(mixer_away).astype(bf16)
    out_sum = SlowScatter(
        lambda begin, number: out_blocks(mixer_keep[begin : begin + number]), out_away, device_count
    )
    out_near = out_sum.to_mate()
    d_mixer_input = dot_nt(after(d_mix_out, out_away), out_weight).astype(bf16)
    [d_mixed_heads] = exchange(5, 15, ("narrow", d_mixer_input))
    d_mixed_heads, out_near = meet(d_mixed_heads.reshape(group_rows, own_width), out_near)
    operands = (projected, start_column, own_floor, own_group_gain, state_out, d_mixed_heads)

    def edge_specs(place):
        def rows(columns):
            return pl.BlockSpec((MAXLEN, columns), lambda i: (place, 0))

        return [rows(3 * own_width), rows(1), VMEM, VMEM, rows(own_width), rows(own_width)]

    first_grad = pl.pallas_call(
        functools.partial(first_grad_kernel, heads),
        grid=(1,),
        out_shape=state_type,
        in_specs=[SMEM] + edge_specs(0),
        out_specs=VMEM,
        compiler_params=pltpu.CompilerParams(vmem_limit_bytes=56 * 2**20),
        cost_estimate=cost(3),
    )(last_starts, *operands)
    entering_grad = lax.ppermute(first_grad, "fsdp", down_line)
    out_near = after(out_near, first_grad)
    out_far = out_sum.to_second(out_sum.onward(out_near))
    dproj_type = jax.ShapeDtypeStruct((group_rows, 3 * own_width), bf16)
    dfloor_type = jax.ShapeDtypeStruct((1, own_width), f32)
    d_projected, floor_most = pl.pallas_call(
        functools.partial(backward_kernel, heads),
        grid=(tile_count,),
        out_shape=(dproj_type, dfloor_type),
        in_specs=[
            SMEM,
            row_tiles(3 * own_width, True),
            row_tiles(1, True),
            VMEM,
            VMEM,
            row_tiles(own_width, True),
            row_tiles(own_width, True),
            state_tiles(True),
        ],
        out_specs=(row_tiles(3 * own_width, True), VMEM),
        scratch_shapes=[state_scratch],
        compiler_params=pltpu.CompilerParams(vmem_limit_bytes=56 * 2**20),
        cost_estimate=cost(30),
    )(last_starts, *operands, entering)
    d_projected, entering_grad = meet(d_projected, entering_grad)
    last_tile = group_rows // MAXLEN - 1
    d_projected, floor_rest = pl.pallas_call(
        functools.partial(backward_edge_kernel, heads),
        grid=(1,),
        out_shape=(dproj_type, dfloor_type),
        in_specs=[SMEM]
        + edge_specs(last_tile)
        + [pl.BlockSpec((edge, heads, dim, dim), lambda i: (last_tile, 0, 0, 0)), VMEM, ANY],
        out_specs=(
            pl.BlockSpec((MAXLEN, 3 * own_width), lambda i: (last_tile, 0)),
            VMEM,
        ),
        scratch_shapes=[state_scratch],
        input_output_aliases={9: 0},
        compiler_params=pltpu.CompilerParams(vmem_limit_bytes=56 * 2**20),
        cost_estimate=cost(4),
    )(last_starts, *operands, entering, entering_grad, d_projected)
    d_projected, out_far = meet(d_projected, out_far)
    out_both = out_sum.both(out_near, out_far)
    d_projected = after(d_projected, out_both)
    floor_grad = floor_most + floor_rest
    by_sender = (GROUP, weight_rows, -1)
    floor_column = lax.dynamic_update_slice_in_dim(
        jnp.zeros((width, 128), f32), jnp.pad(floor_grad.T, ((0, 0), (0, 127))), slot * own_width, 0
    ).astype(bf16)
    mixer_grad = rows_product(first_all, d_projected, 11, floor_column)
    mixer_summed = line_scatter(mixer_grad)
    d_first, ffn_swapped = product_scatter(
        d_projected.reshape(GROUP, row_count, -1),
        after(mixer_weight, mixer_grad),
        8,
        False,
        ffn_summed.reshape(by_sender),
    )
    d_first, mixer_summed, out_last = meet(d_first, mixer_summed, out_sum.to_first(out_both))
    out_total = out_sum.total(out_near, out_far, out_last).astype(bf16)
    out_summed = line_scatter(out_total.reshape(groups * weight_rows, width))

    def swap(x):
        x = x.reshape(by_sender)
        return lax.all_to_all(x, "fsdp", 0, 0, axis_index_groups=planes, tiled=True)

    mixer_swapped = swap(mixer_summed)
    down_swapped = swap(after(down_summed, d_first))
    layer_out = residual + ffn_sum.total(ffn_near, ffn_far, after(ffn_last, d_first))
    d_gate_up, ffn_gain_sum, _ = home(ffn_swapped, gate_up, 2)
    d_mixer_in, norm_gain_sum, d_forget_floor = home(mixer_swapped, mixer_in, 3)
    d_down_proj, _, _ = home(down_swapped, down_proj, 1)
    d_out_proj = out_summed.astype(f32)
    d_dealt = d_residual + rms_back(d_first * first_gain, first_scaled, first_inverse)

    group_gain_sum = jnp.sum(out_proj.astype(f32) * d_out_proj, axis=1)
    return (
        layer_out,
        d_dealt,
        norm_gain_sum[:, 0] / norm_gain.astype(f32),
        d_mixer_in,
        d_forget_floor[:, 0],
        group_gain_sum / group_gain.astype(f32),
        d_out_proj,
        ffn_gain_sum[:, 0] / ffn_gain.astype(f32),
        d_gate_up,
        d_down_proj,
    )


def solution(mesh):
    by_rows = P("fsdp", None)
    by_one = P("fsdp")
    return jax.shard_map(
        body,
        mesh=mesh,
        in_specs=(
            by_rows,
            by_rows,
            P(),
            P(),
            by_one,
            by_rows,
            by_one,
            by_one,
            by_rows,
            by_one,
            by_rows,
            by_rows,
        ),
        out_specs=(
            by_rows,
            by_rows,
            by_one,
            by_rows,
            by_one,
            by_one,
            by_rows,
            by_one,
            by_rows,
            by_rows,
        ),
        check_vma=False,
    )
```

```python
import functools

import jax
import jax.numpy as jnp
from jax import lax
from jax.experimental import pallas as pl
from jax.experimental.pallas import tpu as pltpu
from jax.sharding import PartitionSpec as P

HEADS = 16
CHUNK = 64
HALF = 32
TILE_ROWS = 512
UNROLL = 2
MAXLEN = 128
GROUP = 8
MESH_ID = pl.DeviceIdType.MESH
VMEM = pl.BlockSpec(memory_space=pltpu.VMEM)
SMEM = pl.BlockSpec(memory_space=pltpu.SMEM)
ANY = pl.BlockSpec(memory_space=pl.ANY)

norm_eps = 1e-05
f32 = jnp.float32
bf16 = jnp.bfloat16


def inverse_rms(values):
    return lax.rsqrt(jnp.mean(values * values, axis=-1, keepdims=True) + norm_eps)


def rms_back(grad_scaled, scaled, inverse):
    return inverse * (grad_scaled - scaled * jnp.mean(grad_scaled * scaled, axis=-1, keepdims=True))


def dot_nt(left, right):
    return lax.dot_general(left, right, (((1,), (1,)), ((), ())), preferred_element_type=f32)


def dot_nn(left, right):
    return lax.dot_general(left, right, (((1,), (0,)), ((), ())), preferred_element_type=f32)


def dot_tn(left, right):
    return lax.dot_general(left, right, (((0,), (0,)), ((), ())), preferred_element_type=f32)


def cost(micros):
    return pl.CostEstimate(flops=0, transcendentals=0, bytes_accessed=int(micros * 36_900))


def places():
    me = lax.axis_index("fsdp")
    slot = lax.rem(me, GROUP)
    core = lax.rem(slot, 2)
    step_low = 2 - 4 * lax.rem(slot // 2, 2)
    step_high = 4 - 8 * (slot // 4)
    step_core = 1 - 2 * core
    first_step = (1 - core) * step_low + core * step_high
    second_step = core * step_low + (1 - core) * step_high
    return me, slot, step_core, first_step, second_step


def greet(others):
    barrier = pltpu.get_barrier_semaphore()
    for other in others:
        pl.semaphore_signal(barrier, inc=1, device_id=(other,), device_id_type=MESH_ID)
    pl.semaphore_wait(barrier, len(others))


def remote(source, target, send_sem, recv_sem, device):
    return pltpu.make_async_remote_copy(
        src_ref=source,
        dst_ref=target,
        send_sem=send_sem,
        recv_sem=recv_sem,
        device_id=(device,),
        device_id_type=MESH_ID,
    )


def plane_steps(step_core, step_low, step_high):
    return [
        (number, (number & 1) * step_core + ((number >> 1) & 1) * step_low + (number >> 2) * step_high)
        for number in range(1, GROUP)
    ]


AROUND = (1, 2, 4, 3, 5, 6, 7)


def exchange_kernel(plan, *refs):
    count = len(plan)
    ins, outs = refs[:count], refs[count : 2 * count]
    send_sem, recv_sem, own_sem = refs[2 * count :]
    me, slot, step_core, first_step, second_step = places()
    core = lax.rem(slot, 2)
    step_low = (1 - core) * first_step + core * second_step
    step_high = core * first_step + (1 - core) * second_step
    others = plane_steps(step_core, step_low, step_high)
    group = me // GROUP
    groups = lax.axis_size("fsdp") // GROUP
    greeted = [me + first_step, me + second_step, me + step_core]
    if not set(plan) <= {"gather", "around"}:
        greeted = [me + step for _, step in others]
    line = []
    if "all" in plan:
        line = [
            (
                number,
                lax.rem(group + number, groups) * GROUP + slot,
                lax.rem(group + groups - number, groups),
            )
            for number in range(1, groups)
        ]
        greeted = greeted + [target for _, target, _ in line]
    greet(greeted)
    sent = []

    def copy_of(item, source, target, number, device):
        return remote(source, target, send_sem.at[item, number], recv_sem.at[item, number], device)

    def send(item, source, target, number, device):
        copy = copy_of(item, source, target, number, device)
        copy.start()
        sent.append(copy)

    def arrived(item, target, number):
        copy_of(item, target, target, number, me).wait_recv()

    def keep(item, source, target):
        copy = pltpu.make_async_copy(source, target, own_sem.at[item])
        copy.start()
        return copy

    def block(item, place):
        kind, out = plan[item], outs[item]
        if kind == "widen":
            columns = out.shape[1] // GROUP
            return out.at[:, pl.ds(pl.multiple_of(place * columns, columns), columns)]
        if kind in ("gather", "around"):
            return out.at[:, place]
        return out.at[place]

    def landing(item, place, number):
        return block(item, AROUND[number] if plan[item] == "around" else place)

    def piece(item, place):
        if plan[item] == "narrow":
            columns = ins[item].shape[1] // GROUP
            return ins[item].at[:, pl.ds(pl.multiple_of(place * columns, columns), columns)]
        return ins[item].at[place]

    own = []
    for item, kind in enumerate(plan):
        if kind == "all":
            keep(item, ins[item], outs[item].at[group, slot]).wait()
            for number, target, _ in line:
                send(item, ins[item], outs[item].at[group, slot], GROUP - 1 + number, target)
        elif kind in ("gather", "around"):
            for number, step in enumerate((first_step, second_step, step_core)):
                send(item, ins[item], landing(item, slot, number), number, me + step)
            own.append(keep(item, ins[item], block(item, 0 if kind == "around" else slot)))
    for item, kind in enumerate(plan):
        if kind in ("swap", "widen", "narrow"):
            for number, step in others:
                send(item, piece(item, slot + step), block(item, slot), number - 1, me + step)
            own.append(keep(item, piece(item, slot), block(item, slot)))
    for item, kind in enumerate(plan):
        if kind == "all":
            for number, _, sender in line:
                arrived(item, outs[item].at[sender, slot], GROUP - 1 + number)
            for number, step in others:
                send(item, outs[item].at[:, slot], outs[item].at[:, slot], number - 1, me + step)
    corner_step = first_step + second_step
    for item, kind in enumerate(plan):
        if kind in ("gather", "around"):
            for place, number, onward in (
                (slot + first_step, 0, ((3, second_step), (4, step_core))),
                (slot + second_step, 1, ((5, step_core),)),
                (slot + corner_step, 3, ((6, step_core),)),
            ):
                here = landing(item, place, number)
                arrived(item, here, number)
                for then, step in onward:
                    send(item, here, landing(item, place, then), then, me + step)
    for item, kind in enumerate(plan):
        if kind in ("gather", "around"):
            for step, number in ((0, 2), (second_step, 4), (first_step, 5), (corner_step, 6)):
                arrived(item, landing(item, slot + step_core + step, number), number)
        elif kind == "all":
            for number, step in others:
                arrived(item, outs[item].at[:, slot + step], number - 1)
        else:
            for number, step in others:
                arrived(item, block(item, slot + step), number - 1)
    for copy in sent:
        copy.wait_send()
    for copy in own:
        copy.wait()


def exchange(number, micros, *items):
    groups = lax.axis_size("fsdp") // GROUP
    kinds = [kind for kind, _ in items]
    arrays = [array for _, array in items]
    shapes = []
    for kind, array in items:
        if kind in ("gather", "around"):
            shape = (array.shape[0], GROUP) + array.shape[1:]
        elif kind == "swap":
            shape = array.shape
        elif kind == "widen":
            shape = (array.shape[1], GROUP * array.shape[2])
        elif kind == "narrow":
            shape = (GROUP, array.shape[0], array.shape[1] // GROUP)
        else:
            shape = (groups, GROUP) + array.shape
        shapes.append(jax.ShapeDtypeStruct(shape, array.dtype))
    numbers = GROUP - 1 + (groups if "all" in kinds else 0)
    return pl.pallas_call(
        functools.partial(exchange_kernel, kinds),
        out_shape=tuple(shapes),
        in_specs=[ANY] * len(items),
        out_specs=tuple([ANY] * len(items)),
        scratch_shapes=[
            pltpu.SemaphoreType.DMA((len(items), numbers)),
            pltpu.SemaphoreType.DMA((len(items), numbers)),
            pltpu.SemaphoreType.DMA((len(items),)),
        ],
        compiler_params=pltpu.CompilerParams(collective_id=number, has_side_effects=True),
        cost_estimate=cost(micros),
    )(*arrays)


def owners_kernel(pieces, in_ref, out_ref):
    columns = out_ref.shape[2] // pieces
    for piece in range(pieces):
        for owner in range(GROUP):
            lo = (piece * GROUP + owner) * columns
            out_ref[owner, :, piece * columns : (piece + 1) * columns] = in_ref[:, lo : lo + columns]


def by_owner(weight, pieces):
    rows, columns = weight.shape
    return pl.pallas_call(
        functools.partial(owners_kernel, pieces),
        out_shape=jax.ShapeDtypeStruct((GROUP, rows, columns // GROUP), weight.dtype),
        in_specs=[VMEM],
        out_specs=VMEM,
        compiler_params=pltpu.CompilerParams(vmem_limit_bytes=32 * 2**20),
        cost_estimate=cost(3),
    )(weight)


def dealt_columns_kernel(piece, in_ref, out_ref):
    for owner in range(GROUP):
        for part in range(out_ref.shape[2] // piece):
            lo = (part * GROUP + owner) * piece
            out_ref[owner, :, part * piece : (part + 1) * piece] = in_ref[:, lo : lo + piece]


def dealt_columns(x, piece):
    rows, columns = x.shape
    return pl.pallas_call(
        functools.partial(dealt_columns_kernel, piece),
        out_shape=jax.ShapeDtypeStruct((GROUP, rows, columns // GROUP), x.dtype),
        in_specs=[VMEM],
        out_specs=VMEM,
        compiler_params=pltpu.CompilerParams(vmem_limit_bytes=32 * 2**20),
        cost_estimate=cost(2),
    )(x)


def home_kernel(pieces, got_ref, weight_ref, out_ref, gain_ref):
    columns = got_ref.shape[2] // pieces
    for sender in range(GROUP):
        for piece in range(pieces):
            lo = (piece * GROUP + sender) * columns
            out_ref[:, lo : lo + columns] = got_ref[
                sender, :, piece * columns : (piece + 1) * columns
            ].astype(f32)
    gain_ref[...] = jnp.sum(out_ref[...] * weight_ref[...].astype(f32), axis=1, keepdims=True)


def home(got, weight, pieces):
    rows, columns = weight.shape
    return pl.pallas_call(
        functools.partial(home_kernel, pieces),
        out_shape=(
            jax.ShapeDtypeStruct((rows, columns), f32),
            jax.ShapeDtypeStruct((rows, 1), f32),
        ),
        in_specs=[VMEM, VMEM],
        out_specs=(VMEM, VMEM),
        compiler_params=pltpu.CompilerParams(vmem_limit_bytes=32 * 2**20),
        cost_estimate=cost(5),
    )(got, weight)


TILE = 1024


def product_scatter_kernel(swaps, around, a_far, w_far, *refs):
    swap_refs, out_ref, swapped_refs = refs[:swaps], refs[swaps], refs[swaps + 1 : 2 * swaps + 1]
    near, far, away, going, send_sem, recv_sem, a_ref, w_ref, a_sem, w_sem = refs[
        2 * swaps + 1 : 2 * swaps + 11
    ]
    me, slot, step_core, first_step, second_step = places()
    first, second, mate = me + first_step, me + second_step, me + step_core
    core = lax.rem(slot, 2)
    others = plane_steps(
        step_core,
        (1 - core) * first_step + core * second_step,
        core * first_step + (1 - core) * second_step,
    )
    corner_step = first_step + second_step
    if around:
        own_places, mate_places = (3, 1, 2, 0), (7, 5, 6, 4)
    else:
        own_places = (slot + corner_step, slot + first_step, slot + second_step, slot)
        mate_slot = slot + step_core
        mate_places = (
            mate_slot + corner_step,
            mate_slot + second_step,
            mate_slot + first_step,
            mate_slot,
        )

    def a_load(place):
        return pltpu.make_async_copy(a_far.at[place], a_ref.at[place], a_sem.at[place])

    def w_load(i):
        at = pl.ds(i * TILE, TILE)
        return pltpu.make_async_copy(w_far.at[at, :], w_ref.at[at, :], w_sem.at[i])

    a_load(mate_places[0]).start()
    for i in range(out_ref.shape[1] // TILE):
        w_load(i).start()
    for place in (
        mate_places[2],
        own_places[0],
        own_places[2],
        mate_places[1],
        mate_places[3],
        own_places[3],
        own_places[1],
    ):
        a_load(place).start()
    greet([me + step for _, step in others] if swaps else (first, second, mate))
    sent = []

    def send(source, target, number, device):
        copy = remote(source, target, send_sem.at[number], recv_sem.at[number], device)
        copy.start()
        sent.append(copy)

    def arrived(ref, number, source):
        remote(ref, ref, send_sem.at[number], recv_sem.at[number], source).wait_recv()

    def product(place, extra, target):
        a_load(place).wait()

        def tile(i, _):
            at = pl.ds(pl.multiple_of(i * TILE, TILE), TILE)
            total = dot_nt(a_ref[place], w_ref[at, :])
            for ref in extra:
                total = total + ref[:, at].astype(f32)
            target[:, at] = total.astype(target.dtype)
            return 0

        lax.fori_loop(0, out_ref.shape[1] // TILE, tile, 0)

    def to_mate(kind):
        product(mate_places[kind], (), away.at[kind])
        send(away.at[kind], near.at[kind], kind, mate)

    def add(ref):
        def tile(i, _):
            at = pl.ds(pl.multiple_of(i * TILE, TILE), TILE)
            out_ref[:, at] = out_ref[:, at] + ref[:, at].astype(f32)
            return 0

        lax.fori_loop(0, out_ref.shape[1] // TILE, tile, 0)

    swapping, kept = [], []
    if swaps:
        swap_send, swap_recv, swap_own = refs[2 * swaps + 11 :]

    def start_swaps():
        for item in range(swaps):
            for number, step in others:
                copy = remote(
                    swap_refs[item].at[slot + step],
                    swapped_refs[item].at[slot],
                    swap_send.at[item, number - 1],
                    swap_recv.at[item, number - 1],
                    me + step,
                )
                copy.start()
                swapping.append(copy)
            copy = pltpu.make_async_copy(
                swap_refs[item].at[slot], swapped_refs[item].at[slot], swap_own.at[item]
            )
            copy.start()
            kept.append(copy)

    for i in range(out_ref.shape[1] // TILE):
        w_load(i).wait()
    to_mate(0)
    to_mate(2)
    arrived(near.at[0], 0, mate)
    product(own_places[0], (near.at[0],), going.at[0])
    send(going.at[0], far.at[0], 4, second)
    arrived(near.at[2], 2, mate)
    product(own_places[2], (near.at[2],), going.at[2])
    send(going.at[2], far.at[2], 5, second)
    start_swaps()
    to_mate(1)
    to_mate(3)
    arrived(near.at[3], 3, mate)
    product(own_places[3], (near.at[3],), out_ref)
    arrived(near.at[1], 1, mate)
    arrived(far.at[0], 4, second)
    product(own_places[1], (near.at[1], far.at[0]), going.at[1])
    send(going.at[1], far.at[1], 6, first)
    arrived(far.at[2], 5, second)
    add(far.at[2])
    arrived(far.at[1], 6, first)
    add(far.at[1])
    for item in range(swaps):
        for number, step in others:
            target = swapped_refs[item].at[slot + step]
            remote(
                target,
                target,
                swap_send.at[item, number - 1],
                swap_recv.at[item, number - 1],
                me + step,
            ).wait_recv()
    for copy in sent + swapping:
        copy.wait_send()
    for copy in kept:
        copy.wait()


def product_scatter(a, w, number, around, *swaps):
    _, rows, depth = a.shape
    columns = w.shape[0]
    count = len(swaps)
    swap_sems = [
        pltpu.SemaphoreType.DMA((count, GROUP - 1)),
        pltpu.SemaphoreType.DMA((count, GROUP - 1)),
        pltpu.SemaphoreType.DMA((count,)),
    ]
    return pl.pallas_call(
        functools.partial(product_scatter_kernel, count, around),
        out_shape=(jax.ShapeDtypeStruct((rows, columns), f32),)
        + tuple(jax.ShapeDtypeStruct(x.shape, x.dtype) for x in swaps),
        in_specs=[ANY, ANY] + [ANY] * count,
        out_specs=(VMEM,) + (ANY,) * count,
        scratch_shapes=[
            pltpu.VMEM((4, rows, columns), bf16),
            pltpu.VMEM((3, rows, columns), bf16),
            pltpu.VMEM((4, rows, columns), bf16),
            pltpu.VMEM((3, rows, columns), bf16),
            pltpu.SemaphoreType.DMA((7,)),
            pltpu.SemaphoreType.DMA((7,)),
            pltpu.VMEM(a.shape, bf16),
            pltpu.VMEM(w.shape, bf16),
            pltpu.SemaphoreType.DMA((GROUP,)),
            pltpu.SemaphoreType.DMA((columns // TILE,)),
        ]
        + (swap_sems if swaps else []),
        compiler_params=pltpu.CompilerParams(
            collective_id=number, has_side_effects=True, vmem_limit_bytes=56 * 2**20
        ),
        cost_estimate=cost(50),
    )(a, w, *swaps)


def residual_back_kernel(
    d_second_ref,
    residual_ref,
    cot_ref,
    gain_ref,
    w_far,
    mixer_ref,
    down_ref,
    d_residual_ref,
    d_mix_ref,
    heads_ref,
    near_ref,
    swapped_ref,
    w_ref,
    parts_ref,
    away_ref,
    send_sem,
    recv_sem,
    own_sem,
    w_sem,
):
    me, slot, step_core, first_step, second_step = places()
    core = lax.rem(slot, 2)
    others = plane_steps(
        step_core,
        (1 - core) * first_step + core * second_step,
        core * first_step + (1 - core) * second_step,
    )
    mate = me + step_core
    width = parts_ref.shape[2]

    def w_load(i):
        at = pl.ds(i * width, width)
        return pltpu.make_async_copy(w_far.at[at, :], w_ref.at[i], w_sem.at[i])

    for i in range(GROUP):
        w_load(i).start()
    greet([me + step for _, step in others])
    sent = []

    def send(source, target, item, number, device):
        copy = remote(source, target, send_sem.at[item, number], recv_sem.at[item, number], device)
        copy.start()
        sent.append(copy)

    def arrived(target, item, number):
        remote(target, target, send_sem.at[item, number], recv_sem.at[item, number], me).wait_recv()

    for number, step in others:
        send(down_ref.at[slot + step], swapped_ref.at[slot], 2, number - 1, me + step)
    own_down = pltpu.make_async_copy(down_ref.at[slot], swapped_ref.at[slot], own_sem.at[0])
    own_down.start()
    rows = d_residual_ref.shape[0]
    slab_rows = 32

    def slab(i, _):
        at = pl.ds(pl.multiple_of(i * slab_rows, slab_rows), slab_rows)
        residual = residual_ref[at, :]
        inverse = inverse_rms(residual)
        grad = rms_back(d_second_ref[at, :] * gain_ref[...], residual * inverse, inverse)
        total = cot_ref[at, :].astype(f32) + grad
        d_residual_ref[at, :] = total
        d_mix_ref[at, :] = total.astype(bf16)
        return 0

    lax.fori_loop(0, rows // slab_rows, slab, 0)
    for i in range(GROUP):
        w_load(i).wait()

    def part(place):
        parts_ref[place] = dot_nt(d_mix_ref[...], w_ref[place]).astype(bf16)

    for number, step in reversed(others):
        part(slot + step)
        send(parts_ref.at[slot + step], heads_ref.at[slot], 0, number - 1, me + step)
    part(slot)
    own_part = pltpu.make_async_copy(parts_ref.at[slot], heads_ref.at[slot], own_sem.at[1])
    own_part.start()
    for kind in (3, 2, 1, 0):
        away_ref[kind] = dot_tn(mixer_ref[kind], d_mix_ref[...]).astype(bf16)
        send(away_ref.at[kind], near_ref.at[kind], 1, kind, mate)
    for number, step in others:
        arrived(heads_ref.at[slot + step], 0, number - 1)
        arrived(swapped_ref.at[slot + step], 2, number - 1)
    for kind in range(4):
        arrived(near_ref.at[kind], 1, kind)
    for copy in sent:
        copy.wait_send()
    own_down.wait()
    own_part.wait()


def residual_back(d_second, residual, cot, gain, w, mixer_away, down, number):
    rows, columns = residual.shape
    width = columns // GROUP
    blocks = mixer_away.shape[0]
    return pl.pallas_call(
        residual_back_kernel,
        out_shape=(
            jax.ShapeDtypeStruct((rows, columns), f32),
            jax.ShapeDtypeStruct((rows, columns), bf16),
            jax.ShapeDtypeStruct((GROUP, rows, width), bf16),
            jax.ShapeDtypeStruct((blocks, mixer_away.shape[2], columns), bf16),
            jax.ShapeDtypeStruct(down.shape, down.dtype),
        ),
        in_specs=[VMEM, VMEM, VMEM, VMEM, ANY, VMEM, ANY],
        out_specs=(VMEM, VMEM, ANY, ANY, ANY),
        scratch_shapes=[
            pltpu.VMEM((GROUP, width, columns), bf16),
            pltpu.VMEM((GROUP, rows, width), bf16),
            pltpu.VMEM((blocks, mixer_away.shape[2], columns), bf16),
            pltpu.SemaphoreType.DMA((3, GROUP - 1)),
            pltpu.SemaphoreType.DMA((3, GROUP - 1)),
            pltpu.SemaphoreType.DMA((2,)),
            pltpu.SemaphoreType.DMA((GROUP,)),
        ],
        compiler_params=pltpu.CompilerParams(
            collective_id=number, has_side_effects=True, vmem_limit_bytes=48 * 2**20
        ),
        cost_estimate=cost(20),
    )(d_second, residual, cot, gain, w, mixer_away, down)


def gate_gather_kernel(
    own_ref,
    x_far,
    w_far,
    all_ref,
    gate_far,
    up_far,
    hidden_far,
    x_ref,
    w_ref,
    gate_ref,
    up_ref,
    hidden_ref,
    send_sem,
    recv_sem,
    own_sem,
    x_sem,
    w_sem,
    store_sem,
):
    me, slot, step_core, first_step, second_step = places()
    first, second, mate = me + first_step, me + second_step, me + step_core
    w_load = pltpu.make_async_copy(w_far, w_ref, w_sem)
    w_load.start()
    tiles, tile_rows = x_ref.shape[:2]
    half = gate_ref.shape[2]

    def rows_of(i):
        return pl.ds(pl.multiple_of(i * tile_rows, tile_rows), tile_rows)

    def x_load(i):
        return pltpu.make_async_copy(x_far.at[rows_of(i), :], x_ref.at[i], x_sem.at[i])

    for i in range(tiles):
        x_load(i).start()
    greet((first, second, mate))
    sent = []

    def send(source, number, device):
        copy = remote(
            source, all_ref.at[AROUND[number]], send_sem.at[number], recv_sem.at[number], device
        )
        copy.start()
        sent.append(copy)

    def arrived(number):
        target = all_ref.at[AROUND[number]]
        remote(target, target, send_sem.at[number], recv_sem.at[number], me).wait_recv()
        return target

    own = pltpu.make_async_copy(own_ref, all_ref.at[0], own_sem)
    send(own_ref, 0, first)
    send(own_ref, 1, second)
    send(own_ref, 2, mate)
    own.start()

    def stores(i, spot):
        return [
            pltpu.make_async_copy(near.at[spot], far.at[rows_of(i), :], store_sem.at[spot, number])
            for number, (near, far) in enumerate(
                ((gate_ref, gate_far), (up_ref, up_far), (hidden_ref, hidden_far))
            )
        ]

    def tile(i, _):
        spot = lax.rem(i, 2)
        x_load(i).wait()

        @pl.when(i >= 2)
        def _():
            for copy in stores(i - 2, spot):
                copy.wait()

        both = dot_nn(x_ref[i], w_ref[...])
        gate = both[:, :half]
        up = both[:, half:]
        gate_ref[spot] = gate
        up_ref[spot] = up
        hidden_ref[spot] = (gate * jax.nn.sigmoid(gate) * up).astype(bf16)
        for copy in stores(i, spot):
            copy.start()
        return 0

    w_load.wait()
    lax.fori_loop(0, tiles // 2, tile, 0)
    block = arrived(0)
    send(block, 3, second)
    send(block, 4, mate)
    send(arrived(1), 5, mate)
    lax.fori_loop(tiles // 2, tiles, tile, 0)
    for i in (tiles - 2, tiles - 1):
        for copy in stores(i, i % 2):
            copy.wait()
    send(arrived(3), 6, mate)
    for number in (2, 4, 5, 6):
        arrived(number)
    for copy in sent:
        copy.wait_send()
    own.wait()


def gate_gather(own, x, w, number):
    rows, columns = own.shape
    half = w.shape[1] // 2
    tiles = x.shape[0] // rows
    wide = jax.ShapeDtypeStruct((x.shape[0], half), f32)
    return pl.pallas_call(
        gate_gather_kernel,
        out_shape=(
            jax.ShapeDtypeStruct((GROUP, rows, columns), own.dtype),
            wide,
            wide,
            jax.ShapeDtypeStruct((x.shape[0], half), bf16),
        ),
        in_specs=[ANY, ANY, ANY],
        out_specs=(ANY, ANY, ANY, ANY),
        scratch_shapes=[
            pltpu.VMEM((tiles, rows, x.shape[1]), bf16),
            pltpu.VMEM(w.shape, bf16),
            pltpu.VMEM((2, rows, half), f32),
            pltpu.VMEM((2, rows, half), f32),
            pltpu.VMEM((2, rows, half), bf16),
            pltpu.SemaphoreType.DMA((7,)),
            pltpu.SemaphoreType.DMA((7,)),
            pltpu.SemaphoreType.DMA,
            pltpu.SemaphoreType.DMA((tiles,)),
            pltpu.SemaphoreType.DMA,
            pltpu.SemaphoreType.DMA((2, 3)),
        ],
        compiler_params=pltpu.CompilerParams(
            collective_id=number, has_side_effects=True, vmem_limit_bytes=56 * 2**20
        ),
        cost_estimate=cost(45),
    )(own, x, w)


def hidden_back_kernel(cot_ref, gate_ref, up_ref, w_ref, grad_ref):
    half = gate_ref.shape[1]
    d_hidden = dot_nn(cot_ref[...], w_ref[...])
    gate = gate_ref[...]
    sigmoid = jax.nn.sigmoid(gate)
    grad_ref[:, :half] = (
        d_hidden * up_ref[...] * sigmoid * (1.0 + gate * (1.0 - sigmoid))
    ).astype(bf16)
    grad_ref[:, half:] = (d_hidden * gate * sigmoid).astype(bf16)


def hidden_back(cot, gate, up, w):
    rows, columns = cot.shape
    half = w.shape[1]
    tile_rows = 256

    def tiles(width):
        return pl.BlockSpec((tile_rows, width), lambda i: (i, 0))

    return pl.pallas_call(
        hidden_back_kernel,
        grid=(rows // tile_rows,),
        in_specs=[
            tiles(columns),
            tiles(half),
            tiles(half),
            pl.BlockSpec(w.shape, lambda i: (0, 0)),
        ],
        out_specs=tiles(2 * half),
        out_shape=jax.ShapeDtypeStruct((rows, 2 * half), bf16),
        compiler_params=pltpu.CompilerParams(vmem_limit_bytes=56 * 2**20),
        cost_estimate=cost(20),
    )(cot, gate, up, w)


def away_product_kernel(x_ref, w_ref, out_ref):
    out_ref[...] = dot_nt(x_ref[...], w_ref[...]).astype(bf16)


def away_product(x, w, tile_rows):
    rows, depth = x.shape
    tiles = rows // tile_rows // 2
    return pl.pallas_call(
        away_product_kernel,
        grid=(tiles,),
        in_specs=[
            pl.BlockSpec((tile_rows, depth), lambda i: (tiles + i, 0)),
            pl.BlockSpec(w.shape, lambda i: (0, 0)),
        ],
        out_specs=pl.BlockSpec((tile_rows, w.shape[0]), lambda i: (i, 0)),
        out_shape=jax.ShapeDtypeStruct((rows // 2, w.shape[0]), bf16),
        compiler_params=pltpu.CompilerParams(vmem_limit_bytes=56 * 2**20),
        cost_estimate=cost(6),
    )(x, w)


def keep_product_kernel(x_ref, w_ref, near_ref, out_ref):
    total = dot_nt(x_ref[...], w_ref[...]) + near_ref[0].astype(f32)
    out_ref[0] = total.astype(out_ref.dtype)


def keep_product(x, w, near, begin, number, out_type):
    _, rows, columns = near.shape
    return pl.pallas_call(
        keep_product_kernel,
        grid=(number,),
        in_specs=[
            pl.BlockSpec((rows, x.shape[1]), lambda i: (begin + i, 0)),
            pl.BlockSpec(w.shape, lambda i: (0, 0)),
            pl.BlockSpec((1, rows, columns), lambda i: (begin + i, 0, 0)),
        ],
        out_specs=pl.BlockSpec((1, rows, columns), lambda i: (i, 0, 0)),
        out_shape=jax.ShapeDtypeStruct((number, rows, columns), out_type),
        compiler_params=pltpu.CompilerParams(vmem_limit_bytes=56 * 2**20),
        cost_estimate=cost(5),
    )(x, w, near)


def rows_product_kernel(x_ref, y_ref, out_ref):
    out_ref[...] = dot_tn(x_ref[...], y_ref[...]).astype(bf16)


def rows_product(x, y, micros):
    rows, columns = x.shape
    wide = y.shape[1]
    tile_columns = 512
    return pl.pallas_call(
        rows_product_kernel,
        grid=(columns // tile_columns,),
        in_specs=[
            pl.BlockSpec((rows, tile_columns), lambda i: (0, i)),
            pl.BlockSpec((rows, wide), lambda i: (0, 0)),
        ],
        out_specs=pl.BlockSpec((tile_columns, wide), lambda i: (i, 0)),
        out_shape=jax.ShapeDtypeStruct((columns, wide), bf16),
        compiler_params=pltpu.CompilerParams(vmem_limit_bytes=56 * 2**20),
        cost_estimate=cost(micros),
    )(x, y)


def plane_permutes(device_count):
    first, second, mate = [], [], []
    for i in range(device_count):
        low_bit, high_bit = (2, 4) if i % 2 == 0 else (4, 2)
        first.append((i, i ^ low_bit))
        second.append((i, i ^ high_bit))
        mate.append((i, i ^ 1))
    return first, second, mate


def after(values, *earlier):
    return lax.optimization_barrier((values, earlier))[0]


def meet(*values):
    return lax.optimization_barrier(values)


def assemble_kernel(*refs):
    blocks, out_ref = refs[:GROUP], refs[GROUP]
    _, slot, step_core, first_step, second_step = places()
    corner_step = first_step + second_step
    here = (0, first_step, second_step, corner_step)
    there = (step_core, step_core + second_step, step_core + first_step, step_core + corner_step)
    for number, step in enumerate(here + there):
        out_ref[:, slot + step] = blocks[number][...]


def assemble(x, from_first, from_second, from_corner, mates):
    parts, rows, columns = x.shape
    return pl.pallas_call(
        assemble_kernel,
        out_shape=jax.ShapeDtypeStruct((parts, GROUP, rows, columns), x.dtype),
        in_specs=[VMEM] * GROUP,
        out_specs=VMEM,
        compiler_params=pltpu.CompilerParams(vmem_limit_bytes=32 * 2**20),
        cost_estimate=cost(8),
    )(x, from_first, from_second, from_corner, *mates)


class SlowScatter:
    def __init__(self, keep, away, device_count):
        self.keep = keep
        self.away = away
        self.first, self.second, self.mate = plane_permutes(device_count)

    def to_mate(self):
        return lax.ppermute(self.away, "fsdp", self.mate)

    def onward(self, near):
        return (self.keep(2, 2) + near[2:].astype(f32)).astype(bf16)

    def to_second(self, sums):
        return lax.ppermute(sums, "fsdp", self.second)

    def half(self, near):
        return self.keep(1, 1)[0] + near[1].astype(f32)

    def both(self, half, far):
        return (half + far[1].astype(f32)).astype(bf16)

    def to_first(self, both):
        return lax.ppermute(both, "fsdp", self.first)

    def total(self, near, far, last):
        own = self.keep(0, 1)[0] + near[0].astype(f32)
        return own + far[0].astype(f32) + last.astype(f32)


def low(values):
    return values.astype(bf16).astype(f32)


def gates(proj_ref, floor_ref, rows, head, heads):
    dim = floor_ref.shape[1] // heads
    wide = heads * dim
    lo = head * dim
    q_pre = proj_ref[rows, lo : lo + dim]
    f_pre = proj_ref[rows, wide + lo : wide + lo + dim]
    value = proj_ref[rows, 2 * wide + lo : 2 * wide + lo + dim].astype(bf16)
    floor = floor_ref[:, lo : lo + dim]
    q_sigmoid = jax.nn.sigmoid(q_pre)
    query = low(q_pre * q_sigmoid)
    f_sigmoid = jax.nn.sigmoid(f_pre)
    forget = floor + (1.0 - floor) * f_sigmoid
    key = low(1.0 - forget)
    row = lax.broadcasted_iota(jnp.int32, (CHUNK, dim), 0)
    in_half = lax.rem(row, HALF)
    product = forget
    step = 1
    while step < HALF:
        product = jnp.where(in_half >= step, product * pltpu.roll(product, step, 0), product)
        step *= 2
    middle = product[HALF - 1 : HALF, :]
    end = product[CHUNK - 1 : CHUNK, :]
    ratio = jnp.where(row < HALF, product / middle, product)
    inverse = 1.0 / ratio
    return {
        "q_pre": q_pre,
        "q_sigmoid": q_sigmoid,
        "f_sigmoid": f_sigmoid,
        "forget": forget,
        "value": value,
        "floor": floor,
        "middle": middle,
        "end": end,
        "ratio": ratio,
        "inverse": inverse,
        "row": row,
        "query_mid": query * ratio,
        "key_mid": key * inverse,
    }


def whole_fade(g, last):
    return g["middle"] * g["end"] * jnp.where(last < 0, 1.0, 0.0)


def tail_keys(g, last):
    return jnp.where(g["row"] >= last, g["key_mid"] * g["end"], 0.0).astype(bf16)


def entry_queries(g, carried):
    return jnp.where(carried, g["query_mid"] * g["middle"], 0.0).astype(bf16)


def next_state(g, last, state):
    return state * whole_fade(g, last) + dot_tn(g["value"], tail_keys(g, last))


def forward_kernel(
    heads, last_ref, proj_ref, start_ref, floor_ref, gain_ref, in_ref, mix_ref, out_ref, enter_ref, state
):
    dim = floor_ref.shape[1] // heads
    chunks = proj_ref.shape[0] // CHUNK
    tile = pl.program_id(0)

    @pl.when(tile == 0)
    def _():
        state[...] = in_ref[...]

    def step(n, _):
        base = pl.multiple_of(n * CHUNK, CHUNK)
        rows = pl.ds(base, CHUNK)
        place = (tile * chunks + n) * CHUNK
        starts = start_ref[rows, :] - place
        last = last_ref[tile * chunks + n] - place
        column = lax.broadcasted_iota(jnp.int32, (CHUNK, CHUNK), 1)
        line = lax.broadcasted_iota(jnp.int32, (CHUNK, CHUNK), 0)
        within = (column <= line) & (column >= starts)
        carried = starts < 0
        for head in range(heads):
            lo = head * dim
            g = gates(proj_ref, floor_ref, rows, head, heads)
            now = state[head]
            enter_ref[n, head] = now
            scores = dot_nt(g["query_mid"].astype(bf16), g["key_mid"].astype(bf16))
            scores = jnp.where(within, scores, 0.0).astype(bf16)
            out = dot_nn(scores, g["value"]) + dot_nt(entry_queries(g, carried), now.astype(bf16))
            state[head] = next_state(g, last, now)
            out_ref[rows, lo : lo + dim] = out
            mix_ref[rows, lo : lo + dim] = (
                out * inverse_rms(out) * gain_ref[:, lo : lo + dim]
            ).astype(bf16)
        return 0

    lax.fori_loop(0, chunks, step, 0, unroll=UNROLL)


def last_state_kernel(heads, last_ref, proj_ref, floor_ref, out_ref):
    for head in range(heads):
        state = jnp.zeros(out_ref.shape[1:], f32)
        for n in range(proj_ref.shape[0] // CHUNK):
            g = gates(proj_ref, floor_ref, pl.ds(n * CHUNK, CHUNK), head, heads)
            state = next_state(g, last_ref[n] - n * CHUNK, state)
        out_ref[head] = state


def state_grad(out_ref, dmix_ref, gain_ref, rows, lo, dim):
    out = out_ref[rows, lo : lo + dim]
    inverse = inverse_rms(out)
    scaled = out * inverse
    dmix = dmix_ref[rows, lo : lo + dim].astype(f32)
    return rms_back(dmix * gain_ref[:, lo : lo + dim], scaled, inverse)


def backward_chunk(heads, n, at, refs, outs, later, before=0):
    last_ref, proj_ref, start_ref, floor_ref, gain_ref, out_ref, dmix_ref, enter_ref = refs
    dproj_ref, dfloor_ref = outs
    dim = floor_ref.shape[1] // heads
    wide = heads * dim
    base = n * CHUNK
    rows = pl.ds(base, CHUNK)
    place = (before + n) * CHUNK
    starts = start_ref[rows, :] - place
    last = last_ref[before + n] - place
    column = lax.broadcasted_iota(jnp.int32, (CHUNK, CHUNK), 1)
    line = lax.broadcasted_iota(jnp.int32, (CHUNK, CHUNK), 0)
    within = (column <= line) & (column >= starts)
    carried = starts < 0
    for head in range(heads):
        lo = head * dim
        g = gates(proj_ref, floor_ref, rows, head, heads)
        grad = state_grad(out_ref, dmix_ref, gain_ref, rows, lo, dim)
        grad_hi = grad.astype(bf16)
        grad_lo = (grad - grad_hi.astype(f32)).astype(bf16)
        state = enter_ref[n, head]
        after = later[head]
        after_low = after.astype(bf16)
        query_mid = g["query_mid"].astype(bf16)
        key_mid = g["key_mid"].astype(bf16)
        scores = jnp.where(within, dot_nt(query_mid, key_mid), 0.0).astype(bf16)
        d_scores = dot_nt(grad_hi, g["value"]) + dot_nt(grad_lo, g["value"])
        d_scores = jnp.where(within, d_scores, 0.0).astype(bf16)
        query_in = entry_queries(g, carried)
        key_out = tail_keys(g, last)
        d_query_mid = dot_nn(d_scores, key_mid)
        d_query_in = jnp.where(carried, dot_nn(grad_hi, state.astype(bf16)), 0.0)
        d_key_mid = dot_tn(d_scores, query_mid)
        d_key_out = jnp.where(g["row"] >= last, dot_nn(g["value"], after_low), 0.0)
        d_value = dot_tn(scores, grad_hi) + dot_nt(key_out, after_low)
        d_query = (d_query_mid + d_query_in * g["middle"]) * g["ratio"]
        d_key = (d_key_mid + d_key_out * g["end"]) * g["inverse"]
        tail = d_key_out * key_out.astype(f32)
        term = (
            d_query_mid * query_mid.astype(f32)
            + d_query_in * query_in.astype(f32)
            - d_key_mid * key_mid.astype(f32)
            - tail
        )
        fade = whole_fade(g, last)
        final = jnp.sum(tail, axis=0, keepdims=True) + fade * jnp.sum(
            state * after, axis=0, keepdims=True
        )
        step_rows = 1
        while step_rows < CHUNK:
            term = jnp.where(
                g["row"] < CHUNK - step_rows,
                term + pltpu.roll(term, CHUNK - step_rows, 0),
                term,
            )
            step_rows *= 2
        d_forget = (term + final) / g["forget"] - d_key
        q_sigmoid, f_sigmoid = g["q_sigmoid"], g["f_sigmoid"]
        d_q_pre = d_query * q_sigmoid * (1.0 + g["q_pre"] * (1.0 - q_sigmoid))
        d_floor = d_forget * (1.0 - f_sigmoid)
        d_f_pre = d_floor * (1.0 - g["floor"]) * f_sigmoid
        dproj_ref[at, lo : lo + dim] = d_q_pre.astype(bf16)
        dproj_ref[at, wide + lo : wide + lo + dim] = d_f_pre.astype(bf16)
        dproj_ref[at, 2 * wide + lo : 2 * wide + lo + dim] = d_value.astype(bf16)
        dfloor_ref[:, lo : lo + dim] += jnp.sum(d_floor, axis=0, keepdims=True)
        later[head] = after * fade + dot_tn(grad_hi, query_in)


def backward_rest(heads, n, refs, later, before=0):
    last_ref, proj_ref, start_ref, floor_ref, gain_ref, out_ref, dmix_ref = refs
    dim = floor_ref.shape[1] // heads
    rows = pl.ds(n * CHUNK, CHUNK)
    for head in range(heads):
        g = gates(proj_ref, floor_ref, rows, head, heads)
        grad = state_grad(out_ref, dmix_ref, gain_ref, rows, head * dim, dim)
        place = (before + n) * CHUNK
        queries = entry_queries(g, start_ref[rows, :] < place)
        fade = whole_fade(g, last_ref[before + n] - place)
        later[head] = later[head] * fade + dot_tn(grad.astype(bf16), queries)


def backward_kernel(heads, *refs):
    ins, outs, later = refs[:8], refs[8:10], refs[10]
    chunks = ins[1].shape[0] // CHUNK
    edge = MAXLEN // CHUNK
    tile = pl.num_programs(0) - 1 - pl.program_id(0)
    before = tile * chunks

    def step(i, first):
        n = first - i
        at = pl.ds(pl.multiple_of(n * CHUNK, CHUNK), CHUNK)
        backward_chunk(heads, n, at, ins, outs, later, before)
        return first

    @pl.when(pl.program_id(0) == 0)
    def _():
        later[...] = jnp.zeros_like(later)
        outs[1][...] = jnp.zeros_like(outs[1])
        for n in range(chunks - 1, chunks - 1 - edge, -1):
            backward_rest(heads, n, ins[:7], later, before)
        lax.fori_loop(0, chunks - edge, step, chunks - 1 - edge, unroll=UNROLL)

    @pl.when(pl.program_id(0) != 0)
    def _():
        lax.fori_loop(0, chunks, step, chunks - 1, unroll=UNROLL)


def backward_edge_kernel(heads, *refs):
    ins, in_ref, _, outs, later = refs[:8], refs[8], refs[9], refs[10:12], refs[12]
    later[...] = in_ref[...]
    outs[1][...] = jnp.zeros_like(outs[1])
    edge = MAXLEN // CHUNK
    before = ins[0].shape[0] - edge
    for n in range(edge - 1, -1, -1):
        backward_chunk(heads, n, pl.ds(n * CHUNK, CHUNK), ins, outs, later, before)


def first_grad_kernel(heads, *refs):
    ins, grad_ref = refs[:7], refs[7]
    grad_ref[...] = jnp.zeros_like(grad_ref)
    for n in range(ins[1].shape[0] // CHUNK - 1, -1, -1):
        backward_rest(heads, n, ins, grad_ref)


def local_call(kernel, heads, micros, out_shape, scratch, *operands):
    return pl.pallas_call(
        functools.partial(kernel, heads),
        out_shape=out_shape,
        in_specs=[SMEM] + [VMEM] * (len(operands) - 1),
        out_specs=jax.tree.map(lambda _: VMEM, out_shape),
        scratch_shapes=scratch,
        compiler_params=pltpu.CompilerParams(vmem_limit_bytes=56 * 2**20),
        cost_estimate=cost(micros),
    )(*operands)


def body(
    tokens,
    cotangent,
    dealt_lengths,
    deal,
    norm_gain,
    mixer_in,
    forget_floor,
    group_gain,
    out_proj,
    ffn_gain,
    gate_up,
    down_proj,
):
    row_count, width = tokens.shape
    weight_rows = mixer_in.shape[0]
    device_count = lax.axis_size("fsdp")
    groups = device_count // GROUP
    own_index = lax.axis_index("fsdp")
    slot = lax.rem(own_index, GROUP)
    group = own_index // GROUP
    group_rows = GROUP * row_count
    heads = HEADS // GROUP
    own_width = width // GROUP
    dim = width // HEADS
    ffn_width = down_proj.shape[1]
    own_ffn = ffn_width // GROUP
    planes = [[g * GROUP + s for s in range(GROUP)] for g in range(groups)]
    lines = [[g * GROUP + s for g in range(groups)] for s in range(GROUP)]

    def line_gather(x):
        return lax.all_gather(x, "fsdp", axis=0, axis_index_groups=lines, tiled=True)

    def line_scatter(x):
        return lax.psum_scatter(
            x, "fsdp", scatter_dimension=0, axis_index_groups=lines, tiled=True
        )

    def whole_rows(x):
        return line_gather(x.reshape(GROUP * weight_rows, -1))

    low_step = 2 - 4 * (slot // 2 % 2)
    high_step = 4 - 8 * (slot // 4)
    odd = slot % 2
    moves = (
        slot,
        1 - 2 * odd,
        jnp.where(odd == 0, low_step, high_step),
        jnp.where(odd == 0, high_step, low_step),
    )

    seq_count = deal.shape[0]
    seq_ids = jnp.arange(seq_count, dtype=jnp.int32)
    matches = deal[:, None] == seq_ids[None, :]
    lengths = jnp.sum(jnp.where(matches, dealt_lengths[:, None], 0), axis=0)
    seq_starts = jnp.sum(
        jnp.where(seq_ids[:, None] < seq_ids[None, :], lengths[:, None], 0), axis=0
    )
    group_start = group * group_rows
    rows_here = group_start + jnp.arange(group_rows, dtype=jnp.int32)
    starts = (
        jnp.max(jnp.where(seq_starts[None, :] <= rows_here[:, None], seq_starts[None, :], 0), axis=1)
        - group_start
    )
    start_column = starts[:, None]
    last_starts = starts[CHUNK - 1 :: CHUNK]

    out_lines = lax.all_gather(out_proj, "fsdp", axis=0, axis_index_groups=lines)
    gain_block = jnp.zeros((16, 128), bf16)
    for number, gain in enumerate((norm_gain, forget_floor, group_gain, ffn_gain)):
        gain_block = gain_block.at[number, :weight_rows].set(gain)
    gain_blocks, mixer_swapped = exchange(
        0, 15, ("all", gain_block), ("swap", by_owner(mixer_in, 3))
    )
    mixer_weight = whole_rows(mixer_swapped)
    gains = (
        gain_blocks[:, :, :4, :weight_rows].transpose(2, 0, 1, 3).reshape(4, width).astype(f32)
    )
    first_gain = gains[0:1]
    second_gain = gains[3:4]
    own_gains = lax.dynamic_slice_in_dim(gains, slot * own_width, own_width, 1)
    own_floor = own_gains[1:2]
    own_group_gain = own_gains[2:3]

    inputs = tokens.astype(f32)
    first_inverse = inverse_rms(inputs)
    first_scaled = inputs * first_inverse
    first_normed = (first_scaled * first_gain).astype(bf16)
    late_gate_up, late_down = after((gate_up, down_proj), mixer_swapped)
    first_all, ffn_swapped, down_swapped = exchange(
        1,
        58,
        ("gather", first_normed[None]),
        ("swap", by_owner(late_gate_up, 2)),
        ("swap", by_owner(late_down, 1)),
    )
    first_all = first_all.reshape(group_rows, width)
    ffn_weight = whole_rows(ffn_swapped)
    first, second, mate = plane_permutes(device_count)
    out_own = after(out_lines, first_all)
    from_first = lax.ppermute(out_own, "fsdp", first)
    from_second = lax.ppermute(out_own, "fsdp", second)
    tail_projected = dot_nn(first_all[group_rows - MAXLEN :], mixer_weight)
    edge = MAXLEN // CHUNK
    state_type = jax.ShapeDtypeStruct((heads, dim, dim), f32)
    last_state = local_call(
        last_state_kernel,
        heads,
        3,
        state_type,
        [],
        last_starts[-edge:] - (group_rows - MAXLEN),
        tail_projected,
        own_floor,
    )
    up_line = [(i, i + GROUP) for i in range(device_count - GROUP)]
    down_line = [(i + GROUP, i) for i in range(device_count - GROUP)]
    entering_state = lax.ppermute(last_state, "fsdp", up_line)
    projected = dot_nn(after(first_all, last_state), mixer_weight)
    projected, entering_state, from_first, from_second = meet(
        projected, entering_state, from_first, from_second
    )
    from_corner = lax.ppermute(from_first, "fsdp", second)
    mates = [lax.ppermute(block, "fsdp", mate) for block in (out_own, from_first, from_second)]
    chunks = group_rows // CHUNK
    tile_count = group_rows // TILE_ROWS

    def row_tiles(columns, turned=False):
        return pl.BlockSpec(
            (TILE_ROWS, columns), lambda i: (tile_count - 1 - i if turned else i, 0)
        )

    def state_tiles(turned=False):
        return pl.BlockSpec(
            (TILE_ROWS // CHUNK, heads, dim, dim),
            lambda i: (tile_count - 1 - i if turned else i, 0, 0, 0),
        )

    state_scratch = pltpu.VMEM((heads, dim, dim), f32)
    mixed_heads, state_out, entering = pl.pallas_call(
        functools.partial(forward_kernel, heads),
        grid=(tile_count,),
        out_shape=(
            jax.ShapeDtypeStruct((group_rows, own_width), bf16),
            jax.ShapeDtypeStruct((group_rows, own_width), f32),
            jax.ShapeDtypeStruct((chunks, heads, dim, dim), f32),
        ),
        in_specs=[SMEM, row_tiles(3 * own_width), row_tiles(1), VMEM, VMEM, VMEM],
        out_specs=(row_tiles(own_width), row_tiles(own_width), state_tiles()),
        scratch_shapes=[state_scratch],
        compiler_params=pltpu.CompilerParams(vmem_limit_bytes=56 * 2**20),
        cost_estimate=cost(18),
    )(last_starts, projected, start_column, own_floor, own_group_gain, entering_state)
    mixed_heads, from_corner = meet(mixed_heads, from_corner)
    mates = mates + [lax.ppermute(from_corner, "fsdp", mate)]
    [mixer_input] = exchange(
        3, 15, ("widen", mixed_heads.reshape(GROUP, row_count, own_width))
    )
    mixer_input, mates = meet(mixer_input, mates)
    _, step_core, first_step, second_step = moves
    steps = (0, first_step, second_step, first_step + second_step)
    mate_steps = [step_core + steps[kind] for kind in (0, 2, 1, 3)]
    mixer_blocks = dealt_columns(mixer_input, weight_rows)
    mixer_around = [
        lax.dynamic_index_in_dim(mixer_blocks, slot + step, 0) for step in (*steps, *mate_steps)
    ]
    mixer_keep = jnp.concatenate(mixer_around[:4])
    mixer_away = jnp.concatenate(mixer_around[4:])
    out_weight = assemble(out_own, from_first, from_second, from_corner, mates).reshape(width, width)
    down_weight = whole_rows(after(down_swapped, mixed_heads))
    residual = inputs + dot_nn(mixer_input, out_weight)
    second_inverse = inverse_rms(residual)
    second_scaled = residual * second_inverse
    second_normed = (second_scaled * second_gain).astype(bf16)
    second_normed, mixer_keep, mixer_away = meet(second_normed, mixer_keep, mixer_away)
    [second_all] = exchange(2, 43, ("around", second_normed[None]))
    second_all = second_all.reshape(group_rows, width)
    cot_blocks, gate_part, up_part, hidden_act = gate_gather(
        cotangent, second_all, ffn_weight, 6
    )
    cot_all = cot_blocks.reshape(group_rows, width)
    down_grad = rows_product(cot_all, hidden_act, 11)
    down_summed = line_scatter(down_grad)
    hidden_act = after(hidden_act, down_grad)

    ffn_away = away_product(hidden_act, down_weight, row_count).reshape(4, row_count, width)
    ffn_near = lax.ppermute(ffn_away, "fsdp", mate)
    d_gate_pre = hidden_back(after(cot_all, ffn_away), gate_part, up_part, down_weight)
    d_gate_pre, ffn_near = meet(d_gate_pre, ffn_near)
    ffn_sums = keep_product(hidden_act, down_weight, ffn_near, 2, 2, bf16)
    ffn_grad = rows_product(after(second_all, ffn_sums), d_gate_pre, 18)
    ffn_rest = keep_product(hidden_act, down_weight, after(ffn_near, ffn_grad), 0, 2, f32)
    ffn_grad, ffn_rest, ffn_far = meet(ffn_grad, ffn_rest, lax.ppermute(ffn_sums, "fsdp", second))
    ffn_both = (ffn_rest[1] + ffn_far[1].astype(f32)).astype(bf16)
    ffn_summed = line_scatter(ffn_grad)
    [d_second] = product_scatter(
        d_gate_pre.reshape(GROUP, row_count, -1), after(ffn_weight, ffn_grad, ffn_both), 4, True
    )
    d_second, ffn_last, down_summed = meet(
        d_second, lax.ppermute(ffn_both, "fsdp", first), down_summed
    )

    d_residual, d_mix_out, d_mixed_heads, out_near, down_swapped = residual_back(
        d_second,
        residual,
        cotangent,
        second_gain,
        out_weight,
        mixer_away,
        down_summed.reshape(GROUP, weight_rows, -1),
        5,
    )
    d_mixed_heads = d_mixed_heads.reshape(group_rows, own_width)

    def out_blocks(blocks):
        return lax.dot_general(
            blocks, d_mix_out, (((1,), (0,)), ((), ())), preferred_element_type=f32
        )

    out_sum = SlowScatter(
        lambda begin, number: out_blocks(mixer_keep[begin : begin + number]), None, device_count
    )
    operands = (projected, start_column, own_floor, own_group_gain, state_out, d_mixed_heads)

    def edge_specs(place):
        def rows(columns):
            return pl.BlockSpec((MAXLEN, columns), lambda i: (place, 0))

        return [rows(3 * own_width), rows(1), VMEM, VMEM, rows(own_width), rows(own_width)]

    first_grad = pl.pallas_call(
        functools.partial(first_grad_kernel, heads),
        grid=(1,),
        out_shape=state_type,
        in_specs=[SMEM] + edge_specs(0),
        out_specs=VMEM,
        compiler_params=pltpu.CompilerParams(vmem_limit_bytes=56 * 2**20),
        cost_estimate=cost(3),
    )(last_starts, *operands)
    entering_grad = lax.ppermute(first_grad, "fsdp", down_line)
    out_near = after(out_near, first_grad)
    out_far = out_sum.to_second(out_sum.onward(out_near))
    dproj_type = jax.ShapeDtypeStruct((group_rows, 3 * own_width), bf16)
    dfloor_type = jax.ShapeDtypeStruct((1, own_width), f32)
    d_projected, floor_most = pl.pallas_call(
        functools.partial(backward_kernel, heads),
        grid=(tile_count,),
        out_shape=(dproj_type, dfloor_type),
        in_specs=[
            SMEM,
            row_tiles(3 * own_width, True),
            row_tiles(1, True),
            VMEM,
            VMEM,
            row_tiles(own_width, True),
            row_tiles(own_width, True),
            state_tiles(True),
        ],
        out_specs=(row_tiles(3 * own_width, True), VMEM),
        scratch_shapes=[state_scratch],
        compiler_params=pltpu.CompilerParams(vmem_limit_bytes=56 * 2**20),
        cost_estimate=cost(30),
    )(last_starts, *operands, entering)
    d_projected, entering_grad = meet(d_projected, entering_grad)
    last_tile = group_rows // MAXLEN - 1
    d_projected, floor_rest = pl.pallas_call(
        functools.partial(backward_edge_kernel, heads),
        grid=(1,),
        out_shape=(dproj_type, dfloor_type),
        in_specs=[SMEM]
        + edge_specs(last_tile)
        + [pl.BlockSpec((edge, heads, dim, dim), lambda i: (last_tile, 0, 0, 0)), VMEM, ANY],
        out_specs=(
            pl.BlockSpec((MAXLEN, 3 * own_width), lambda i: (last_tile, 0)),
            VMEM,
        ),
        scratch_shapes=[state_scratch],
        input_output_aliases={9: 0},
        compiler_params=pltpu.CompilerParams(vmem_limit_bytes=56 * 2**20),
        cost_estimate=cost(4),
    )(last_starts, *operands, entering, entering_grad, d_projected)
    d_projected, out_far = meet(d_projected, out_far)
    out_both = out_sum.both(out_sum.half(out_near), out_far)
    d_projected = after(d_projected, out_both)
    floor_grad = floor_most + floor_rest
    by_sender = (GROUP, weight_rows, -1)
    floor_parts = lax.dynamic_update_slice_in_dim(
        jnp.zeros((width,), f32), floor_grad[0], slot * own_width, 0
    ).reshape(device_count, weight_rows)
    floor_parts = lax.all_to_all(floor_parts, "fsdp", 0, 0, tiled=True)
    mixer_grad = rows_product(first_all, d_projected, 11)
    mixer_grad, out_last = meet(mixer_grad, out_sum.to_first(out_both))
    mixer_summed = line_scatter(mixer_grad)
    out_total = out_sum.total(after(out_near, mixer_grad), out_far, out_last).astype(bf16)
    out_summed = line_scatter(out_total.reshape(groups * weight_rows, width))
    d_first, ffn_swapped = product_scatter(
        d_projected.reshape(GROUP, row_count, -1),
        after(mixer_weight, out_total),
        8,
        False,
        ffn_summed.reshape(by_sender),
    )
    d_first, mixer_summed, floor_parts = meet(d_first, mixer_summed, floor_parts)
    d_forget_floor = jnp.sum(floor_parts, axis=0)

    def swap(x):
        x = x.reshape(by_sender)
        return lax.all_to_all(x, "fsdp", 0, 0, axis_index_groups=planes, tiled=True)

    mixer_swapped = swap(mixer_summed)
    ffn_last = after(ffn_last, d_first)
    layer_out = residual + (ffn_rest[0] + ffn_far[0].astype(f32) + ffn_last.astype(f32))
    d_gate_up, ffn_gain_sum = home(ffn_swapped, gate_up, 2)
    d_mixer_in, norm_gain_sum = home(mixer_swapped, mixer_in, 3)
    d_down_proj, _ = home(down_swapped, down_proj, 1)
    d_dealt = d_residual + rms_back(d_first * first_gain, first_scaled, first_inverse)

    d_out_proj = after(out_summed, d_dealt, mixer_swapped).astype(f32)

    group_gain_sum = jnp.sum(out_proj.astype(f32) * d_out_proj, axis=1)
    return (
        layer_out,
        d_dealt,
        norm_gain_sum[:, 0] / norm_gain.astype(f32),
        d_mixer_in,
        d_forget_floor,
        group_gain_sum / group_gain.astype(f32),
        d_out_proj,
        ffn_gain_sum[:, 0] / ffn_gain.astype(f32),
        d_gate_up,
        d_down_proj,
    )


def solution(mesh):
    by_rows = P("fsdp", None)
    by_one = P("fsdp")
    return jax.shard_map(
        body,
        mesh=mesh,
        in_specs=(
            by_rows,
            by_rows,
            P(),
            P(),
            by_one,
            by_rows,
            by_one,
            by_one,
            by_rows,
            by_one,
            by_rows,
            by_rows,
        ),
        out_specs=(
            by_rows,
            by_rows,
            by_one,
            by_rows,
            by_one,
            by_one,
            by_rows,
            by_one,
            by_rows,
            by_rows,
        ),
        check_vma=False,
    )
```

```python
import functools

import jax
import jax.numpy as jnp
from jax import lax
from jax.experimental import pallas as pl
from jax.experimental.pallas import tpu as pltpu
from jax.sharding import PartitionSpec as P

HEADS = 16
CHUNK = 64
HALF = 32
TILE_ROWS = 512
UNROLL = 2
MAXLEN = 128
GROUP = 8
MESH_ID = pl.DeviceIdType.MESH
VMEM = pl.BlockSpec(memory_space=pltpu.VMEM)
SMEM = pl.BlockSpec(memory_space=pltpu.SMEM)
ANY = pl.BlockSpec(memory_space=pl.ANY)

norm_eps = 1e-05
f32 = jnp.float32
bf16 = jnp.bfloat16


def inverse_rms(values):
    return lax.rsqrt(jnp.mean(values * values, axis=-1, keepdims=True) + norm_eps)


def rms_back(grad_scaled, scaled, inverse):
    return inverse * (grad_scaled - scaled * jnp.mean(grad_scaled * scaled, axis=-1, keepdims=True))


def dot_nt(left, right):
    return lax.dot_general(left, right, (((1,), (1,)), ((), ())), preferred_element_type=f32)


def dot_nn(left, right):
    return lax.dot_general(left, right, (((1,), (0,)), ((), ())), preferred_element_type=f32)


def dot_tn(left, right):
    return lax.dot_general(left, right, (((0,), (0,)), ((), ())), preferred_element_type=f32)


def cost(micros):
    return pl.CostEstimate(flops=0, transcendentals=0, bytes_accessed=int(micros * 36_900))


def places():
    me = lax.axis_index("fsdp")
    slot = lax.rem(me, GROUP)
    core = lax.rem(slot, 2)
    step_low = 2 - 4 * lax.rem(slot // 2, 2)
    step_high = 4 - 8 * (slot // 4)
    step_core = 1 - 2 * core
    first_step = (1 - core) * step_low + core * step_high
    second_step = core * step_low + (1 - core) * step_high
    return me, slot, step_core, first_step, second_step


def greet(others):
    barrier = pltpu.get_barrier_semaphore()
    for other in others:
        pl.semaphore_signal(barrier, inc=1, device_id=(other,), device_id_type=MESH_ID)
    pl.semaphore_wait(barrier, len(others))


def remote(source, target, send_sem, recv_sem, device):
    return pltpu.make_async_remote_copy(
        src_ref=source,
        dst_ref=target,
        send_sem=send_sem,
        recv_sem=recv_sem,
        device_id=(device,),
        device_id_type=MESH_ID,
    )


def plane_steps(step_core, step_low, step_high):
    return [
        (number, (number & 1) * step_core + ((number >> 1) & 1) * step_low + (number >> 2) * step_high)
        for number in range(1, GROUP)
    ]


AROUND = (1, 2, 4, 3, 5, 6, 7)


def exchange_kernel(plan, *refs):
    count = len(plan)
    ins, outs = refs[:count], refs[count : 2 * count]
    send_sem, recv_sem, own_sem = refs[2 * count :]
    me, slot, step_core, first_step, second_step = places()
    core = lax.rem(slot, 2)
    step_low = (1 - core) * first_step + core * second_step
    step_high = core * first_step + (1 - core) * second_step
    others = plane_steps(step_core, step_low, step_high)
    group = me // GROUP
    groups = lax.axis_size("fsdp") // GROUP
    greeted = [me + first_step, me + second_step, me + step_core]
    if not set(plan) <= {"gather", "around"}:
        greeted = [me + step for _, step in others]
    line = []
    if "all" in plan:
        line = [
            (
                number,
                lax.rem(group + number, groups) * GROUP + slot,
                lax.rem(group + groups - number, groups),
            )
            for number in range(1, groups)
        ]
        greeted = greeted + [target for _, target, _ in line]
    greet(greeted)
    sent = []

    def copy_of(item, source, target, number, device):
        return remote(source, target, send_sem.at[item, number], recv_sem.at[item, number], device)

    def send(item, source, target, number, device):
        copy = copy_of(item, source, target, number, device)
        copy.start()
        sent.append(copy)

    def arrived(item, target, number):
        copy_of(item, target, target, number, me).wait_recv()

    def keep(item, source, target):
        copy = pltpu.make_async_copy(source, target, own_sem.at[item])
        copy.start()
        return copy

    def block(item, place):
        kind, out = plan[item], outs[item]
        if kind == "widen":
            columns = out.shape[1] // GROUP
            return out.at[:, pl.ds(pl.multiple_of(place * columns, columns), columns)]
        if kind in ("gather", "around"):
            return out.at[:, place]
        return out.at[place]

    def landing(item, place, number):
        return block(item, AROUND[number] if plan[item] == "around" else place)

    def piece(item, place):
        if plan[item] == "narrow":
            columns = ins[item].shape[1] // GROUP
            return ins[item].at[:, pl.ds(pl.multiple_of(place * columns, columns), columns)]
        return ins[item].at[place]

    own = []
    for item, kind in enumerate(plan):
        if kind == "all":
            keep(item, ins[item], outs[item].at[group, slot]).wait()
            for number, target, _ in line:
                send(item, ins[item], outs[item].at[group, slot], GROUP - 1 + number, target)
        elif kind in ("gather", "around"):
            for number, step in enumerate((first_step, second_step, step_core)):
                send(item, ins[item], landing(item, slot, number), number, me + step)
            own.append(keep(item, ins[item], block(item, 0 if kind == "around" else slot)))
    for item, kind in enumerate(plan):
        if kind in ("swap", "widen", "narrow"):
            for number, step in others:
                send(item, piece(item, slot + step), block(item, slot), number - 1, me + step)
            own.append(keep(item, piece(item, slot), block(item, slot)))
    for item, kind in enumerate(plan):
        if kind == "all":
            for number, _, sender in line:
                arrived(item, outs[item].at[sender, slot], GROUP - 1 + number)
            for number, step in others:
                send(item, outs[item].at[:, slot], outs[item].at[:, slot], number - 1, me + step)
    corner_step = first_step + second_step
    for item, kind in enumerate(plan):
        if kind in ("gather", "around"):
            for place, number, onward in (
                (slot + first_step, 0, ((3, second_step), (4, step_core))),
                (slot + second_step, 1, ((5, step_core),)),
                (slot + corner_step, 3, ((6, step_core),)),
            ):
                here = landing(item, place, number)
                arrived(item, here, number)
                for then, step in onward:
                    send(item, here, landing(item, place, then), then, me + step)
    for item, kind in enumerate(plan):
        if kind in ("gather", "around"):
            for step, number in ((0, 2), (second_step, 4), (first_step, 5), (corner_step, 6)):
                arrived(item, landing(item, slot + step_core + step, number), number)
        elif kind == "all":
            for number, step in others:
                arrived(item, outs[item].at[:, slot + step], number - 1)
        else:
            for number, step in others:
                arrived(item, block(item, slot + step), number - 1)
    for copy in sent:
        copy.wait_send()
    for copy in own:
        copy.wait()


def exchange(number, micros, *items):
    groups = lax.axis_size("fsdp") // GROUP
    kinds = [kind for kind, _ in items]
    arrays = [array for _, array in items]
    shapes = []
    for kind, array in items:
        if kind in ("gather", "around"):
            shape = (array.shape[0], GROUP) + array.shape[1:]
        elif kind == "swap":
            shape = array.shape
        elif kind == "widen":
            shape = (array.shape[1], GROUP * array.shape[2])
        elif kind == "narrow":
            shape = (GROUP, array.shape[0], array.shape[1] // GROUP)
        else:
            shape = (groups, GROUP) + array.shape
        shapes.append(jax.ShapeDtypeStruct(shape, array.dtype))
    numbers = GROUP - 1 + (groups if "all" in kinds else 0)
    return pl.pallas_call(
        functools.partial(exchange_kernel, kinds),
        out_shape=tuple(shapes),
        in_specs=[ANY] * len(items),
        out_specs=tuple([ANY] * len(items)),
        scratch_shapes=[
            pltpu.SemaphoreType.DMA((len(items), numbers)),
            pltpu.SemaphoreType.DMA((len(items), numbers)),
            pltpu.SemaphoreType.DMA((len(items),)),
        ],
        compiler_params=pltpu.CompilerParams(collective_id=number, has_side_effects=True),
        cost_estimate=cost(micros),
    )(*arrays)


def owners_kernel(pieces, in_ref, out_ref):
    columns = out_ref.shape[2] // pieces
    for piece in range(pieces):
        for owner in range(GROUP):
            lo = (piece * GROUP + owner) * columns
            out_ref[owner, :, piece * columns : (piece + 1) * columns] = in_ref[:, lo : lo + columns]


def by_owner(weight, pieces):
    rows, columns = weight.shape
    return pl.pallas_call(
        functools.partial(owners_kernel, pieces),
        out_shape=jax.ShapeDtypeStruct((GROUP, rows, columns // GROUP), weight.dtype),
        in_specs=[VMEM],
        out_specs=VMEM,
        compiler_params=pltpu.CompilerParams(vmem_limit_bytes=32 * 2**20),
        cost_estimate=cost(3),
    )(weight)


def dealt_columns_kernel(piece, in_ref, out_ref):
    for owner in range(GROUP):
        for part in range(out_ref.shape[2] // piece):
            lo = (part * GROUP + owner) * piece
            out_ref[owner, :, part * piece : (part + 1) * piece] = in_ref[:, lo : lo + piece]


def dealt_columns(x, piece):
    rows, columns = x.shape
    return pl.pallas_call(
        functools.partial(dealt_columns_kernel, piece),
        out_shape=jax.ShapeDtypeStruct((GROUP, rows, columns // GROUP), x.dtype),
        in_specs=[VMEM],
        out_specs=VMEM,
        compiler_params=pltpu.CompilerParams(vmem_limit_bytes=32 * 2**20),
        cost_estimate=cost(2),
    )(x)


def home_kernel(pieces, got_ref, weight_ref, out_ref, gain_ref):
    columns = got_ref.shape[2] // pieces
    for sender in range(GROUP):
        for piece in range(pieces):
            lo = (piece * GROUP + sender) * columns
            out_ref[:, lo : lo + columns] = got_ref[
                sender, :, piece * columns : (piece + 1) * columns
            ].astype(f32)
    gain_ref[...] = jnp.sum(out_ref[...] * weight_ref[...].astype(f32), axis=1, keepdims=True)


def home(got, weight, pieces):
    rows, columns = weight.shape
    return pl.pallas_call(
        functools.partial(home_kernel, pieces),
        out_shape=(
            jax.ShapeDtypeStruct((rows, columns), f32),
            jax.ShapeDtypeStruct((rows, 1), f32),
        ),
        in_specs=[VMEM, VMEM],
        out_specs=(VMEM, VMEM),
        compiler_params=pltpu.CompilerParams(vmem_limit_bytes=32 * 2**20),
        cost_estimate=cost(5),
    )(got, weight)


TILE = 1024


def product_scatter_kernel(swaps, around, a_far, w_far, *refs):
    swap_refs, out_ref, swapped_refs = refs[:swaps], refs[swaps], refs[swaps + 1 : 2 * swaps + 1]
    near, far, away, going, send_sem, recv_sem, a_ref, w_ref, a_sem, w_sem = refs[
        2 * swaps + 1 : 2 * swaps + 11
    ]
    me, slot, step_core, first_step, second_step = places()
    first, second, mate = me + first_step, me + second_step, me + step_core
    core = lax.rem(slot, 2)
    others = plane_steps(
        step_core,
        (1 - core) * first_step + core * second_step,
        core * first_step + (1 - core) * second_step,
    )
    corner_step = first_step + second_step
    if around:
        own_places, mate_places = (3, 1, 2, 0), (7, 5, 6, 4)
    else:
        own_places = (slot + corner_step, slot + first_step, slot + second_step, slot)
        mate_slot = slot + step_core
        mate_places = (
            mate_slot + corner_step,
            mate_slot + second_step,
            mate_slot + first_step,
            mate_slot,
        )

    def a_load(place):
        return pltpu.make_async_copy(a_far.at[place], a_ref.at[place], a_sem.at[place])

    def w_load(i):
        at = pl.ds(i * TILE, TILE)
        return pltpu.make_async_copy(w_far.at[at, :], w_ref.at[at, :], w_sem.at[i])

    a_load(mate_places[0]).start()
    for i in range(out_ref.shape[1] // TILE):
        w_load(i).start()
    for place in (
        mate_places[2],
        own_places[0],
        own_places[2],
        mate_places[1],
        mate_places[3],
        own_places[3],
        own_places[1],
    ):
        a_load(place).start()
    greet([me + step for _, step in others] if swaps else (first, second, mate))
    sent = []

    def send(source, target, number, device):
        copy = remote(source, target, send_sem.at[number], recv_sem.at[number], device)
        copy.start()
        sent.append(copy)

    def arrived(ref, number, source):
        remote(ref, ref, send_sem.at[number], recv_sem.at[number], source).wait_recv()

    def product(place, extra, target):
        a_load(place).wait()

        def tile(i, _):
            at = pl.ds(pl.multiple_of(i * TILE, TILE), TILE)
            total = dot_nt(a_ref[place], w_ref[at, :])
            for ref in extra:
                total = total + ref[:, at].astype(f32)
            target[:, at] = total.astype(target.dtype)
            return 0

        lax.fori_loop(0, out_ref.shape[1] // TILE, tile, 0)

    def to_mate(kind):
        product(mate_places[kind], (), away.at[kind])
        send(away.at[kind], near.at[kind], kind, mate)

    def add(ref):
        def tile(i, _):
            at = pl.ds(pl.multiple_of(i * TILE, TILE), TILE)
            out_ref[:, at] = out_ref[:, at] + ref[:, at].astype(f32)
            return 0

        lax.fori_loop(0, out_ref.shape[1] // TILE, tile, 0)

    swapping, kept = [], []
    if swaps:
        swap_send, swap_recv, swap_own = refs[2 * swaps + 11 :]

    def start_swaps():
        for item in range(swaps):
            for number, step in others:
                copy = remote(
                    swap_refs[item].at[slot + step],
                    swapped_refs[item].at[slot],
                    swap_send.at[item, number - 1],
                    swap_recv.at[item, number - 1],
                    me + step,
                )
                copy.start()
                swapping.append(copy)
            copy = pltpu.make_async_copy(
                swap_refs[item].at[slot], swapped_refs[item].at[slot], swap_own.at[item]
            )
            copy.start()
            kept.append(copy)

    start_swaps()
    for i in range(out_ref.shape[1] // TILE):
        w_load(i).wait()
    to_mate(0)
    to_mate(2)
    arrived(near.at[0], 0, mate)
    product(own_places[0], (near.at[0],), going.at[0])
    send(going.at[0], far.at[0], 4, second)
    arrived(near.at[2], 2, mate)
    product(own_places[2], (near.at[2],), going.at[2])
    send(going.at[2], far.at[2], 5, second)
    to_mate(1)
    to_mate(3)
    arrived(near.at[3], 3, mate)
    product(own_places[3], (near.at[3],), out_ref)
    arrived(near.at[1], 1, mate)
    arrived(far.at[0], 4, second)
    product(own_places[1], (near.at[1], far.at[0]), going.at[1])
    send(going.at[1], far.at[1], 6, first)
    arrived(far.at[2], 5, second)
    add(far.at[2])
    arrived(far.at[1], 6, first)
    add(far.at[1])
    for item in range(swaps):
        for number, step in others:
            target = swapped_refs[item].at[slot + step]
            remote(
                target,
                target,
                swap_send.at[item, number - 1],
                swap_recv.at[item, number - 1],
                me + step,
            ).wait_recv()
    for copy in sent + swapping:
        copy.wait_send()
    for copy in kept:
        copy.wait()


def product_scatter(a, w, number, around, *swaps):
    _, rows, depth = a.shape
    columns = w.shape[0]
    count = len(swaps)
    swap_sems = [
        pltpu.SemaphoreType.DMA((count, GROUP - 1)),
        pltpu.SemaphoreType.DMA((count, GROUP - 1)),
        pltpu.SemaphoreType.DMA((count,)),
    ]
    return pl.pallas_call(
        functools.partial(product_scatter_kernel, count, around),
        out_shape=(jax.ShapeDtypeStruct((rows, columns), f32),)
        + tuple(jax.ShapeDtypeStruct(x.shape, x.dtype) for x in swaps),
        in_specs=[ANY, ANY] + [ANY] * count,
        out_specs=(VMEM,) + (ANY,) * count,
        scratch_shapes=[
            pltpu.VMEM((4, rows, columns), bf16),
            pltpu.VMEM((3, rows, columns), bf16),
            pltpu.VMEM((4, rows, columns), bf16),
            pltpu.VMEM((3, rows, columns), bf16),
            pltpu.SemaphoreType.DMA((7,)),
            pltpu.SemaphoreType.DMA((7,)),
            pltpu.VMEM(a.shape, bf16),
            pltpu.VMEM(w.shape, bf16),
            pltpu.SemaphoreType.DMA((GROUP,)),
            pltpu.SemaphoreType.DMA((columns // TILE,)),
        ]
        + (swap_sems if swaps else []),
        compiler_params=pltpu.CompilerParams(
            collective_id=number, has_side_effects=True, vmem_limit_bytes=56 * 2**20
        ),
        cost_estimate=cost(50),
    )(a, w, *swaps)


def residual_back_kernel(
    d_second_ref,
    residual_ref,
    cot_ref,
    gain_ref,
    w_far,
    mixer_ref,
    down_ref,
    d_residual_ref,
    d_mix_ref,
    heads_ref,
    near_ref,
    swapped_ref,
    w_ref,
    parts_ref,
    away_ref,
    send_sem,
    recv_sem,
    own_sem,
    w_sem,
):
    me, slot, step_core, first_step, second_step = places()
    core = lax.rem(slot, 2)
    others = plane_steps(
        step_core,
        (1 - core) * first_step + core * second_step,
        core * first_step + (1 - core) * second_step,
    )
    mate = me + step_core
    width = parts_ref.shape[2]

    def w_load(i):
        at = pl.ds(i * width, width)
        return pltpu.make_async_copy(w_far.at[at, :], w_ref.at[i], w_sem.at[i])

    for i in range(GROUP):
        w_load(i).start()
    greet([me + step for _, step in others])
    sent = []

    def send(source, target, item, number, device):
        copy = remote(source, target, send_sem.at[item, number], recv_sem.at[item, number], device)
        copy.start()
        sent.append(copy)

    def arrived(target, item, number):
        remote(target, target, send_sem.at[item, number], recv_sem.at[item, number], me).wait_recv()

    for number, step in others:
        send(down_ref.at[slot + step], swapped_ref.at[slot], 2, number - 1, me + step)
    own_down = pltpu.make_async_copy(down_ref.at[slot], swapped_ref.at[slot], own_sem.at[0])
    own_down.start()
    rows = d_residual_ref.shape[0]
    slab_rows = 32

    def slab(i, _):
        at = pl.ds(pl.multiple_of(i * slab_rows, slab_rows), slab_rows)
        residual = residual_ref[at, :]
        inverse = inverse_rms(residual)
        grad = rms_back(d_second_ref[at, :] * gain_ref[...], residual * inverse, inverse)
        total = cot_ref[at, :].astype(f32) + grad
        d_residual_ref[at, :] = total
        d_mix_ref[at, :] = total.astype(bf16)
        return 0

    lax.fori_loop(0, rows // slab_rows, slab, 0)
    for i in range(GROUP):
        w_load(i).wait()

    def part(place):
        parts_ref[place] = dot_nt(d_mix_ref[...], w_ref[place]).astype(bf16)

    for number, step in reversed(others):
        part(slot + step)
        send(parts_ref.at[slot + step], heads_ref.at[slot], 0, number - 1, me + step)
    part(slot)
    own_part = pltpu.make_async_copy(parts_ref.at[slot], heads_ref.at[slot], own_sem.at[1])
    own_part.start()
    for kind in (3, 2, 1, 0):
        away_ref[kind] = dot_tn(mixer_ref[kind], d_mix_ref[...]).astype(bf16)
        send(away_ref.at[kind], near_ref.at[kind], 1, kind, mate)
    for number, step in others:
        arrived(heads_ref.at[slot + step], 0, number - 1)
        arrived(swapped_ref.at[slot + step], 2, number - 1)
    for kind in range(4):
        arrived(near_ref.at[kind], 1, kind)
    for copy in sent:
        copy.wait_send()
    own_down.wait()
    own_part.wait()


def residual_back(d_second, residual, cot, gain, w, mixer_away, down, number):
    rows, columns = residual.shape
    width = columns // GROUP
    blocks = mixer_away.shape[0]
    return pl.pallas_call(
        residual_back_kernel,
        out_shape=(
            jax.ShapeDtypeStruct((rows, columns), f32),
            jax.ShapeDtypeStruct((rows, columns), bf16),
            jax.ShapeDtypeStruct((GROUP, rows, width), bf16),
            jax.ShapeDtypeStruct((blocks, mixer_away.shape[2], columns), bf16),
            jax.ShapeDtypeStruct(down.shape, down.dtype),
        ),
        in_specs=[VMEM, VMEM, VMEM, VMEM, ANY, VMEM, ANY],
        out_specs=(VMEM, VMEM, ANY, ANY, ANY),
        scratch_shapes=[
            pltpu.VMEM((GROUP, width, columns), bf16),
            pltpu.VMEM((GROUP, rows, width), bf16),
            pltpu.VMEM((blocks, mixer_away.shape[2], columns), bf16),
            pltpu.SemaphoreType.DMA((3, GROUP - 1)),
            pltpu.SemaphoreType.DMA((3, GROUP - 1)),
            pltpu.SemaphoreType.DMA((2,)),
            pltpu.SemaphoreType.DMA((GROUP,)),
        ],
        compiler_params=pltpu.CompilerParams(
            collective_id=number, has_side_effects=True, vmem_limit_bytes=48 * 2**20
        ),
        cost_estimate=cost(20),
    )(d_second, residual, cot, gain, w, mixer_away, down)


def gate_gather_kernel(
    own_ref,
    x_far,
    w_far,
    all_ref,
    gate_far,
    up_far,
    hidden_far,
    x_ref,
    w_ref,
    gate_ref,
    up_ref,
    hidden_ref,
    send_sem,
    recv_sem,
    own_sem,
    x_sem,
    w_sem,
    store_sem,
):
    me, slot, step_core, first_step, second_step = places()
    first, second, mate = me + first_step, me + second_step, me + step_core
    w_load = pltpu.make_async_copy(w_far, w_ref, w_sem)
    w_load.start()
    tiles, tile_rows = x_ref.shape[:2]
    half = gate_ref.shape[2]

    def rows_of(i):
        return pl.ds(pl.multiple_of(i * tile_rows, tile_rows), tile_rows)

    def x_load(i):
        return pltpu.make_async_copy(x_far.at[rows_of(i), :], x_ref.at[i], x_sem.at[i])

    for i in range(tiles):
        x_load(i).start()
    greet((first, second, mate))
    sent = []

    def send(source, number, device):
        copy = remote(
            source, all_ref.at[AROUND[number]], send_sem.at[number], recv_sem.at[number], device
        )
        copy.start()
        sent.append(copy)

    def arrived(number):
        target = all_ref.at[AROUND[number]]
        remote(target, target, send_sem.at[number], recv_sem.at[number], me).wait_recv()
        return target

    own = pltpu.make_async_copy(own_ref, all_ref.at[0], own_sem)
    send(own_ref, 0, first)
    send(own_ref, 1, second)
    send(own_ref, 2, mate)
    own.start()

    def stores(i, spot):
        return [
            pltpu.make_async_copy(near.at[spot], far.at[rows_of(i), :], store_sem.at[spot, number])
            for number, (near, far) in enumerate(
                ((gate_ref, gate_far), (up_ref, up_far), (hidden_ref, hidden_far))
            )
        ]

    def tile(i, _):
        spot = lax.rem(i, 2)
        x_load(i).wait()

        @pl.when(i >= 2)
        def _():
            for copy in stores(i - 2, spot):
                copy.wait()

        both = dot_nn(x_ref[i], w_ref[...])
        gate = both[:, :half]
        up = both[:, half:]
        gate_ref[spot] = gate
        up_ref[spot] = up
        hidden_ref[spot] = (gate * jax.nn.sigmoid(gate) * up).astype(bf16)
        for copy in stores(i, spot):
            copy.start()
        return 0

    w_load.wait()
    lax.fori_loop(0, tiles // 2, tile, 0)
    block = arrived(0)
    send(block, 3, second)
    send(block, 4, mate)
    send(arrived(1), 5, mate)
    lax.fori_loop(tiles // 2, tiles, tile, 0)
    for i in (tiles - 2, tiles - 1):
        for copy in stores(i, i % 2):
            copy.wait()
    send(arrived(3), 6, mate)
    for number in (2, 4, 5, 6):
        arrived(number)
    for copy in sent:
        copy.wait_send()
    own.wait()


def gate_gather(own, x, w, number):
    rows, columns = own.shape
    half = w.shape[1] // 2
    tiles = x.shape[0] // rows
    wide = jax.ShapeDtypeStruct((x.shape[0], half), f32)
    return pl.pallas_call(
        gate_gather_kernel,
        out_shape=(
            jax.ShapeDtypeStruct((GROUP, rows, columns), own.dtype),
            wide,
            wide,
            jax.ShapeDtypeStruct((x.shape[0], half), bf16),
        ),
        in_specs=[ANY, ANY, ANY],
        out_specs=(ANY, ANY, ANY, ANY),
        scratch_shapes=[
            pltpu.VMEM((tiles, rows, x.shape[1]), bf16),
            pltpu.VMEM(w.shape, bf16),
            pltpu.VMEM((2, rows, half), f32),
            pltpu.VMEM((2, rows, half), f32),
            pltpu.VMEM((2, rows, half), bf16),
            pltpu.SemaphoreType.DMA((7,)),
            pltpu.SemaphoreType.DMA((7,)),
            pltpu.SemaphoreType.DMA,
            pltpu.SemaphoreType.DMA((tiles,)),
            pltpu.SemaphoreType.DMA,
            pltpu.SemaphoreType.DMA((2, 3)),
        ],
        compiler_params=pltpu.CompilerParams(
            collective_id=number, has_side_effects=True, vmem_limit_bytes=56 * 2**20
        ),
        cost_estimate=cost(45),
    )(own, x, w)


def hidden_back_kernel(cot_ref, gate_ref, up_ref, w_ref, grad_ref):
    half = gate_ref.shape[1]
    d_hidden = dot_nn(cot_ref[...], w_ref[...])
    gate = gate_ref[...]
    sigmoid = jax.nn.sigmoid(gate)
    grad_ref[:, :half] = (
        d_hidden * up_ref[...] * sigmoid * (1.0 + gate * (1.0 - sigmoid))
    ).astype(bf16)
    grad_ref[:, half:] = (d_hidden * gate * sigmoid).astype(bf16)


def hidden_back(cot, gate, up, w):
    rows, columns = cot.shape
    half = w.shape[1]
    tile_rows = 256

    def tiles(width):
        return pl.BlockSpec((tile_rows, width), lambda i: (i, 0))

    return pl.pallas_call(
        hidden_back_kernel,
        grid=(rows // tile_rows,),
        in_specs=[
            tiles(columns),
            tiles(half),
            tiles(half),
            pl.BlockSpec(w.shape, lambda i: (0, 0)),
        ],
        out_specs=tiles(2 * half),
        out_shape=jax.ShapeDtypeStruct((rows, 2 * half), bf16),
        compiler_params=pltpu.CompilerParams(vmem_limit_bytes=56 * 2**20),
        cost_estimate=cost(20),
    )(cot, gate, up, w)


def away_product_kernel(x_ref, w_ref, out_ref):
    out_ref[...] = dot_nt(x_ref[...], w_ref[...]).astype(bf16)


def away_product(x, w, tile_rows):
    rows, depth = x.shape
    tiles = rows // tile_rows // 2
    return pl.pallas_call(
        away_product_kernel,
        grid=(tiles,),
        in_specs=[
            pl.BlockSpec((tile_rows, depth), lambda i: (tiles + i, 0)),
            pl.BlockSpec(w.shape, lambda i: (0, 0)),
        ],
        out_specs=pl.BlockSpec((tile_rows, w.shape[0]), lambda i: (i, 0)),
        out_shape=jax.ShapeDtypeStruct((rows // 2, w.shape[0]), bf16),
        compiler_params=pltpu.CompilerParams(vmem_limit_bytes=56 * 2**20),
        cost_estimate=cost(6),
    )(x, w)


def keep_product_kernel(x_ref, w_ref, near_ref, out_ref):
    total = dot_nt(x_ref[...], w_ref[...]) + near_ref[0].astype(f32)
    out_ref[0] = total.astype(out_ref.dtype)


def keep_product(x, w, near, begin, number, out_type):
    _, rows, columns = near.shape
    return pl.pallas_call(
        keep_product_kernel,
        grid=(number,),
        in_specs=[
            pl.BlockSpec((rows, x.shape[1]), lambda i: (begin + i, 0)),
            pl.BlockSpec(w.shape, lambda i: (0, 0)),
            pl.BlockSpec((1, rows, columns), lambda i: (begin + i, 0, 0)),
        ],
        out_specs=pl.BlockSpec((1, rows, columns), lambda i: (i, 0, 0)),
        out_shape=jax.ShapeDtypeStruct((number, rows, columns), out_type),
        compiler_params=pltpu.CompilerParams(vmem_limit_bytes=56 * 2**20),
        cost_estimate=cost(5),
    )(x, w, near)


def rows_product_kernel(x_ref, y_ref, out_ref):
    out_ref[...] = dot_tn(x_ref[...], y_ref[...]).astype(bf16)


def rows_product(x, y, micros):
    rows, columns = x.shape
    wide = y.shape[1]
    tile_columns = 512
    return pl.pallas_call(
        rows_product_kernel,
        grid=(columns // tile_columns,),
        in_specs=[
            pl.BlockSpec((rows, tile_columns), lambda i: (0, i)),
            pl.BlockSpec((rows, wide), lambda i: (0, 0)),
        ],
        out_specs=pl.BlockSpec((tile_columns, wide), lambda i: (i, 0)),
        out_shape=jax.ShapeDtypeStruct((columns, wide), bf16),
        compiler_params=pltpu.CompilerParams(vmem_limit_bytes=56 * 2**20),
        cost_estimate=cost(micros),
    )(x, y)


def plane_permutes(device_count):
    first, second, mate = [], [], []
    for i in range(device_count):
        low_bit, high_bit = (2, 4) if i % 2 == 0 else (4, 2)
        first.append((i, i ^ low_bit))
        second.append((i, i ^ high_bit))
        mate.append((i, i ^ 1))
    return first, second, mate


def after(values, *earlier):
    return lax.optimization_barrier((values, earlier))[0]


def meet(*values):
    return lax.optimization_barrier(values)


def assemble_kernel(*refs):
    blocks, out_ref = refs[:GROUP], refs[GROUP]
    _, slot, step_core, first_step, second_step = places()
    corner_step = first_step + second_step
    here = (0, first_step, second_step, corner_step)
    there = (step_core, step_core + second_step, step_core + first_step, step_core + corner_step)
    for number, step in enumerate(here + there):
        out_ref[:, slot + step] = blocks[number][...]


def assemble(x, from_first, from_second, from_corner, mates):
    parts, rows, columns = x.shape
    return pl.pallas_call(
        assemble_kernel,
        out_shape=jax.ShapeDtypeStruct((parts, GROUP, rows, columns), x.dtype),
        in_specs=[VMEM] * GROUP,
        out_specs=VMEM,
        compiler_params=pltpu.CompilerParams(vmem_limit_bytes=32 * 2**20),
        cost_estimate=cost(8),
    )(x, from_first, from_second, from_corner, *mates)


class SlowScatter:
    def __init__(self, keep, away, device_count):
        self.keep = keep
        self.away = away
        self.first, self.second, self.mate = plane_permutes(device_count)

    def to_mate(self):
        return lax.ppermute(self.away, "fsdp", self.mate)

    def onward(self, near):
        return (self.keep(2, 2) + near[2:].astype(f32)).astype(bf16)

    def to_second(self, sums):
        return lax.ppermute(sums, "fsdp", self.second)

    def half(self, near):
        return self.keep(1, 1)[0] + near[1].astype(f32)

    def both(self, half, far):
        return (half + far[1].astype(f32)).astype(bf16)

    def to_first(self, both):
        return lax.ppermute(both, "fsdp", self.first)

    def total(self, near, far, last):
        own = self.keep(0, 1)[0] + near[0].astype(f32)
        return own + far[0].astype(f32) + last.astype(f32)


def low(values):
    return values.astype(bf16).astype(f32)


def gates(proj_ref, floor_ref, rows, head, heads):
    dim = floor_ref.shape[1] // heads
    wide = heads * dim
    lo = head * dim
    q_pre = proj_ref[rows, lo : lo + dim]
    f_pre = proj_ref[rows, wide + lo : wide + lo + dim]
    value = proj_ref[rows, 2 * wide + lo : 2 * wide + lo + dim].astype(bf16)
    floor = floor_ref[:, lo : lo + dim]
    q_sigmoid = jax.nn.sigmoid(q_pre)
    query = low(q_pre * q_sigmoid)
    f_sigmoid = jax.nn.sigmoid(f_pre)
    forget = floor + (1.0 - floor) * f_sigmoid
    key = low(1.0 - forget)
    row = lax.broadcasted_iota(jnp.int32, (CHUNK, dim), 0)
    in_half = lax.rem(row, HALF)
    product = forget
    step = 1
    while step < HALF:
        product = jnp.where(in_half >= step, product * pltpu.roll(product, step, 0), product)
        step *= 2
    middle = product[HALF - 1 : HALF, :]
    end = product[CHUNK - 1 : CHUNK, :]
    ratio = jnp.where(row < HALF, product / middle, product)
    inverse = 1.0 / ratio
    return {
        "q_pre": q_pre,
        "q_sigmoid": q_sigmoid,
        "f_sigmoid": f_sigmoid,
        "forget": forget,
        "value": value,
        "floor": floor,
        "middle": middle,
        "end": end,
        "ratio": ratio,
        "inverse": inverse,
        "row": row,
        "query_mid": query * ratio,
        "key_mid": key * inverse,
    }


def whole_fade(g, last):
    return g["middle"] * g["end"] * jnp.where(last < 0, 1.0, 0.0)


def tail_keys(g, last):
    return jnp.where(g["row"] >= last, g["key_mid"] * g["end"], 0.0).astype(bf16)


def entry_queries(g, carried):
    return jnp.where(carried, g["query_mid"] * g["middle"], 0.0).astype(bf16)


def next_state(g, last, state):
    return state * whole_fade(g, last) + dot_tn(g["value"], tail_keys(g, last))


def forward_kernel(
    heads, last_ref, proj_ref, start_ref, floor_ref, gain_ref, in_ref, mix_ref, out_ref, enter_ref, state
):
    dim = floor_ref.shape[1] // heads
    chunks = proj_ref.shape[0] // CHUNK
    tile = pl.program_id(0)

    @pl.when(tile == 0)
    def _():
        state[...] = in_ref[...]

    def step(n, _):
        base = pl.multiple_of(n * CHUNK, CHUNK)
        rows = pl.ds(base, CHUNK)
        place = (tile * chunks + n) * CHUNK
        starts = start_ref[rows, :] - place
        last = last_ref[tile * chunks + n] - place
        column = lax.broadcasted_iota(jnp.int32, (CHUNK, CHUNK), 1)
        line = lax.broadcasted_iota(jnp.int32, (CHUNK, CHUNK), 0)
        within = (column <= line) & (column >= starts)
        carried = starts < 0
        for head in range(heads):
            lo = head * dim
            g = gates(proj_ref, floor_ref, rows, head, heads)
            now = state[head]
            enter_ref[n, head] = now
            scores = dot_nt(g["query_mid"].astype(bf16), g["key_mid"].astype(bf16))
            scores = jnp.where(within, scores, 0.0).astype(bf16)
            out = dot_nn(scores, g["value"]) + dot_nt(entry_queries(g, carried), now.astype(bf16))
            state[head] = next_state(g, last, now)
            out_ref[rows, lo : lo + dim] = out
            mix_ref[rows, lo : lo + dim] = (
                out * inverse_rms(out) * gain_ref[:, lo : lo + dim]
            ).astype(bf16)
        return 0

    lax.fori_loop(0, chunks, step, 0, unroll=UNROLL)


def last_state_kernel(heads, last_ref, proj_ref, floor_ref, out_ref):
    for head in range(heads):
        state = jnp.zeros(out_ref.shape[1:], f32)
        for n in range(proj_ref.shape[0] // CHUNK):
            g = gates(proj_ref, floor_ref, pl.ds(n * CHUNK, CHUNK), head, heads)
            state = next_state(g, last_ref[n] - n * CHUNK, state)
        out_ref[head] = state


def state_grad(out_ref, dmix_ref, gain_ref, rows, lo, dim):
    out = out_ref[rows, lo : lo + dim]
    inverse = inverse_rms(out)
    scaled = out * inverse
    dmix = dmix_ref[rows, lo : lo + dim].astype(f32)
    return rms_back(dmix * gain_ref[:, lo : lo + dim], scaled, inverse)


def backward_chunk(heads, n, at, refs, outs, later, before=0):
    last_ref, proj_ref, start_ref, floor_ref, gain_ref, out_ref, dmix_ref, enter_ref = refs
    dproj_ref, dfloor_ref = outs
    dim = floor_ref.shape[1] // heads
    wide = heads * dim
    base = n * CHUNK
    rows = pl.ds(base, CHUNK)
    place = (before + n) * CHUNK
    starts = start_ref[rows, :] - place
    last = last_ref[before + n] - place
    column = lax.broadcasted_iota(jnp.int32, (CHUNK, CHUNK), 1)
    line = lax.broadcasted_iota(jnp.int32, (CHUNK, CHUNK), 0)
    within = (column <= line) & (column >= starts)
    carried = starts < 0
    for head in range(heads):
        lo = head * dim
        g = gates(proj_ref, floor_ref, rows, head, heads)
        grad = state_grad(out_ref, dmix_ref, gain_ref, rows, lo, dim)
        grad_hi = grad.astype(bf16)
        grad_lo = (grad - grad_hi.astype(f32)).astype(bf16)
        state = enter_ref[n, head]
        after = later[head]
        after_low = after.astype(bf16)
        query_mid = g["query_mid"].astype(bf16)
        key_mid = g["key_mid"].astype(bf16)
        scores = jnp.where(within, dot_nt(query_mid, key_mid), 0.0).astype(bf16)
        d_scores = dot_nt(grad_hi, g["value"]) + dot_nt(grad_lo, g["value"])
        d_scores = jnp.where(within, d_scores, 0.0).astype(bf16)
        query_in = entry_queries(g, carried)
        key_out = tail_keys(g, last)
        d_query_mid = dot_nn(d_scores, key_mid)
        d_query_in = jnp.where(carried, dot_nn(grad_hi, state.astype(bf16)), 0.0)
        d_key_mid = dot_tn(d_scores, query_mid)
        d_key_out = jnp.where(g["row"] >= last, dot_nn(g["value"], after_low), 0.0)
        d_value = dot_tn(scores, grad_hi) + dot_nt(key_out, after_low)
        d_query = (d_query_mid + d_query_in * g["middle"]) * g["ratio"]
        d_key = (d_key_mid + d_key_out * g["end"]) * g["inverse"]
        tail = d_key_out * key_out.astype(f32)
        term = (
            d_query_mid * query_mid.astype(f32)
            + d_query_in * query_in.astype(f32)
            - d_key_mid * key_mid.astype(f32)
            - tail
        )
        fade = whole_fade(g, last)
        final = jnp.sum(tail, axis=0, keepdims=True) + fade * jnp.sum(
            state * after, axis=0, keepdims=True
        )
        step_rows = 1
        while step_rows < CHUNK:
            term = jnp.where(
                g["row"] < CHUNK - step_rows,
                term + pltpu.roll(term, CHUNK - step_rows, 0),
                term,
            )
            step_rows *= 2
        d_forget = (term + final) / g["forget"] - d_key
        q_sigmoid, f_sigmoid = g["q_sigmoid"], g["f_sigmoid"]
        d_q_pre = d_query * q_sigmoid * (1.0 + g["q_pre"] * (1.0 - q_sigmoid))
        d_floor = d_forget * (1.0 - f_sigmoid)
        d_f_pre = d_floor * (1.0 - g["floor"]) * f_sigmoid
        dproj_ref[at, lo : lo + dim] = d_q_pre.astype(bf16)
        dproj_ref[at, wide + lo : wide + lo + dim] = d_f_pre.astype(bf16)
        dproj_ref[at, 2 * wide + lo : 2 * wide + lo + dim] = d_value.astype(bf16)
        dfloor_ref[:, lo : lo + dim] += jnp.sum(d_floor, axis=0, keepdims=True)
        later[head] = after * fade + dot_tn(grad_hi, query_in)


def backward_rest(heads, n, refs, later, before=0):
    last_ref, proj_ref, start_ref, floor_ref, gain_ref, out_ref, dmix_ref = refs
    dim = floor_ref.shape[1] // heads
    rows = pl.ds(n * CHUNK, CHUNK)
    for head in range(heads):
        g = gates(proj_ref, floor_ref, rows, head, heads)
        grad = state_grad(out_ref, dmix_ref, gain_ref, rows, head * dim, dim)
        place = (before + n) * CHUNK
        queries = entry_queries(g, start_ref[rows, :] < place)
        fade = whole_fade(g, last_ref[before + n] - place)
        later[head] = later[head] * fade + dot_tn(grad.astype(bf16), queries)


def backward_kernel(heads, *refs):
    ins, outs, later = refs[:8], refs[8:10], refs[10]
    chunks = ins[1].shape[0] // CHUNK
    edge = MAXLEN // CHUNK
    tile = pl.num_programs(0) - 1 - pl.program_id(0)
    before = tile * chunks

    def step(i, first):
        n = first - i
        at = pl.ds(pl.multiple_of(n * CHUNK, CHUNK), CHUNK)
        backward_chunk(heads, n, at, ins, outs, later, before)
        return first

    @pl.when(pl.program_id(0) == 0)
    def _():
        later[...] = jnp.zeros_like(later)
        outs[1][...] = jnp.zeros_like(outs[1])
        for n in range(chunks - 1, chunks - 1 - edge, -1):
            backward_rest(heads, n, ins[:7], later, before)
        lax.fori_loop(0, chunks - edge, step, chunks - 1 - edge, unroll=UNROLL)

    @pl.when(pl.program_id(0) != 0)
    def _():
        lax.fori_loop(0, chunks, step, chunks - 1, unroll=UNROLL)


def backward_edge_kernel(heads, *refs):
    ins, in_ref, _, outs, later = refs[:8], refs[8], refs[9], refs[10:12], refs[12]
    later[...] = in_ref[...]
    outs[1][...] = jnp.zeros_like(outs[1])
    edge = MAXLEN // CHUNK
    before = ins[0].shape[0] - edge
    for n in range(edge - 1, -1, -1):
        backward_chunk(heads, n, pl.ds(n * CHUNK, CHUNK), ins, outs, later, before)


def first_grad_kernel(heads, *refs):
    ins, grad_ref = refs[:7], refs[7]
    grad_ref[...] = jnp.zeros_like(grad_ref)
    for n in range(ins[1].shape[0] // CHUNK - 1, -1, -1):
        backward_rest(heads, n, ins, grad_ref)


def local_call(kernel, heads, micros, out_shape, scratch, *operands):
    return pl.pallas_call(
        functools.partial(kernel, heads),
        out_shape=out_shape,
        in_specs=[SMEM] + [VMEM] * (len(operands) - 1),
        out_specs=jax.tree.map(lambda _: VMEM, out_shape),
        scratch_shapes=scratch,
        compiler_params=pltpu.CompilerParams(vmem_limit_bytes=56 * 2**20),
        cost_estimate=cost(micros),
    )(*operands)


def body(
    tokens,
    cotangent,
    dealt_lengths,
    deal,
    norm_gain,
    mixer_in,
    forget_floor,
    group_gain,
    out_proj,
    ffn_gain,
    gate_up,
    down_proj,
):
    row_count, width = tokens.shape
    weight_rows = mixer_in.shape[0]
    device_count = lax.axis_size("fsdp")
    groups = device_count // GROUP
    own_index = lax.axis_index("fsdp")
    slot = lax.rem(own_index, GROUP)
    group = own_index // GROUP
    group_rows = GROUP * row_count
    heads = HEADS // GROUP
    own_width = width // GROUP
    dim = width // HEADS
    ffn_width = down_proj.shape[1]
    own_ffn = ffn_width // GROUP
    planes = [[g * GROUP + s for s in range(GROUP)] for g in range(groups)]
    lines = [[g * GROUP + s for g in range(groups)] for s in range(GROUP)]

    def line_gather(x):
        return lax.all_gather(x, "fsdp", axis=0, axis_index_groups=lines, tiled=True)

    def line_scatter(x):
        return lax.psum_scatter(
            x, "fsdp", scatter_dimension=0, axis_index_groups=lines, tiled=True
        )

    def whole_rows(x):
        return line_gather(x.reshape(GROUP * weight_rows, -1))

    low_step = 2 - 4 * (slot // 2 % 2)
    high_step = 4 - 8 * (slot // 4)
    odd = slot % 2
    moves = (
        slot,
        1 - 2 * odd,
        jnp.where(odd == 0, low_step, high_step),
        jnp.where(odd == 0, high_step, low_step),
    )

    seq_count = deal.shape[0]
    seq_ids = jnp.arange(seq_count, dtype=jnp.int32)
    matches = deal[:, None] == seq_ids[None, :]
    lengths = jnp.sum(jnp.where(matches, dealt_lengths[:, None], 0), axis=0)
    seq_starts = jnp.sum(
        jnp.where(seq_ids[:, None] < seq_ids[None, :], lengths[:, None], 0), axis=0
    )
    group_start = group * group_rows
    rows_here = group_start + jnp.arange(group_rows, dtype=jnp.int32)
    starts = (
        jnp.max(jnp.where(seq_starts[None, :] <= rows_here[:, None], seq_starts[None, :], 0), axis=1)
        - group_start
    )
    start_column = starts[:, None]
    last_starts = starts[CHUNK - 1 :: CHUNK]

    out_lines = lax.all_gather(out_proj, "fsdp", axis=0, axis_index_groups=lines)
    gain_block = jnp.zeros((16, 128), bf16)
    for number, gain in enumerate((norm_gain, forget_floor, group_gain, ffn_gain)):
        gain_block = gain_block.at[number, :weight_rows].set(gain)
    gain_blocks, mixer_swapped = exchange(
        0, 15, ("all", gain_block), ("swap", by_owner(mixer_in, 3))
    )
    mixer_weight = whole_rows(mixer_swapped)
    gains = (
        gain_blocks[:, :, :4, :weight_rows].transpose(2, 0, 1, 3).reshape(4, width).astype(f32)
    )
    first_gain = gains[0:1]
    second_gain = gains[3:4]
    own_gains = lax.dynamic_slice_in_dim(gains, slot * own_width, own_width, 1)
    own_floor = own_gains[1:2]
    own_group_gain = own_gains[2:3]

    inputs = tokens.astype(f32)
    first_inverse = inverse_rms(inputs)
    first_scaled = inputs * first_inverse
    first_normed = (first_scaled * first_gain).astype(bf16)
    late_gate_up, late_down = after((gate_up, down_proj), mixer_swapped)
    first_all, ffn_swapped, down_swapped = exchange(
        1,
        58,
        ("gather", first_normed[None]),
        ("swap", by_owner(late_gate_up, 2)),
        ("swap", by_owner(late_down, 1)),
    )
    first_all = first_all.reshape(group_rows, width)
    ffn_weight = whole_rows(ffn_swapped)
    first, second, mate = plane_permutes(device_count)
    out_own = after(out_lines, first_all)
    from_first = lax.ppermute(out_own, "fsdp", first)
    from_second = lax.ppermute(out_own, "fsdp", second)
    tail_projected = dot_nn(first_all[group_rows - MAXLEN :], mixer_weight)
    edge = MAXLEN // CHUNK
    state_type = jax.ShapeDtypeStruct((heads, dim, dim), f32)
    last_state = local_call(
        last_state_kernel,
        heads,
        3,
        state_type,
        [],
        last_starts[-edge:] - (group_rows - MAXLEN),
        tail_projected,
        own_floor,
    )
    up_line = [(i, i + GROUP) for i in range(device_count - GROUP)]
    down_line = [(i + GROUP, i) for i in range(device_count - GROUP)]
    entering_state = lax.ppermute(last_state, "fsdp", up_line)
    projected = dot_nn(after(first_all, last_state), mixer_weight)
    projected, entering_state, from_first, from_second = meet(
        projected, entering_state, from_first, from_second
    )
    from_corner = lax.ppermute(from_first, "fsdp", second)
    mates = [lax.ppermute(block, "fsdp", mate) for block in (out_own, from_first, from_second)]
    chunks = group_rows // CHUNK
    tile_count = group_rows // TILE_ROWS

    def row_tiles(columns, turned=False):
        return pl.BlockSpec(
            (TILE_ROWS, columns), lambda i: (tile_count - 1 - i if turned else i, 0)
        )

    def state_tiles(turned=False):
        return pl.BlockSpec(
            (TILE_ROWS // CHUNK, heads, dim, dim),
            lambda i: (tile_count - 1 - i if turned else i, 0, 0, 0),
        )

    state_scratch = pltpu.VMEM((heads, dim, dim), f32)
    mixed_heads, state_out, entering = pl.pallas_call(
        functools.partial(forward_kernel, heads),
        grid=(tile_count,),
        out_shape=(
            jax.ShapeDtypeStruct((group_rows, own_width), bf16),
            jax.ShapeDtypeStruct((group_rows, own_width), f32),
            jax.ShapeDtypeStruct((chunks, heads, dim, dim), f32),
        ),
        in_specs=[SMEM, row_tiles(3 * own_width), row_tiles(1), VMEM, VMEM, VMEM],
        out_specs=(row_tiles(own_width), row_tiles(own_width), state_tiles()),
        scratch_shapes=[state_scratch],
        compiler_params=pltpu.CompilerParams(vmem_limit_bytes=56 * 2**20),
        cost_estimate=cost(18),
    )(last_starts, projected, start_column, own_floor, own_group_gain, entering_state)
    mixed_heads, from_corner = meet(mixed_heads, from_corner)
    mates = mates + [lax.ppermute(from_corner, "fsdp", mate)]
    [mixer_input] = exchange(
        3, 15, ("widen", mixed_heads.reshape(GROUP, row_count, own_width))
    )
    mixer_input, mates = meet(mixer_input, mates)
    _, step_core, first_step, second_step = moves
    steps = (0, first_step, second_step, first_step + second_step)
    mate_steps = [step_core + steps[kind] for kind in (0, 2, 1, 3)]
    mixer_blocks = dealt_columns(mixer_input, weight_rows)
    mixer_around = [
        lax.dynamic_index_in_dim(mixer_blocks, slot + step, 0) for step in (*steps, *mate_steps)
    ]
    mixer_keep = jnp.concatenate(mixer_around[:4])
    mixer_away = jnp.concatenate(mixer_around[4:])
    out_weight = assemble(out_own, from_first, from_second, from_corner, mates).reshape(width, width)
    down_weight = whole_rows(after(down_swapped, mixed_heads))
    residual = inputs + dot_nn(mixer_input, out_weight)
    second_inverse = inverse_rms(residual)
    second_scaled = residual * second_inverse
    second_normed = (second_scaled * second_gain).astype(bf16)
    second_normed, mixer_keep, mixer_away = meet(second_normed, mixer_keep, mixer_away)
    [second_all] = exchange(2, 43, ("around", second_normed[None]))
    second_all = second_all.reshape(group_rows, width)
    cot_blocks, gate_part, up_part, hidden_act = gate_gather(
        cotangent, second_all, ffn_weight, 6
    )
    cot_all = cot_blocks.reshape(group_rows, width)
    down_grad = rows_product(cot_all, hidden_act, 11)
    down_summed = line_scatter(down_grad)
    hidden_act = after(hidden_act, down_grad)

    ffn_away = away_product(hidden_act, down_weight, row_count).reshape(4, row_count, width)
    ffn_near = lax.ppermute(ffn_away, "fsdp", mate)
    d_gate_pre = hidden_back(after(cot_all, ffn_away), gate_part, up_part, down_weight)
    d_gate_pre, ffn_near = meet(d_gate_pre, ffn_near)
    ffn_sums = keep_product(hidden_act, down_weight, ffn_near, 2, 2, bf16)
    ffn_grad = rows_product(after(second_all, ffn_sums), d_gate_pre, 18)
    ffn_rest = keep_product(hidden_act, down_weight, after(ffn_near, ffn_grad), 0, 2, f32)
    ffn_grad, ffn_rest, ffn_far = meet(ffn_grad, ffn_rest, lax.ppermute(ffn_sums, "fsdp", second))
    ffn_both = (ffn_rest[1] + ffn_far[1].astype(f32)).astype(bf16)
    ffn_summed = line_scatter(ffn_grad)
    [d_second] = product_scatter(
        d_gate_pre.reshape(GROUP, row_count, -1), after(ffn_weight, ffn_grad, ffn_both), 4, True
    )
    d_second, ffn_last, down_summed = meet(
        d_second, lax.ppermute(ffn_both, "fsdp", first), down_summed
    )

    d_residual, d_mix_out, d_mixed_heads, out_near, down_swapped = residual_back(
        d_second,
        residual,
        cotangent,
        second_gain,
        out_weight,
        mixer_away,
        down_summed.reshape(GROUP, weight_rows, -1),
        5,
    )
    d_mixed_heads = d_mixed_heads.reshape(group_rows, own_width)

    def out_blocks(blocks):
        return lax.dot_general(
            blocks, d_mix_out, (((1,), (0,)), ((), ())), preferred_element_type=f32
        )

    out_sum = SlowScatter(
        lambda begin, number: out_blocks(mixer_keep[begin : begin + number]), None, device_count
    )
    operands = (projected, start_column, own_floor, own_group_gain, state_out, d_mixed_heads)

    def edge_specs(place):
        def rows(columns):
            return pl.BlockSpec((MAXLEN, columns), lambda i: (place, 0))

        return [rows(3 * own_width), rows(1), VMEM, VMEM, rows(own_width), rows(own_width)]

    first_grad = pl.pallas_call(
        functools.partial(first_grad_kernel, heads),
        grid=(1,),
        out_shape=state_type,
        in_specs=[SMEM] + edge_specs(0),
        out_specs=VMEM,
        compiler_params=pltpu.CompilerParams(vmem_limit_bytes=56 * 2**20),
        cost_estimate=cost(3),
    )(last_starts, *operands)
    entering_grad = lax.ppermute(first_grad, "fsdp", down_line)
    out_near = after(out_near, first_grad)
    out_far = out_sum.to_second(out_sum.onward(out_near))
    dproj_type = jax.ShapeDtypeStruct((group_rows, 3 * own_width), bf16)
    dfloor_type = jax.ShapeDtypeStruct((1, own_width), f32)
    d_projected, floor_most = pl.pallas_call(
        functools.partial(backward_kernel, heads),
        grid=(tile_count,),
        out_shape=(dproj_type, dfloor_type),
        in_specs=[
            SMEM,
            row_tiles(3 * own_width, True),
            row_tiles(1, True),
            VMEM,
            VMEM,
            row_tiles(own_width, True),
            row_tiles(own_width, True),
            state_tiles(True),
        ],
        out_specs=(row_tiles(3 * own_width, True), VMEM),
        scratch_shapes=[state_scratch],
        compiler_params=pltpu.CompilerParams(vmem_limit_bytes=56 * 2**20),
        cost_estimate=cost(30),
    )(last_starts, *operands, entering)
    d_projected, entering_grad = meet(d_projected, entering_grad)
    last_tile = group_rows // MAXLEN - 1
    d_projected, floor_rest = pl.pallas_call(
        functools.partial(backward_edge_kernel, heads),
        grid=(1,),
        out_shape=(dproj_type, dfloor_type),
        in_specs=[SMEM]
        + edge_specs(last_tile)
        + [pl.BlockSpec((edge, heads, dim, dim), lambda i: (last_tile, 0, 0, 0)), VMEM, ANY],
        out_specs=(
            pl.BlockSpec((MAXLEN, 3 * own_width), lambda i: (last_tile, 0)),
            VMEM,
        ),
        scratch_shapes=[state_scratch],
        input_output_aliases={9: 0},
        compiler_params=pltpu.CompilerParams(vmem_limit_bytes=56 * 2**20),
        cost_estimate=cost(4),
    )(last_starts, *operands, entering, entering_grad, d_projected)
    d_projected, out_far = meet(d_projected, out_far)
    out_both = out_sum.both(out_sum.half(out_near), out_far)
    d_projected = after(d_projected, out_both)
    floor_grad = floor_most + floor_rest
    by_sender = (GROUP, weight_rows, -1)
    floor_parts = lax.dynamic_update_slice_in_dim(
        jnp.zeros((width,), f32), floor_grad[0], slot * own_width, 0
    ).reshape(device_count, weight_rows)
    floor_parts = lax.all_to_all(floor_parts, "fsdp", 0, 0, tiled=True)
    mixer_grad = rows_product(first_all, d_projected, 11)
    mixer_grad, out_last = meet(mixer_grad, out_sum.to_first(out_both))
    mixer_summed = line_scatter(mixer_grad)
    out_total = out_sum.total(after(out_near, mixer_grad), out_far, out_last).astype(bf16)
    out_summed = line_scatter(out_total.reshape(groups * weight_rows, width))
    d_first, ffn_swapped = product_scatter(
        d_projected.reshape(GROUP, row_count, -1),
        after(mixer_weight, out_total),
        8,
        False,
        ffn_summed.reshape(by_sender),
    )
    d_first, mixer_summed, floor_parts = meet(d_first, mixer_summed, floor_parts)
    d_forget_floor = jnp.sum(floor_parts, axis=0)

    def swap(x):
        x = x.reshape(by_sender)
        return lax.all_to_all(x, "fsdp", 0, 0, axis_index_groups=planes, tiled=True)

    mixer_swapped = swap(mixer_summed)
    ffn_last = after(ffn_last, d_first)
    layer_out = residual + (ffn_rest[0] + ffn_far[0].astype(f32) + ffn_last.astype(f32))
    d_gate_up, ffn_gain_sum = home(ffn_swapped, gate_up, 2)
    d_mixer_in, norm_gain_sum = home(mixer_swapped, mixer_in, 3)
    d_down_proj, _ = home(down_swapped, down_proj, 1)
    d_dealt = d_residual + rms_back(d_first * first_gain, first_scaled, first_inverse)

    d_out_proj = after(out_summed, d_dealt, mixer_swapped).astype(f32)

    group_gain_sum = jnp.sum(out_proj.astype(f32) * d_out_proj, axis=1)
    return (
        layer_out,
        d_dealt,
        norm_gain_sum[:, 0] / norm_gain.astype(f32),
        d_mixer_in,
        d_forget_floor,
        group_gain_sum / group_gain.astype(f32),
        d_out_proj,
        ffn_gain_sum[:, 0] / ffn_gain.astype(f32),
        d_gate_up,
        d_down_proj,
    )


def solution(mesh):
    by_rows = P("fsdp", None)
    by_one = P("fsdp")
    return jax.shard_map(
        body,
        mesh=mesh,
        in_specs=(
            by_rows,
            by_rows,
            P(),
            P(),
            by_one,
            by_rows,
            by_one,
            by_one,
            by_rows,
            by_one,
            by_rows,
            by_rows,
        ),
        out_specs=(
            by_rows,
            by_rows,
            by_one,
            by_rows,
            by_one,
            by_one,
            by_rows,
            by_one,
            by_rows,
            by_rows,
        ),
        check_vma=False,
    )
```

```python
import functools

import jax
import jax.numpy as jnp
from jax import lax
from jax.experimental import pallas as pl
from jax.experimental.pallas import tpu as pltpu
from jax.sharding import PartitionSpec as P

HEADS = 16
CHUNK = 64
HALF = 32
TILE_ROWS = 512
UNROLL = 2
MAXLEN = 128
GROUP = 8
MESH_ID = pl.DeviceIdType.MESH
VMEM = pl.BlockSpec(memory_space=pltpu.VMEM)
SMEM = pl.BlockSpec(memory_space=pltpu.SMEM)
ANY = pl.BlockSpec(memory_space=pl.ANY)

norm_eps = 1e-05
f32 = jnp.float32
bf16 = jnp.bfloat16


def inverse_rms(values):
    return lax.rsqrt(jnp.mean(values * values, axis=-1, keepdims=True) + norm_eps)


def rms_back(grad_scaled, scaled, inverse):
    return inverse * (grad_scaled - scaled * jnp.mean(grad_scaled * scaled, axis=-1, keepdims=True))


def dot_nt(left, right):
    return lax.dot_general(left, right, (((1,), (1,)), ((), ())), preferred_element_type=f32)


def dot_nn(left, right):
    return lax.dot_general(left, right, (((1,), (0,)), ((), ())), preferred_element_type=f32)


def dot_tn(left, right):
    return lax.dot_general(left, right, (((0,), (0,)), ((), ())), preferred_element_type=f32)


def cost(micros):
    return pl.CostEstimate(flops=0, transcendentals=0, bytes_accessed=int(micros * 36_900))


def places():
    me = lax.axis_index("fsdp")
    slot = lax.rem(me, GROUP)
    core = lax.rem(slot, 2)
    step_low = 2 - 4 * lax.rem(slot // 2, 2)
    step_high = 4 - 8 * (slot // 4)
    step_core = 1 - 2 * core
    first_step = (1 - core) * step_low + core * step_high
    second_step = core * step_low + (1 - core) * step_high
    return me, slot, step_core, first_step, second_step


def greet(others):
    barrier = pltpu.get_barrier_semaphore()
    for other in others:
        pl.semaphore_signal(barrier, inc=1, device_id=(other,), device_id_type=MESH_ID)
    pl.semaphore_wait(barrier, len(others))


def remote(source, target, send_sem, recv_sem, device):
    return pltpu.make_async_remote_copy(
        src_ref=source,
        dst_ref=target,
        send_sem=send_sem,
        recv_sem=recv_sem,
        device_id=(device,),
        device_id_type=MESH_ID,
    )


def plane_steps(step_core, step_low, step_high):
    return [
        (number, (number & 1) * step_core + ((number >> 1) & 1) * step_low + (number >> 2) * step_high)
        for number in range(1, GROUP)
    ]


AROUND = (1, 2, 4, 3, 5, 6, 7)


def exchange_kernel(plan, *refs):
    count = len(plan)
    ins, outs = refs[:count], refs[count : 2 * count]
    send_sem, recv_sem, own_sem = refs[2 * count :]
    me, slot, step_core, first_step, second_step = places()
    core = lax.rem(slot, 2)
    step_low = (1 - core) * first_step + core * second_step
    step_high = core * first_step + (1 - core) * second_step
    others = plane_steps(step_core, step_low, step_high)
    group = me // GROUP
    groups = lax.axis_size("fsdp") // GROUP
    greeted = [me + first_step, me + second_step, me + step_core]
    if not set(plan) <= {"gather", "around"}:
        greeted = [me + step for _, step in others]
    line = []
    if "all" in plan:
        line = [
            (
                number,
                lax.rem(group + number, groups) * GROUP + slot,
                lax.rem(group + groups - number, groups),
            )
            for number in range(1, groups)
        ]
        greeted = greeted + [target for _, target, _ in line]
    greet(greeted)
    sent = []

    def copy_of(item, source, target, number, device):
        return remote(source, target, send_sem.at[item, number], recv_sem.at[item, number], device)

    def send(item, source, target, number, device):
        copy = copy_of(item, source, target, number, device)
        copy.start()
        sent.append(copy)

    def arrived(item, target, number):
        copy_of(item, target, target, number, me).wait_recv()

    def keep(item, source, target):
        copy = pltpu.make_async_copy(source, target, own_sem.at[item])
        copy.start()
        return copy

    def block(item, place):
        kind, out = plan[item], outs[item]
        if kind == "widen":
            columns = out.shape[1] // GROUP
            return out.at[:, pl.ds(pl.multiple_of(place * columns, columns), columns)]
        if kind in ("gather", "around"):
            return out.at[:, place]
        return out.at[place]

    def landing(item, place, number):
        return block(item, AROUND[number] if plan[item] == "around" else place)

    def piece(item, place):
        if plan[item] == "narrow":
            columns = ins[item].shape[1] // GROUP
            return ins[item].at[:, pl.ds(pl.multiple_of(place * columns, columns), columns)]
        return ins[item].at[place]

    own = []
    for item, kind in enumerate(plan):
        if kind == "all":
            keep(item, ins[item], outs[item].at[group, slot]).wait()
            for number, target, _ in line:
                send(item, ins[item], outs[item].at[group, slot], GROUP - 1 + number, target)
        elif kind in ("gather", "around"):
            for number, step in enumerate((first_step, second_step, step_core)):
                send(item, ins[item], landing(item, slot, number), number, me + step)
            own.append(keep(item, ins[item], block(item, 0 if kind == "around" else slot)))
    for item, kind in enumerate(plan):
        if kind in ("swap", "widen", "narrow"):
            for number, step in others:
                send(item, piece(item, slot + step), block(item, slot), number - 1, me + step)
            own.append(keep(item, piece(item, slot), block(item, slot)))
    for item, kind in enumerate(plan):
        if kind == "all":
            for number, _, sender in line:
                arrived(item, outs[item].at[sender, slot], GROUP - 1 + number)
            for number, step in others:
                send(item, outs[item].at[:, slot], outs[item].at[:, slot], number - 1, me + step)
    corner_step = first_step + second_step
    for item, kind in enumerate(plan):
        if kind in ("gather", "around"):
            for place, number, onward in (
                (slot + first_step, 0, ((3, second_step), (4, step_core))),
                (slot + second_step, 1, ((5, step_core),)),
                (slot + corner_step, 3, ((6, step_core),)),
            ):
                here = landing(item, place, number)
                arrived(item, here, number)
                for then, step in onward:
                    send(item, here, landing(item, place, then), then, me + step)
    for item, kind in enumerate(plan):
        if kind in ("gather", "around"):
            for step, number in ((0, 2), (second_step, 4), (first_step, 5), (corner_step, 6)):
                arrived(item, landing(item, slot + step_core + step, number), number)
        elif kind == "all":
            for number, step in others:
                arrived(item, outs[item].at[:, slot + step], number - 1)
        else:
            for number, step in others:
                arrived(item, block(item, slot + step), number - 1)
    for copy in sent:
        copy.wait_send()
    for copy in own:
        copy.wait()


def exchange(number, micros, *items):
    groups = lax.axis_size("fsdp") // GROUP
    kinds = [kind for kind, _ in items]
    arrays = [array for _, array in items]
    shapes = []
    for kind, array in items:
        if kind in ("gather", "around"):
            shape = (array.shape[0], GROUP) + array.shape[1:]
        elif kind == "swap":
            shape = array.shape
        elif kind == "widen":
            shape = (array.shape[1], GROUP * array.shape[2])
        elif kind == "narrow":
            shape = (GROUP, array.shape[0], array.shape[1] // GROUP)
        else:
            shape = (groups, GROUP) + array.shape
        shapes.append(jax.ShapeDtypeStruct(shape, array.dtype))
    numbers = GROUP - 1 + (groups if "all" in kinds else 0)
    return pl.pallas_call(
        functools.partial(exchange_kernel, kinds),
        out_shape=tuple(shapes),
        in_specs=[ANY] * len(items),
        out_specs=tuple([ANY] * len(items)),
        scratch_shapes=[
            pltpu.SemaphoreType.DMA((len(items), numbers)),
            pltpu.SemaphoreType.DMA((len(items), numbers)),
            pltpu.SemaphoreType.DMA((len(items),)),
        ],
        compiler_params=pltpu.CompilerParams(collective_id=number, has_side_effects=True),
        cost_estimate=cost(micros),
    )(*arrays)


def owners_kernel(pieces, in_ref, out_ref):
    columns = out_ref.shape[2] // pieces
    for piece in range(pieces):
        for owner in range(GROUP):
            lo = (piece * GROUP + owner) * columns
            out_ref[owner, :, piece * columns : (piece + 1) * columns] = in_ref[:, lo : lo + columns]


def by_owner(weight, pieces):
    rows, columns = weight.shape
    return pl.pallas_call(
        functools.partial(owners_kernel, pieces),
        out_shape=jax.ShapeDtypeStruct((GROUP, rows, columns // GROUP), weight.dtype),
        in_specs=[VMEM],
        out_specs=VMEM,
        compiler_params=pltpu.CompilerParams(vmem_limit_bytes=32 * 2**20),
        cost_estimate=cost(3),
    )(weight)


def dealt_columns_kernel(piece, in_ref, out_ref):
    for owner in range(GROUP):
        for part in range(out_ref.shape[2] // piece):
            lo = (part * GROUP + owner) * piece
            out_ref[owner, :, part * piece : (part + 1) * piece] = in_ref[:, lo : lo + piece]


def dealt_columns(x, piece):
    rows, columns = x.shape
    return pl.pallas_call(
        functools.partial(dealt_columns_kernel, piece),
        out_shape=jax.ShapeDtypeStruct((GROUP, rows, columns // GROUP), x.dtype),
        in_specs=[VMEM],
        out_specs=VMEM,
        compiler_params=pltpu.CompilerParams(vmem_limit_bytes=32 * 2**20),
        cost_estimate=cost(2),
    )(x)


def home_kernel(pieces, got_ref, weight_ref, out_ref, gain_ref):
    columns = got_ref.shape[2] // pieces
    for sender in range(GROUP):
        for piece in range(pieces):
            lo = (piece * GROUP + sender) * columns
            out_ref[:, lo : lo + columns] = got_ref[
                sender, :, piece * columns : (piece + 1) * columns
            ].astype(f32)
    gain_ref[...] = jnp.sum(out_ref[...] * weight_ref[...].astype(f32), axis=1, keepdims=True)


def home(got, weight, pieces):
    rows, columns = weight.shape
    return pl.pallas_call(
        functools.partial(home_kernel, pieces),
        out_shape=(
            jax.ShapeDtypeStruct((rows, columns), f32),
            jax.ShapeDtypeStruct((rows, 1), f32),
        ),
        in_specs=[VMEM, VMEM],
        out_specs=(VMEM, VMEM),
        compiler_params=pltpu.CompilerParams(vmem_limit_bytes=32 * 2**20),
        cost_estimate=cost(5),
    )(got, weight)


TILE = 1024


def product_scatter_kernel(swaps, around, a_far, w_far, *refs):
    swap_refs, out_ref, swapped_refs = refs[:swaps], refs[swaps], refs[swaps + 1 : 2 * swaps + 1]
    near, far, away, going, send_sem, recv_sem, a_ref, w_ref, a_sem, w_sem = refs[
        2 * swaps + 1 : 2 * swaps + 11
    ]
    me, slot, step_core, first_step, second_step = places()
    first, second, mate = me + first_step, me + second_step, me + step_core
    core = lax.rem(slot, 2)
    others = plane_steps(
        step_core,
        (1 - core) * first_step + core * second_step,
        core * first_step + (1 - core) * second_step,
    )
    corner_step = first_step + second_step
    if around:
        own_places, mate_places = (3, 1, 2, 0), (7, 5, 6, 4)
    else:
        own_places = (slot + corner_step, slot + first_step, slot + second_step, slot)
        mate_slot = slot + step_core
        mate_places = (
            mate_slot + corner_step,
            mate_slot + second_step,
            mate_slot + first_step,
            mate_slot,
        )

    def a_load(place):
        return pltpu.make_async_copy(a_far.at[place], a_ref.at[place], a_sem.at[place])

    def w_load(i):
        at = pl.ds(i * TILE, TILE)
        return pltpu.make_async_copy(w_far.at[at, :], w_ref.at[at, :], w_sem.at[i])

    a_load(mate_places[0]).start()
    for i in range(out_ref.shape[1] // TILE):
        w_load(i).start()
    for place in (
        mate_places[2],
        own_places[0],
        own_places[2],
        mate_places[1],
        mate_places[3],
        own_places[3],
        own_places[1],
    ):
        a_load(place).start()
    greet([me + step for _, step in others] if swaps else (first, second, mate))
    sent = []

    def send(source, target, number, device):
        copy = remote(source, target, send_sem.at[number], recv_sem.at[number], device)
        copy.start()
        sent.append(copy)

    def arrived(ref, number, source):
        remote(ref, ref, send_sem.at[number], recv_sem.at[number], source).wait_recv()

    def product(place, extra, target):
        a_load(place).wait()

        def tile(i, _):
            at = pl.ds(pl.multiple_of(i * TILE, TILE), TILE)
            total = dot_nt(a_ref[place], w_ref[at, :])
            for ref in extra:
                total = total + ref[:, at].astype(f32)
            target[:, at] = total.astype(target.dtype)
            return 0

        lax.fori_loop(0, out_ref.shape[1] // TILE, tile, 0)

    def to_mate(kind):
        product(mate_places[kind], (), away.at[kind])
        send(away.at[kind], near.at[kind], kind, mate)

    def add(ref):
        def tile(i, _):
            at = pl.ds(pl.multiple_of(i * TILE, TILE), TILE)
            out_ref[:, at] = out_ref[:, at] + ref[:, at].astype(f32)
            return 0

        lax.fori_loop(0, out_ref.shape[1] // TILE, tile, 0)

    swapping, kept = [], []
    if swaps:
        swap_send, swap_recv, swap_own = refs[2 * swaps + 11 :]

    def start_swaps():
        for item in range(swaps):
            for number, step in others:
                copy = remote(
                    swap_refs[item].at[slot + step],
                    swapped_refs[item].at[slot],
                    swap_send.at[item, number - 1],
                    swap_recv.at[item, number - 1],
                    me + step,
                )
                copy.start()
                swapping.append(copy)
            copy = pltpu.make_async_copy(
                swap_refs[item].at[slot], swapped_refs[item].at[slot], swap_own.at[item]
            )
            copy.start()
            kept.append(copy)

    start_swaps()
    for i in range(out_ref.shape[1] // TILE):
        w_load(i).wait()
    to_mate(0)
    to_mate(2)
    arrived(near.at[0], 0, mate)
    product(own_places[0], (near.at[0],), going.at[0])
    send(going.at[0], far.at[0], 4, second)
    arrived(near.at[2], 2, mate)
    product(own_places[2], (near.at[2],), going.at[2])
    send(going.at[2], far.at[2], 5, second)
    to_mate(1)
    to_mate(3)
    arrived(near.at[3], 3, mate)
    product(own_places[3], (near.at[3],), out_ref)
    arrived(near.at[1], 1, mate)
    arrived(far.at[0], 4, second)
    product(own_places[1], (near.at[1], far.at[0]), going.at[1])
    send(going.at[1], far.at[1], 6, first)
    arrived(far.at[2], 5, second)
    add(far.at[2])
    arrived(far.at[1], 6, first)
    add(far.at[1])
    for item in range(swaps):
        for number, step in others:
            target = swapped_refs[item].at[slot + step]
            remote(
                target,
                target,
                swap_send.at[item, number - 1],
                swap_recv.at[item, number - 1],
                me + step,
            ).wait_recv()
    for copy in sent + swapping:
        copy.wait_send()
    for copy in kept:
        copy.wait()


def product_scatter(a, w, number, around, *swaps):
    _, rows, depth = a.shape
    columns = w.shape[0]
    count = len(swaps)
    swap_sems = [
        pltpu.SemaphoreType.DMA((count, GROUP - 1)),
        pltpu.SemaphoreType.DMA((count, GROUP - 1)),
        pltpu.SemaphoreType.DMA((count,)),
    ]
    return pl.pallas_call(
        functools.partial(product_scatter_kernel, count, around),
        out_shape=(jax.ShapeDtypeStruct((rows, columns), f32),)
        + tuple(jax.ShapeDtypeStruct(x.shape, x.dtype) for x in swaps),
        in_specs=[ANY, ANY] + [ANY] * count,
        out_specs=(VMEM,) + (ANY,) * count,
        scratch_shapes=[
            pltpu.VMEM((4, rows, columns), bf16),
            pltpu.VMEM((3, rows, columns), bf16),
            pltpu.VMEM((4, rows, columns), bf16),
            pltpu.VMEM((3, rows, columns), bf16),
            pltpu.SemaphoreType.DMA((7,)),
            pltpu.SemaphoreType.DMA((7,)),
            pltpu.VMEM(a.shape, bf16),
            pltpu.VMEM(w.shape, bf16),
            pltpu.SemaphoreType.DMA((GROUP,)),
            pltpu.SemaphoreType.DMA((columns // TILE,)),
        ]
        + (swap_sems if swaps else []),
        compiler_params=pltpu.CompilerParams(
            collective_id=number, has_side_effects=True, vmem_limit_bytes=56 * 2**20
        ),
        cost_estimate=cost(50),
    )(a, w, *swaps)


def residual_back_kernel(
    d_second_ref,
    residual_ref,
    cot_ref,
    gain_ref,
    w_far,
    mixer_ref,
    down_ref,
    d_residual_ref,
    d_mix_ref,
    heads_ref,
    near_ref,
    swapped_ref,
    w_ref,
    parts_ref,
    away_ref,
    send_sem,
    recv_sem,
    own_sem,
    w_sem,
):
    me, slot, step_core, first_step, second_step = places()
    core = lax.rem(slot, 2)
    others = plane_steps(
        step_core,
        (1 - core) * first_step + core * second_step,
        core * first_step + (1 - core) * second_step,
    )
    mate = me + step_core
    width = parts_ref.shape[2]

    def w_load(i):
        at = pl.ds(i * width, width)
        return pltpu.make_async_copy(w_far.at[at, :], w_ref.at[i], w_sem.at[i])

    for i in range(GROUP):
        w_load(i).start()
    greet([me + step for _, step in others])
    sent = []

    def send(source, target, item, number, device):
        copy = remote(source, target, send_sem.at[item, number], recv_sem.at[item, number], device)
        copy.start()
        sent.append(copy)

    def arrived(target, item, number):
        remote(target, target, send_sem.at[item, number], recv_sem.at[item, number], me).wait_recv()

    for number, step in others:
        send(down_ref.at[slot + step], swapped_ref.at[slot], 2, number - 1, me + step)
    own_down = pltpu.make_async_copy(down_ref.at[slot], swapped_ref.at[slot], own_sem.at[0])
    own_down.start()
    rows = d_residual_ref.shape[0]
    slab_rows = 32

    def slab(i, _):
        at = pl.ds(pl.multiple_of(i * slab_rows, slab_rows), slab_rows)
        residual = residual_ref[at, :]
        inverse = inverse_rms(residual)
        grad = rms_back(d_second_ref[at, :] * gain_ref[...], residual * inverse, inverse)
        total = cot_ref[at, :].astype(f32) + grad
        d_residual_ref[at, :] = total
        d_mix_ref[at, :] = total.astype(bf16)
        return 0

    lax.fori_loop(0, rows // slab_rows, slab, 0)
    for i in range(GROUP):
        w_load(i).wait()

    def part(place):
        parts_ref[place] = dot_nt(d_mix_ref[...], w_ref[place]).astype(bf16)

    for number, step in reversed(others):
        part(slot + step)
        send(parts_ref.at[slot + step], heads_ref.at[slot], 0, number - 1, me + step)
    part(slot)
    own_part = pltpu.make_async_copy(parts_ref.at[slot], heads_ref.at[slot], own_sem.at[1])
    own_part.start()
    for kind in (3, 2, 1, 0):
        away_ref[kind] = dot_tn(mixer_ref[kind], d_mix_ref[...]).astype(bf16)
        send(away_ref.at[kind], near_ref.at[kind], 1, kind, mate)
    for number, step in others:
        arrived(heads_ref.at[slot + step], 0, number - 1)
        arrived(swapped_ref.at[slot + step], 2, number - 1)
    for kind in range(4):
        arrived(near_ref.at[kind], 1, kind)
    for copy in sent:
        copy.wait_send()
    own_down.wait()
    own_part.wait()


def residual_back(d_second, residual, cot, gain, w, mixer_away, down, number):
    rows, columns = residual.shape
    width = columns // GROUP
    blocks = mixer_away.shape[0]
    return pl.pallas_call(
        residual_back_kernel,
        out_shape=(
            jax.ShapeDtypeStruct((rows, columns), f32),
            jax.ShapeDtypeStruct((rows, columns), bf16),
            jax.ShapeDtypeStruct((GROUP, rows, width), bf16),
            jax.ShapeDtypeStruct((blocks, mixer_away.shape[2], columns), bf16),
            jax.ShapeDtypeStruct(down.shape, down.dtype),
        ),
        in_specs=[VMEM, VMEM, VMEM, VMEM, ANY, VMEM, ANY],
        out_specs=(VMEM, VMEM, ANY, ANY, ANY),
        scratch_shapes=[
            pltpu.VMEM((GROUP, width, columns), bf16),
            pltpu.VMEM((GROUP, rows, width), bf16),
            pltpu.VMEM((blocks, mixer_away.shape[2], columns), bf16),
            pltpu.SemaphoreType.DMA((3, GROUP - 1)),
            pltpu.SemaphoreType.DMA((3, GROUP - 1)),
            pltpu.SemaphoreType.DMA((2,)),
            pltpu.SemaphoreType.DMA((GROUP,)),
        ],
        compiler_params=pltpu.CompilerParams(
            collective_id=number, has_side_effects=True, vmem_limit_bytes=48 * 2**20
        ),
        cost_estimate=cost(20),
    )(d_second, residual, cot, gain, w, mixer_away, down)


def gate_gather_kernel(
    own_ref,
    x_far,
    w_far,
    all_ref,
    gate_far,
    up_far,
    hidden_far,
    x_ref,
    w_ref,
    gate_ref,
    up_ref,
    hidden_ref,
    send_sem,
    recv_sem,
    own_sem,
    x_sem,
    w_sem,
    store_sem,
):
    me, slot, step_core, first_step, second_step = places()
    first, second, mate = me + first_step, me + second_step, me + step_core
    w_load = pltpu.make_async_copy(w_far, w_ref, w_sem)
    w_load.start()
    tiles, tile_rows = x_ref.shape[:2]
    half = gate_ref.shape[2]

    def rows_of(i):
        return pl.ds(pl.multiple_of(i * tile_rows, tile_rows), tile_rows)

    def x_load(i):
        return pltpu.make_async_copy(x_far.at[rows_of(i), :], x_ref.at[i], x_sem.at[i])

    for i in range(tiles):
        x_load(i).start()
    greet((first, second, mate))
    sent = []

    def send(source, number, device):
        copy = remote(
            source, all_ref.at[AROUND[number]], send_sem.at[number], recv_sem.at[number], device
        )
        copy.start()
        sent.append(copy)

    def arrived(number):
        target = all_ref.at[AROUND[number]]
        remote(target, target, send_sem.at[number], recv_sem.at[number], me).wait_recv()
        return target

    own = pltpu.make_async_copy(own_ref, all_ref.at[0], own_sem)
    send(own_ref, 0, first)
    send(own_ref, 1, second)
    send(own_ref, 2, mate)
    own.start()

    def stores(i, spot):
        return [
            pltpu.make_async_copy(near.at[spot], far.at[rows_of(i), :], store_sem.at[spot, number])
            for number, (near, far) in enumerate(
                ((gate_ref, gate_far), (up_ref, up_far), (hidden_ref, hidden_far))
            )
        ]

    def tile(i, _):
        spot = lax.rem(i, 2)
        x_load(i).wait()

        @pl.when(i >= 2)
        def _():
            for copy in stores(i - 2, spot):
                copy.wait()

        both = dot_nn(x_ref[i], w_ref[...])
        gate = both[:, :half]
        up = both[:, half:]
        gate_ref[spot] = gate
        up_ref[spot] = up
        hidden_ref[spot] = (gate * jax.nn.sigmoid(gate) * up).astype(bf16)
        for copy in stores(i, spot):
            copy.start()
        return 0

    w_load.wait()
    lax.fori_loop(0, tiles // 2, tile, 0)
    block = arrived(0)
    send(block, 3, second)
    send(block, 4, mate)
    send(arrived(1), 5, mate)
    lax.fori_loop(tiles // 2, tiles, tile, 0)
    for i in (tiles - 2, tiles - 1):
        for copy in stores(i, i % 2):
            copy.wait()
    send(arrived(3), 6, mate)
    for number in (2, 4, 5, 6):
        arrived(number)
    for copy in sent:
        copy.wait_send()
    own.wait()


def gate_gather(own, x, w, number):
    rows, columns = own.shape
    half = w.shape[1] // 2
    tiles = x.shape[0] // rows
    wide = jax.ShapeDtypeStruct((x.shape[0], half), f32)
    return pl.pallas_call(
        gate_gather_kernel,
        out_shape=(
            jax.ShapeDtypeStruct((GROUP, rows, columns), own.dtype),
            wide,
            wide,
            jax.ShapeDtypeStruct((x.shape[0], half), bf16),
        ),
        in_specs=[ANY, ANY, ANY],
        out_specs=(ANY, ANY, ANY, ANY),
        scratch_shapes=[
            pltpu.VMEM((tiles, rows, x.shape[1]), bf16),
            pltpu.VMEM(w.shape, bf16),
            pltpu.VMEM((2, rows, half), f32),
            pltpu.VMEM((2, rows, half), f32),
            pltpu.VMEM((2, rows, half), bf16),
            pltpu.SemaphoreType.DMA((7,)),
            pltpu.SemaphoreType.DMA((7,)),
            pltpu.SemaphoreType.DMA,
            pltpu.SemaphoreType.DMA((tiles,)),
            pltpu.SemaphoreType.DMA,
            pltpu.SemaphoreType.DMA((2, 3)),
        ],
        compiler_params=pltpu.CompilerParams(
            collective_id=number, has_side_effects=True, vmem_limit_bytes=56 * 2**20
        ),
        cost_estimate=cost(45),
    )(own, x, w)


def hidden_back_kernel(cot_ref, gate_ref, up_ref, w_ref, grad_ref):
    half = gate_ref.shape[1]
    d_hidden = dot_nn(cot_ref[...], w_ref[...])
    gate = gate_ref[...]
    sigmoid = jax.nn.sigmoid(gate)
    grad_ref[:, :half] = (
        d_hidden * up_ref[...] * sigmoid * (1.0 + gate * (1.0 - sigmoid))
    ).astype(bf16)
    grad_ref[:, half:] = (d_hidden * gate * sigmoid).astype(bf16)


def hidden_back(cot, gate, up, w):
    rows, columns = cot.shape
    half = w.shape[1]
    tile_rows = 256

    def tiles(width):
        return pl.BlockSpec((tile_rows, width), lambda i: (i, 0))

    return pl.pallas_call(
        hidden_back_kernel,
        grid=(rows // tile_rows,),
        in_specs=[
            tiles(columns),
            tiles(half),
            tiles(half),
            pl.BlockSpec(w.shape, lambda i: (0, 0)),
        ],
        out_specs=tiles(2 * half),
        out_shape=jax.ShapeDtypeStruct((rows, 2 * half), bf16),
        compiler_params=pltpu.CompilerParams(vmem_limit_bytes=56 * 2**20),
        cost_estimate=cost(20),
    )(cot, gate, up, w)


def away_product_kernel(x_ref, w_ref, out_ref):
    out_ref[...] = dot_nt(x_ref[...], w_ref[...]).astype(bf16)


def away_product(x, w, tile_rows):
    rows, depth = x.shape
    tiles = rows // tile_rows // 2
    return pl.pallas_call(
        away_product_kernel,
        grid=(tiles,),
        in_specs=[
            pl.BlockSpec((tile_rows, depth), lambda i: (tiles + i, 0)),
            pl.BlockSpec(w.shape, lambda i: (0, 0)),
        ],
        out_specs=pl.BlockSpec((tile_rows, w.shape[0]), lambda i: (i, 0)),
        out_shape=jax.ShapeDtypeStruct((rows // 2, w.shape[0]), bf16),
        compiler_params=pltpu.CompilerParams(vmem_limit_bytes=56 * 2**20),
        cost_estimate=cost(6),
    )(x, w)


def keep_product_kernel(x_ref, w_ref, near_ref, out_ref):
    total = dot_nt(x_ref[...], w_ref[...]) + near_ref[0].astype(f32)
    out_ref[0] = total.astype(out_ref.dtype)


def keep_product(x, w, near, begin, number, out_type):
    _, rows, columns = near.shape
    return pl.pallas_call(
        keep_product_kernel,
        grid=(number,),
        in_specs=[
            pl.BlockSpec((rows, x.shape[1]), lambda i: (begin + i, 0)),
            pl.BlockSpec(w.shape, lambda i: (0, 0)),
            pl.BlockSpec((1, rows, columns), lambda i: (begin + i, 0, 0)),
        ],
        out_specs=pl.BlockSpec((1, rows, columns), lambda i: (i, 0, 0)),
        out_shape=jax.ShapeDtypeStruct((number, rows, columns), out_type),
        compiler_params=pltpu.CompilerParams(vmem_limit_bytes=56 * 2**20),
        cost_estimate=cost(5),
    )(x, w, near)


def rows_product_kernel(x_ref, y_ref, out_ref):
    out_ref[...] = dot_tn(x_ref[...], y_ref[...]).astype(bf16)


def rows_product(x, y, micros):
    rows, columns = x.shape
    wide = y.shape[1]
    tile_columns = 512
    return pl.pallas_call(
        rows_product_kernel,
        grid=(columns // tile_columns,),
        in_specs=[
            pl.BlockSpec((rows, tile_columns), lambda i: (0, i)),
            pl.BlockSpec((rows, wide), lambda i: (0, 0)),
        ],
        out_specs=pl.BlockSpec((tile_columns, wide), lambda i: (i, 0)),
        out_shape=jax.ShapeDtypeStruct((columns, wide), bf16),
        compiler_params=pltpu.CompilerParams(vmem_limit_bytes=56 * 2**20),
        cost_estimate=cost(micros),
    )(x, y)


def plane_permutes(device_count):
    first, second, mate = [], [], []
    for i in range(device_count):
        low_bit, high_bit = (2, 4) if i % 2 == 0 else (4, 2)
        first.append((i, i ^ low_bit))
        second.append((i, i ^ high_bit))
        mate.append((i, i ^ 1))
    return first, second, mate


def after(values, *earlier):
    return lax.optimization_barrier((values, earlier))[0]


def meet(*values):
    return lax.optimization_barrier(values)


def assemble_kernel(*refs):
    blocks, out_ref = refs[:GROUP], refs[GROUP]
    _, slot, step_core, first_step, second_step = places()
    corner_step = first_step + second_step
    here = (0, first_step, second_step, corner_step)
    there = (step_core, step_core + second_step, step_core + first_step, step_core + corner_step)
    for number, step in enumerate(here + there):
        out_ref[:, slot + step] = blocks[number][...]


def assemble(x, from_first, from_second, from_corner, mates):
    parts, rows, columns = x.shape
    return pl.pallas_call(
        assemble_kernel,
        out_shape=jax.ShapeDtypeStruct((parts, GROUP, rows, columns), x.dtype),
        in_specs=[VMEM] * GROUP,
        out_specs=VMEM,
        compiler_params=pltpu.CompilerParams(vmem_limit_bytes=32 * 2**20),
        cost_estimate=cost(8),
    )(x, from_first, from_second, from_corner, *mates)


class SlowScatter:
    def __init__(self, keep, away, device_count):
        self.keep = keep
        self.away = away
        self.first, self.second, self.mate = plane_permutes(device_count)

    def to_mate(self):
        return lax.ppermute(self.away, "fsdp", self.mate)

    def onward(self, near):
        return (self.keep(2, 2) + near[2:].astype(f32)).astype(bf16)

    def to_second(self, sums):
        return lax.ppermute(sums, "fsdp", self.second)

    def half(self, near):
        return self.keep(1, 1)[0] + near[1].astype(f32)

    def both(self, half, far):
        return (half + far[1].astype(f32)).astype(bf16)

    def to_first(self, both):
        return lax.ppermute(both, "fsdp", self.first)

    def total(self, near, far, last):
        own = self.keep(0, 1)[0] + near[0].astype(f32)
        return own + far[0].astype(f32) + last.astype(f32)


def low(values):
    return values.astype(bf16).astype(f32)


def gates(proj_ref, floor_ref, rows, head, heads):
    dim = floor_ref.shape[1] // heads
    wide = heads * dim
    lo = head * dim
    q_pre = proj_ref[rows, lo : lo + dim]
    f_pre = proj_ref[rows, wide + lo : wide + lo + dim]
    value = proj_ref[rows, 2 * wide + lo : 2 * wide + lo + dim].astype(bf16)
    floor = floor_ref[:, lo : lo + dim]
    q_sigmoid = jax.nn.sigmoid(q_pre)
    query = low(q_pre * q_sigmoid)
    f_sigmoid = jax.nn.sigmoid(f_pre)
    forget = floor + (1.0 - floor) * f_sigmoid
    key = low(1.0 - forget)
    row = lax.broadcasted_iota(jnp.int32, (CHUNK, dim), 0)
    in_half = lax.rem(row, HALF)
    product = forget
    step = 1
    while step < HALF:
        product = jnp.where(in_half >= step, product * pltpu.roll(product, step, 0), product)
        step *= 2
    middle = product[HALF - 1 : HALF, :]
    end = product[CHUNK - 1 : CHUNK, :]
    ratio = jnp.where(row < HALF, product / middle, product)
    inverse = 1.0 / ratio
    return {
        "q_pre": q_pre,
        "q_sigmoid": q_sigmoid,
        "f_sigmoid": f_sigmoid,
        "forget": forget,
        "value": value,
        "floor": floor,
        "middle": middle,
        "end": end,
        "ratio": ratio,
        "inverse": inverse,
        "row": row,
        "query_mid": query * ratio,
        "key_mid": key * inverse,
    }


def whole_fade(g, last):
    return g["middle"] * g["end"] * jnp.where(last < 0, 1.0, 0.0)


def tail_keys(g, last):
    return jnp.where(g["row"] >= last, g["key_mid"] * g["end"], 0.0).astype(bf16)


def entry_queries(g, carried):
    return jnp.where(carried, g["query_mid"] * g["middle"], 0.0).astype(bf16)


def next_state(g, last, state):
    return state * whole_fade(g, last) + dot_tn(g["value"], tail_keys(g, last))


def forward_kernel(
    heads, last_ref, proj_ref, start_ref, floor_ref, gain_ref, in_ref, mix_ref, out_ref, enter_ref, state
):
    dim = floor_ref.shape[1] // heads
    chunks = proj_ref.shape[0] // CHUNK
    tile = pl.program_id(0)

    @pl.when(tile == 0)
    def _():
        state[...] = in_ref[...]

    def step(n, _):
        base = pl.multiple_of(n * CHUNK, CHUNK)
        rows = pl.ds(base, CHUNK)
        place = (tile * chunks + n) * CHUNK
        starts = start_ref[rows, :] - place
        last = last_ref[tile * chunks + n] - place
        column = lax.broadcasted_iota(jnp.int32, (CHUNK, CHUNK), 1)
        line = lax.broadcasted_iota(jnp.int32, (CHUNK, CHUNK), 0)
        within = (column <= line) & (column >= starts)
        carried = starts < 0
        for head in range(heads):
            lo = head * dim
            g = gates(proj_ref, floor_ref, rows, head, heads)
            now = state[head]
            enter_ref[n, head] = now
            scores = dot_nt(g["query_mid"].astype(bf16), g["key_mid"].astype(bf16))
            scores = jnp.where(within, scores, 0.0).astype(bf16)
            out = dot_nn(scores, g["value"]) + dot_nt(entry_queries(g, carried), now.astype(bf16))
            state[head] = next_state(g, last, now)
            out_ref[rows, lo : lo + dim] = out
            mix_ref[rows, lo : lo + dim] = (
                out * inverse_rms(out) * gain_ref[:, lo : lo + dim]
            ).astype(bf16)
        return 0

    lax.fori_loop(0, chunks, step, 0, unroll=UNROLL)


def last_state_kernel(heads, last_ref, proj_ref, floor_ref, out_ref):
    for head in range(heads):
        state = jnp.zeros(out_ref.shape[1:], f32)
        for n in range(proj_ref.shape[0] // CHUNK):
            g = gates(proj_ref, floor_ref, pl.ds(n * CHUNK, CHUNK), head, heads)
            state = next_state(g, last_ref[n] - n * CHUNK, state)
        out_ref[head] = state


def state_grad(out_ref, dmix_ref, gain_ref, rows, lo, dim):
    out = out_ref[rows, lo : lo + dim]
    inverse = inverse_rms(out)
    scaled = out * inverse
    dmix = dmix_ref[rows, lo : lo + dim].astype(f32)
    return rms_back(dmix * gain_ref[:, lo : lo + dim], scaled, inverse)


def backward_chunk(heads, n, at, refs, outs, later, before=0):
    last_ref, proj_ref, start_ref, floor_ref, gain_ref, out_ref, dmix_ref, enter_ref = refs
    dproj_ref, dfloor_ref = outs
    dim = floor_ref.shape[1] // heads
    wide = heads * dim
    base = n * CHUNK
    rows = pl.ds(base, CHUNK)
    place = (before + n) * CHUNK
    starts = start_ref[rows, :] - place
    last = last_ref[before + n] - place
    column = lax.broadcasted_iota(jnp.int32, (CHUNK, CHUNK), 1)
    line = lax.broadcasted_iota(jnp.int32, (CHUNK, CHUNK), 0)
    within = (column <= line) & (column >= starts)
    carried = starts < 0
    for head in range(heads):
        lo = head * dim
        g = gates(proj_ref, floor_ref, rows, head, heads)
        grad = state_grad(out_ref, dmix_ref, gain_ref, rows, lo, dim)
        grad_hi = grad.astype(bf16)
        grad_lo = (grad - grad_hi.astype(f32)).astype(bf16)
        state = enter_ref[n, head]
        after = later[head]
        after_low = after.astype(bf16)
        query_mid = g["query_mid"].astype(bf16)
        key_mid = g["key_mid"].astype(bf16)
        scores = jnp.where(within, dot_nt(query_mid, key_mid), 0.0).astype(bf16)
        d_scores = dot_nt(grad_hi, g["value"]) + dot_nt(grad_lo, g["value"])
        d_scores = jnp.where(within, d_scores, 0.0).astype(bf16)
        query_in = entry_queries(g, carried)
        key_out = tail_keys(g, last)
        d_query_mid = dot_nn(d_scores, key_mid)
        d_query_in = jnp.where(carried, dot_nn(grad_hi, state.astype(bf16)), 0.0)
        d_key_mid = dot_tn(d_scores, query_mid)
        d_key_out = jnp.where(g["row"] >= last, dot_nn(g["value"], after_low), 0.0)
        d_value = dot_tn(scores, grad_hi) + dot_nt(key_out, after_low)
        d_query = (d_query_mid + d_query_in * g["middle"]) * g["ratio"]
        d_key = (d_key_mid + d_key_out * g["end"]) * g["inverse"]
        tail = d_key_out * key_out.astype(f32)
        term = (
            d_query_mid * query_mid.astype(f32)
            + d_query_in * query_in.astype(f32)
            - d_key_mid * key_mid.astype(f32)
            - tail
        )
        fade = whole_fade(g, last)
        final = jnp.sum(tail, axis=0, keepdims=True) + fade * jnp.sum(
            state * after, axis=0, keepdims=True
        )
        step_rows = 1
        while step_rows < CHUNK:
            term = jnp.where(
                g["row"] < CHUNK - step_rows,
                term + pltpu.roll(term, CHUNK - step_rows, 0),
                term,
            )
            step_rows *= 2
        d_forget = (term + final) / g["forget"] - d_key
        q_sigmoid, f_sigmoid = g["q_sigmoid"], g["f_sigmoid"]
        d_q_pre = d_query * q_sigmoid * (1.0 + g["q_pre"] * (1.0 - q_sigmoid))
        d_floor = d_forget * (1.0 - f_sigmoid)
        d_f_pre = d_floor * (1.0 - g["floor"]) * f_sigmoid
        dproj_ref[at, lo : lo + dim] = d_q_pre.astype(bf16)
        dproj_ref[at, wide + lo : wide + lo + dim] = d_f_pre.astype(bf16)
        dproj_ref[at, 2 * wide + lo : 2 * wide + lo + dim] = d_value.astype(bf16)
        dfloor_ref[:, lo : lo + dim] += jnp.sum(d_floor, axis=0, keepdims=True)
        later[head] = after * fade + dot_tn(grad_hi, query_in)


def backward_rest(heads, n, refs, later, before=0):
    last_ref, proj_ref, start_ref, floor_ref, gain_ref, out_ref, dmix_ref = refs
    dim = floor_ref.shape[1] // heads
    rows = pl.ds(n * CHUNK, CHUNK)
    for head in range(heads):
        g = gates(proj_ref, floor_ref, rows, head, heads)
        grad = state_grad(out_ref, dmix_ref, gain_ref, rows, head * dim, dim)
        place = (before + n) * CHUNK
        queries = entry_queries(g, start_ref[rows, :] < place)
        fade = whole_fade(g, last_ref[before + n] - place)
        later[head] = later[head] * fade + dot_tn(grad.astype(bf16), queries)


def backward_kernel(heads, *refs):
    ins, outs, later = refs[:8], refs[8:10], refs[10]
    chunks = ins[1].shape[0] // CHUNK
    edge = MAXLEN // CHUNK
    tile = pl.num_programs(0) - 1 - pl.program_id(0)
    before = tile * chunks

    def step(i, first):
        n = first - i
        at = pl.ds(pl.multiple_of(n * CHUNK, CHUNK), CHUNK)
        backward_chunk(heads, n, at, ins, outs, later, before)
        return first

    @pl.when(pl.program_id(0) == 0)
    def _():
        later[...] = jnp.zeros_like(later)
        outs[1][...] = jnp.zeros_like(outs[1])
        for n in range(chunks - 1, chunks - 1 - edge, -1):
            backward_rest(heads, n, ins[:7], later, before)
        lax.fori_loop(0, chunks - edge, step, chunks - 1 - edge, unroll=UNROLL)

    @pl.when(pl.program_id(0) != 0)
    def _():
        lax.fori_loop(0, chunks, step, chunks - 1, unroll=2 * UNROLL)


def backward_edge_kernel(heads, *refs):
    ins, in_ref, _, outs, later = refs[:8], refs[8], refs[9], refs[10:12], refs[12]
    later[...] = in_ref[...]
    outs[1][...] = jnp.zeros_like(outs[1])
    edge = MAXLEN // CHUNK
    before = ins[0].shape[0] - edge
    for n in range(edge - 1, -1, -1):
        backward_chunk(heads, n, pl.ds(n * CHUNK, CHUNK), ins, outs, later, before)


def first_grad_kernel(heads, *refs):
    ins, grad_ref = refs[:7], refs[7]
    grad_ref[...] = jnp.zeros_like(grad_ref)
    for n in range(ins[1].shape[0] // CHUNK - 1, -1, -1):
        backward_rest(heads, n, ins, grad_ref)


def local_call(kernel, heads, micros, out_shape, scratch, *operands):
    return pl.pallas_call(
        functools.partial(kernel, heads),
        out_shape=out_shape,
        in_specs=[SMEM] + [VMEM] * (len(operands) - 1),
        out_specs=jax.tree.map(lambda _: VMEM, out_shape),
        scratch_shapes=scratch,
        compiler_params=pltpu.CompilerParams(vmem_limit_bytes=56 * 2**20),
        cost_estimate=cost(micros),
    )(*operands)


def body(
    tokens,
    cotangent,
    dealt_lengths,
    deal,
    norm_gain,
    mixer_in,
    forget_floor,
    group_gain,
    out_proj,
    ffn_gain,
    gate_up,
    down_proj,
):
    row_count, width = tokens.shape
    weight_rows = mixer_in.shape[0]
    device_count = lax.axis_size("fsdp")
    groups = device_count // GROUP
    own_index = lax.axis_index("fsdp")
    slot = lax.rem(own_index, GROUP)
    group = own_index // GROUP
    group_rows = GROUP * row_count
    heads = HEADS // GROUP
    own_width = width // GROUP
    dim = width // HEADS
    ffn_width = down_proj.shape[1]
    own_ffn = ffn_width // GROUP
    planes = [[g * GROUP + s for s in range(GROUP)] for g in range(groups)]
    lines = [[g * GROUP + s for g in range(groups)] for s in range(GROUP)]

    def line_gather(x):
        return lax.all_gather(x, "fsdp", axis=0, axis_index_groups=lines, tiled=True)

    def line_scatter(x):
        return lax.psum_scatter(
            x, "fsdp", scatter_dimension=0, axis_index_groups=lines, tiled=True
        )

    def whole_rows(x):
        return line_gather(x.reshape(GROUP * weight_rows, -1))

    low_step = 2 - 4 * (slot // 2 % 2)
    high_step = 4 - 8 * (slot // 4)
    odd = slot % 2
    moves = (
        slot,
        1 - 2 * odd,
        jnp.where(odd == 0, low_step, high_step),
        jnp.where(odd == 0, high_step, low_step),
    )

    seq_count = deal.shape[0]
    seq_ids = jnp.arange(seq_count, dtype=jnp.int32)
    matches = deal[:, None] == seq_ids[None, :]
    lengths = jnp.sum(jnp.where(matches, dealt_lengths[:, None], 0), axis=0)
    seq_starts = jnp.sum(
        jnp.where(seq_ids[:, None] < seq_ids[None, :], lengths[:, None], 0), axis=0
    )
    group_start = group * group_rows
    rows_here = group_start + jnp.arange(group_rows, dtype=jnp.int32)
    starts = (
        jnp.max(jnp.where(seq_starts[None, :] <= rows_here[:, None], seq_starts[None, :], 0), axis=1)
        - group_start
    )
    start_column = starts[:, None]
    last_starts = starts[CHUNK - 1 :: CHUNK]

    out_lines = lax.all_gather(out_proj, "fsdp", axis=0, axis_index_groups=lines)
    gain_block = jnp.zeros((16, 128), bf16)
    for number, gain in enumerate((norm_gain, forget_floor, group_gain, ffn_gain)):
        gain_block = gain_block.at[number, :weight_rows].set(gain)
    gain_blocks, mixer_swapped = exchange(
        0, 15, ("all", gain_block), ("swap", by_owner(mixer_in, 3))
    )
    mixer_weight = whole_rows(mixer_swapped)
    gains = (
        gain_blocks[:, :, :4, :weight_rows].transpose(2, 0, 1, 3).reshape(4, width).astype(f32)
    )
    first_gain = gains[0:1]
    second_gain = gains[3:4]
    own_gains = lax.dynamic_slice_in_dim(gains, slot * own_width, own_width, 1)
    own_floor = own_gains[1:2]
    own_group_gain = own_gains[2:3]

    inputs = tokens.astype(f32)
    first_inverse = inverse_rms(inputs)
    first_scaled = inputs * first_inverse
    first_normed = (first_scaled * first_gain).astype(bf16)
    late_gate_up, late_down = after((gate_up, down_proj), mixer_swapped)
    first_all, ffn_swapped, down_swapped = exchange(
        1,
        58,
        ("gather", first_normed[None]),
        ("swap", by_owner(late_gate_up, 2)),
        ("swap", by_owner(late_down, 1)),
    )
    first_all = first_all.reshape(group_rows, width)
    ffn_weight = whole_rows(ffn_swapped)
    first, second, mate = plane_permutes(device_count)
    out_own = after(out_lines, first_all)
    from_first = lax.ppermute(out_own, "fsdp", first)
    from_second = lax.ppermute(out_own, "fsdp", second)
    tail_projected = dot_nn(first_all[group_rows - MAXLEN :], mixer_weight)
    edge = MAXLEN // CHUNK
    state_type = jax.ShapeDtypeStruct((heads, dim, dim), f32)
    last_state = local_call(
        last_state_kernel,
        heads,
        3,
        state_type,
        [],
        last_starts[-edge:] - (group_rows - MAXLEN),
        tail_projected,
        own_floor,
    )
    up_line = [(i, i + GROUP) for i in range(device_count - GROUP)]
    down_line = [(i + GROUP, i) for i in range(device_count - GROUP)]
    entering_state = lax.ppermute(last_state, "fsdp", up_line)
    projected = dot_nn(after(first_all, last_state), mixer_weight)
    projected, entering_state, from_first, from_second = meet(
        projected, entering_state, from_first, from_second
    )
    from_corner = lax.ppermute(from_first, "fsdp", second)
    mates = [lax.ppermute(block, "fsdp", mate) for block in (out_own, from_first, from_second)]
    chunks = group_rows // CHUNK
    tile_count = group_rows // TILE_ROWS

    def row_tiles(columns, turned=False):
        return pl.BlockSpec(
            (TILE_ROWS, columns), lambda i: (tile_count - 1 - i if turned else i, 0)
        )

    def state_tiles(turned=False):
        return pl.BlockSpec(
            (TILE_ROWS // CHUNK, heads, dim, dim),
            lambda i: (tile_count - 1 - i if turned else i, 0, 0, 0),
        )

    state_scratch = pltpu.VMEM((heads, dim, dim), f32)
    mixed_heads, state_out, entering = pl.pallas_call(
        functools.partial(forward_kernel, heads),
        grid=(tile_count,),
        out_shape=(
            jax.ShapeDtypeStruct((group_rows, own_width), bf16),
            jax.ShapeDtypeStruct((group_rows, own_width), f32),
            jax.ShapeDtypeStruct((chunks, heads, dim, dim), f32),
        ),
        in_specs=[SMEM, row_tiles(3 * own_width), row_tiles(1), VMEM, VMEM, VMEM],
        out_specs=(row_tiles(own_width), row_tiles(own_width), state_tiles()),
        scratch_shapes=[state_scratch],
        compiler_params=pltpu.CompilerParams(vmem_limit_bytes=56 * 2**20),
        cost_estimate=cost(18),
    )(last_starts, projected, start_column, own_floor, own_group_gain, entering_state)
    mixed_heads, from_corner = meet(mixed_heads, from_corner)
    mates = mates + [lax.ppermute(from_corner, "fsdp", mate)]
    [mixer_input] = exchange(
        3, 15, ("widen", mixed_heads.reshape(GROUP, row_count, own_width))
    )
    mixer_input, mates = meet(mixer_input, mates)
    _, step_core, first_step, second_step = moves
    steps = (0, first_step, second_step, first_step + second_step)
    mate_steps = [step_core + steps[kind] for kind in (0, 2, 1, 3)]
    mixer_blocks = dealt_columns(mixer_input, weight_rows)
    mixer_around = [
        lax.dynamic_index_in_dim(mixer_blocks, slot + step, 0) for step in (*steps, *mate_steps)
    ]
    mixer_keep = jnp.concatenate(mixer_around[:4])
    mixer_away = jnp.concatenate(mixer_around[4:])
    out_weight = assemble(out_own, from_first, from_second, from_corner, mates).reshape(width, width)
    down_weight = whole_rows(after(down_swapped, mixed_heads))
    residual = inputs + dot_nn(mixer_input, out_weight)
    second_inverse = inverse_rms(residual)
    second_scaled = residual * second_inverse
    second_normed = (second_scaled * second_gain).astype(bf16)
    second_normed, mixer_keep, mixer_away = meet(second_normed, mixer_keep, mixer_away)
    [second_all] = exchange(2, 43, ("around", second_normed[None]))
    second_all = second_all.reshape(group_rows, width)
    cot_blocks, gate_part, up_part, hidden_act = gate_gather(
        cotangent, second_all, ffn_weight, 6
    )
    cot_all = cot_blocks.reshape(group_rows, width)
    down_grad = rows_product(cot_all, hidden_act, 11)
    down_summed = line_scatter(down_grad)
    hidden_act = after(hidden_act, down_grad)

    ffn_away = away_product(hidden_act, down_weight, row_count).reshape(4, row_count, width)
    ffn_near = lax.ppermute(ffn_away, "fsdp", mate)
    d_gate_pre = hidden_back(after(cot_all, ffn_away), gate_part, up_part, down_weight)
    d_gate_pre, ffn_near = meet(d_gate_pre, ffn_near)
    ffn_sums = keep_product(hidden_act, down_weight, ffn_near, 2, 2, bf16)
    ffn_grad = rows_product(after(second_all, ffn_sums), d_gate_pre, 18)
    ffn_rest = keep_product(hidden_act, down_weight, after(ffn_near, ffn_grad), 0, 2, f32)
    ffn_grad, ffn_rest, ffn_far = meet(ffn_grad, ffn_rest, lax.ppermute(ffn_sums, "fsdp", second))
    ffn_both = (ffn_rest[1] + ffn_far[1].astype(f32)).astype(bf16)
    ffn_summed = line_scatter(ffn_grad)
    [d_second] = product_scatter(
        d_gate_pre.reshape(GROUP, row_count, -1), after(ffn_weight, ffn_grad, ffn_both), 4, True
    )
    d_second, ffn_last, down_summed = meet(
        d_second, lax.ppermute(ffn_both, "fsdp", first), down_summed
    )

    d_residual, d_mix_out, d_mixed_heads, out_near, down_swapped = residual_back(
        d_second,
        residual,
        cotangent,
        second_gain,
        out_weight,
        mixer_away,
        down_summed.reshape(GROUP, weight_rows, -1),
        5,
    )
    d_mixed_heads = d_mixed_heads.reshape(group_rows, own_width)

    def out_blocks(blocks):
        return lax.dot_general(
            blocks, d_mix_out, (((1,), (0,)), ((), ())), preferred_element_type=f32
        )

    out_sum = SlowScatter(
        lambda begin, number: out_blocks(mixer_keep[begin : begin + number]), None, device_count
    )
    out_sums = out_sum.onward(out_near)
    d_mixed_heads = after(d_mixed_heads, out_sums)
    out_far = out_sum.to_second(out_sums)
    operands = (projected, start_column, own_floor, own_group_gain, state_out, d_mixed_heads)

    def edge_specs(place):
        def rows(columns):
            return pl.BlockSpec((MAXLEN, columns), lambda i: (place, 0))

        return [rows(3 * own_width), rows(1), VMEM, VMEM, rows(own_width), rows(own_width)]

    first_grad = pl.pallas_call(
        functools.partial(first_grad_kernel, heads),
        grid=(1,),
        out_shape=state_type,
        in_specs=[SMEM] + edge_specs(0),
        out_specs=VMEM,
        compiler_params=pltpu.CompilerParams(vmem_limit_bytes=56 * 2**20),
        cost_estimate=cost(3),
    )(last_starts, *operands)
    entering_grad = lax.ppermute(first_grad, "fsdp", down_line)
    dproj_type = jax.ShapeDtypeStruct((group_rows, 3 * own_width), bf16)
    dfloor_type = jax.ShapeDtypeStruct((1, own_width), f32)
    d_projected, floor_most = pl.pallas_call(
        functools.partial(backward_kernel, heads),
        grid=(tile_count,),
        out_shape=(dproj_type, dfloor_type),
        in_specs=[
            SMEM,
            row_tiles(3 * own_width, True),
            row_tiles(1, True),
            VMEM,
            VMEM,
            row_tiles(own_width, True),
            row_tiles(own_width, True),
            state_tiles(True),
        ],
        out_specs=(row_tiles(3 * own_width, True), VMEM),
        scratch_shapes=[state_scratch],
        compiler_params=pltpu.CompilerParams(vmem_limit_bytes=56 * 2**20),
        cost_estimate=cost(30),
    )(last_starts, *operands, entering)
    d_projected, entering_grad = meet(d_projected, entering_grad)
    last_tile = group_rows // MAXLEN - 1
    d_projected, floor_rest = pl.pallas_call(
        functools.partial(backward_edge_kernel, heads),
        grid=(1,),
        out_shape=(dproj_type, dfloor_type),
        in_specs=[SMEM]
        + edge_specs(last_tile)
        + [pl.BlockSpec((edge, heads, dim, dim), lambda i: (last_tile, 0, 0, 0)), VMEM, ANY],
        out_specs=(
            pl.BlockSpec((MAXLEN, 3 * own_width), lambda i: (last_tile, 0)),
            VMEM,
        ),
        scratch_shapes=[state_scratch],
        input_output_aliases={9: 0},
        compiler_params=pltpu.CompilerParams(vmem_limit_bytes=56 * 2**20),
        cost_estimate=cost(4),
    )(last_starts, *operands, entering, entering_grad, d_projected)
    d_projected, out_far = meet(d_projected, out_far)
    out_both = out_sum.both(out_sum.half(out_near), out_far)
    d_projected = after(d_projected, out_both)
    floor_grad = floor_most + floor_rest
    by_sender = (GROUP, weight_rows, -1)
    floor_parts = lax.dynamic_update_slice_in_dim(
        jnp.zeros((width,), f32), floor_grad[0], slot * own_width, 0
    ).reshape(device_count, weight_rows)
    floor_parts = lax.all_to_all(floor_parts, "fsdp", 0, 0, tiled=True)
    mixer_grad = rows_product(first_all, d_projected, 11)
    mixer_grad, out_last = meet(mixer_grad, out_sum.to_first(out_both))
    mixer_summed = line_scatter(mixer_grad)
    out_total = out_sum.total(after(out_near, mixer_grad), out_far, out_last).astype(bf16)
    out_summed = line_scatter(out_total.reshape(groups * weight_rows, width))
    d_first, ffn_swapped = product_scatter(
        d_projected.reshape(GROUP, row_count, -1),
        after(mixer_weight, out_total),
        8,
        False,
        ffn_summed.reshape(by_sender),
    )
    d_first, mixer_summed, floor_parts = meet(d_first, mixer_summed, floor_parts)
    d_forget_floor = jnp.sum(floor_parts, axis=0)

    def swap(x):
        x = x.reshape(by_sender)
        return lax.all_to_all(x, "fsdp", 0, 0, axis_index_groups=planes, tiled=True)

    mixer_swapped = swap(mixer_summed)
    ffn_last = after(ffn_last, d_first)
    layer_out = residual + (ffn_rest[0] + ffn_far[0].astype(f32) + ffn_last.astype(f32))
    d_gate_up, ffn_gain_sum = home(ffn_swapped, gate_up, 2)
    d_mixer_in, norm_gain_sum = home(mixer_swapped, mixer_in, 3)
    d_down_proj, _ = home(down_swapped, down_proj, 1)
    d_dealt = d_residual + rms_back(d_first * first_gain, first_scaled, first_inverse)

    d_out_proj = after(out_summed, d_dealt, mixer_swapped).astype(f32)

    group_gain_sum = jnp.sum(out_proj.astype(f32) * d_out_proj, axis=1)
    return (
        layer_out,
        d_dealt,
        norm_gain_sum[:, 0] / norm_gain.astype(f32),
        d_mixer_in,
        d_forget_floor,
        group_gain_sum / group_gain.astype(f32),
        d_out_proj,
        ffn_gain_sum[:, 0] / ffn_gain.astype(f32),
        d_gate_up,
        d_down_proj,
    )


def solution(mesh):
    by_rows = P("fsdp", None)
    by_one = P("fsdp")
    return jax.shard_map(
        body,
        mesh=mesh,
        in_specs=(
            by_rows,
            by_rows,
            P(),
            P(),
            by_one,
            by_rows,
            by_one,
            by_one,
            by_rows,
            by_one,
            by_rows,
            by_rows,
        ),
        out_specs=(
            by_rows,
            by_rows,
            by_one,
            by_rows,
            by_one,
            by_one,
            by_rows,
            by_one,
            by_rows,
            by_rows,
        ),
        check_vma=False,
    )
```

```python
import functools

import jax
import jax.numpy as jnp
from jax import lax
from jax.experimental import pallas as pl
from jax.experimental.pallas import tpu as pltpu
from jax.sharding import PartitionSpec as P

HEADS = 16
CHUNK = 64
HALF = 32
TILE_ROWS = 512
UNROLL = 2
MAXLEN = 128
GROUP = 8
MESH_ID = pl.DeviceIdType.MESH
VMEM = pl.BlockSpec(memory_space=pltpu.VMEM)
SMEM = pl.BlockSpec(memory_space=pltpu.SMEM)
ANY = pl.BlockSpec(memory_space=pl.ANY)

norm_eps = 1e-05
f32 = jnp.float32
bf16 = jnp.bfloat16


def inverse_rms(values):
    return lax.rsqrt(jnp.mean(values * values, axis=-1, keepdims=True) + norm_eps)


def rms_back(grad_scaled, scaled, inverse):
    return inverse * (grad_scaled - scaled * jnp.mean(grad_scaled * scaled, axis=-1, keepdims=True))


def dot_nt(left, right):
    return lax.dot_general(left, right, (((1,), (1,)), ((), ())), preferred_element_type=f32)


def dot_nn(left, right):
    return lax.dot_general(left, right, (((1,), (0,)), ((), ())), preferred_element_type=f32)


def dot_tn(left, right):
    return lax.dot_general(left, right, (((0,), (0,)), ((), ())), preferred_element_type=f32)


def cost(micros):
    return pl.CostEstimate(flops=0, transcendentals=0, bytes_accessed=int(micros * 36_900))


def places():
    me = lax.axis_index("fsdp")
    slot = lax.rem(me, GROUP)
    core = lax.rem(slot, 2)
    step_low = 2 - 4 * lax.rem(slot // 2, 2)
    step_high = 4 - 8 * (slot // 4)
    step_core = 1 - 2 * core
    first_step = (1 - core) * step_low + core * step_high
    second_step = core * step_low + (1 - core) * step_high
    return me, slot, step_core, first_step, second_step


def greet(others):
    barrier = pltpu.get_barrier_semaphore()
    for other in others:
        pl.semaphore_signal(barrier, inc=1, device_id=(other,), device_id_type=MESH_ID)
    pl.semaphore_wait(barrier, len(others))


def remote(source, target, send_sem, recv_sem, device):
    return pltpu.make_async_remote_copy(
        src_ref=source,
        dst_ref=target,
        send_sem=send_sem,
        recv_sem=recv_sem,
        device_id=(device,),
        device_id_type=MESH_ID,
    )


def plane_steps(step_core, step_low, step_high):
    return [
        (number, (number & 1) * step_core + ((number >> 1) & 1) * step_low + (number >> 2) * step_high)
        for number in range(1, GROUP)
    ]


AROUND = (1, 2, 4, 3, 5, 6, 7)


def exchange_kernel(plan, *refs):
    count = len(plan)
    ins, outs = refs[:count], refs[count : 2 * count]
    send_sem, recv_sem, own_sem = refs[2 * count :]
    me, slot, step_core, first_step, second_step = places()
    core = lax.rem(slot, 2)
    step_low = (1 - core) * first_step + core * second_step
    step_high = core * first_step + (1 - core) * second_step
    others = plane_steps(step_core, step_low, step_high)
    group = me // GROUP
    groups = lax.axis_size("fsdp") // GROUP
    greeted = [me + first_step, me + second_step, me + step_core]
    if not set(plan) <= {"gather", "around"}:
        greeted = [me + step for _, step in others]
    line = []
    if "all" in plan:
        line = [
            (
                number,
                lax.rem(group + number, groups) * GROUP + slot,
                lax.rem(group + groups - number, groups),
            )
            for number in range(1, groups)
        ]
        greeted = greeted + [target for _, target, _ in line]
    greet(greeted)
    sent = []

    def copy_of(item, source, target, number, device):
        return remote(source, target, send_sem.at[item, number], recv_sem.at[item, number], device)

    def send(item, source, target, number, device):
        copy = copy_of(item, source, target, number, device)
        copy.start()
        sent.append(copy)

    def arrived(item, target, number):
        copy_of(item, target, target, number, me).wait_recv()

    def keep(item, source, target):
        copy = pltpu.make_async_copy(source, target, own_sem.at[item])
        copy.start()
        return copy

    def block(item, place):
        kind, out = plan[item], outs[item]
        if kind == "widen":
            columns = out.shape[1] // GROUP
            return out.at[:, pl.ds(pl.multiple_of(place * columns, columns), columns)]
        if kind in ("gather", "around"):
            return out.at[:, place]
        return out.at[place]

    def landing(item, place, number):
        return block(item, AROUND[number] if plan[item] == "around" else place)

    def piece(item, place):
        if plan[item] == "narrow":
            columns = ins[item].shape[1] // GROUP
            return ins[item].at[:, pl.ds(pl.multiple_of(place * columns, columns), columns)]
        return ins[item].at[place]

    own = []
    for item, kind in enumerate(plan):
        if kind == "all":
            keep(item, ins[item], outs[item].at[group, slot]).wait()
            for number, target, _ in line:
                send(item, ins[item], outs[item].at[group, slot], GROUP - 1 + number, target)
        elif kind in ("gather", "around"):
            for number, step in enumerate((first_step, second_step, step_core)):
                send(item, ins[item], landing(item, slot, number), number, me + step)
            own.append(keep(item, ins[item], block(item, 0 if kind == "around" else slot)))
    for item, kind in enumerate(plan):
        if kind in ("swap", "widen", "narrow"):
            for number, step in others:
                send(item, piece(item, slot + step), block(item, slot), number - 1, me + step)
            own.append(keep(item, piece(item, slot), block(item, slot)))
    for item, kind in enumerate(plan):
        if kind == "all":
            for number, _, sender in line:
                arrived(item, outs[item].at[sender, slot], GROUP - 1 + number)
            for number, step in others:
                send(item, outs[item].at[:, slot], outs[item].at[:, slot], number - 1, me + step)
    corner_step = first_step + second_step
    for item, kind in enumerate(plan):
        if kind in ("gather", "around"):
            for place, number, onward in (
                (slot + first_step, 0, ((3, second_step), (4, step_core))),
                (slot + second_step, 1, ((5, step_core),)),
                (slot + corner_step, 3, ((6, step_core),)),
            ):
                here = landing(item, place, number)
                arrived(item, here, number)
                for then, step in onward:
                    send(item, here, landing(item, place, then), then, me + step)
    for item, kind in enumerate(plan):
        if kind in ("gather", "around"):
            for step, number in ((0, 2), (second_step, 4), (first_step, 5), (corner_step, 6)):
                arrived(item, landing(item, slot + step_core + step, number), number)
        elif kind == "all":
            for number, step in others:
                arrived(item, outs[item].at[:, slot + step], number - 1)
        else:
            for number, step in others:
                arrived(item, block(item, slot + step), number - 1)
    for copy in sent:
        copy.wait_send()
    for copy in own:
        copy.wait()


def exchange(number, micros, *items):
    groups = lax.axis_size("fsdp") // GROUP
    kinds = [kind for kind, _ in items]
    arrays = [array for _, array in items]
    shapes = []
    for kind, array in items:
        if kind in ("gather", "around"):
            shape = (array.shape[0], GROUP) + array.shape[1:]
        elif kind == "swap":
            shape = array.shape
        elif kind == "widen":
            shape = (array.shape[1], GROUP * array.shape[2])
        elif kind == "narrow":
            shape = (GROUP, array.shape[0], array.shape[1] // GROUP)
        else:
            shape = (groups, GROUP) + array.shape
        shapes.append(jax.ShapeDtypeStruct(shape, array.dtype))
    numbers = GROUP - 1 + (groups if "all" in kinds else 0)
    return pl.pallas_call(
        functools.partial(exchange_kernel, kinds),
        out_shape=tuple(shapes),
        in_specs=[ANY] * len(items),
        out_specs=tuple([ANY] * len(items)),
        scratch_shapes=[
            pltpu.SemaphoreType.DMA((len(items), numbers)),
            pltpu.SemaphoreType.DMA((len(items), numbers)),
            pltpu.SemaphoreType.DMA((len(items),)),
        ],
        compiler_params=pltpu.CompilerParams(collective_id=number, has_side_effects=True),
        cost_estimate=cost(micros),
    )(*arrays)


def owners_kernel(pieces, in_ref, out_ref):
    columns = out_ref.shape[2] // pieces
    for piece in range(pieces):
        for owner in range(GROUP):
            lo = (piece * GROUP + owner) * columns
            out_ref[owner, :, piece * columns : (piece + 1) * columns] = in_ref[:, lo : lo + columns]


def by_owner(weight, pieces):
    rows, columns = weight.shape
    return pl.pallas_call(
        functools.partial(owners_kernel, pieces),
        out_shape=jax.ShapeDtypeStruct((GROUP, rows, columns // GROUP), weight.dtype),
        in_specs=[VMEM],
        out_specs=VMEM,
        compiler_params=pltpu.CompilerParams(vmem_limit_bytes=32 * 2**20),
        cost_estimate=cost(3),
    )(weight)


def dealt_columns_kernel(piece, in_ref, out_ref):
    for owner in range(GROUP):
        for part in range(out_ref.shape[2] // piece):
            lo = (part * GROUP + owner) * piece
            out_ref[owner, :, part * piece : (part + 1) * piece] = in_ref[:, lo : lo + piece]


def dealt_columns(x, piece):
    rows, columns = x.shape
    return pl.pallas_call(
        functools.partial(dealt_columns_kernel, piece),
        out_shape=jax.ShapeDtypeStruct((GROUP, rows, columns // GROUP), x.dtype),
        in_specs=[VMEM],
        out_specs=VMEM,
        compiler_params=pltpu.CompilerParams(vmem_limit_bytes=32 * 2**20),
        cost_estimate=cost(2),
    )(x)


def home_kernel(pieces, got_ref, weight_ref, out_ref, gain_ref):
    columns = got_ref.shape[2] // pieces
    for sender in range(GROUP):
        for piece in range(pieces):
            lo = (piece * GROUP + sender) * columns
            out_ref[:, lo : lo + columns] = got_ref[
                sender, :, piece * columns : (piece + 1) * columns
            ].astype(f32)
    gain_ref[...] = jnp.sum(out_ref[...] * weight_ref[...].astype(f32), axis=1, keepdims=True)


def home(got, weight, pieces):
    rows, columns = weight.shape
    return pl.pallas_call(
        functools.partial(home_kernel, pieces),
        out_shape=(
            jax.ShapeDtypeStruct((rows, columns), f32),
            jax.ShapeDtypeStruct((rows, 1), f32),
        ),
        in_specs=[VMEM, VMEM],
        out_specs=(VMEM, VMEM),
        compiler_params=pltpu.CompilerParams(vmem_limit_bytes=32 * 2**20),
        cost_estimate=cost(5),
    )(got, weight)


TILE = 1024


def product_scatter_kernel(swaps, around, a_far, w_far, *refs):
    swap_refs, out_ref, swapped_refs = refs[:swaps], refs[swaps], refs[swaps + 1 : 2 * swaps + 1]
    near, far, away, going, send_sem, recv_sem, a_ref, w_ref, a_sem, w_sem = refs[
        2 * swaps + 1 : 2 * swaps + 11
    ]
    me, slot, step_core, first_step, second_step = places()
    first, second, mate = me + first_step, me + second_step, me + step_core
    core = lax.rem(slot, 2)
    others = plane_steps(
        step_core,
        (1 - core) * first_step + core * second_step,
        core * first_step + (1 - core) * second_step,
    )
    corner_step = first_step + second_step
    if around:
        own_places, mate_places = (3, 1, 2, 0), (7, 5, 6, 4)
    else:
        own_places = (slot + corner_step, slot + first_step, slot + second_step, slot)
        mate_slot = slot + step_core
        mate_places = (
            mate_slot + corner_step,
            mate_slot + second_step,
            mate_slot + first_step,
            mate_slot,
        )

    def a_load(place):
        return pltpu.make_async_copy(a_far.at[place], a_ref.at[place], a_sem.at[place])

    def w_load(i):
        at = pl.ds(i * TILE, TILE)
        return pltpu.make_async_copy(w_far.at[at, :], w_ref.at[at, :], w_sem.at[i])

    a_load(mate_places[0]).start()
    for i in range(out_ref.shape[1] // TILE):
        w_load(i).start()
    for place in (
        mate_places[2],
        own_places[0],
        own_places[2],
        mate_places[1],
        mate_places[3],
        own_places[3],
        own_places[1],
    ):
        a_load(place).start()
    greet([me + step for _, step in others] if swaps else (first, second, mate))
    sent = []

    def send(source, target, number, device):
        copy = remote(source, target, send_sem.at[number], recv_sem.at[number], device)
        copy.start()
        sent.append(copy)

    def arrived(ref, number, source):
        remote(ref, ref, send_sem.at[number], recv_sem.at[number], source).wait_recv()

    def product(place, extra, target):
        a_load(place).wait()

        def tile(i, _):
            at = pl.ds(pl.multiple_of(i * TILE, TILE), TILE)
            total = dot_nt(a_ref[place], w_ref[at, :])
            for ref in extra:
                total = total + ref[:, at].astype(f32)
            target[:, at] = total.astype(target.dtype)
            return 0

        lax.fori_loop(0, out_ref.shape[1] // TILE, tile, 0)

    def to_mate(kind):
        product(mate_places[kind], (), away.at[kind])
        send(away.at[kind], near.at[kind], kind, mate)

    def add(ref):
        def tile(i, _):
            at = pl.ds(pl.multiple_of(i * TILE, TILE), TILE)
            out_ref[:, at] = out_ref[:, at] + ref[:, at].astype(f32)
            return 0

        lax.fori_loop(0, out_ref.shape[1] // TILE, tile, 0)

    swapping, kept = [], []
    if swaps:
        swap_send, swap_recv, swap_own = refs[2 * swaps + 11 :]

    def start_swaps():
        for item in range(swaps):
            for number, step in others:
                copy = remote(
                    swap_refs[item].at[slot + step],
                    swapped_refs[item].at[slot],
                    swap_send.at[item, number - 1],
                    swap_recv.at[item, number - 1],
                    me + step,
                )
                copy.start()
                swapping.append(copy)
            copy = pltpu.make_async_copy(
                swap_refs[item].at[slot], swapped_refs[item].at[slot], swap_own.at[item]
            )
            copy.start()
            kept.append(copy)

    start_swaps()
    for i in range(out_ref.shape[1] // TILE):
        w_load(i).wait()
    to_mate(0)
    to_mate(2)
    arrived(near.at[0], 0, mate)
    product(own_places[0], (near.at[0],), going.at[0])
    send(going.at[0], far.at[0], 4, second)
    arrived(near.at[2], 2, mate)
    product(own_places[2], (near.at[2],), going.at[2])
    send(going.at[2], far.at[2], 5, second)
    to_mate(1)
    to_mate(3)
    arrived(near.at[3], 3, mate)
    product(own_places[3], (near.at[3],), out_ref)
    arrived(near.at[1], 1, mate)
    arrived(far.at[0], 4, second)
    product(own_places[1], (near.at[1], far.at[0]), going.at[1])
    send(going.at[1], far.at[1], 6, first)
    arrived(far.at[2], 5, second)
    add(far.at[2])
    arrived(far.at[1], 6, first)
    add(far.at[1])
    for item in range(swaps):
        for number, step in others:
            target = swapped_refs[item].at[slot + step]
            remote(
                target,
                target,
                swap_send.at[item, number - 1],
                swap_recv.at[item, number - 1],
                me + step,
            ).wait_recv()
    for copy in sent + swapping:
        copy.wait_send()
    for copy in kept:
        copy.wait()


def product_scatter(a, w, number, around, *swaps):
    _, rows, depth = a.shape
    columns = w.shape[0]
    count = len(swaps)
    swap_sems = [
        pltpu.SemaphoreType.DMA((count, GROUP - 1)),
        pltpu.SemaphoreType.DMA((count, GROUP - 1)),
        pltpu.SemaphoreType.DMA((count,)),
    ]
    return pl.pallas_call(
        functools.partial(product_scatter_kernel, count, around),
        out_shape=(jax.ShapeDtypeStruct((rows, columns), f32),)
        + tuple(jax.ShapeDtypeStruct(x.shape, x.dtype) for x in swaps),
        in_specs=[ANY, ANY] + [ANY] * count,
        out_specs=(VMEM,) + (ANY,) * count,
        scratch_shapes=[
            pltpu.VMEM((4, rows, columns), bf16),
            pltpu.VMEM((3, rows, columns), bf16),
            pltpu.VMEM((4, rows, columns), bf16),
            pltpu.VMEM((3, rows, columns), bf16),
            pltpu.SemaphoreType.DMA((7,)),
            pltpu.SemaphoreType.DMA((7,)),
            pltpu.VMEM(a.shape, bf16),
            pltpu.VMEM(w.shape, bf16),
            pltpu.SemaphoreType.DMA((GROUP,)),
            pltpu.SemaphoreType.DMA((columns // TILE,)),
        ]
        + (swap_sems if swaps else []),
        compiler_params=pltpu.CompilerParams(
            collective_id=number, has_side_effects=True, vmem_limit_bytes=56 * 2**20
        ),
        cost_estimate=cost(50),
    )(a, w, *swaps)


def residual_back_kernel(
    d_second_ref,
    residual_ref,
    cot_ref,
    gain_ref,
    w_far,
    mixer_ref,
    d_residual_ref,
    d_mix_ref,
    heads_ref,
    near_ref,
    w_ref,
    parts_ref,
    away_ref,
    send_sem,
    recv_sem,
    own_sem,
    w_sem,
):
    me, slot, step_core, first_step, second_step = places()
    core = lax.rem(slot, 2)
    others = plane_steps(
        step_core,
        (1 - core) * first_step + core * second_step,
        core * first_step + (1 - core) * second_step,
    )
    mate = me + step_core
    width = parts_ref.shape[2]

    def w_load(i):
        at = pl.ds(i * width, width)
        return pltpu.make_async_copy(w_far.at[at, :], w_ref.at[i], w_sem.at[i])

    for i in range(GROUP):
        w_load(i).start()
    greet([me + step for _, step in others])
    sent = []

    def send(source, target, item, number, device):
        copy = remote(source, target, send_sem.at[item, number], recv_sem.at[item, number], device)
        copy.start()
        sent.append(copy)

    def arrived(target, item, number):
        remote(target, target, send_sem.at[item, number], recv_sem.at[item, number], me).wait_recv()

    rows = d_residual_ref.shape[0]
    slab_rows = 32

    def slab(i, _):
        at = pl.ds(pl.multiple_of(i * slab_rows, slab_rows), slab_rows)
        residual = residual_ref[at, :]
        inverse = inverse_rms(residual)
        grad = rms_back(d_second_ref[at, :] * gain_ref[...], residual * inverse, inverse)
        total = cot_ref[at, :].astype(f32) + grad
        d_residual_ref[at, :] = total
        d_mix_ref[at, :] = total.astype(bf16)
        return 0

    lax.fori_loop(0, rows // slab_rows, slab, 0)
    for i in range(GROUP):
        w_load(i).wait()

    def part(place):
        parts_ref[place] = dot_nt(d_mix_ref[...], w_ref[place]).astype(bf16)

    for number, step in reversed(others):
        part(slot + step)
        send(parts_ref.at[slot + step], heads_ref.at[slot], 0, number - 1, me + step)
    part(slot)
    own_part = pltpu.make_async_copy(parts_ref.at[slot], heads_ref.at[slot], own_sem)
    own_part.start()
    for kind in (3, 2, 1, 0):
        away_ref[kind] = dot_tn(mixer_ref[kind], d_mix_ref[...]).astype(bf16)
        send(away_ref.at[kind], near_ref.at[kind], 1, kind, mate)
    for number, step in others:
        arrived(heads_ref.at[slot + step], 0, number - 1)
    for kind in range(4):
        arrived(near_ref.at[kind], 1, kind)
    for copy in sent:
        copy.wait_send()
    own_part.wait()


def residual_back(d_second, residual, cot, gain, w, mixer_away, number):
    rows, columns = residual.shape
    width = columns // GROUP
    blocks = mixer_away.shape[0]
    return pl.pallas_call(
        residual_back_kernel,
        out_shape=(
            jax.ShapeDtypeStruct((rows, columns), f32),
            jax.ShapeDtypeStruct((rows, columns), bf16),
            jax.ShapeDtypeStruct((GROUP, rows, width), bf16),
            jax.ShapeDtypeStruct((blocks, mixer_away.shape[2], columns), bf16),
        ),
        in_specs=[VMEM, VMEM, VMEM, VMEM, ANY, VMEM],
        out_specs=(VMEM, VMEM, ANY, ANY),
        scratch_shapes=[
            pltpu.VMEM((GROUP, width, columns), bf16),
            pltpu.VMEM((GROUP, rows, width), bf16),
            pltpu.VMEM((blocks, mixer_away.shape[2], columns), bf16),
            pltpu.SemaphoreType.DMA((2, GROUP - 1)),
            pltpu.SemaphoreType.DMA((2, GROUP - 1)),
            pltpu.SemaphoreType.DMA,
            pltpu.SemaphoreType.DMA((GROUP,)),
        ],
        compiler_params=pltpu.CompilerParams(
            collective_id=number, has_side_effects=True, vmem_limit_bytes=48 * 2**20
        ),
        cost_estimate=cost(20),
    )(d_second, residual, cot, gain, w, mixer_away)


def gate_gather_kernel(
    own_ref,
    x_far,
    w_far,
    all_ref,
    gate_far,
    up_far,
    hidden_far,
    x_ref,
    w_ref,
    gate_ref,
    up_ref,
    hidden_ref,
    send_sem,
    recv_sem,
    own_sem,
    x_sem,
    w_sem,
    store_sem,
):
    me, slot, step_core, first_step, second_step = places()
    first, second, mate = me + first_step, me + second_step, me + step_core
    w_load = pltpu.make_async_copy(w_far, w_ref, w_sem)
    w_load.start()
    tiles, tile_rows = x_ref.shape[:2]
    half = gate_ref.shape[2]

    def rows_of(i):
        return pl.ds(pl.multiple_of(i * tile_rows, tile_rows), tile_rows)

    def x_load(i):
        return pltpu.make_async_copy(x_far.at[rows_of(i), :], x_ref.at[i], x_sem.at[i])

    for i in range(tiles):
        x_load(i).start()
    greet((first, second, mate))
    sent = []

    def send(source, number, device):
        copy = remote(
            source, all_ref.at[AROUND[number]], send_sem.at[number], recv_sem.at[number], device
        )
        copy.start()
        sent.append(copy)

    def arrived(number):
        target = all_ref.at[AROUND[number]]
        remote(target, target, send_sem.at[number], recv_sem.at[number], me).wait_recv()
        return target

    own = pltpu.make_async_copy(own_ref, all_ref.at[0], own_sem)
    send(own_ref, 0, first)
    send(own_ref, 1, second)
    send(own_ref, 2, mate)
    own.start()

    def stores(i, spot):
        return [
            pltpu.make_async_copy(near.at[spot], far.at[rows_of(i), :], store_sem.at[spot, number])
            for number, (near, far) in enumerate(
                ((gate_ref, gate_far), (up_ref, up_far), (hidden_ref, hidden_far))
            )
        ]

    def tile(i, _):
        spot = lax.rem(i, 2)
        x_load(i).wait()

        @pl.when(i >= 2)
        def _():
            for copy in stores(i - 2, spot):
                copy.wait()

        both = dot_nn(x_ref[i], w_ref[...])
        gate = both[:, :half]
        up = both[:, half:]
        gate_ref[spot] = gate
        up_ref[spot] = up
        hidden_ref[spot] = (gate * jax.nn.sigmoid(gate) * up).astype(bf16)
        for copy in stores(i, spot):
            copy.start()
        return 0

    w_load.wait()
    lax.fori_loop(0, tiles // 2, tile, 0)
    block = arrived(0)
    send(block, 3, second)
    send(block, 4, mate)
    send(arrived(1), 5, mate)
    lax.fori_loop(tiles // 2, tiles, tile, 0)
    for i in (tiles - 2, tiles - 1):
        for copy in stores(i, i % 2):
            copy.wait()
    send(arrived(3), 6, mate)
    for number in (2, 4, 5, 6):
        arrived(number)
    for copy in sent:
        copy.wait_send()
    own.wait()


def gate_gather(own, x, w, number):
    rows, columns = own.shape
    half = w.shape[1] // 2
    tiles = x.shape[0] // rows
    wide = jax.ShapeDtypeStruct((x.shape[0], half), f32)
    return pl.pallas_call(
        gate_gather_kernel,
        out_shape=(
            jax.ShapeDtypeStruct((GROUP, rows, columns), own.dtype),
            wide,
            wide,
            jax.ShapeDtypeStruct((x.shape[0], half), bf16),
        ),
        in_specs=[ANY, ANY, ANY],
        out_specs=(ANY, ANY, ANY, ANY),
        scratch_shapes=[
            pltpu.VMEM((tiles, rows, x.shape[1]), bf16),
            pltpu.VMEM(w.shape, bf16),
            pltpu.VMEM((2, rows, half), f32),
            pltpu.VMEM((2, rows, half), f32),
            pltpu.VMEM((2, rows, half), bf16),
            pltpu.SemaphoreType.DMA((7,)),
            pltpu.SemaphoreType.DMA((7,)),
            pltpu.SemaphoreType.DMA,
            pltpu.SemaphoreType.DMA((tiles,)),
            pltpu.SemaphoreType.DMA,
            pltpu.SemaphoreType.DMA((2, 3)),
        ],
        compiler_params=pltpu.CompilerParams(
            collective_id=number, has_side_effects=True, vmem_limit_bytes=56 * 2**20
        ),
        cost_estimate=cost(45),
    )(own, x, w)


def hidden_back_kernel(cot_ref, gate_ref, up_ref, w_ref, grad_ref):
    half = gate_ref.shape[1]
    d_hidden = dot_nn(cot_ref[...], w_ref[...])
    gate = gate_ref[...]
    sigmoid = jax.nn.sigmoid(gate)
    grad_ref[:, :half] = (
        d_hidden * up_ref[...] * sigmoid * (1.0 + gate * (1.0 - sigmoid))
    ).astype(bf16)
    grad_ref[:, half:] = (d_hidden * gate * sigmoid).astype(bf16)


def hidden_back(cot, gate, up, w):
    rows, columns = cot.shape
    half = w.shape[1]
    tile_rows = 256

    def tiles(width):
        return pl.BlockSpec((tile_rows, width), lambda i: (i, 0))

    return pl.pallas_call(
        hidden_back_kernel,
        grid=(rows // tile_rows,),
        in_specs=[
            tiles(columns),
            tiles(half),
            tiles(half),
            pl.BlockSpec(w.shape, lambda i: (0, 0)),
        ],
        out_specs=tiles(2 * half),
        out_shape=jax.ShapeDtypeStruct((rows, 2 * half), bf16),
        compiler_params=pltpu.CompilerParams(vmem_limit_bytes=56 * 2**20),
        cost_estimate=cost(20),
    )(cot, gate, up, w)


def away_product_kernel(x_ref, w_ref, out_ref):
    out_ref[...] = dot_nt(x_ref[...], w_ref[...]).astype(bf16)


def away_product(x, w, tile_rows):
    rows, depth = x.shape
    tiles = rows // tile_rows // 2
    return pl.pallas_call(
        away_product_kernel,
        grid=(tiles,),
        in_specs=[
            pl.BlockSpec((tile_rows, depth), lambda i: (tiles + i, 0)),
            pl.BlockSpec(w.shape, lambda i: (0, 0)),
        ],
        out_specs=pl.BlockSpec((tile_rows, w.shape[0]), lambda i: (i, 0)),
        out_shape=jax.ShapeDtypeStruct((rows // 2, w.shape[0]), bf16),
        compiler_params=pltpu.CompilerParams(vmem_limit_bytes=56 * 2**20),
        cost_estimate=cost(6),
    )(x, w)


def keep_product_kernel(x_ref, w_ref, near_ref, out_ref):
    total = dot_nt(x_ref[...], w_ref[...]) + near_ref[0].astype(f32)
    out_ref[0] = total.astype(out_ref.dtype)


def keep_product(x, w, near, begin, number, out_type):
    _, rows, columns = near.shape
    return pl.pallas_call(
        keep_product_kernel,
        grid=(number,),
        in_specs=[
            pl.BlockSpec((rows, x.shape[1]), lambda i: (begin + i, 0)),
            pl.BlockSpec(w.shape, lambda i: (0, 0)),
            pl.BlockSpec((1, rows, columns), lambda i: (begin + i, 0, 0)),
        ],
        out_specs=pl.BlockSpec((1, rows, columns), lambda i: (i, 0, 0)),
        out_shape=jax.ShapeDtypeStruct((number, rows, columns), out_type),
        compiler_params=pltpu.CompilerParams(vmem_limit_bytes=56 * 2**20),
        cost_estimate=cost(5),
    )(x, w, near)


def rows_product_kernel(x_ref, y_ref, out_ref):
    out_ref[...] = dot_tn(x_ref[...], y_ref[...]).astype(bf16)


def rows_product(x, y, micros):
    rows, columns = x.shape
    wide = y.shape[1]
    tile_columns = 512
    return pl.pallas_call(
        rows_product_kernel,
        grid=(columns // tile_columns,),
        in_specs=[
            pl.BlockSpec((rows, tile_columns), lambda i: (0, i)),
            pl.BlockSpec((rows, wide), lambda i: (0, 0)),
        ],
        out_specs=pl.BlockSpec((tile_columns, wide), lambda i: (i, 0)),
        out_shape=jax.ShapeDtypeStruct((columns, wide), bf16),
        compiler_params=pltpu.CompilerParams(vmem_limit_bytes=56 * 2**20),
        cost_estimate=cost(micros),
    )(x, y)


def plane_permutes(device_count):
    first, second, mate = [], [], []
    for i in range(device_count):
        low_bit, high_bit = (2, 4) if i % 2 == 0 else (4, 2)
        first.append((i, i ^ low_bit))
        second.append((i, i ^ high_bit))
        mate.append((i, i ^ 1))
    return first, second, mate


def after(values, *earlier):
    return lax.optimization_barrier((values, earlier))[0]


def meet(*values):
    return lax.optimization_barrier(values)


def assemble_kernel(*refs):
    blocks, out_ref = refs[:GROUP], refs[GROUP]
    _, slot, step_core, first_step, second_step = places()
    corner_step = first_step + second_step
    here = (0, first_step, second_step, corner_step)
    there = (step_core, step_core + second_step, step_core + first_step, step_core + corner_step)
    for number, step in enumerate(here + there):
        out_ref[:, slot + step] = blocks[number][...]


def assemble(x, from_first, from_second, from_corner, mates):
    parts, rows, columns = x.shape
    return pl.pallas_call(
        assemble_kernel,
        out_shape=jax.ShapeDtypeStruct((parts, GROUP, rows, columns), x.dtype),
        in_specs=[VMEM] * GROUP,
        out_specs=VMEM,
        compiler_params=pltpu.CompilerParams(vmem_limit_bytes=32 * 2**20),
        cost_estimate=cost(8),
    )(x, from_first, from_second, from_corner, *mates)


class SlowScatter:
    def __init__(self, keep, away, device_count):
        self.keep = keep
        self.away = away
        self.first, self.second, self.mate = plane_permutes(device_count)

    def to_mate(self):
        return lax.ppermute(self.away, "fsdp", self.mate)

    def onward(self, near):
        return (self.keep(2, 2) + near[2:].astype(f32)).astype(bf16)

    def to_second(self, sums):
        return lax.ppermute(sums, "fsdp", self.second)

    def half(self, near):
        return self.keep(1, 1)[0] + near[1].astype(f32)

    def both(self, half, far):
        return (half + far[1].astype(f32)).astype(bf16)

    def to_first(self, both):
        return lax.ppermute(both, "fsdp", self.first)

    def total(self, near, far, last):
        own = self.keep(0, 1)[0] + near[0].astype(f32)
        return own + far[0].astype(f32) + last.astype(f32)


def low(values):
    return values.astype(bf16).astype(f32)


def gates(proj_ref, floor_ref, rows, head, heads):
    dim = floor_ref.shape[1] // heads
    wide = heads * dim
    lo = head * dim
    q_pre = proj_ref[rows, lo : lo + dim]
    f_pre = proj_ref[rows, wide + lo : wide + lo + dim]
    value = proj_ref[rows, 2 * wide + lo : 2 * wide + lo + dim].astype(bf16)
    floor = floor_ref[:, lo : lo + dim]
    q_sigmoid = jax.nn.sigmoid(q_pre)
    query = low(q_pre * q_sigmoid)
    f_sigmoid = jax.nn.sigmoid(f_pre)
    forget = floor + (1.0 - floor) * f_sigmoid
    key = low(1.0 - forget)
    row = lax.broadcasted_iota(jnp.int32, (CHUNK, dim), 0)
    in_half = lax.rem(row, HALF)
    product = forget
    step = 1
    while step < HALF:
        product = jnp.where(in_half >= step, product * pltpu.roll(product, step, 0), product)
        step *= 2
    middle = product[HALF - 1 : HALF, :]
    end = product[CHUNK - 1 : CHUNK, :]
    ratio = jnp.where(row < HALF, product / middle, product)
    inverse = 1.0 / ratio
    return {
        "q_pre": q_pre,
        "q_sigmoid": q_sigmoid,
        "f_sigmoid": f_sigmoid,
        "forget": forget,
        "value": value,
        "floor": floor,
        "middle": middle,
        "end": end,
        "ratio": ratio,
        "inverse": inverse,
        "row": row,
        "query_mid": query * ratio,
        "key_mid": key * inverse,
    }


def whole_fade(g, last):
    return g["middle"] * g["end"] * jnp.where(last < 0, 1.0, 0.0)


def tail_keys(g, last):
    return jnp.where(g["row"] >= last, g["key_mid"] * g["end"], 0.0).astype(bf16)


def entry_queries(g, carried):
    return jnp.where(carried, g["query_mid"] * g["middle"], 0.0).astype(bf16)


def next_state(g, last, state):
    return state * whole_fade(g, last) + dot_tn(g["value"], tail_keys(g, last))


def forward_kernel(
    heads, last_ref, proj_ref, start_ref, floor_ref, gain_ref, in_ref, mix_ref, out_ref, enter_ref, state
):
    dim = floor_ref.shape[1] // heads
    chunks = proj_ref.shape[0] // CHUNK
    tile = pl.program_id(0)

    @pl.when(tile == 0)
    def _():
        state[...] = in_ref[...]

    def step(n, _):
        base = pl.multiple_of(n * CHUNK, CHUNK)
        rows = pl.ds(base, CHUNK)
        place = (tile * chunks + n) * CHUNK
        starts = start_ref[rows, :] - place
        last = last_ref[tile * chunks + n] - place
        column = lax.broadcasted_iota(jnp.int32, (CHUNK, CHUNK), 1)
        line = lax.broadcasted_iota(jnp.int32, (CHUNK, CHUNK), 0)
        within = (column <= line) & (column >= starts)
        carried = starts < 0
        for head in range(heads):
            lo = head * dim
            g = gates(proj_ref, floor_ref, rows, head, heads)
            now = state[head]
            enter_ref[n, head] = now
            scores = dot_nt(g["query_mid"].astype(bf16), g["key_mid"].astype(bf16))
            scores = jnp.where(within, scores, 0.0).astype(bf16)
            out = dot_nn(scores, g["value"]) + dot_nt(entry_queries(g, carried), now.astype(bf16))
            state[head] = next_state(g, last, now)
            out_ref[rows, lo : lo + dim] = out
            mix_ref[rows, lo : lo + dim] = (
                out * inverse_rms(out) * gain_ref[:, lo : lo + dim]
            ).astype(bf16)
        return 0

    lax.fori_loop(0, chunks, step, 0, unroll=UNROLL)


def last_state_kernel(heads, last_ref, proj_ref, floor_ref, out_ref):
    for head in range(heads):
        state = jnp.zeros(out_ref.shape[1:], f32)
        for n in range(proj_ref.shape[0] // CHUNK):
            g = gates(proj_ref, floor_ref, pl.ds(n * CHUNK, CHUNK), head, heads)
            state = next_state(g, last_ref[n] - n * CHUNK, state)
        out_ref[head] = state


def state_grad(out_ref, dmix_ref, gain_ref, rows, lo, dim):
    out = out_ref[rows, lo : lo + dim]
    inverse = inverse_rms(out)
    scaled = out * inverse
    dmix = dmix_ref[rows, lo : lo + dim].astype(f32)
    return rms_back(dmix * gain_ref[:, lo : lo + dim], scaled, inverse)


def backward_chunk(heads, n, at, refs, outs, later, before=0):
    last_ref, proj_ref, start_ref, floor_ref, gain_ref, out_ref, dmix_ref, enter_ref = refs
    dproj_ref, dfloor_ref = outs
    dim = floor_ref.shape[1] // heads
    wide = heads * dim
    base = n * CHUNK
    rows = pl.ds(base, CHUNK)
    place = (before + n) * CHUNK
    starts = start_ref[rows, :] - place
    last = last_ref[before + n] - place
    column = lax.broadcasted_iota(jnp.int32, (CHUNK, CHUNK), 1)
    line = lax.broadcasted_iota(jnp.int32, (CHUNK, CHUNK), 0)
    within = (column <= line) & (column >= starts)
    carried = starts < 0
    for head in range(heads):
        lo = head * dim
        g = gates(proj_ref, floor_ref, rows, head, heads)
        grad = state_grad(out_ref, dmix_ref, gain_ref, rows, lo, dim)
        grad_hi = grad.astype(bf16)
        grad_lo = (grad - grad_hi.astype(f32)).astype(bf16)
        state = enter_ref[n, head]
        after = later[head]
        after_low = after.astype(bf16)
        query_mid = g["query_mid"].astype(bf16)
        key_mid = g["key_mid"].astype(bf16)
        scores = jnp.where(within, dot_nt(query_mid, key_mid), 0.0).astype(bf16)
        d_scores = dot_nt(grad_hi, g["value"]) + dot_nt(grad_lo, g["value"])
        d_scores = jnp.where(within, d_scores, 0.0).astype(bf16)
        query_in = entry_queries(g, carried)
        key_out = tail_keys(g, last)
        d_query_mid = dot_nn(d_scores, key_mid)
        d_query_in = jnp.where(carried, dot_nn(grad_hi, state.astype(bf16)), 0.0)
        d_key_mid = dot_tn(d_scores, query_mid)
        d_key_out = jnp.where(g["row"] >= last, dot_nn(g["value"], after_low), 0.0)
        d_value = dot_tn(scores, grad_hi) + dot_nt(key_out, after_low)
        d_query = (d_query_mid + d_query_in * g["middle"]) * g["ratio"]
        d_key = (d_key_mid + d_key_out * g["end"]) * g["inverse"]
        tail = d_key_out * key_out.astype(f32)
        term = (
            d_query_mid * query_mid.astype(f32)
            + d_query_in * query_in.astype(f32)
            - d_key_mid * key_mid.astype(f32)
            - tail
        )
        fade = whole_fade(g, last)
        final = jnp.sum(tail, axis=0, keepdims=True) + fade * jnp.sum(
            state * after, axis=0, keepdims=True
        )
        step_rows = 1
        while step_rows < CHUNK:
            term = jnp.where(
                g["row"] < CHUNK - step_rows,
                term + pltpu.roll(term, CHUNK - step_rows, 0),
                term,
            )
            step_rows *= 2
        d_forget = (term + final) / g["forget"] - d_key
        q_sigmoid, f_sigmoid = g["q_sigmoid"], g["f_sigmoid"]
        d_q_pre = d_query * q_sigmoid * (1.0 + g["q_pre"] * (1.0 - q_sigmoid))
        d_floor = d_forget * (1.0 - f_sigmoid)
        d_f_pre = d_floor * (1.0 - g["floor"]) * f_sigmoid
        dproj_ref[at, lo : lo + dim] = d_q_pre.astype(bf16)
        dproj_ref[at, wide + lo : wide + lo + dim] = d_f_pre.astype(bf16)
        dproj_ref[at, 2 * wide + lo : 2 * wide + lo + dim] = d_value.astype(bf16)
        dfloor_ref[:, lo : lo + dim] += jnp.sum(d_floor, axis=0, keepdims=True)
        later[head] = after * fade + dot_tn(grad_hi, query_in)


def backward_rest(heads, n, refs, later, before=0):
    last_ref, proj_ref, start_ref, floor_ref, gain_ref, out_ref, dmix_ref = refs
    dim = floor_ref.shape[1] // heads
    rows = pl.ds(n * CHUNK, CHUNK)
    for head in range(heads):
        g = gates(proj_ref, floor_ref, rows, head, heads)
        grad = state_grad(out_ref, dmix_ref, gain_ref, rows, head * dim, dim)
        place = (before + n) * CHUNK
        queries = entry_queries(g, start_ref[rows, :] < place)
        fade = whole_fade(g, last_ref[before + n] - place)
        later[head] = later[head] * fade + dot_tn(grad.astype(bf16), queries)


def backward_kernel(heads, *refs):
    ins, outs, later = refs[:8], refs[8:10], refs[10]
    chunks = ins[1].shape[0] // CHUNK
    edge = MAXLEN // CHUNK
    tile = pl.num_programs(0) - 1 - pl.program_id(0)
    before = tile * chunks

    def step(i, first):
        n = first - i
        at = pl.ds(pl.multiple_of(n * CHUNK, CHUNK), CHUNK)
        backward_chunk(heads, n, at, ins, outs, later, before)
        return first

    @pl.when(pl.program_id(0) == 0)
    def _():
        later[...] = jnp.zeros_like(later)
        outs[1][...] = jnp.zeros_like(outs[1])
        for n in range(chunks - 1, chunks - 1 - edge, -1):
            backward_rest(heads, n, ins[:7], later, before)
        lax.fori_loop(0, chunks - edge, step, chunks - 1 - edge, unroll=UNROLL)

    @pl.when(pl.program_id(0) != 0)
    def _():
        lax.fori_loop(0, chunks, step, chunks - 1, unroll=2 * UNROLL)


def backward_edge_kernel(heads, *refs):
    ins, in_ref, _, outs, later = refs[:8], refs[8], refs[9], refs[10:12], refs[12]
    later[...] = in_ref[...]
    outs[1][...] = jnp.zeros_like(outs[1])
    edge = MAXLEN // CHUNK
    before = ins[0].shape[0] - edge
    for n in range(edge - 1, -1, -1):
        backward_chunk(heads, n, pl.ds(n * CHUNK, CHUNK), ins, outs, later, before)


def first_grad_kernel(heads, *refs):
    ins, grad_ref = refs[:7], refs[7]
    grad_ref[...] = jnp.zeros_like(grad_ref)
    for n in range(ins[1].shape[0] // CHUNK - 1, -1, -1):
        backward_rest(heads, n, ins, grad_ref)


def local_call(kernel, heads, micros, out_shape, scratch, *operands):
    return pl.pallas_call(
        functools.partial(kernel, heads),
        out_shape=out_shape,
        in_specs=[SMEM] + [VMEM] * (len(operands) - 1),
        out_specs=jax.tree.map(lambda _: VMEM, out_shape),
        scratch_shapes=scratch,
        compiler_params=pltpu.CompilerParams(vmem_limit_bytes=56 * 2**20),
        cost_estimate=cost(micros),
    )(*operands)


def body(
    tokens,
    cotangent,
    dealt_lengths,
    deal,
    norm_gain,
    mixer_in,
    forget_floor,
    group_gain,
    out_proj,
    ffn_gain,
    gate_up,
    down_proj,
):
    row_count, width = tokens.shape
    weight_rows = mixer_in.shape[0]
    device_count = lax.axis_size("fsdp")
    groups = device_count // GROUP
    own_index = lax.axis_index("fsdp")
    slot = lax.rem(own_index, GROUP)
    group = own_index // GROUP
    group_rows = GROUP * row_count
    heads = HEADS // GROUP
    own_width = width // GROUP
    dim = width // HEADS
    ffn_width = down_proj.shape[1]
    own_ffn = ffn_width // GROUP
    planes = [[g * GROUP + s for s in range(GROUP)] for g in range(groups)]
    lines = [[g * GROUP + s for g in range(groups)] for s in range(GROUP)]

    def line_gather(x):
        return lax.all_gather(x, "fsdp", axis=0, axis_index_groups=lines, tiled=True)

    def line_scatter(x):
        return lax.psum_scatter(
            x, "fsdp", scatter_dimension=0, axis_index_groups=lines, tiled=True
        )

    def whole_rows(x):
        return line_gather(x.reshape(GROUP * weight_rows, -1))

    low_step = 2 - 4 * (slot // 2 % 2)
    high_step = 4 - 8 * (slot // 4)
    odd = slot % 2
    moves = (
        slot,
        1 - 2 * odd,
        jnp.where(odd == 0, low_step, high_step),
        jnp.where(odd == 0, high_step, low_step),
    )

    seq_count = deal.shape[0]
    seq_ids = jnp.arange(seq_count, dtype=jnp.int32)
    matches = deal[:, None] == seq_ids[None, :]
    lengths = jnp.sum(jnp.where(matches, dealt_lengths[:, None], 0), axis=0)
    seq_starts = jnp.sum(
        jnp.where(seq_ids[:, None] < seq_ids[None, :], lengths[:, None], 0), axis=0
    )
    group_start = group * group_rows
    rows_here = group_start + jnp.arange(group_rows, dtype=jnp.int32)
    starts = (
        jnp.max(jnp.where(seq_starts[None, :] <= rows_here[:, None], seq_starts[None, :], 0), axis=1)
        - group_start
    )
    start_column = starts[:, None]
    last_starts = starts[CHUNK - 1 :: CHUNK]

    out_lines = lax.all_gather(out_proj, "fsdp", axis=0, axis_index_groups=lines)
    gain_block = jnp.zeros((16, 128), bf16)
    for number, gain in enumerate((norm_gain, forget_floor, group_gain, ffn_gain)):
        gain_block = gain_block.at[number, :weight_rows].set(gain)
    gain_blocks, mixer_swapped = exchange(
        0, 15, ("all", gain_block), ("swap", by_owner(mixer_in, 3))
    )
    mixer_weight = whole_rows(mixer_swapped)
    gains = (
        gain_blocks[:, :, :4, :weight_rows].transpose(2, 0, 1, 3).reshape(4, width).astype(f32)
    )
    first_gain = gains[0:1]
    second_gain = gains[3:4]
    own_gains = lax.dynamic_slice_in_dim(gains, slot * own_width, own_width, 1)
    own_floor = own_gains[1:2]
    own_group_gain = own_gains[2:3]

    inputs = tokens.astype(f32)
    first_inverse = inverse_rms(inputs)
    first_scaled = inputs * first_inverse
    first_normed = (first_scaled * first_gain).astype(bf16)
    late_gate_up, late_down = after((gate_up, down_proj), mixer_swapped)
    first_all, ffn_swapped, down_swapped = exchange(
        1,
        58,
        ("gather", first_normed[None]),
        ("swap", by_owner(late_gate_up, 2)),
        ("swap", by_owner(late_down, 1)),
    )
    first_all = first_all.reshape(group_rows, width)
    ffn_weight = whole_rows(ffn_swapped)
    first, second, mate = plane_permutes(device_count)
    out_own = after(out_lines, first_all)
    from_first = lax.ppermute(out_own, "fsdp", first)
    from_second = lax.ppermute(out_own, "fsdp", second)
    tail_projected = dot_nn(first_all[group_rows - MAXLEN :], mixer_weight)
    edge = MAXLEN // CHUNK
    state_type = jax.ShapeDtypeStruct((heads, dim, dim), f32)
    last_state = local_call(
        last_state_kernel,
        heads,
        3,
        state_type,
        [],
        last_starts[-edge:] - (group_rows - MAXLEN),
        tail_projected,
        own_floor,
    )
    up_line = [(i, i + GROUP) for i in range(device_count - GROUP)]
    down_line = [(i + GROUP, i) for i in range(device_count - GROUP)]
    entering_state = lax.ppermute(last_state, "fsdp", up_line)
    projected = dot_nn(after(first_all, last_state), mixer_weight)
    projected, entering_state, from_first, from_second = meet(
        projected, entering_state, from_first, from_second
    )
    from_corner = lax.ppermute(from_first, "fsdp", second)
    mates = [lax.ppermute(block, "fsdp", mate) for block in (out_own, from_first, from_second)]
    chunks = group_rows // CHUNK
    tile_count = group_rows // TILE_ROWS

    def row_tiles(columns, turned=False):
        return pl.BlockSpec(
            (TILE_ROWS, columns), lambda i: (tile_count - 1 - i if turned else i, 0)
        )

    def state_tiles(turned=False):
        return pl.BlockSpec(
            (TILE_ROWS // CHUNK, heads, dim, dim),
            lambda i: (tile_count - 1 - i if turned else i, 0, 0, 0),
        )

    state_scratch = pltpu.VMEM((heads, dim, dim), f32)
    mixed_heads, state_out, entering = pl.pallas_call(
        functools.partial(forward_kernel, heads),
        grid=(tile_count,),
        out_shape=(
            jax.ShapeDtypeStruct((group_rows, own_width), bf16),
            jax.ShapeDtypeStruct((group_rows, own_width), f32),
            jax.ShapeDtypeStruct((chunks, heads, dim, dim), f32),
        ),
        in_specs=[SMEM, row_tiles(3 * own_width), row_tiles(1), VMEM, VMEM, VMEM],
        out_specs=(row_tiles(own_width), row_tiles(own_width), state_tiles()),
        scratch_shapes=[state_scratch],
        compiler_params=pltpu.CompilerParams(vmem_limit_bytes=56 * 2**20),
        cost_estimate=cost(18),
    )(last_starts, projected, start_column, own_floor, own_group_gain, entering_state)
    mixed_heads, from_corner = meet(mixed_heads, from_corner)
    mates = mates + [lax.ppermute(from_corner, "fsdp", mate)]
    [mixer_input] = exchange(
        3, 15, ("widen", mixed_heads.reshape(GROUP, row_count, own_width))
    )
    mixer_input, mates = meet(mixer_input, mates)
    _, step_core, first_step, second_step = moves
    steps = (0, first_step, second_step, first_step + second_step)
    mate_steps = [step_core + steps[kind] for kind in (0, 2, 1, 3)]
    mixer_blocks = dealt_columns(mixer_input, weight_rows)
    mixer_around = [
        lax.dynamic_index_in_dim(mixer_blocks, slot + step, 0) for step in (*steps, *mate_steps)
    ]
    mixer_keep = jnp.concatenate(mixer_around[:4])
    mixer_away = jnp.concatenate(mixer_around[4:])
    out_weight = assemble(out_own, from_first, from_second, from_corner, mates).reshape(width, width)
    down_weight = whole_rows(after(down_swapped, mixed_heads))
    residual = inputs + dot_nn(mixer_input, out_weight)
    second_inverse = inverse_rms(residual)
    second_scaled = residual * second_inverse
    second_normed = (second_scaled * second_gain).astype(bf16)
    second_normed, mixer_keep, mixer_away = meet(second_normed, mixer_keep, mixer_away)
    [second_all] = exchange(2, 43, ("around", second_normed[None]))
    second_all = second_all.reshape(group_rows, width)
    cot_blocks, gate_part, up_part, hidden_act = gate_gather(
        cotangent, second_all, ffn_weight, 6
    )
    cot_all = cot_blocks.reshape(group_rows, width)
    down_grad = rows_product(cot_all, hidden_act, 11)
    down_summed = line_scatter(down_grad)
    hidden_act = after(hidden_act, down_grad)

    ffn_away = away_product(hidden_act, down_weight, row_count).reshape(4, row_count, width)
    ffn_near = lax.ppermute(ffn_away, "fsdp", mate)
    d_gate_pre = hidden_back(after(cot_all, ffn_away), gate_part, up_part, down_weight)
    d_gate_pre, ffn_near = meet(d_gate_pre, ffn_near)
    ffn_sums = keep_product(hidden_act, down_weight, ffn_near, 2, 2, bf16)
    ffn_grad = rows_product(after(second_all, ffn_sums), d_gate_pre, 18)
    ffn_rest = keep_product(hidden_act, down_weight, after(ffn_near, ffn_grad), 0, 2, f32)
    ffn_grad, ffn_rest, ffn_far = meet(ffn_grad, ffn_rest, lax.ppermute(ffn_sums, "fsdp", second))
    ffn_both = (ffn_rest[1] + ffn_far[1].astype(f32)).astype(bf16)
    ffn_summed = line_scatter(ffn_grad)
    d_second, down_swapped = product_scatter(
        d_gate_pre.reshape(GROUP, row_count, -1),
        after(ffn_weight, ffn_grad, ffn_both),
        4,
        True,
        down_summed.reshape(GROUP, weight_rows, -1),
    )
    d_second, ffn_last = meet(d_second, lax.ppermute(ffn_both, "fsdp", first))
    d_residual, d_mix_out, d_mixed_heads, out_near = residual_back(
        d_second,
        residual,
        cotangent,
        second_gain,
        out_weight,
        mixer_away,
        5,
    )
    d_mixed_heads = d_mixed_heads.reshape(group_rows, own_width)

    def out_blocks(blocks):
        return lax.dot_general(
            blocks, d_mix_out, (((1,), (0,)), ((), ())), preferred_element_type=f32
        )

    out_sum = SlowScatter(
        lambda begin, number: out_blocks(mixer_keep[begin : begin + number]), None, device_count
    )
    out_sums = out_sum.onward(out_near)
    d_mixed_heads = after(d_mixed_heads, out_sums)
    out_far = out_sum.to_second(out_sums)
    operands = (projected, start_column, own_floor, own_group_gain, state_out, d_mixed_heads)

    def edge_specs(place):
        def rows(columns):
            return pl.BlockSpec((MAXLEN, columns), lambda i: (place, 0))

        return [rows(3 * own_width), rows(1), VMEM, VMEM, rows(own_width), rows(own_width)]

    first_grad = pl.pallas_call(
        functools.partial(first_grad_kernel, heads),
        grid=(1,),
        out_shape=state_type,
        in_specs=[SMEM] + edge_specs(0),
        out_specs=VMEM,
        compiler_params=pltpu.CompilerParams(vmem_limit_bytes=56 * 2**20),
        cost_estimate=cost(3),
    )(last_starts, *operands)
    entering_grad = lax.ppermute(first_grad, "fsdp", down_line)
    dproj_type = jax.ShapeDtypeStruct((group_rows, 3 * own_width), bf16)
    dfloor_type = jax.ShapeDtypeStruct((1, own_width), f32)
    d_projected, floor_most = pl.pallas_call(
        functools.partial(backward_kernel, heads),
        grid=(tile_count,),
        out_shape=(dproj_type, dfloor_type),
        in_specs=[
            SMEM,
            row_tiles(3 * own_width, True),
            row_tiles(1, True),
            VMEM,
            VMEM,
            row_tiles(own_width, True),
            row_tiles(own_width, True),
            state_tiles(True),
        ],
        out_specs=(row_tiles(3 * own_width, True), VMEM),
        scratch_shapes=[state_scratch],
        compiler_params=pltpu.CompilerParams(vmem_limit_bytes=56 * 2**20),
        cost_estimate=cost(30),
    )(last_starts, *operands, entering)
    d_projected, entering_grad = meet(d_projected, entering_grad)
    last_tile = group_rows // MAXLEN - 1
    d_projected, floor_rest = pl.pallas_call(
        functools.partial(backward_edge_kernel, heads),
        grid=(1,),
        out_shape=(dproj_type, dfloor_type),
        in_specs=[SMEM]
        + edge_specs(last_tile)
        + [pl.BlockSpec((edge, heads, dim, dim), lambda i: (last_tile, 0, 0, 0)), VMEM, ANY],
        out_specs=(
            pl.BlockSpec((MAXLEN, 3 * own_width), lambda i: (last_tile, 0)),
            VMEM,
        ),
        scratch_shapes=[state_scratch],
        input_output_aliases={9: 0},
        compiler_params=pltpu.CompilerParams(vmem_limit_bytes=56 * 2**20),
        cost_estimate=cost(4),
    )(last_starts, *operands, entering, entering_grad, d_projected)
    d_projected, out_far = meet(d_projected, out_far)
    out_both = out_sum.both(out_sum.half(out_near), out_far)
    d_projected = after(d_projected, out_both)
    floor_grad = floor_most + floor_rest
    by_sender = (GROUP, weight_rows, -1)
    floor_parts = lax.dynamic_update_slice_in_dim(
        jnp.zeros((width,), f32), floor_grad[0], slot * own_width, 0
    ).reshape(device_count, weight_rows)
    floor_parts = lax.all_to_all(floor_parts, "fsdp", 0, 0, tiled=True)
    mixer_grad = rows_product(first_all, d_projected, 11)
    mixer_grad, out_last = meet(mixer_grad, out_sum.to_first(out_both))
    mixer_summed = line_scatter(mixer_grad)
    out_total = out_sum.total(after(out_near, mixer_grad), out_far, out_last).astype(bf16)
    out_summed = line_scatter(out_total.reshape(groups * weight_rows, width))
    d_first, ffn_swapped = product_scatter(
        d_projected.reshape(GROUP, row_count, -1),
        after(mixer_weight, out_total),
        8,
        False,
        ffn_summed.reshape(by_sender),
    )
    d_first, mixer_summed, floor_parts = meet(d_first, mixer_summed, floor_parts)
    d_forget_floor = jnp.sum(floor_parts, axis=0)

    def swap(x):
        x = x.reshape(by_sender)
        return lax.all_to_all(x, "fsdp", 0, 0, axis_index_groups=planes, tiled=True)

    mixer_swapped = swap(mixer_summed)
    ffn_last = after(ffn_last, d_first)
    layer_out = residual + (ffn_rest[0] + ffn_far[0].astype(f32) + ffn_last.astype(f32))
    d_gate_up, ffn_gain_sum = home(ffn_swapped, gate_up, 2)
    d_mixer_in, norm_gain_sum = home(mixer_swapped, mixer_in, 3)
    d_down_proj, _ = home(down_swapped, down_proj, 1)
    d_dealt = d_residual + rms_back(d_first * first_gain, first_scaled, first_inverse)

    d_out_proj = after(out_summed, d_dealt, mixer_swapped).astype(f32)

    group_gain_sum = jnp.sum(out_proj.astype(f32) * d_out_proj, axis=1)
    return (
        layer_out,
        d_dealt,
        norm_gain_sum[:, 0] / norm_gain.astype(f32),
        d_mixer_in,
        d_forget_floor,
        group_gain_sum / group_gain.astype(f32),
        d_out_proj,
        ffn_gain_sum[:, 0] / ffn_gain.astype(f32),
        d_gate_up,
        d_down_proj,
    )


def solution(mesh):
    by_rows = P("fsdp", None)
    by_one = P("fsdp")
    return jax.shard_map(
        body,
        mesh=mesh,
        in_specs=(
            by_rows,
            by_rows,
            P(),
            P(),
            by_one,
            by_rows,
            by_one,
            by_one,
            by_rows,
            by_one,
            by_rows,
            by_rows,
        ),
        out_specs=(
            by_rows,
            by_rows,
            by_one,
            by_rows,
            by_one,
            by_one,
            by_rows,
            by_one,
            by_rows,
            by_rows,
        ),
        check_vma=False,
    )
```
